32 devices in a mesh: dp: 8 (over z, x), tensor: 4 (over y, core).
Axes of the slice: x: 2, y: 2, z: 4, core: 2. Of those that a mesh axis runs over, the one named last changes fastest.
Arguments:
- layer_input: bfloat16 [8192, 2048], P(('dp', 'tensor')), may hold values from -6 to 6
- out_grad: bfloat16 [8192, 2048], P(('dp', 'tensor')), may hold values from -6 to 6
- doc_starts: int32 [6], replicated, may hold values from 0 to 8191, as said below
- mixer_gain: bfloat16 [2048], P('dp'), may hold values from 0.099609375 to 1.8984375
- branch_gate: bfloat16 [2048, 2560], P('dp', 'tensor'), may hold values from -0.125 to 0.125
- branch_input: bfloat16 [2048, 2560], P('dp', 'tensor'), may hold values from -0.125 to 0.125
- conv_taps: bfloat16 [4, 16, 160], P(None, 'tensor', 'dp'), may hold values from -3 to 3
- rate_gate: bfloat16 [16, 160, 160], P('tensor', 'dp'), may hold values from -0.5 to 0.5
- input_gate: bfloat16 [16, 160, 160], P('tensor', 'dp'), may hold values from -0.5 to 0.5
- decay_param: bfloat16 [16, 160], P('tensor', 'dp'), may hold values from 3 to 30
- mixer_out: bfloat16 [2560, 2048], P('tensor', 'dp'), may hold values from -0.125 to 0.125
- feed_gain: bfloat16 [2048], P('dp'), may hold values from 0.099609375 to 1.8984375
- feed_gate: bfloat16 [2048, 6144], P('dp', 'tensor'), may hold values from -0.125 to 0.125
- feed_up: bfloat16 [2048, 6144], P('dp', 'tensor'), may hold values from -0.125 to 0.125
- feed_down: bfloat16 [6144, 2048], P('tensor', 'dp'), may hold values from -0.078125 to 0.078125
Outputs:
- layer_output: bfloat16 [8192, 2048], P(('dp', 'tensor'))
- input_grad: bfloat16 [8192, 2048], P(('dp', 'tensor'))
- mixer_gain_grad: float32 [2048], P('dp')
- branch_gate_grad: float32 [2048, 2560], P('dp', 'tensor')
- branch_input_grad: float32 [2048, 2560], P('dp', 'tensor')
- conv_taps_grad: float32 [4, 16, 160], P(None, 'tensor', 'dp')
- rate_gate_grad: float32 [16, 160, 160], P('tensor', 'dp')
- input_gate_grad: float32 [16, 160, 160], P('tensor', 'dp')
- decay_param_grad: float32 [16, 160], P('tensor', 'dp')
- mixer_out_grad: float32 [2560, 2048], P('tensor', 'dp')
- feed_gain_grad: float32 [2048], P('dp')
- feed_gate_grad: float32 [2048, 6144], P('dp', 'tensor')
- feed_up_grad: float32 [2048, 6144], P('dp', 'tensor')
- feed_down_grad: float32 [6144, 2048], P('tensor', 'dp')
The draws below stay inside these ranges and needn't reach their ends.
Inputs may be any that keep to these rules, and one draw needn't show every extreme that they name: `doc_starts`: the starts rise strictly and the first is 0. One document, which one drawn from the seed, begins within the first 1024 positions and reaches position 7168; every other start lies within the first or the last 1024 positions.
All inputs are finite; a program needn't handle non-finite values.
Results may differ from the reference program's by a relative error of at most 0.02.
Values may be sent and summed in bfloat16 or wider, within the bound.
A program may use at most 256 MiB of HBM per device.

```python
import math
import jax
import jax.numpy as jnp
from jax import lax

D = 2048
H = 16
HD = 160
FF = 6144
TAPS = 4
DOCS = 6
R = 2560
GROUP = 1024
TOKENS = 8192


def draw_doc_starts(key, part):
    key = jax.random.fold_in(key, 11)
    pick_key, early_key, late_key, edge_key = jax.random.split(key, 4)
    longest = jax.random.randint(pick_key, (), 0, DOCS - 1)
    early_side = jnp.sort(jax.random.permutation(early_key, GROUP - 1)[:DOCS - 2] + 1)
    late_side = jnp.sort(jax.random.permutation(late_key, GROUP - TAPS + 1)[:DOCS - 2] + TOKENS - GROUP + TAPS - 1)
    edge_start = TOKENS - GROUP + 1 + jax.random.randint(edge_key, (), 0, TAPS - 2)
    slots = jnp.arange(1, DOCS)
    early_pick = jnp.take(early_side, jnp.clip(slots - 1, 0, DOCS - 3))
    late_pick = jnp.take(late_side, jnp.clip(slots - longest - 2, 0, DOCS - 3))
    rest = jnp.where(slots <= longest, early_pick, jnp.where(slots == longest + 1, edge_start, late_pick))
    return jnp.concatenate([jnp.zeros((1,), jnp.int32), rest.astype(jnp.int32)])


def draw_decay_param(key, part):
    key = jax.random.fold_in(key, 5)
    choose_key, slow_key, fast_key = jax.random.split(key, 3)
    share = 0.4
    picker = jax.random.uniform(choose_key, (H, HD), jnp.float32)
    slow_rate = jnp.exp(jax.random.uniform(slow_key, (H, HD), jnp.float32, math.log(0.05), math.log(0.5))) / TOKENS
    fast_rate = jnp.exp(jax.random.uniform(fast_key, (H, HD), jnp.float32, math.log(0.003), math.log(0.03)))
    chosen = jnp.where(picker < share, fast_rate, slow_rate)
    return (-jnp.log(jnp.expm1(chosen))).astype(jnp.bfloat16)


def levels(key, extent, cuts, smallest, high):
    loudness = 1.0
    for dim, parts in cuts:
        steps = jax.random.uniform(jax.random.fold_in(jax.random.fold_in(key, 6), dim), (parts,), jnp.float32, smallest / len(cuts), high / len(cuts))
        loudness = loudness * jnp.repeat(jnp.exp(steps), extent[dim] // parts).reshape((-1,) + (1,) * (len(extent) - 1 - dim))
    return loudness


def centred(stream_key, dims, deviation, limit, shards=(), kind=jnp.bfloat16):
    values = jax.random.normal(stream_key, dims, jnp.float32) * deviation
    if len(shards) > 0:
        values = levels(stream_key, dims, shards, -0.22, 0.18) * values
    return jnp.clip(values, min=-limit, max=limit).astype(kind)


def setup_inputs(seed: int = 0) -> dict:
    seeds = jax.random.split(jax.random.key(seed), 16)
    layer_input = centred(seeds[0], (TOKENS, D), 1.0, 6.0, ((0, 32),))
    out_grad = centred(seeds[1], (TOKENS, D), 1.0, 6.0, ((0, 32),))
    doc_starts = draw_doc_starts(jax.random.fold_in(seeds[15], 71), 0)
    mixer_gain = jnp.clip(1.0 + 0.18 * jax.random.normal(seeds[3], (D,), jnp.float32), 0.099609375, 1.8984375).astype(jnp.bfloat16)
    branch_gate = centred(seeds[4], (D, R), D ** -0.5, 0.125, ((0, 8), (1, 4)))
    branch_input = centred(seeds[5], (D, R), D ** -0.5, 0.125, ((0, 8), (1, 4)))
    conv_taps = centred(seeds[6], (TAPS, H, HD), TAPS ** -0.5, 3.0, ((1, 4), (2, 8)))
    rate_gate = centred(seeds[7], (H, HD, HD), HD ** -0.5, 0.5, ((0, 4), (1, 8)))
    input_gate = centred(seeds[8], (H, HD, HD), HD ** -0.5, 0.5, ((0, 4), (1, 8)))
    decay_param = draw_decay_param(jax.random.fold_in(seeds[15], 71), 0)
    mixer_out = centred(seeds[10], (R, D), R ** -0.5, 0.125, ((0, 4), (1, 8)))
    feed_gain = jnp.clip(1.0 + 0.18 * jax.random.normal(seeds[11], (D,), jnp.float32), 0.099609375, 1.8984375).astype(jnp.bfloat16)
    feed_gate = centred(seeds[12], (D, FF), D ** -0.5, 0.125, ((0, 8), (1, 4)))
    feed_up = centred(seeds[13], (D, FF), D ** -0.5, 0.125, ((0, 8), (1, 4)))
    feed_down = centred(seeds[14], (FF, D), FF ** -0.5, 0.078125, ((0, 4), (1, 8)))
    return dict(layer_input=layer_input, out_grad=out_grad, doc_starts=doc_starts, mixer_gain=mixer_gain, branch_gate=branch_gate, branch_input=branch_input, conv_taps=conv_taps, rate_gate=rate_gate, input_gate=input_gate, decay_param=decay_param, mixer_out=mixer_out, feed_gain=feed_gain, feed_gate=feed_gate, feed_up=feed_up, feed_down=feed_down)


@jax.custom_vjp
def low(v):
    return lax.optimization_barrier(v.astype(jnp.bfloat16)).astype(jnp.float32)

@jax.custom_vjp
def low_back(v):
    return v

def low_keep(v):
    return (low(v), None)

def low_pass(kept, grad):
    return (grad,)

def back_keep(v):
    return (v, None)

def back_low(kept, grad):
    return (low(grad),)
low.defvjp(low_keep, low_pass)
low_back.defvjp(back_keep, back_low)
EPSILON = 1e-06
GUARD = 0.001
HIGH = lax.Precision.HIGHEST

def product(left, right):
    return jnp.dot(left, right, precision=HIGH)

def pair_join(earlier, later):
    return (earlier[0] * later[0], earlier[1] * later[0] + later[1])

def rms_unit(values):
    return values * lax.rsqrt(lax.optimization_barrier(jnp.mean(values * values, axis=1, keepdims=True)) + EPSILON)

def forward(layer_input, mixer_gain, branch_gate, branch_input, conv_taps, rate_gate, input_gate, decay_param, mixer_out, feed_gain, feed_gate, feed_up, feed_down, doc_starts):
    lanes = H * HD
    normed_one = low(rms_unit(layer_input) * mixer_gain)
    gate_pre = low_back(product(normed_one, branch_gate))
    entry_pre = low_back(product(normed_one, branch_input))
    places = jnp.arange(TOKENS, dtype=jnp.int32)
    segment = lax.optimization_barrier(jnp.sum((doc_starts[None, :] <= places[:, None]).astype(jnp.int32), axis=1))
    starts_here = jnp.any(doc_starts[None, :] == places[:, None], axis=1)[:, None]
    tap_table = conv_taps.reshape(TAPS, lanes)
    convolved = jnp.zeros_like(entry_pre)
    for offset in range(TAPS):
        shifted = jnp.pad(entry_pre, ((offset, 0), (0, 0)))[:TOKENS]
        earlier_seg = jnp.pad(segment, (offset, 0))[:TOKENS]
        same_doc = (earlier_seg == segment).astype(entry_pre.dtype)[:, None]
        convolved = convolved + tap_table[offset] * shifted * same_doc
    conv_low = low(convolved)
    blocked = conv_low.reshape(TOKENS, H, HD)
    rate_pre = low_back(jnp.einsum('thc,hcd->thd', blocked, rate_gate, precision=HIGH).reshape(TOKENS, lanes))
    inlet_pre = low_back(jnp.einsum('thc,hcd->thd', blocked, input_gate, precision=HIGH).reshape(TOKENS, lanes))
    recur_gate = jax.nn.sigmoid(rate_pre)
    admit_gate = jax.nn.sigmoid(inlet_pre)
    softened = jax.nn.softplus(-decay_param.reshape(lanes))
    log_decay = -8.0 * recur_gate * softened
    decays = jnp.exp(log_decay)
    root_norm = jnp.sqrt(GUARD - jnp.expm1(2.0 * log_decay))
    carry_decay = jnp.where(starts_here, 0.0, decays)
    norm_root = jnp.where(starts_here, 1.0, root_norm)
    unused, state = lax.associative_scan(pair_join, (carry_decay, norm_root * admit_gate * convolved), axis=0)
    merged = low(state * jax.nn.gelu(gate_pre))
    hidden_one = layer_input + low_back(product(merged, mixer_out))
    normed_two = low(rms_unit(hidden_one) * feed_gain)
    gating = low_back(product(normed_two, feed_gate))
    lifting = low_back(product(normed_two, feed_up))
    hidden = low(jax.nn.gelu(gating) * lifting)
    return hidden_one + low_back(product(hidden, feed_down))

def reference(layer_input, out_grad, doc_starts, mixer_gain, branch_gate, branch_input, conv_taps, rate_gate, input_gate, decay_param, mixer_out, feed_gain, feed_gate, feed_up, feed_down):
    params = [w.astype(jnp.float32) for w in (mixer_gain, branch_gate, branch_input, conv_taps, rate_gate, input_gate, decay_param, mixer_out, feed_gain, feed_gate, feed_up, feed_down)]

    def run(values, *weights):
        return forward(values, *weights, doc_starts)
    result, pull = jax.vjp(run, layer_input.astype(jnp.float32), *params)
    grads = pull(out_grad.astype(jnp.float32))
    return (result.astype(jnp.bfloat16), grads[0].astype(jnp.bfloat16), grads[1], grads[2], grads[3], grads[4], grads[5], grads[6], grads[7], grads[8], grads[9], grads[10], grads[11], grads[12])
```

```python
import functools

import jax
import jax.numpy as jnp
from jax import lax
from jax.experimental import pallas as pl
from jax.experimental.pallas import tpu as pltpu
from jax.sharding import PartitionSpec as P

TAPS = 4
EPSILON = 1e-06
GUARD = 0.001
GELU_SCALE = 0.7978845608028654
GELU_CUBE = 0.044715
MESH = pl.DeviceIdType.MESH
F32, BF16 = jnp.float32, jnp.bfloat16
ANY = pl.BlockSpec(memory_space=pl.ANY)
VMEM = pl.BlockSpec(memory_space=pltpu.VMEM)
GRANT = 60 * 1024 * 1024
NT = (((1,), (1,)), ((), ()))
TN = (((0,), (0,)), ((), ()))
CHUNK = 256


def spot():
    dp, tensor = lax.axis_index("dp"), lax.axis_index("tensor")
    return dp // 2, dp % 2, tensor // 2, tensor % 2


def seat(line, side, deck, core):
    return (line * 2 + side, deck * 2 + core)


def rank(side, deck, core):
    return side * 4 + deck * 2 + core


def greet(peers):
    barrier = pltpu.get_barrier_semaphore()
    for peer in peers:
        pl.semaphore_signal(barrier, inc=1, device_id=peer, device_id_type=MESH)
    pl.semaphore_wait(barrier, len(peers))


def remote(source, target, send, receive, peer):
    return pltpu.make_async_remote_copy(
        src_ref=source,
        dst_ref=target,
        send_sem=send,
        recv_sem=receive,
        device_id=peer,
        device_id_type=MESH,
    )


def line_peers(count):
    line, side, deck, core = spot()
    return [seat((line + k) % count, side, deck, core) for k in range(1, count)]


def group_peers():
    line, side, deck, core = spot()
    return [
        seat(line, side, deck, 1 - core),
        seat(line, 1 - side, deck, core),
        seat(line, side, 1 - deck, core),
    ]


PIECES = 2


class LineGather:
    def __init__(self, count, source, target, sems):
        self.count, self.source, self.target = count, source, target
        self.send, self.receive, self.local = sems
        self.here = spot()

    @staticmethod
    def scratch(count):
        steps = 5 if count == 4 else count - 1
        return [
            pltpu.SemaphoreType.DMA((steps, PIECES)),
            pltpu.SemaphoreType.DMA((count, PIECES)),
            pltpu.SemaphoreType.DMA,
        ]

    def part(self, ref, piece):
        rows = self.source.shape[0] // PIECES
        return ref.at[pl.ds(piece * rows, rows)]

    def copy(self, origin, place, index, piece, source):
        line, side, deck, core = self.here
        return remote(
            source,
            self.part(self.target.at[origin], piece),
            self.send.at[index, piece],
            self.receive.at[origin, piece],
            seat(place, side, deck, core),
        )

    def own(self, place, index, piece):
        return self.copy(self.here[0], place, index, piece, self.part(self.source, piece))

    def arrival(self, origin, piece):
        return self.copy(origin, origin, 0, piece, self.part(self.source, piece))

    def keep(self):
        return pltpu.make_async_copy(self.source, self.target.at[self.here[0]], self.local)

    def steps(self):
        if self.count == 4:
            return [1, -1, 2, -2]
        return list(range(1, self.count))

    def guarded(self, index, step, action):
        line = self.here[0]
        if self.count == 4:
            place = line + step

            @pl.when((place >= 0) & (place < self.count))
            def _():
                action(place)

        else:
            action((line + step) % self.count)

    def start(self):
        for piece in range(PIECES):
            for index, step in enumerate(self.steps()):
                self.guarded(
                    index, step, lambda place, i=index, p=piece: self.own(place, i, p).start()
                )
        self.keep().start()

    def middle(self, action):
        line = self.here[0]
        if self.count == 4:

            @pl.when((line == 1) | (line == 2))
            def _():
                action(6 - 3 * line, 3 * line - 3)

    def onward(self, origin, place, piece):
        return self.copy(origin, place, 4, piece, self.part(self.target.at[origin], piece))

    def forward(self):
        for piece in range(PIECES):

            def action(origin, place, piece=piece):
                self.arrival(origin, piece).wait_recv()
                self.onward(origin, place, piece).start()

            self.middle(action)

    def finish(self):
        line = self.here[0]
        for piece in range(PIECES):
            for index, step in enumerate(self.steps()):
                self.guarded(
                    index, step, lambda place, i=index, p=piece: self.own(place, i, p).wait_send()
                )
            self.middle(
                lambda origin, place, p=piece: self.onward(origin, place, p).wait_send()
            )
            for origin in range(self.count):
                pending = line != origin
                if self.count == 4 and origin == 0:
                    pending = pending & (line != 2)
                if self.count == 4 and origin == 3:
                    pending = pending & (line != 1)

                @pl.when(pending)
                def _(origin=origin, piece=piece):
                    self.arrival(origin, piece).wait_recv()

        self.keep().wait()


def call(kernel, outs, ins, scratch, identity, name):
    results = pl.pallas_call(
        kernel,
        out_shape=[jax.ShapeDtypeStruct(shape, kind) for shape, kind, _ in outs],
        in_specs=[space for _, space in ins],
        out_specs=[space for _, _, space in outs],
        scratch_shapes=scratch,
        compiler_params=pltpu.CompilerParams(
            collective_id=identity, has_side_effects=True, vmem_limit_bytes=GRANT
        ),
        name=name,
    )(*[value for value, _ in ins])
    return list(results)


def spread_kernel(count, halves, small, pair, everyone, send, receive, local):
    dp, tensor = lax.axis_index("dp"), lax.axis_index("tensor")
    line, side, deck, core = spot()
    greet([((dp + k) % count, tensor) for k in range(1, count)])
    copies = [
        remote(
            small,
            everyone.at[dp],
            send.at[k],
            receive.at[k],
            ((dp + k) % count, tensor),
        )
        for k in range(1, count)
    ]
    copies.append(
        remote(
            halves.at[1 - side],
            pair.at[side],
            send.at[0],
            receive.at[0],
            seat(line, 1 - side, deck, core),
        )
    )
    copies.append(pltpu.make_async_copy(small, everyone.at[dp], local.at[0]))
    copies.append(pltpu.make_async_copy(halves.at[side], pair.at[side], local.at[1]))
    for copy in copies:
        copy.start()
    for copy in copies:
        copy.wait()


def spread(count, halves, small):
    return call(
        functools.partial(spread_kernel, count),
        [(halves.shape, BF16, ANY), ((count,) + small.shape, BF16, ANY)],
        [(halves, ANY), (small, ANY)],
        [
            pltpu.SemaphoreType.DMA((count,)),
            pltpu.SemaphoreType.DMA((count,)),
            pltpu.SemaphoreType.DMA((2,)),
        ],
        0,
        "spread",
    )


class GroupGather:
    def __init__(self, source, target, send, receive, local):
        self.source, self.target = source, target
        self.send, self.receive = send, receive
        self.local = local
        self.here = spot()

    @staticmethod
    def scratch():
        return [
            pltpu.SemaphoreType.DMA((11,)),
            pltpu.SemaphoreType.DMA((11,)),
            pltpu.SemaphoreType.DMA,
        ]

    def half(self, ref, h):
        rows = self.source.shape[0] // 2
        return ref.at[pl.ds(h * rows, rows)]

    def make(self):
        line, side, deck, core = self.here
        sibling, across, above = group_peers()
        mine = rank(side, deck, core)
        beside = rank(1 - side, deck, core)
        over = rank(side, 1 - deck, core)
        corner = rank(1 - side, 1 - deck, core)

        def own(h, peer, index):
            return remote(
                self.half(self.source, h),
                self.half(self.target.at[mine], h),
                self.send.at[index],
                self.receive.at[index],
                peer,
            )

        def relay(block, h, peer, index):
            ref = self.half(self.target.at[block], h)
            return remote(ref, ref, self.send.at[index], self.receive.at[index], peer)

        self.keep = pltpu.make_async_copy(self.source, self.target.at[mine], self.local)
        self.first = [
            own(0, across, 0),
            own(1, above, 1),
            own(0, above, 2),
            own(1, across, 3),
        ]
        self.near = remote(
            self.source, self.target.at[mine], self.send.at[4], self.receive.at[4], sibling
        )
        self.second = [relay(beside, 0, above, 5), relay(over, 1, across, 6)]
        self.last = [
            relay(beside, 0, sibling, 7),
            relay(over, 1, sibling, 8),
            relay(over, 0, sibling, 9),
            relay(beside, 1, sibling, 10),
        ]
        self.corner = corner

    def start(self):
        self.make()
        for copy in self.first:
            copy.start()
        self.near.start()
        self.keep.start()

    def forward(self):
        for k in range(2):
            self.first[k].wait_recv()
            self.second[k].start()
            self.last[k].start()
        for k in range(2, 4):
            self.first[k].wait_recv()
            self.last[k].start()


def corner_relay(gather, send, receive):
    sibling = group_peers()[0]
    out = []
    for h in range(2):
        ref = gather.half(gather.target.at[gather.corner], h)
        out.append(remote(ref, ref, send.at[h], receive.at[h], sibling))
    return out


def group_finish(gather, send, receive):
    relays = corner_relay(gather, send, receive)
    for k in range(2):
        gather.second[k].wait_recv()
        relays[k].start()
    gather.keep.wait()
    gather.near.wait()
    for copy in gather.first:
        copy.wait_send()
    for copy in gather.second:
        copy.wait_send()
    for copy in gather.last:
        copy.wait()
    for copy in relays:
        copy.wait()


def rows_scratch():
    return GroupGather.scratch() + [
        pltpu.SemaphoreType.DMA((2,)),
        pltpu.SemaphoreType.DMA((2,)),
    ]


def rows_kernel(count, swaps, *refs):
    rows, block = refs[0], refs[1]
    halves = refs[2 : 2 + swaps]
    outs = refs[2 + swaps : 4 + swaps + swaps]
    sems = refs[4 + swaps + swaps :]
    everything, blocks = outs[:2]
    pairs = outs[2:]
    gather = GroupGather(rows, everything, *sems[:3])
    corner = sems[3:5]
    freight = LineGather(count, block, blocks, sems[5:8])
    line, side, deck, core = spot()
    greet(group_peers() + line_peers(count))
    gather.start()
    freight.start()
    moves = []
    if swaps:
        send, receive, local = sems[8:]
        for k in range(swaps):
            moves.append(
                remote(
                    halves[k].at[1 - side],
                    pairs[k].at[side],
                    send.at[k],
                    receive.at[k],
                    seat(line, 1 - side, deck, core),
                )
            )
            moves.append(
                pltpu.make_async_copy(halves[k].at[side], pairs[k].at[side], local.at[k])
            )
        for move in moves:
            move.start()
    gather.forward()
    freight.forward()
    group_finish(gather, *corner)
    for move in moves:
        move.wait()
    freight.finish()


def gather_rows(count, rows, block, identity, halves=()):
    scratch = rows_scratch() + LineGather.scratch(count)
    if halves:
        scratch += [pltpu.SemaphoreType.DMA((len(halves),))] * 3
    out = call(
        functools.partial(rows_kernel, count, len(halves)),
        [((8,) + rows.shape, BF16, ANY), ((count,) + block.shape, BF16, ANY)]
        + [(half.shape, BF16, ANY) for half in halves],
        [(rows, ANY), (block, ANY)] + [(half, ANY) for half in halves],
        scratch,
        identity,
        "gather_rows",
    )
    full = out[0].reshape(-1, rows.shape[1])
    line = out[1].reshape(-1, block.shape[1])
    return [full, line] + [pair.reshape(-1, pair.shape[2]) for pair in out[2:]]


def plain_rows_kernel(rows, everything, *sems):
    gather = GroupGather(rows, everything, *sems[:3])
    greet(group_peers())
    gather.start()
    gather.forward()
    group_finish(gather, *sems[3:5])


def gather_plain(rows, identity):
    out = call(
        plain_rows_kernel,
        [((8,) + rows.shape, BF16, ANY)],
        [(rows, ANY)],
        rows_scratch(),
        identity,
        "gather_rows",
    )
    return out[0].reshape(-1, rows.shape[1])


def fold_kernel(count, pairs, cargo, *refs):
    lefts, rights = refs[:pairs], refs[pairs : 2 * pairs]
    refs = refs[2 * pairs :]
    block = None
    if cargo:
        block, refs = refs[0], refs[1:]
    out, refs = refs[0], refs[1:]
    if cargo:
        blocks, refs = refs[0], refs[1:]
    mine, stage, near, leaving, arriving, refs = *refs[:5], refs[5:]
    send, receive, near_send, near_receive = refs[:4]
    line, side, deck, core = spot()
    sibling, across, above = group_peers()
    if cargo:
        freight = LineGather(count, block, blocks, refs[4:])
        greet(group_peers() + line_peers(count))
        freight.start()
    else:
        greet(group_peers())
    rows = out.shape[0]
    half = rows // 2
    width = out.shape[1]
    step = 512

    def product(which, store):
        base = pl.multiple_of(which * rows, rows)

        def body(j, carry):
            columns = pl.ds(pl.multiple_of(j * step, step), step)
            total = None
            for left, right in zip(lefts, rights):
                part = lax.dot_general(
                    left[pl.ds(base, rows), :],
                    right[columns, :],
                    NT,
                    preferred_element_type=F32,
                )
                total = part if total is None else total + part
            store(columns, total)
            return carry

        lax.fori_loop(0, width // step, body, 0)

    def sweep(action):
        def body(i, carry):
            action(pl.multiple_of(i * 16, 16))
            return carry

        lax.fori_loop(0, half // 16, body, 0)

    def chip_sum(q, h, r):
        place = pl.ds(h * half + r, 16)
        return mine[q, place, :] + near[q, place, :].astype(F32)

    def ship(index, peer):
        return remote(
            leaving.at[index], arriving.at[index], send.at[index], receive.at[index], peer
        )

    ships = [ship(k, peer) for k, peer in enumerate((above, across, above, across, across, above))]
    OWN, ACROSS, ABOVE, CORNER = 0, 1, 2, 3
    seats = {
        CORNER: (1 - side, 1 - deck),
        ABOVE: (side, 1 - deck),
        ACROSS: (1 - side, deck),
        OWN: (side, deck),
    }
    nears = []
    for q in (CORNER, ABOVE, ACROSS, OWN):
        s, d = seats[q]

        def put_stage(columns, total, q=q):
            stage[q, :, columns] = total.astype(BF16)

        def put_mine(columns, total, q=q):
            mine[q, :, columns] = total

        product(rank(s, d, 1 - core), put_stage)
        copy = remote(stage.at[q], near.at[q], near_send.at[q], near_receive.at[q], sibling)
        copy.start()
        nears.append(copy)
        product(rank(s, d, core), put_mine)
        copy.wait_recv()
        if q == CORNER:

            def corner_sum(r):
                for h in range(2):
                    leaving[h, pl.ds(r, 16), :] = chip_sum(CORNER, h, r).astype(BF16)

            sweep(corner_sum)
            ships[0].start()
            ships[1].start()
        if q == ABOVE:

            def above_sum(r):
                leaving[2, pl.ds(r, 16), :] = chip_sum(ABOVE, 0, r).astype(BF16)

            sweep(above_sum)
            ships[2].start()
        if q == ACROSS:

            def across_sum(r):
                leaving[3, pl.ds(r, 16), :] = chip_sum(ACROSS, 1, r).astype(BF16)

            sweep(across_sum)
            ships[3].start()
    if cargo:
        freight.forward()
    ships[0].wait_recv()

    def pass_across(r):
        total = chip_sum(ACROSS, 0, r) + arriving[0, pl.ds(r, 16), :].astype(F32)
        leaving[4, pl.ds(r, 16), :] = total.astype(BF16)

    sweep(pass_across)
    ships[4].start()
    ships[1].wait_recv()

    def pass_above(r):
        total = chip_sum(ABOVE, 1, r) + arriving[1, pl.ds(r, 16), :].astype(F32)
        leaving[5, pl.ds(r, 16), :] = total.astype(BF16)

    sweep(pass_above)
    ships[5].start()
    for k in range(2, 6):
        ships[k].wait_recv()

    def finish(r):
        place = pl.ds(r, 16)
        first = arriving[2, place, :].astype(F32) + arriving[4, place, :].astype(F32)
        out[place, :] = chip_sum(OWN, 0, r) + first
        second = arriving[3, place, :].astype(F32) + arriving[5, place, :].astype(F32)
        out[pl.ds(half + r, 16), :] = chip_sum(OWN, 1, r) + second

    sweep(finish)
    for k in range(6):
        ships[k].wait_send()
    for copy in nears:
        copy.wait_send()
    if cargo:
        freight.finish()


def fold(count, lefts, rights, identity, block=None):
    rows, width = lefts[0].shape[0] // 8, rights[0].shape[0]
    outs = [((rows, width), F32, VMEM)]
    ins = [(value, VMEM) for value in list(lefts) + list(rights)]
    scratch = [
        pltpu.VMEM((4, rows, width), F32),
        pltpu.VMEM((4, rows, width), BF16),
        pltpu.VMEM((4, rows, width), BF16),
        pltpu.VMEM((6, rows // 2, width), BF16),
        pltpu.VMEM((6, rows // 2, width), BF16),
        pltpu.SemaphoreType.DMA((6,)),
        pltpu.SemaphoreType.DMA((6,)),
        pltpu.SemaphoreType.DMA((4,)),
        pltpu.SemaphoreType.DMA((4,)),
    ]
    if block is not None:
        outs.append(((count,) + block.shape, BF16, ANY))
        ins.append((block, ANY))
        scratch += LineGather.scratch(count)
    out = call(
        functools.partial(fold_kernel, count, len(lefts), block is not None),
        outs,
        ins,
        scratch,
        identity,
        "fold",
    )
    if block is not None:
        return out[0], out[1].reshape(-1, block.shape[1])
    return out[0]


def gelu_both(value):
    square = value * value
    bend = jnp.tanh(GELU_SCALE * value * (1.0 + GELU_CUBE * square))
    act = 0.5 * value * (1.0 + bend)
    slope = 0.5 * (1.0 + bend) + 0.5 * value * (1.0 - bend * bend) * GELU_SCALE * (
        1.0 + 3.0 * GELU_CUBE * square
    )
    return act, slope


def chunks(rows, action, size=CHUNK):
    def body(i, carry):
        action(pl.multiple_of(i * size, size))
        return carry

    lax.fori_loop(0, rows // size, body, 0)


def tile_scan(mults, adds, rows, width, backward):
    place = lax.broadcasted_iota(jnp.int32, (8, width), 0)

    def inside(base):
        where = pl.ds(base, 8)
        a, b = mults[where, :], adds[where, :]
        for k in (1, 2, 4):
            if backward:
                away, mask = pltpu.roll(a, 8 - k, 0), place < 8 - k
                back = pltpu.roll(b, 8 - k, 0)
            else:
                away, mask = pltpu.roll(a, k, 0), place >= k
                back = pltpu.roll(b, k, 0)
            b = jnp.where(mask, b + a * back, b)
            a = jnp.where(mask, a * away, a)
        return where, a, b

    unroll = 4
    tiles = rows // 8

    def body(i, carry):
        prod, total = carry
        work = []
        for u in range(unroll):
            index = i * unroll + u
            if backward:
                index = tiles - 1 - index
            work.append(inside(pl.multiple_of(index * 8, 8)))
        for where, a, b in work:
            edge = 0 if backward else 7
            adds[where, :] = b + a * total
            mults[where, :] = a * prod
            whole = jnp.broadcast_to(a[edge : edge + 1, :], (8, width))
            extra = jnp.broadcast_to(b[edge : edge + 1, :], (8, width))
            total = extra + whole * total
            prod = whole * prod
        return prod, total

    return lax.fori_loop(
        0, tiles // unroll, body, (jnp.ones((8, width), F32), jnp.zeros((8, width), F32))
    )


def pool(count, prod, total, outgoing, slots, send, receive, backward):
    line, side, deck, core = spot()
    outgoing[0:8, :] = prod
    outgoing[8:16, :] = total
    slots[line, 0:8, :] = prod
    slots[line, 8:16, :] = total
    copies = []
    for k in range(1, count):
        copy = remote(
            outgoing,
            slots.at[line],
            send.at[k],
            receive.at[k],
            seat((line + k) % count, side, deck, core),
        )
        copy.start()
        copies.append(copy)
    for copy in copies:
        copy.wait()
    entering = jnp.zeros_like(prod)
    order = range(count - 1, -1, -1) if backward else range(count)
    for place in order:
        longer = slots[place, 8:16, :] + slots[place, 0:8, :] * entering
        before = (line < place) if backward else (line > place)
        entering = jnp.where(before, longer, entering)
    return entering


def gates(values, soft):
    recur = values
    low = -8.0 * recur * soft
    decay = jnp.exp(low)
    root = jnp.sqrt((1.0 + GUARD) - decay * decay)
    return decay, root


def scan_kernel(
    count,
    pre,
    masks,
    table,
    gate_weights,
    block,
    conv,
    recur_out,
    admit_out,
    state,
    merged,
    entry,
    blocks,
    prods,
    sums,
    halo,
    outgoing,
    slots,
    edge_sems,
    send,
    receive,
    *sems,
):
    line, side, deck, core = spot()
    rows, width = conv.shape
    freight = LineGather(count, block, blocks, sems)
    greet(line_peers(count))

    def edge(place):
        return remote(
            pre.at[pl.ds(rows - 8, 8), pl.ds(width, width)],
            halo,
            edge_sems.at[0],
            edge_sems.at[1],
            seat(place, side, deck, core),
        )

    @pl.when(line < count - 1)
    def _():
        edge(line + 1).start()

    freight.start()

    def copy_entry(r):
        entry[pl.ds(r + 8, CHUNK), :] = pre[pl.ds(r, CHUNK), width:]

    chunks(rows, copy_entry)

    @pl.when(line > 0)
    def _():
        edge(line - 1).wait_recv()
        entry[0:8, :] = halo[...]

    @pl.when(line == 0)
    def _():
        entry[0:8, :] = jnp.zeros((8, width), F32)

    @pl.when(line < count - 1)
    def _():
        edge(line + 1).wait_send()

    def gate_chunk(r):
        wide = entry[pl.ds(r, CHUNK + 8), :]
        mask = masks[pl.ds(r, CHUNK), :]
        value = table[0:1, :] * wide[8:, :]
        for k in range(1, TAPS):
            value = (
                value + table[k : k + 1, :] * wide[8 - k : 8 - k + CHUNK, :] * mask[:, k - 1 : k]
            )
        where = pl.ds(r, CHUNK)
        conv[where, :] = value
        both = jnp.dot(value.astype(BF16), gate_weights[...], preferred_element_type=F32)
        recur = jax.nn.sigmoid(both[:, :width])
        admit = jax.nn.sigmoid(both[:, width:])
        recur_out[where, :] = recur
        admit_out[where, :] = admit
        decay, root = gates(recur, table[4:5, :])
        opened = mask[:, 3:4]
        norm = root * opened + (1.0 - opened)
        prods[where, :] = decay * opened
        sums[where, :] = norm * admit * value

    chunks(rows, gate_chunk)
    prod, total = tile_scan(prods, sums, rows, width, False)
    entering = pool(count, prod, total, outgoing, slots, send, receive, False)
    state[0:8, :] = entering

    def state_chunk(r):
        where = pl.ds(r, CHUNK)
        value = sums[where, :] + prods[where, :] * entering[0:1, :]
        state[pl.ds(r + 8, CHUNK), :] = value
        act, _ = gelu_both(pre[where, :width])
        merged[where, :] = (value * act).astype(BF16)

    chunks(rows, state_chunk)
    freight.forward()
    freight.finish()


def scan_forward(count, pre, masks, table, gate_weights, block):
    rows, width = pre.shape[0], pre.shape[1] // 2
    out = call(
        functools.partial(scan_kernel, count),
        [
            ((rows, width), F32, VMEM),
            ((rows, width), F32, VMEM),
            ((rows, width), F32, VMEM),
            ((rows + 8, width), F32, VMEM),
            ((rows, width), BF16, VMEM),
            ((rows + 8, width), F32, VMEM),
            ((count,) + block.shape, BF16, ANY),
        ],
        [(pre, VMEM), (masks, VMEM), (table, VMEM), (gate_weights, VMEM), (block, ANY)],
        [
            pltpu.VMEM((rows, width), F32),
            pltpu.VMEM((rows, width), F32),
            pltpu.VMEM((8, width), F32),
            pltpu.VMEM((16, width), F32),
            pltpu.VMEM((count, 16, width), F32),
            pltpu.SemaphoreType.DMA((2,)),
            pltpu.SemaphoreType.DMA((count,)),
            pltpu.SemaphoreType.DMA((count,)),
        ]
        + LineGather.scratch(count),
        2,
        "scan_forward",
    )
    return out[:-1] + [out[-1].reshape(-1, block.shape[1])]


def back_kernel(
    count,
    pre,
    grad_merged,
    conv,
    recur_in,
    admit_in,
    state,
    entry,
    masks,
    table,
    gate_weights,
    grad_pre,
    grad_gates,
    grad_table,
    prods,
    sums,
    mixes,
    outgoing,
    slots,
    edge_sems,
    send,
    receive,
):
    line, side, deck, core = spot()
    rows, width = conv.shape
    greet(line_peers(count))

    def direct_chunk(r):
        where = pl.ds(r, CHUNK)
        act, slope = gelu_both(pre[where, :width])
        grad = grad_merged[where, :]
        grad_pre[where, :width] = (grad * state[pl.ds(r + 8, CHUNK), :] * slope).astype(BF16)
        direct = grad * act
        decay, _ = gates(recur_in[where, :], table[4:5, :])
        carry = decay * masks[where, 3:4]
        mixes[where, :] = direct
        prods[where, :] = carry
        sums[where, :] = carry * direct

    chunks(rows, direct_chunk)
    prods[rows : rows + 8, :] = jnp.ones((8, width), F32)
    sums[rows : rows + 8, :] = jnp.zeros((8, width), F32)
    prod, total = tile_scan(prods, sums, rows, width, True)
    entering = pool(count, prod, total, outgoing, slots, send, receive, True)
    grad_gates[...] = jnp.zeros_like(grad_gates)
    grad_table[...] = jnp.zeros_like(grad_table)

    def fold_rows(value):
        return jnp.sum(value, axis=0, keepdims=True)

    def gate_chunk(r):
        where = pl.ds(r, CHUNK)
        wide = pl.ds(r, CHUNK + 8)
        later = sums[wide, :] + prods[wide, :] * entering[0:1, :]
        grad = mixes[where, :] + later[1 : CHUNK + 1, :]
        before = state[wide, :][7 : CHUNK + 7, :]
        soft = table[4:5, :]
        recur, admit, value = recur_in[where, :], admit_in[where, :], conv[where, :]
        decay, root = gates(recur, soft)
        opened = masks[where, 3:4]
        norm = root * opened + (1.0 - opened)
        flow = grad * admit
        grad_log = opened * (grad * before * decay - flow * value * decay * decay / root)
        grad_table[4:5, :] += fold_rows(grad_log * (-8.0 * recur))
        grad_rate = (grad_log * (-8.0 * soft) * recur * (1.0 - recur)).astype(BF16)
        grad_inlet = (flow * norm * value * (1.0 - admit)).astype(BF16)
        both = jnp.concatenate([grad_rate, grad_inlet], axis=1)
        grad_gates[...] += lax.dot_general(
            value.astype(BF16), both, TN, preferred_element_type=F32
        )
        mixes[where, :] = flow * norm + lax.dot_general(
            both, gate_weights[...], NT, preferred_element_type=F32
        )

    gate_chunk(0)

    def edge(place):
        return remote(
            mixes.at[pl.ds(0, 8)],
            mixes.at[pl.ds(rows, 8)],
            edge_sems.at[0],
            edge_sems.at[1],
            seat(place, side, deck, core),
        )

    @pl.when(line > 0)
    def _():
        edge(line - 1).start()

    def other(i, carry):
        gate_chunk(pl.multiple_of(i * CHUNK, CHUNK))
        return carry

    lax.fori_loop(1, rows // CHUNK, other, 0)

    @pl.when(line < count - 1)
    def _():
        edge(line + 1).wait_recv()

    @pl.when(line == count - 1)
    def _():
        mixes[rows : rows + 8, :] = jnp.zeros((8, width), F32)

    def entry_chunk(r):
        where, wide = pl.ds(r, CHUNK), pl.ds(r, CHUNK + 8)
        ahead, mask = mixes[wide, :], masks[where, :]
        source = entry[wide, :]
        here = ahead[:CHUNK, :]
        total = table[0:1, :] * here
        grad_table[0:1, :] += fold_rows(here * source[8:, :])
        for k in range(1, TAPS):
            total = total + table[k : k + 1, :] * ahead[k : k + CHUNK, :] * mask[:, 3 + k : 4 + k]
            grad_table[k : k + 1, :] += fold_rows(
                here * source[8 - k : 8 - k + CHUNK, :] * mask[:, k - 1 : k]
            )
        grad_pre[where, width:] = total.astype(BF16)

    chunks(rows, entry_chunk)

    @pl.when(line > 0)
    def _():
        edge(line - 1).wait_send()


def scan_backward(count, pre, grad_merged, saved, masks, table, gate_weights):
    rows, width = grad_merged.shape
    values = [pre, grad_merged, *saved, masks, table, gate_weights]
    return call(
        functools.partial(back_kernel, count),
        [
            ((rows, 2 * width), BF16, VMEM),
            ((width, 2 * width), F32, VMEM),
            ((8, width), F32, VMEM),
        ],
        [(value, VMEM) for value in values],
        [
            pltpu.VMEM((rows + 8, width), F32),
            pltpu.VMEM((rows + 8, width), F32),
            pltpu.VMEM((rows + 8, width), F32),
            pltpu.VMEM((16, width), F32),
            pltpu.VMEM((count, 16, width), F32),
            pltpu.SemaphoreType.DMA((2,)),
            pltpu.SemaphoreType.DMA((count,)),
            pltpu.SemaphoreType.DMA((count,)),
        ],
        7,
        "scan_backward",
    )


def doc_index(places, doc_starts):
    return jnp.sum((doc_starts[None, :] <= places[:, None]).astype(jnp.int32), axis=1)


def norm_back(grad_unit, unit_rows, scale_rows):
    return scale_rows * (
        grad_unit - unit_rows * jnp.mean(grad_unit * unit_rows, axis=1, keepdims=True)
    )


def unit_norm(values):
    scale = lax.rsqrt(jnp.mean(values * values, axis=1, keepdims=True) + EPSILON)
    return values * scale, scale


def split_columns(value):
    rows, columns = value.shape
    return value.reshape(rows, 2, columns // 2).transpose(1, 0, 2)


def widen(value, width):
    return jnp.pad(value, [(0, 0)] * (value.ndim - 1) + [(0, width - value.shape[-1])])


def by_rows(left, right):
    return lax.dot_general(left, right, TN, preferred_element_type=F32).astype(BF16)


def shards(
    layer_input,
    out_grad,
    doc_starts,
    mixer_gain,
    branch_gate,
    branch_input,
    conv_taps,
    rate_gate,
    input_gate,
    decay_param,
    mixer_out,
    feed_gain,
    feed_gate,
    feed_up,
    feed_down,
):
    shares = lax.axis_size("dp")
    count = shares // 2
    side = lax.axis_index("dp") % 2
    slim, feature_count = mixer_gain.shape[0], layer_input.shape[1]
    heads, piece, head_width = rate_gate.shape
    half_heads = heads // 2
    lanes = half_heads * head_width
    width = -(-lanes // 128) * 128
    row_count = layer_input.shape[0]
    rows = row_count * 8
    line_groups = [[2 * k + s for k in range(count)] for s in range(2)]

    branch_halves = jnp.concatenate(
        [split_columns(branch_gate), split_columns(branch_input)], axis=2
    )
    mixer_halves = widen(split_columns(mixer_out.T), width)
    gate_halves, up_halves = split_columns(feed_gate), split_columns(feed_up)
    down_halves = split_columns(feed_down.T)
    flat = jnp.concatenate(
        [
            mixer_gain,
            feed_gain,
            rate_gate.reshape(-1),
            input_gate.reshape(-1),
            conv_taps.reshape(-1),
            decay_param.reshape(-1),
        ]
    )
    small_rows = -(-flat.shape[0] // (128 * 16)) * 16
    small = jnp.pad(flat, (0, small_rows * 128 - flat.shape[0])).reshape(small_rows, 128)
    branch_pair, small_all = spread(shares, branch_halves, small)

    small_all = small_all.reshape(shares, -1)
    cuts = [slim, slim, rate_gate.size, input_gate.size, conv_taps.size, decay_param.size]
    parts, start = [], 0
    for size in cuts:
        parts.append(small_all[:, start : start + size])
        start += size
    gain_first = parts[0].reshape(feature_count).astype(F32)
    gain_second = parts[1].reshape(feature_count).astype(F32)

    def own_heads(value, axis):
        return lax.dynamic_slice_in_dim(value, side * half_heads, half_heads, axis)

    rate_weights, inlet_weights = [
        own_heads(
            part.reshape(shares, heads, piece, head_width)
            .transpose(1, 0, 2, 3)
            .reshape(heads, shares * piece, head_width),
            0,
        )
        for part in parts[2:4]
    ]
    taps = own_heads(
        parts[4].reshape(shares, TAPS, heads, piece).transpose(1, 2, 0, 3), 1
    ).reshape(TAPS, lanes)
    decay_flat = own_heads(
        parts[5].reshape(shares, heads, piece).transpose(1, 0, 2), 0
    ).reshape(lanes).astype(F32)
    table = widen(
        jnp.concatenate(
            [
                taps.astype(F32),
                jax.nn.softplus(-decay_flat)[None],
                jnp.zeros((3, lanes), F32),
            ]
        ),
        width,
    )

    def diagonal(blocks):
        bands = [
            jnp.pad(
                blocks[h],
                ((0, 0), (h * head_width, width - (h + 1) * head_width)),
            )
            for h in range(half_heads)
        ]
        return jnp.pad(jnp.concatenate(bands, axis=0), ((0, width - lanes), (0, 0)))

    gate_weights = jnp.concatenate([diagonal(rate_weights), diagonal(inlet_weights)], axis=1)

    anchor = lax.axis_index("dp") // 2 * rows
    places = anchor + jnp.arange(rows, dtype=jnp.int32)
    here = doc_index(places, doc_starts)
    columns = [doc_index(places - k, doc_starts) == here for k in range(1, TAPS)]
    columns.append(~jnp.any(doc_starts[None, :] == places[:, None], axis=1))
    columns += [doc_index(places + k, doc_starts) == here for k in range(1, TAPS)]
    columns.append(columns[0])
    masks = jnp.stack(columns, axis=1).astype(F32)

    residual = layer_input.astype(F32)
    unit_one, scale_one = unit_norm(residual)
    normed_own = (unit_one * gain_first).astype(BF16)
    normed_one, branch_all, mixer_pair, gate_pair, up_pair, down_pair = gather_rows(
        count,
        normed_own,
        branch_pair.reshape(-1, 2 * lanes),
        1,
        (mixer_halves, gate_halves, up_halves, down_halves),
    )
    branch_wide = jnp.concatenate(
        [widen(branch_all[:, :lanes], width), widen(branch_all[:, lanes:], width)], axis=1
    )
    pre = jnp.dot(normed_one, branch_wide, preferred_element_type=F32)
    conv, recur, admit, state, merged, entry, mixer_all = scan_forward(
        count, pre, masks, table, gate_weights, mixer_pair
    )
    mixer_own, gating_weights = fold(count, [merged], [mixer_all], 3, gate_pair)
    hidden_one = residual + mixer_own
    unit_two, scale_two = unit_norm(hidden_one)
    normed_two, lifting_weights = gather_rows(
        count, (unit_two * gain_second).astype(BF16), up_pair, 4
    )
    cot_all, lowering_weights = gather_rows(count, out_grad, down_pair, 5)

    gating_pre = jnp.dot(normed_two, gating_weights, preferred_element_type=F32)
    lifting_pre = jnp.dot(normed_two, lifting_weights, preferred_element_type=F32)
    gating_act, gating_slope = gelu_both(gating_pre)
    hidden = (gating_act * lifting_pre).astype(BF16)

    def line_sum(value):
        return lax.psum_scatter(
            value, "dp", scatter_dimension=0, axis_index_groups=line_groups, tiled=True
        )

    down_sum = line_sum(by_rows(cot_all, hidden))
    grad_hidden = lax.dot_general(cot_all, lowering_weights, (((1,), (0,)), ((), ())), preferred_element_type=F32)
    grad_gating = (grad_hidden * lifting_pre * gating_slope).astype(BF16)
    grad_lifting = (grad_hidden * gating_act).astype(BF16)
    gate_sum = line_sum(by_rows(normed_two, grad_gating))
    up_sum = line_sum(by_rows(normed_two, grad_lifting))
    grad_normed_two = fold(
        count, [grad_gating, grad_lifting], [gating_weights, lifting_weights], 6
    )
    grad_hidden_one = out_grad.astype(F32) + norm_back(
        grad_normed_two * gain_second, unit_two, scale_two
    )
    back_low = gather_plain(grad_hidden_one.astype(BF16), 8)
    outlet_sum = line_sum(by_rows(back_low, merged))
    grad_merged = jnp.dot(back_low, mixer_all, preferred_element_type=F32)
    grad_pre, grad_gates, grad_table = scan_backward(
        count, pre, grad_merged, [conv, recur, admit, state, entry], masks, table, gate_weights
    )
    branch_grads = by_rows(normed_one, grad_pre)
    branch_sum = line_sum(
        jnp.concatenate([branch_grads[:, :lanes], branch_grads[:, width : width + lanes]], axis=1)
    )
    feed_own = fold(count, [hidden], [lowering_weights], 9)
    layer_output = (hidden_one + feed_own).astype(BF16)
    grad_normed_one = fold(count, [grad_pre], [branch_wide], 10)
    input_grad = (
        grad_hidden_one + norm_back(grad_normed_one * gain_first, unit_one, scale_one)
    ).astype(BF16)

    gains = jnp.stack(
        [jnp.sum(grad_normed_one * unit_one, axis=0), jnp.sum(grad_normed_two * unit_two, axis=0)]
    )
    gains = lax.psum(gains, ("dp", "tensor"))
    gains = lax.dynamic_slice_in_dim(gains, lax.axis_index("dp") * slim, slim, 1)

    def spots(value):
        blocks = [
            value[
                h * head_width : (h + 1) * head_width, h * head_width : (h + 1) * head_width
            ].reshape(shares, -1)
            for h in range(half_heads)
        ]
        return jnp.concatenate(blocks, axis=1)

    grad_decay = -jax.nn.sigmoid(-decay_flat) * grad_table[4, :lanes]
    grad_small = jnp.concatenate(
        [
            spots(grad_gates[:, :width]),
            spots(grad_gates[:, width:]),
            grad_table[:TAPS, :lanes]
            .reshape(TAPS * half_heads, shares, piece)
            .transpose(1, 0, 2)
            .reshape(shares, -1),
            grad_decay.reshape(half_heads, shares, piece).transpose(1, 0, 2).reshape(shares, -1),
        ],
        axis=1,
    )
    flat_size = grad_small.shape[1]
    small_rows = -(-flat_size // (128 * 16)) * 16
    grad_small = widen(grad_small, small_rows * 128).reshape(shares * small_rows, 128)
    small_sum = line_sum(grad_small.astype(BF16)).astype(F32)

    def swap(value):
        pair = value.reshape(2, -1, value.shape[1])
        kept = lax.dynamic_index_in_dim(pair, side, 0, False)
        given = lax.dynamic_index_in_dim(pair, 1 - side, 0, False)
        other = lax.ppermute(given, "dp", [(k, k ^ 1) for k in range(shares)])
        first = jnp.where(side == 0, kept, other).astype(F32)
        second = jnp.where(side == 0, other, kept).astype(F32)
        return first, second

    def joined(value):
        return jnp.concatenate(swap(value), axis=1)

    branch_first, branch_second = swap(branch_sum)
    branch_gate_grad = jnp.concatenate([branch_first[:, :lanes], branch_second[:, :lanes]], axis=1)
    branch_input_grad = jnp.concatenate([branch_first[:, lanes:], branch_second[:, lanes:]], axis=1)
    outlet_first, outlet_second = swap(outlet_sum)
    mixer_out_grad = jnp.concatenate([outlet_first[:, :lanes], outlet_second[:, :lanes]], axis=1).T

    smalls = [value.reshape(-1)[:flat_size] for value in swap(small_sum.astype(BF16))]
    one = half_heads * piece * head_width
    tap_size = TAPS * half_heads * piece
    rate_grad = jnp.concatenate([v[:one].reshape(half_heads, piece, head_width) for v in smalls])
    inlet_grad = jnp.concatenate(
        [v[one : 2 * one].reshape(half_heads, piece, head_width) for v in smalls]
    )
    taps_grad = jnp.concatenate(
        [v[2 * one : 2 * one + tap_size].reshape(TAPS, half_heads, piece) for v in smalls], axis=1
    )
    decay_grad = jnp.concatenate(
        [v[2 * one + tap_size :].reshape(half_heads, piece) for v in smalls]
    )
    return (
        layer_output,
        input_grad,
        gains[0],
        branch_gate_grad,
        branch_input_grad,
        taps_grad,
        rate_grad,
        inlet_grad,
        decay_grad,
        mixer_out_grad,
        gains[1],
        joined(gate_sum),
        joined(up_sum),
        joined(down_sum).T,
    )


def solution(mesh):
    placed = (
        P(("dp", "tensor"), None),
        P(("dp", "tensor"), None),
        P(),
        P("dp"),
        P("dp", "tensor"),
        P("dp", "tensor"),
        P(None, "tensor", "dp"),
        P("tensor", "dp", None),
        P("tensor", "dp", None),
        P("tensor", "dp"),
        P("tensor", "dp"),
        P("dp"),
        P("dp", "tensor"),
        P("dp", "tensor"),
        P("tensor", "dp"),
    )
    return jax.shard_map(
        shards,
        mesh=mesh,
        in_specs=placed,
        out_specs=(
            P(("dp", "tensor"), None),
            P(("dp", "tensor"), None),
            P("dp"),
            P("dp", "tensor"),
            P("dp", "tensor"),
            P(None, "tensor", "dp"),
            P("tensor", "dp", None),
            P("tensor", "dp", None),
            P("tensor", "dp"),
            P("tensor", "dp"),
            P("dp"),
            P("dp", "tensor"),
            P("dp", "tensor"),
            P("tensor", "dp"),
        ),
        check_vma=False,
    )
```

```python
import functools

import jax
import jax.numpy as jnp
from jax import lax
from jax.experimental import pallas as pl
from jax.experimental.pallas import tpu as pltpu
from jax.sharding import PartitionSpec as P

TAPS = 4
EPSILON = 1e-06
GUARD = 0.001
GELU_SCALE = 0.7978845608028654
GELU_CUBE = 0.044715
MESH = pl.DeviceIdType.MESH
F32, BF16 = jnp.float32, jnp.bfloat16
ANY = pl.BlockSpec(memory_space=pl.ANY)
VMEM = pl.BlockSpec(memory_space=pltpu.VMEM)
GRANT = 60 * 1024 * 1024
NT = (((1,), (1,)), ((), ()))
TN = (((0,), (0,)), ((), ()))
CHUNK = 256


def spot():
    dp, tensor = lax.axis_index("dp"), lax.axis_index("tensor")
    return dp // 2, dp % 2, tensor // 2, tensor % 2


def seat(line, side, deck, core):
    return (line * 2 + side, deck * 2 + core)


def rank(side, deck, core):
    return side * 4 + deck * 2 + core


def greet(peers):
    barrier = pltpu.get_barrier_semaphore()
    for peer in peers:
        pl.semaphore_signal(barrier, inc=1, device_id=peer, device_id_type=MESH)
    pl.semaphore_wait(barrier, len(peers))


def remote(source, target, send, receive, peer):
    return pltpu.make_async_remote_copy(
        src_ref=source,
        dst_ref=target,
        send_sem=send,
        recv_sem=receive,
        device_id=peer,
        device_id_type=MESH,
    )


def line_peers(count):
    line, side, deck, core = spot()
    return [seat((line + k) % count, side, deck, core) for k in range(1, count)]


def group_peers():
    line, side, deck, core = spot()
    return [
        seat(line, side, deck, 1 - core),
        seat(line, 1 - side, deck, core),
        seat(line, side, 1 - deck, core),
    ]


class Freight:
    def __init__(self, count, halves, target, sems, start=0):
        self.count, self.halves, self.target = count, halves, target
        self.start_column = start
        self.cross, self.local, self.send, self.receive = sems
        self.line, self.side, self.deck, self.core = spot()

    @staticmethod
    def scratch(count):
        steps = 5 if count == 4 else count - 1
        return [
            pltpu.SemaphoreType.DMA((2,)),
            pltpu.SemaphoreType.DMA,
            pltpu.SemaphoreType.DMA((steps, 2)),
            pltpu.SemaphoreType.DMA((count, 2)),
        ]

    def half(self, which):
        if len(self.halves.shape) == 3:
            return self.halves.at[which]
        offset = which * (self.halves.shape[1] // 2) + self.start_column
        return self.halves.at[:, pl.ds(pl.multiple_of(offset, 128), self.target.shape[2])]

    def place(self, origin, part):
        rows = self.target.shape[1] // 2
        return self.target.at[origin, pl.ds(pl.multiple_of(part * rows, rows), rows)]

    def seat(self, line):
        return seat(line, self.side, self.deck, self.core)

    def swap(self):
        return remote(
            self.half(1 - self.side),
            self.place(self.line, self.side),
            self.cross.at[0],
            self.cross.at[1],
            seat(self.line, 1 - self.side, self.deck, self.core),
        )

    def keep(self):
        return pltpu.make_async_copy(
            self.half(self.side), self.place(self.line, self.side), self.local
        )

    def copy(self, origin, line, index, part, source):
        return remote(
            source,
            self.place(origin, part),
            self.send.at[index, part],
            self.receive.at[origin, part],
            self.seat(line),
        )

    def own(self, line, index, part):
        source = self.half(self.side)
        if part is not self.side:
            source = self.place(self.line, part)
        return self.copy(self.line, line, index, part, source)

    def arrival(self, origin, part):
        return self.copy(origin, origin, 0, part, self.half(self.side))

    def each_step(self, action, phases=(0, 1)):
        if self.count == 4:
            line = self.line
            for index, step in enumerate((1, -1, 2, -2)):
                if index == 0:
                    when = [line == 2, line < 2]
                elif index == 1:
                    when = [line == 1, line > 1]
                else:
                    when = [(line + step >= 0) & (line + step < 4), None]
                for phase in phases:
                    if when[phase] is not None:

                        @pl.when(when[phase])
                        def _(index=index, step=step):
                            action(index, line + step)

        elif 0 in phases:
            for step in range(1, self.count):
                action(step - 1, (self.line + step) % self.count)

    def start(self):
        self.swap().start()
        self.each_step(lambda index, line: self.own(line, index, self.side).start(), (0,))
        self.keep().start()

    def second(self):
        self.swap().wait_recv()
        self.each_step(lambda index, line: self.own(line, index, 1 - self.side).start(), (0,))

    def middle(self, action):
        if self.count == 4:

            @pl.when((self.line == 1) | (self.line == 2))
            def _():
                action(6 - 3 * self.line, 3 * self.line - 3)

    def onward(self, origin, line, part):
        return self.copy(origin, line, 4, part, self.place(origin, part))

    def forward(self):
        for part in (self.side, 1 - self.side):
            self.each_step(
                lambda index, line, part=part: self.own(line, index, part).start(), (1,)
            )

            def action(origin, line, part=part):
                self.arrival(origin, part).wait_recv()
                self.onward(origin, line, part).start()

            self.middle(action)

    def finish(self):
        for part in (self.side, 1 - self.side):
            self.each_step(
                lambda index, line, part=part: self.own(line, index, part).wait_send()
            )
            self.middle(
                lambda origin, line, part=part: self.onward(origin, line, part).wait_send()
            )
            for origin in range(self.count):
                pending = self.line != origin
                if self.count == 4 and origin == 0:
                    pending = pending & (self.line != 2)
                if self.count == 4 and origin == 3:
                    pending = pending & (self.line != 1)

                @pl.when(pending)
                def _(origin=origin, part=part):
                    self.arrival(origin, part).wait_recv()

        self.keep().wait()
        self.swap().wait_send()


def cargo_peers(count):
    return group_peers() + line_peers(count)


def piece_shape(count, piece):
    if isinstance(piece, tuple):
        return count, 2 * piece[0].shape[0], piece[2]
    return count, 2 * piece.shape[1], piece.shape[2]


def cargo_outs(count, cargo):
    return [(piece_shape(count, piece), BF16, ANY) for piece in cargo]


def cargo_ins(cargo):
    return [(piece[0] if isinstance(piece, tuple) else piece, ANY) for piece in cargo]


def cargo_starts(cargo):
    return [piece[1] if isinstance(piece, tuple) else 0 for piece in cargo]


def cargo_scratch(count, cargo):
    return [sem for _ in cargo for sem in Freight.scratch(count)]


def load(count, starts, halves, targets, sems):
    return [
        Freight(count, half, target, sems[4 * k : 4 * k + 4], starts[k])
        for k, (half, target) in enumerate(zip(halves, targets))
    ]


def flat_rows(values):
    return [value.reshape(-1, value.shape[2]) for value in values]


def call(kernel, outs, ins, scratch, identity, name):
    results = pl.pallas_call(
        kernel,
        out_shape=[jax.ShapeDtypeStruct(shape, kind) for shape, kind, _ in outs],
        in_specs=[space for _, space in ins],
        out_specs=[space for _, _, space in outs],
        scratch_shapes=scratch,
        compiler_params=pltpu.CompilerParams(
            collective_id=identity, has_side_effects=True, vmem_limit_bytes=GRANT
        ),
        name=name,
    )(*[value for value, _ in ins])
    return list(results)


class GroupGather:
    def __init__(self, source, target, send, receive, local):
        self.source, self.target = source, target
        self.send, self.receive = send, receive
        self.local = local
        self.here = spot()

    @staticmethod
    def scratch():
        return [
            pltpu.SemaphoreType.DMA((11,)),
            pltpu.SemaphoreType.DMA((11,)),
            pltpu.SemaphoreType.DMA,
        ]

    def half(self, ref, h):
        rows = self.source.shape[0] // 2
        return ref.at[pl.ds(h * rows, rows)]

    def make(self):
        line, side, deck, core = self.here
        sibling, across, above = group_peers()
        mine = rank(side, deck, core)
        beside = rank(1 - side, deck, core)
        over = rank(side, 1 - deck, core)
        corner = rank(1 - side, 1 - deck, core)

        def own(h, peer, index):
            return remote(
                self.half(self.source, h),
                self.half(self.target.at[mine], h),
                self.send.at[index],
                self.receive.at[index],
                peer,
            )

        def relay(block, h, peer, index):
            ref = self.half(self.target.at[block], h)
            return remote(ref, ref, self.send.at[index], self.receive.at[index], peer)

        self.keep = pltpu.make_async_copy(self.source, self.target.at[mine], self.local)
        self.first = [
            own(0, across, 0),
            own(1, above, 1),
            own(0, above, 2),
            own(1, across, 3),
        ]
        self.near = remote(
            self.source, self.target.at[mine], self.send.at[4], self.receive.at[4], sibling
        )
        self.second = [relay(beside, 0, above, 5), relay(over, 1, across, 6)]
        self.last = [
            relay(beside, 0, sibling, 7),
            relay(over, 1, sibling, 8),
            relay(over, 0, sibling, 9),
            relay(beside, 1, sibling, 10),
        ]
        self.corner = corner

    def start(self):
        self.make()
        for copy in self.first:
            copy.start()
        self.near.start()
        self.keep.start()

    def forward(self):
        for k in range(2):
            self.first[k].wait_recv()
            self.second[k].start()
            self.last[k].start()
        for k in range(2, 4):
            self.first[k].wait_recv()
            self.last[k].start()


def corner_relay(gather, send, receive):
    sibling = group_peers()[0]
    out = []
    for h in range(2):
        ref = gather.half(gather.target.at[gather.corner], h)
        out.append(remote(ref, ref, send.at[h], receive.at[h], sibling))
    return out


def group_finish(gather, send, receive):
    relays = corner_relay(gather, send, receive)
    for k in range(2):
        gather.second[k].wait_recv()
        relays[k].start()
    gather.keep.wait()
    gather.near.wait()
    for copy in gather.first:
        copy.wait_send()
    for copy in gather.second:
        copy.wait_send()
    for copy in gather.last:
        copy.wait()
    for copy in relays:
        copy.wait()


def rows_scratch():
    return GroupGather.scratch() + [
        pltpu.SemaphoreType.DMA((2,)),
        pltpu.SemaphoreType.DMA((2,)),
    ]


SMALL_GAINS = 5


def first_kernel(count, starts, small_top, *refs):
    loads = len(starts)
    rows, small = refs[:2]
    halves, refs = refs[2 : 2 + loads], refs[2 + loads :]
    everything, everyone, normed, pre = refs[:4]
    targets, refs = refs[4 : 4 + loads], refs[4 + loads :]
    incoming, table, weights, incoming_sems, out_sems, weight_sems = refs[:6]
    sems = refs[6:]
    dp, tensor = lax.axis_index("dp"), lax.axis_index("tensor")
    gather = GroupGather(rows, everything, *sems[:3])
    corner = sems[3:5]
    send, receive, local = sems[5:8]
    freights = load(count, starts, halves, targets, sems[8:])
    shares = 2 * count
    line, side, deck, core = spot()
    greet(
        [((dp + k) % shares, tensor) for k in range(1, shares)]
        + [seat(line, side, deck, 1 - core), seat(line, side, 1 - deck, core)]
    )
    copies = [
        remote(
            small.at[(dp + k) % 2],
            everyone.at[dp],
            send.at[k],
            receive.at[k],
            ((dp + k) % shares, tensor),
        )
        for k in range(1, shares)
    ]
    copies.append(pltpu.make_async_copy(small.at[side], everyone.at[dp], local))
    freights[0].start()
    gather.start()
    for copy in copies:
        copy.start()
    for freight in freights[1:]:
        freight.start()
    for freight in freights:
        freight.second()
    gather.forward()
    freights[0].forward()
    group_finish(gather, *corner)
    for copy in copies:
        copy.wait()

    block_rows, features = rows.shape

    def fetch(g):
        slot = g % 2
        return pltpu.make_async_copy(
            everything.at[g], incoming.at[slot], incoming_sems.at[slot]
        )

    gain = jnp.concatenate(
        [
            everyone[k, small_top : small_top + 16, : features // shares].astype(F32)[
                SMALL_GAINS : SMALL_GAINS + 1
            ]
            for k in range(shares)
        ],
        axis=1,
    )
    fetch(0).start()
    for g in range(8):
        fetch(g).wait()
        if g < 7:
            fetch(g + 1).start()

        def norm_rows(i, carry, g=g):
            r = pl.multiple_of(i * 32, 32)
            value = incoming[g % 2, pl.ds(r, 32), :].astype(F32)
            mean = jnp.mean(value * value, axis=1, keepdims=True)
            unit = value * lax.rsqrt(mean + EPSILON)
            table[pl.ds(g * block_rows + r, 32), :] = (unit * gain).astype(BF16)
            return carry

        lax.fori_loop(0, block_rows // 32, norm_rows, 0)
        pltpu.make_async_copy(
            table.at[pl.ds(g * block_rows, block_rows)],
            normed.at[pl.ds(g * block_rows, block_rows)],
            out_sems.at[g],
        ).start()
    for freight in freights[1:]:
        freight.forward()
    freights[0].finish()
    depth = targets[0].shape[1]
    loading = [
        pltpu.make_async_copy(
            targets[0].at[k], weights.at[pl.ds(k * depth, depth)], weight_sems.at[k]
        )
        for k in range(count)
    ]
    for copy in loading:
        copy.start()
    for copy in loading:
        copy.wait()
    lanes, width = weights.shape[1] // 2, pre.shape[1] // 2
    shift = lanes - (2 * lanes - width)
    inside = lax.broadcasted_iota(jnp.int32, (CHUNK, width), 1) < lanes

    def product(r):
        where = pl.ds(r, CHUNK)
        both = jnp.dot(table[where, :], weights[...], preferred_element_type=F32)
        pre[where, :width] = jnp.where(inside, both[:, :width], 0.0)
        later = pltpu.roll(both[:, 2 * lanes - width :], width - shift, 1)
        pre[where, width:] = jnp.where(inside, later, 0.0)

    chunks(pre.shape[0], product)
    for g in range(8):
        pltpu.make_async_copy(
            table.at[pl.ds(g * block_rows, block_rows)],
            normed.at[pl.ds(g * block_rows, block_rows)],
            out_sems.at[g],
        ).wait()
    for freight in freights[1:]:
        freight.finish()


def first(count, rows, small, cargo, width):
    shares = 2 * count
    total = 8 * rows.shape[0]
    out = call(
        functools.partial(first_kernel, count, cargo_starts(cargo), small.shape[1] - 16),
        [
            ((8,) + rows.shape, BF16, ANY),
            ((shares,) + small.shape[1:], BF16, VMEM),
            ((total, rows.shape[1]), BF16, ANY),
            ((total, 2 * width), F32, VMEM),
        ]
        + cargo_outs(count, cargo),
        [(rows, ANY), (small, ANY)] + cargo_ins(cargo),
        [
            pltpu.VMEM((2,) + rows.shape, BF16),
            pltpu.VMEM((total, rows.shape[1]), BF16),
            pltpu.VMEM((rows.shape[1], cargo[0].shape[2]), BF16),
            pltpu.SemaphoreType.DMA((2,)),
            pltpu.SemaphoreType.DMA((8,)),
            pltpu.SemaphoreType.DMA((count,)),
        ]
        + rows_scratch()
        + [
            pltpu.SemaphoreType.DMA((shares,)),
            pltpu.SemaphoreType.DMA((shares,)),
            pltpu.SemaphoreType.DMA,
        ]
        + cargo_scratch(count, cargo),
        0,
        "first",
    )
    return out[1:4] + flat_rows(out[4:])


def rows_kernel(count, starts, *refs):
    loads = len(starts)
    rows, halves = refs[0], refs[1 : 1 + loads]
    everything, targets = refs[1 + loads], refs[2 + loads : 2 + 2 * loads]
    sems = refs[2 + 2 * loads :]
    gather = GroupGather(rows, everything, *sems[:3])
    freights = load(count, starts, halves, targets, sems[5:])
    greet(cargo_peers(count))
    gather.start()
    for freight in freights:
        freight.start()
    for freight in freights:
        freight.second()
    gather.forward()
    for freight in freights:
        freight.forward()
    group_finish(gather, *sems[3:5])
    for freight in freights:
        freight.finish()


def gather_rows(count, rows, cargo, identity):
    out = call(
        functools.partial(rows_kernel, count, cargo_starts(cargo)),
        [((8,) + rows.shape, BF16, ANY)] + cargo_outs(count, cargo),
        [(rows, ANY)] + cargo_ins(cargo),
        rows_scratch() + cargo_scratch(count, cargo),
        identity,
        "gather_rows",
    )
    return [out[0].reshape(-1, rows.shape[1])] + flat_rows(out[1:])


def plain_rows_kernel(rows, everything, *sems):
    gather = GroupGather(rows, everything, *sems[:3])
    greet(group_peers())
    gather.start()
    gather.forward()
    group_finish(gather, *sems[3:5])


def gather_plain(rows, identity):
    out = call(
        plain_rows_kernel,
        [((8,) + rows.shape, BF16, ANY)],
        [(rows, ANY)],
        rows_scratch(),
        identity,
        "gather_rows",
    )
    return out[0].reshape(-1, rows.shape[1])


def flip(value, bit):
    return 1 - value if bit else value


def whole_group():
    line, side, deck, core = spot()
    return [
        seat(line, flip(side, k & 4), flip(deck, k & 2), flip(core, k & 1)) for k in range(1, 8)
    ]


class GainSum:
    def __init__(self, count, gains, totals, near, far, send, receive, far_send, far_receive):
        self.gains, self.totals, self.near, self.far = gains, totals, near, far
        self.first = [
            remote(gains, near.at[k], send.at[k], receive.at[k], peer)
            for k, peer in enumerate(whole_group())
        ]
        self.second_copies = [
            remote(far.at[0], far.at[1 + k], far_send.at[k], far_receive.at[k], peer)
            for k, peer in enumerate(line_peers(count))
        ]

    @staticmethod
    def scratch(count, gains):
        return [
            pltpu.VMEM((7,) + gains.shape, F32),
            pltpu.VMEM((count,) + gains.shape, F32),
            pltpu.SemaphoreType.DMA((7,)),
            pltpu.SemaphoreType.DMA((7,)),
            pltpu.SemaphoreType.DMA((count,)),
            pltpu.SemaphoreType.DMA((count,)),
        ]

    def start(self):
        for copy in self.first:
            copy.start()

    def second(self):
        for copy in self.first:
            copy.wait()
        total = self.gains[...]
        for k in range(7):
            total = total + self.near[k]
        self.far[0] = total
        for copy in self.second_copies:
            copy.start()

    def finish(self):
        for copy in self.second_copies:
            copy.wait()
        total = self.far[0]
        for k in range(len(self.second_copies)):
            total = total + self.far[1 + k]
        self.totals[...] = total


def fold_kernel(count, plan, starts, gained, *refs):
    loads = len(starts)
    lefts = refs[: plan[-1][0] + 1]
    rights = refs[len(lefts) : len(lefts) + len(plan)]
    refs = refs[len(lefts) + len(rights) :]
    halves, refs = refs[:loads], refs[loads:]
    gains = None
    if gained:
        gains, refs = refs[0], refs[1:]
    out, refs = refs[0], refs[1:]
    targets, refs = refs[:loads], refs[loads:]
    if gained:
        totals, refs = refs[0], refs[1:]
        gain_sum = GainSum(count, gains, totals, *refs[-6:])
    mine, stage, near, leaving, arriving, refs = *refs[:5], refs[5:]
    send, receive, near_send, near_receive = refs[:4]
    line, side, deck, core = spot()
    sibling, across, above = group_peers()
    freights = load(count, starts, halves, targets, refs[4:])
    if gained:
        greet(whole_group() + line_peers(count))
        gain_sum.start()
    else:
        greet(cargo_peers(count) if loads else group_peers())
    for freight in freights:
        freight.start()
    rows = out.shape[0]
    half = rows // 2
    width = out.shape[1]
    step = 512

    def product(which, store):
        base = pl.multiple_of(which * rows, rows)

        def body(j, carry):
            columns = pl.ds(pl.multiple_of(j * step, step), step)
            total = None
            for (which_left, start), right in zip(plan, rights):
                part = lax.dot_general(
                    lefts[which_left][pl.ds(base, rows), start : start + right.shape[1]],
                    right[columns, :],
                    NT,
                    preferred_element_type=F32,
                )
                total = part if total is None else total + part
            store(columns, total)
            return carry

        lax.fori_loop(0, width // step, body, 0)

    def sweep(action):
        def body(i, carry):
            action(pl.multiple_of(i * 16, 16))
            return carry

        lax.fori_loop(0, half // 16, body, 0)

    def chip_sum(q, h, r):
        place = pl.ds(h * half + r, 16)
        return mine[q, place, :] + near[q, place, :].astype(F32)

    def ship(index, peer):
        return remote(
            leaving.at[index], arriving.at[index], send.at[index], receive.at[index], peer
        )

    ships = [ship(k, peer) for k, peer in enumerate((above, across, above, across, across, above))]
    OWN, ACROSS, ABOVE, CORNER = 0, 1, 2, 3
    seats = {
        CORNER: (1 - side, 1 - deck),
        ABOVE: (side, 1 - deck),
        ACROSS: (1 - side, deck),
        OWN: (side, deck),
    }
    nears = []
    for q in (CORNER, ABOVE, ACROSS, OWN):
        s, d = seats[q]

        def put_stage(columns, total, q=q):
            stage[q, :, columns] = total.astype(BF16)

        def put_mine(columns, total, q=q):
            mine[q, :, columns] = total

        product(rank(s, d, 1 - core), put_stage)
        copy = remote(stage.at[q], near.at[q], near_send.at[q], near_receive.at[q], sibling)
        copy.start()
        nears.append(copy)
        product(rank(s, d, core), put_mine)
        copy.wait_recv()
        if q == CORNER:

            def corner_sum(r):
                for h in range(2):
                    leaving[h, pl.ds(r, 16), :] = chip_sum(CORNER, h, r).astype(BF16)

            sweep(corner_sum)
            ships[0].start()
            ships[1].start()
        if q == ABOVE:

            def above_sum(r):
                leaving[2, pl.ds(r, 16), :] = chip_sum(ABOVE, 0, r).astype(BF16)

            sweep(above_sum)
            ships[2].start()
            for freight in freights:
                freight.second()
            if gained:
                gain_sum.second()
        if q == ACROSS:

            def across_sum(r):
                leaving[3, pl.ds(r, 16), :] = chip_sum(ACROSS, 1, r).astype(BF16)

            sweep(across_sum)
            ships[3].start()
    ships[0].wait_recv()

    def pass_across(r):
        total = chip_sum(ACROSS, 0, r) + arriving[0, pl.ds(r, 16), :].astype(F32)
        leaving[4, pl.ds(r, 16), :] = total.astype(BF16)

    sweep(pass_across)
    ships[4].start()
    ships[1].wait_recv()

    def pass_above(r):
        total = chip_sum(ABOVE, 1, r) + arriving[1, pl.ds(r, 16), :].astype(F32)
        leaving[5, pl.ds(r, 16), :] = total.astype(BF16)

    sweep(pass_above)
    ships[5].start()
    for freight in freights:
        freight.forward()
    if gained:
        gain_sum.finish()
    for k in range(2, 6):
        ships[k].wait_recv()

    def finish(r):
        place = pl.ds(r, 16)
        first = arriving[2, place, :].astype(F32) + arriving[4, place, :].astype(F32)
        out[place, :] = chip_sum(OWN, 0, r) + first
        second = arriving[3, place, :].astype(F32) + arriving[5, place, :].astype(F32)
        out[pl.ds(half + r, 16), :] = chip_sum(OWN, 1, r) + second

    sweep(finish)
    for k in range(6):
        ships[k].wait_send()
    for copy in nears:
        copy.wait_send()
    for freight in freights:
        freight.finish()


def fold(count, pairs, identity, cargo=(), gains=None):
    lefts, rights, plan = [], [], []
    for k, (left, parts) in enumerate(pairs):
        lefts.append(left)
        start = 0
        for part in parts:
            rights.append(part)
            plan.append((k, start))
            start += part.shape[1]
    rows, width = lefts[0].shape[0] // 8, rights[0].shape[0]
    outs = [((rows, width), F32, VMEM)]
    ins = [(value, VMEM) for value in list(lefts) + list(rights)]
    scratch = [
        pltpu.VMEM((4, rows, width), F32),
        pltpu.VMEM((4, rows, width), BF16),
        pltpu.VMEM((4, rows, width), BF16),
        pltpu.VMEM((6, rows // 2, width), BF16),
        pltpu.VMEM((6, rows // 2, width), BF16),
        pltpu.SemaphoreType.DMA((6,)),
        pltpu.SemaphoreType.DMA((6,)),
        pltpu.SemaphoreType.DMA((4,)),
        pltpu.SemaphoreType.DMA((4,)),
    ]
    outs += cargo_outs(count, cargo)
    ins += cargo_ins(cargo)
    scratch += cargo_scratch(count, cargo)
    if gains is not None:
        outs.append((gains.shape, F32, VMEM))
        ins.append((gains, VMEM))
        scratch += GainSum.scratch(count, gains)
    out = call(
        functools.partial(fold_kernel, count, plan, cargo_starts(cargo), gains is not None),
        outs,
        ins,
        scratch,
        identity,
        "fold",
    )
    if gains is not None:
        return out
    return out[:1] + flat_rows(out[1:])


def gelu_both(value):
    square = value * value
    bend = jnp.tanh(GELU_SCALE * value * (1.0 + GELU_CUBE * square))
    act = 0.5 * value * (1.0 + bend)
    slope = 0.5 * (1.0 + bend) + 0.5 * value * (1.0 - bend * bend) * GELU_SCALE * (
        1.0 + 3.0 * GELU_CUBE * square
    )
    return act, slope


def chunks(rows, action, size=CHUNK):
    def body(i, carry):
        action(pl.multiple_of(i * size, size))
        return carry

    lax.fori_loop(0, rows // size, body, 0)


def spans(low, high, action):
    def body(i, carry):
        action(pl.multiple_of(i * CHUNK, CHUNK))
        return carry

    lax.fori_loop(low, high, body, 0)


def tile_scan(mults, adds, rows, width, backward):
    place = lax.broadcasted_iota(jnp.int32, (8, width), 0)

    def inside(base):
        where = pl.ds(base, 8)
        a, b = mults[where, :], adds[where, :]
        for k in (1, 2, 4):
            if backward:
                away, mask = pltpu.roll(a, 8 - k, 0), place < 8 - k
                back = pltpu.roll(b, 8 - k, 0)
            else:
                away, mask = pltpu.roll(a, k, 0), place >= k
                back = pltpu.roll(b, k, 0)
            b = jnp.where(mask, b + a * back, b)
            a = jnp.where(mask, a * away, a)
        return where, a, b

    unroll = 4
    tiles = rows // 8

    def body(i, carry):
        prod, total = carry
        work = []
        for u in range(unroll):
            index = i * unroll + u
            if backward:
                index = tiles - 1 - index
            work.append(inside(pl.multiple_of(index * 8, 8)))
        for where, a, b in work:
            edge = 0 if backward else 7
            adds[where, :] = b + a * total
            mults[where, :] = a * prod
            whole = jnp.broadcast_to(a[edge : edge + 1, :], (8, width))
            extra = jnp.broadcast_to(b[edge : edge + 1, :], (8, width))
            total = extra + whole * total
            prod = whole * prod
        return prod, total

    return lax.fori_loop(
        0, tiles // unroll, body, (jnp.ones((8, width), F32), jnp.zeros((8, width), F32))
    )


def pool(count, prod, total, outgoing, slots, send, receive, backward):
    line, side, deck, core = spot()
    outgoing[0:8, :] = prod
    outgoing[8:16, :] = total
    slots[line, 0:8, :] = prod
    slots[line, 8:16, :] = total
    copies = []
    for k in range(1, count):
        copy = remote(
            outgoing,
            slots.at[line],
            send.at[k],
            receive.at[k],
            seat((line + k) % count, side, deck, core),
        )
        copy.start()
        copies.append(copy)
    for copy in copies:
        copy.wait()
    entering = jnp.zeros_like(prod)
    order = range(count - 1, -1, -1) if backward else range(count)
    for place in order:
        longer = slots[place, 8:16, :] + slots[place, 0:8, :] * entering
        before = (line < place) if backward else (line > place)
        entering = jnp.where(before, longer, entering)
    return entering


def sigmoid(value):
    return 0.5 + 0.5 * jnp.tanh(0.5 * value)


def gates(recur, soft):
    decay = jnp.exp(-8.0 * recur * soft)
    square = (1.0 + GUARD) - decay * decay
    inverse = lax.rsqrt(square)
    return decay, square * inverse, inverse


def scan_kernel(count, starts, *refs):
    loads = len(starts)
    pre, masks, table, gate_weights, cotangent = refs[:5]
    halves, refs = refs[5 : 5 + loads], refs[5 + loads :]
    conv, recur_out, admit_out, state, merged, entry, everything = refs[:7]
    targets, refs = refs[7 : 7 + loads], refs[7 + loads :]
    prods, sums, halo, outgoing, slots, edge_sems, send, receive = refs[:8]
    sems = refs[8:]
    line, side, deck, core = spot()
    rows, width = conv.shape
    gather = GroupGather(cotangent, everything, *sems[:3])
    freights = load(count, starts, halves, targets, sems[5:])
    greet(cargo_peers(count))

    def edge(place):
        return remote(
            pre.at[pl.ds(rows - 8, 8), pl.ds(width, width)],
            halo,
            edge_sems.at[0],
            edge_sems.at[1],
            seat(place, side, deck, core),
        )

    @pl.when(line < count - 1)
    def _():
        edge(line + 1).start()

    for freight in freights:
        freight.start()
    gather.start()

    def copy_entry(r):
        entry[pl.ds(r + 8, CHUNK), :] = pre[pl.ds(r, CHUNK), width:]

    chunks(rows, copy_entry)

    @pl.when(line > 0)
    def _():
        edge(line - 1).wait_recv()
        entry[0:8, :] = halo[...]

    @pl.when(line == 0)
    def _():
        entry[0:8, :] = jnp.zeros((8, width), F32)

    @pl.when(line < count - 1)
    def _():
        edge(line + 1).wait_send()

    def gate_chunk(r):
        wide = entry[pl.ds(r, CHUNK + 8), :]
        mask = masks[pl.ds(r, CHUNK), :]
        value = table[0:1, :] * wide[8:, :]
        for k in range(1, TAPS):
            value = (
                value + table[k : k + 1, :] * wide[8 - k : 8 - k + CHUNK, :] * mask[:, k - 1 : k]
            )
        where = pl.ds(r, CHUNK)
        conv[where, :] = value
        both = jnp.dot(value.astype(BF16), gate_weights[...], preferred_element_type=F32)
        recur = sigmoid(both[:, :width])
        admit = sigmoid(both[:, width:])
        recur_out[where, :] = recur
        admit_out[where, :] = admit
        decay, root, _ = gates(recur, table[4:5, :])
        opened = mask[:, 3:4]
        norm = root * opened + (1.0 - opened)
        prods[where, :] = decay * opened
        sums[where, :] = norm * admit * value

    spans(0, rows // CHUNK // 2, gate_chunk)
    for freight in freights:
        freight.second()
    spans(rows // CHUNK // 2, rows // CHUNK, gate_chunk)
    gather.forward()
    prod, total = tile_scan(prods, sums, rows, width, False)
    entering = pool(count, prod, total, outgoing, slots, send, receive, False)
    for freight in freights:
        freight.forward()
    state[0:8, :] = entering

    def state_chunk(r):
        where = pl.ds(r, CHUNK)
        value = sums[where, :] + prods[where, :] * entering[0:1, :]
        state[pl.ds(r + 8, CHUNK), :] = value
        act, _ = gelu_both(pre[where, :width])
        merged[where, :] = (value * act).astype(BF16)

    chunks(rows, state_chunk)
    group_finish(gather, *sems[3:5])
    for freight in freights:
        freight.finish()


def scan_forward(count, pre, masks, table, gate_weights, cotangent, cargo):
    rows, width = pre.shape[0], pre.shape[1] // 2
    out = call(
        functools.partial(scan_kernel, count, cargo_starts(cargo)),
        [
            ((rows, width), F32, VMEM),
            ((rows, width), F32, VMEM),
            ((rows, width), F32, VMEM),
            ((rows + 8, width), F32, VMEM),
            ((rows, width), BF16, VMEM),
            ((rows + 8, width), F32, VMEM),
            ((8,) + cotangent.shape, BF16, ANY),
        ]
        + cargo_outs(count, cargo),
        [(pre, VMEM), (masks, VMEM), (table, VMEM), (gate_weights, VMEM), (cotangent, ANY)]
        + cargo_ins(cargo),
        [
            pltpu.VMEM((rows, width), F32),
            pltpu.VMEM((rows, width), F32),
            pltpu.VMEM((8, width), F32),
            pltpu.VMEM((16, width), F32),
            pltpu.VMEM((count, 16, width), F32),
            pltpu.SemaphoreType.DMA((2,)),
            pltpu.SemaphoreType.DMA((count,)),
            pltpu.SemaphoreType.DMA((count,)),
        ]
        + rows_scratch()
        + cargo_scratch(count, cargo),
        2,
        "scan_forward",
    )
    return out[:6] + [out[6].reshape(-1, cotangent.shape[1])] + flat_rows(out[7:])


def back_kernel(
    count,
    pre,
    grad_merged,
    conv,
    recur_in,
    admit_in,
    state,
    entry,
    masks,
    table,
    gate_weights,
    grad_pre,
    grad_gates,
    grad_table,
    prods,
    sums,
    mixes,
    outgoing,
    slots,
    edge_sems,
    send,
    receive,
):
    line, side, deck, core = spot()
    rows, width = conv.shape
    greet(line_peers(count))

    def direct_chunk(r):
        where = pl.ds(r, CHUNK)
        act, slope = gelu_both(pre[where, :width])
        grad = grad_merged[where, :]
        grad_pre[where, :width] = (grad * state[pl.ds(r + 8, CHUNK), :] * slope).astype(BF16)
        direct = grad * act
        carry = jnp.exp(-8.0 * recur_in[where, :] * table[4:5, :]) * masks[where, 3:4]
        mixes[where, :] = direct
        prods[where, :] = carry
        sums[where, :] = carry * direct

    chunks(rows, direct_chunk)
    prods[rows : rows + 8, :] = jnp.ones((8, width), F32)
    sums[rows : rows + 8, :] = jnp.zeros((8, width), F32)
    prod, total = tile_scan(prods, sums, rows, width, True)
    entering = pool(count, prod, total, outgoing, slots, send, receive, True)
    grad_gates[...] = jnp.zeros_like(grad_gates)
    grad_table[...] = jnp.zeros_like(grad_table)

    def fold_rows(value):
        return jnp.sum(value, axis=0, keepdims=True)

    def gate_chunk(r):
        where = pl.ds(r, CHUNK)
        wide = pl.ds(r, CHUNK + 8)
        later = sums[wide, :] + prods[wide, :] * entering[0:1, :]
        grad = mixes[where, :] + later[1 : CHUNK + 1, :]
        before = state[wide, :][7 : CHUNK + 7, :]
        soft = table[4:5, :]
        recur, admit, value = recur_in[where, :], admit_in[where, :], conv[where, :]
        decay, root, inverse = gates(recur, soft)
        opened = masks[where, 3:4]
        norm = root * opened + (1.0 - opened)
        flow = grad * admit
        grad_log = opened * (grad * before * decay - flow * value * decay * decay * inverse)
        grad_table[4:5, :] += fold_rows(grad_log * (-8.0 * recur))
        grad_rate = (grad_log * (-8.0 * soft) * recur * (1.0 - recur)).astype(BF16)
        grad_inlet = (flow * norm * value * (1.0 - admit)).astype(BF16)
        both = jnp.concatenate([grad_rate, grad_inlet], axis=1)
        grad_gates[...] += lax.dot_general(
            value.astype(BF16), both, TN, preferred_element_type=F32
        )
        mixes[where, :] = flow * norm + lax.dot_general(
            both, gate_weights[...], NT, preferred_element_type=F32
        )

    gate_chunk(0)

    def edge(place):
        return remote(
            mixes.at[pl.ds(0, 8)],
            mixes.at[pl.ds(rows, 8)],
            edge_sems.at[0],
            edge_sems.at[1],
            seat(place, side, deck, core),
        )

    @pl.when(line > 0)
    def _():
        edge(line - 1).start()

    def other(i, carry):
        gate_chunk(pl.multiple_of(i * CHUNK, CHUNK))
        return carry

    lax.fori_loop(1, rows // CHUNK, other, 0)

    @pl.when(line < count - 1)
    def _():
        edge(line + 1).wait_recv()

    @pl.when(line == count - 1)
    def _():
        mixes[rows : rows + 8, :] = jnp.zeros((8, width), F32)

    def entry_chunk(r):
        where, wide = pl.ds(r, CHUNK), pl.ds(r, CHUNK + 8)
        ahead, mask = mixes[wide, :], masks[where, :]
        source = entry[wide, :]
        here = ahead[:CHUNK, :]
        total = table[0:1, :] * here
        grad_table[0:1, :] += fold_rows(here * source[8:, :])
        for k in range(1, TAPS):
            total = total + table[k : k + 1, :] * ahead[k : k + CHUNK, :] * mask[:, 3 + k : 4 + k]
            grad_table[k : k + 1, :] += fold_rows(
                here * source[8 - k : 8 - k + CHUNK, :] * mask[:, k - 1 : k]
            )
        grad_pre[where, width:] = total.astype(BF16)

    chunks(rows, entry_chunk)

    @pl.when(line > 0)
    def _():
        edge(line - 1).wait_send()


def scan_backward(count, pre, grad_merged, saved, masks, table, gate_weights):
    rows, width = grad_merged.shape
    values = [pre, grad_merged, *saved, masks, table, gate_weights]
    return call(
        functools.partial(back_kernel, count),
        [
            ((rows, 2 * width), BF16, VMEM),
            ((width, 2 * width), F32, VMEM),
            ((8, width), F32, VMEM),
        ],
        [(value, VMEM) for value in values],
        [
            pltpu.VMEM((rows + 8, width), F32),
            pltpu.VMEM((rows + 8, width), F32),
            pltpu.VMEM((rows + 8, width), F32),
            pltpu.VMEM((16, width), F32),
            pltpu.VMEM((count, 16, width), F32),
            pltpu.SemaphoreType.DMA((2,)),
            pltpu.SemaphoreType.DMA((count,)),
            pltpu.SemaphoreType.DMA((count,)),
        ],
        7,
        "scan_backward",
    )


def feed_kernel(count, early, starts, normed, cotangent, *refs):
    loads = len(starts)
    gate_parts, refs = refs[:2], refs[2:]
    up_parts, refs = refs[:2], refs[2:]
    down_parts, refs = refs[:early], refs[early:]
    halves, refs = refs[:loads], refs[loads:]
    hidden, grad_gating, grad_lifting = refs[:3]
    targets, refs = refs[3 : 3 + loads], refs[3 + loads :]
    table, acts, slopes, down, sems = *refs[:4], refs[4:]
    table_sem, down_sems = sems[:2]
    freights = load(count, starts, halves, targets, sems[2:])
    greet(cargo_peers(count))
    for freight in freights:
        freight.start()
    rows, width = hidden.shape
    pieces = rows // CHUNK
    first = pltpu.make_async_copy(normed, table, table_sem)
    first.start()
    first.wait()

    def forward_chunk(r):
        where = pl.ds(r, CHUNK)
        start = 0
        for gate_part, up_part in zip(gate_parts, up_parts):
            columns = slice(start, start + gate_part.shape[1])
            gating = jnp.dot(table[where, :], gate_part[...], preferred_element_type=F32)
            lifting = jnp.dot(table[where, :], up_part[...], preferred_element_type=F32)
            act, slope = gelu_both(gating)
            hidden[where, columns] = (act * lifting).astype(BF16)
            acts[where, columns] = act
            slopes[where, columns] = lifting * slope
            start += gate_part.shape[1]

    spans(0, pieces // 4, forward_chunk)
    for freight in freights:
        freight.second()
    spans(pieces // 4, pieces, forward_chunk)
    second = pltpu.make_async_copy(cotangent, table, table_sem)
    second.start()
    for freight in freights:
        freight.forward()
    for freight in freights:
        freight.finish()
    rows_in = down.shape[0] // count
    copies, start = [], 0
    for k, part in enumerate(down_parts):
        copies.append(
            pltpu.make_async_copy(
                part, down.at[:, pl.ds(start, part.shape[1])], down_sems.at[k]
            )
        )
        start += part.shape[1]
    for k, target in enumerate(targets):
        for place in range(count):
            copies.append(
                pltpu.make_async_copy(
                    target.at[place],
                    down.at[pl.ds(place * rows_in, rows_in), pl.ds(start, target.shape[2])],
                    down_sems.at[early + k * count + place],
                )
            )
        start += target.shape[2]
    for copy in copies:
        copy.start()
    second.wait()
    for copy in copies:
        copy.wait()

    def back_chunk(r):
        where = pl.ds(r, CHUNK)
        for start in range(0, width, width // 3):
            columns = slice(start, start + width // 3)
            grad = jnp.dot(table[where, :], down[:, columns], preferred_element_type=F32)
            grad_gating[where, columns] = (grad * slopes[where, columns]).astype(BF16)
            grad_lifting[where, columns] = (grad * acts[where, columns]).astype(BF16)

    chunks(rows, back_chunk)


def feed(count, normed, cotangent, gate_parts, up_parts, down_parts, cargo):
    rows = normed.shape[0]
    width = sum(part.shape[1] for part in gate_parts)
    out = call(
        functools.partial(feed_kernel, count, len(down_parts), cargo_starts(cargo)),
        [((rows, width), BF16, VMEM)] * 3 + cargo_outs(count, cargo),
        [(normed, ANY), (cotangent, ANY)]
        + [(part, VMEM) for part in list(gate_parts) + list(up_parts)]
        + [(part, ANY) for part in down_parts]
        + cargo_ins(cargo),
        [
            pltpu.VMEM(normed.shape, BF16),
            pltpu.VMEM((rows, width), F32),
            pltpu.VMEM((rows, width), F32),
            pltpu.VMEM((normed.shape[1], width), BF16),
            pltpu.SemaphoreType.DMA,
            pltpu.SemaphoreType.DMA((len(down_parts) + count * len(cargo),)),
        ]
        + cargo_scratch(count, cargo),
        5,
        "feed",
    )
    return out[:3] + flat_rows(out[3:])


def doc_index(places, doc_starts):
    return jnp.sum((doc_starts[None, :] <= places[:, None]).astype(jnp.int32), axis=1)


def norm_back(grad_unit, unit_rows, scale_rows):
    return scale_rows * (
        grad_unit - unit_rows * jnp.mean(grad_unit * unit_rows, axis=1, keepdims=True)
    )


def unit_norm(values):
    scale = lax.rsqrt(jnp.mean(values * values, axis=1, keepdims=True) + EPSILON)
    return values * scale, scale


def split_columns(value):
    rows, columns = value.shape
    return value.reshape(rows, 2, columns // 2).transpose(1, 0, 2)


def widen(value, width):
    return jnp.pad(value, [(0, 0)] * (value.ndim - 1) + [(0, width - value.shape[-1])])


def by_rows(left, right):
    return lax.dot_general(left, right, TN, preferred_element_type=F32).astype(BF16)


def shards(
    layer_input,
    out_grad,
    doc_starts,
    mixer_gain,
    branch_gate,
    branch_input,
    conv_taps,
    rate_gate,
    input_gate,
    decay_param,
    mixer_out,
    feed_gain,
    feed_gate,
    feed_up,
    feed_down,
):
    shares = lax.axis_size("dp")
    count = shares // 2
    side = lax.axis_index("dp") % 2
    slim, feature_count = mixer_gain.shape[0], layer_input.shape[1]
    heads, piece, head_width = rate_gate.shape
    half_heads = heads // 2
    lanes = half_heads * head_width
    width = -(-lanes // 128) * 128
    row_count = layer_input.shape[0]
    rows = row_count * 8
    line_groups = [[2 * k + s for k in range(count)] for s in range(2)]

    branch_halves = jnp.concatenate(
        [split_columns(branch_gate), split_columns(branch_input)], axis=2
    )
    mixer_halves = widen(split_columns(mixer_out.T), width)
    down_rows = feed_down.T
    narrow = feed_gate.shape[1] // 6
    broad = 2 * narrow

    mine = lax.axis_index("dp")
    blocks = jnp.concatenate(
        [
            jnp.stack(
                [
                    jnp.pad(
                        jnp.concatenate(
                            [
                                widen(jnp.pad(rate_gate[h], ((0, 0), (p, 0))), width),
                                widen(jnp.pad(input_gate[h], ((0, 0), (p, 0))), width),
                            ],
                            axis=1,
                        ),
                        ((0, 0), (0, 0)),
                    )
                    for h, p in [(s * half_heads + k, k * head_width) for k in range(half_heads)]
                ]
            ).reshape(1, half_heads * piece, 2 * width)
            for s in range(2)
        ]
    )
    own = jnp.concatenate([conv_taps, decay_param[None]], axis=0)
    own = jnp.pad(own, ((0, 0), (0, 0), (0, head_width - piece)))
    own = jnp.roll(own, mine * piece, axis=2)
    own = own.reshape(TAPS + 1, 2, lanes).transpose(1, 0, 2)
    gains_own = jnp.pad(
        jnp.stack([mixer_gain, feed_gain]), ((0, 16 - TAPS - 3), (0, 2 * width - slim))
    )
    tail = jnp.concatenate(
        [widen(own, 2 * width), jnp.broadcast_to(gains_own, (2,) + gains_own.shape)], axis=1
    )
    small_top = -(-half_heads * piece // 16) * 16
    small = jnp.concatenate(
        [jnp.pad(blocks, ((0, 0), (0, small_top - half_heads * piece), (0, 0))), tail], axis=1
    )

    small_all, normed_one, pre, branch_all, gate_first = first(
        count, layer_input, small, [branch_halves, (feed_gate, 0, narrow)], width
    )

    tails = small_all[:, small_top:].astype(F32)
    gain_first = tails[:, SMALL_GAINS, :slim].reshape(feature_count)
    gain_second = tails[:, SMALL_GAINS + 1, :slim].reshape(feature_count)
    sums = jnp.sum(tails[:, : TAPS + 1, :width], axis=0)
    decay_flat = sums[TAPS, :lanes]
    inside = (jnp.arange(width) < lanes)[None]
    table = jnp.concatenate(
        [
            sums[:TAPS],
            jnp.where(inside, jax.nn.softplus(-sums[TAPS:]), 0.0),
            jnp.zeros((3, width), F32),
        ]
    )
    gate_weights = (
        small_all[:, : half_heads * piece]
        .reshape(shares, half_heads, piece, 2 * width)
        .transpose(1, 0, 2, 3)
        .reshape(lanes, 2 * width)
    )
    gate_weights = jnp.pad(gate_weights, ((0, width - lanes), (0, 0)))

    anchor = lax.axis_index("dp") // 2 * rows
    places = anchor + jnp.arange(rows, dtype=jnp.int32)
    here = doc_index(places, doc_starts)
    columns = [doc_index(places - k, doc_starts) == here for k in range(1, TAPS)]
    columns.append(~jnp.any(doc_starts[None, :] == places[:, None], axis=1))
    columns += [doc_index(places + k, doc_starts) == here for k in range(1, TAPS)]
    columns.append(columns[0])
    masks = jnp.stack(columns, axis=1).astype(F32)

    residual = layer_input.astype(F32)
    unit_one, scale_one = unit_norm(residual)
    branch_wide = jnp.concatenate(
        [widen(branch_all[:, :lanes], width), widen(branch_all[:, lanes:], width)], axis=1
    )
    conv, recur, admit, state, merged, entry, cot_all, mixer_all, up_first = scan_forward(
        count, pre, masks, table, gate_weights, out_grad, [mixer_halves, (feed_up, 0, narrow)]
    )
    mixer_own, gate_second, down_first = fold(
        count, [(merged, [mixer_all])], 3, [(feed_gate, narrow, broad), (down_rows, 0, narrow)]
    )
    hidden_one = residual + mixer_own
    unit_two, scale_two = unit_norm(hidden_one)
    normed_two, up_second = gather_rows(
        count, (unit_two * gain_second).astype(BF16), [(feed_up, narrow, broad)], 4
    )
    gate_parts, up_parts = [gate_first, gate_second], [up_first, up_second]
    hidden, grad_gating, grad_lifting, down_second = feed(
        count, normed_two, cot_all, gate_parts, up_parts, [down_first], [(down_rows, narrow, broad)]
    )
    down_parts = [down_first, down_second]

    def line_sum(value):
        return lax.psum_scatter(
            value, "dp", scatter_dimension=0, axis_index_groups=line_groups, tiled=True
        )

    down_grads = by_rows(cot_all, hidden)
    grad_gating, grad_lifting, down_grads = lax.optimization_barrier(
        (grad_gating, grad_lifting, down_grads)
    )
    gate_grads = by_rows(normed_two, grad_gating)
    up_grads = by_rows(normed_two, grad_lifting)
    grad_gating, grad_lifting, down_grads, gate_grads, up_grads = lax.optimization_barrier(
        (grad_gating, grad_lifting, down_grads, gate_grads, up_grads)
    )
    down_sum, gate_sum, up_sum = line_sum(down_grads), line_sum(gate_grads), line_sum(up_grads)
    grad_normed_two = fold(count, [(grad_gating, gate_parts), (grad_lifting, up_parts)], 6)[0]
    grad_hidden_one = out_grad.astype(F32) + norm_back(
        grad_normed_two * gain_second, unit_two, scale_two
    )
    grad_hidden_one, down_sum = lax.optimization_barrier((grad_hidden_one, down_sum))
    back_low = gather_plain(grad_hidden_one.astype(BF16), 8)
    outlet_grads = by_rows(back_low, merged)
    grad_merged = jnp.dot(back_low, mixer_all, preferred_element_type=F32)
    grad_merged, outlet_grads, gate_sum = lax.optimization_barrier(
        (grad_merged, outlet_grads, gate_sum)
    )
    outlet_sum = line_sum(outlet_grads)
    grad_pre, grad_gates, grad_table = scan_backward(
        count, pre, grad_merged, [conv, recur, admit, state, entry], masks, table, gate_weights
    )
    branch_grads = by_rows(normed_one, grad_pre)
    branch_grads = jnp.concatenate(
        [branch_grads[:, :lanes], branch_grads[:, width : width + lanes]], axis=1
    )
    grad_pre, branch_grads = lax.optimization_barrier((grad_pre, branch_grads))
    branch_sum = line_sum(branch_grads)
    grad_normed_one = fold(count, [(grad_pre, [branch_wide])], 10)[0]
    hidden, grad_normed_one, up_sum = lax.optimization_barrier(
        (hidden, grad_normed_one, up_sum)
    )
    gains = jnp.concatenate(
        [
            jnp.sum(grad_normed_one * unit_one, axis=0).reshape(shares, slim),
            jnp.sum(grad_normed_two * unit_two, axis=0).reshape(shares, slim),
        ]
    )
    feed_own, gains = fold(count, [(hidden, down_parts)], 9, gains=gains)
    first_gain_grad = lax.dynamic_index_in_dim(gains, mine, 0, False)
    second_gain_grad = lax.dynamic_index_in_dim(gains, shares + mine, 0, False)
    layer_output = (hidden_one + feed_own).astype(BF16)
    input_grad = (
        grad_hidden_one + norm_back(grad_normed_one * gain_first, unit_one, scale_one)
    ).astype(BF16)

    def spots(value):
        blocks = [
            value[
                h * head_width : (h + 1) * head_width, h * head_width : (h + 1) * head_width
            ].reshape(shares, -1)
            for h in range(half_heads)
        ]
        return jnp.concatenate(blocks, axis=1)

    grad_decay = -jax.nn.sigmoid(-decay_flat) * grad_table[4, :lanes]
    grad_small = jnp.concatenate(
        [
            spots(grad_gates[:, :width]),
            spots(grad_gates[:, width:]),
            grad_table[:TAPS, :lanes]
            .reshape(TAPS * half_heads, shares, piece)
            .transpose(1, 0, 2)
            .reshape(shares, -1),
            grad_decay.reshape(half_heads, shares, piece).transpose(1, 0, 2).reshape(shares, -1),
        ],
        axis=1,
    )
    flat_size = grad_small.shape[1]
    small_rows = -(-flat_size // (128 * 16)) * 16
    grad_small = widen(grad_small, small_rows * 128).reshape(shares * small_rows, 128)
    small_sum = line_sum(grad_small.astype(BF16)).astype(F32)

    def swap(value):
        pair = value.reshape(2, -1, value.shape[1])
        kept = lax.dynamic_index_in_dim(pair, side, 0, False)
        given = lax.dynamic_index_in_dim(pair, 1 - side, 0, False)
        other = lax.ppermute(given, "dp", [(k, k ^ 1) for k in range(shares)])
        first = jnp.where(side == 0, kept, other).astype(F32)
        second = jnp.where(side == 0, other, kept).astype(F32)
        return first, second

    def joined(value):
        return jnp.concatenate(swap(value), axis=1)

    branch_first, branch_second = swap(branch_sum)
    branch_gate_grad = jnp.concatenate([branch_first[:, :lanes], branch_second[:, :lanes]], axis=1)
    branch_input_grad = jnp.concatenate([branch_first[:, lanes:], branch_second[:, lanes:]], axis=1)
    outlet_first, outlet_second = swap(outlet_sum)
    mixer_out_grad = jnp.concatenate([outlet_first[:, :lanes], outlet_second[:, :lanes]], axis=1).T

    smalls = [value.reshape(-1)[:flat_size] for value in swap(small_sum.astype(BF16))]
    one = half_heads * piece * head_width
    tap_size = TAPS * half_heads * piece
    rate_grad = jnp.concatenate([v[:one].reshape(half_heads, piece, head_width) for v in smalls])
    inlet_grad = jnp.concatenate(
        [v[one : 2 * one].reshape(half_heads, piece, head_width) for v in smalls]
    )
    taps_grad = jnp.concatenate(
        [v[2 * one : 2 * one + tap_size].reshape(TAPS, half_heads, piece) for v in smalls], axis=1
    )
    decay_grad = jnp.concatenate(
        [v[2 * one + tap_size :].reshape(half_heads, piece) for v in smalls]
    )
    return (
        layer_output,
        input_grad,
        first_gain_grad,
        branch_gate_grad,
        branch_input_grad,
        taps_grad,
        rate_grad,
        inlet_grad,
        decay_grad,
        mixer_out_grad,
        second_gain_grad,
        joined(gate_sum),
        joined(up_sum),
        joined(down_sum).T,
    )


def solution(mesh):
    placed = (
        P(("dp", "tensor"), None),
        P(("dp", "tensor"), None),
        P(),
        P("dp"),
        P("dp", "tensor"),
        P("dp", "tensor"),
        P(None, "tensor", "dp"),
        P("tensor", "dp", None),
        P("tensor", "dp", None),
        P("tensor", "dp"),
        P("tensor", "dp"),
        P("dp"),
        P("dp", "tensor"),
        P("dp", "tensor"),
        P("tensor", "dp"),
    )
    return jax.shard_map(
        shards,
        mesh=mesh,
        in_specs=placed,
        out_specs=(
            P(("dp", "tensor"), None),
            P(("dp", "tensor"), None),
            P("dp"),
            P("dp", "tensor"),
            P("dp", "tensor"),
            P(None, "tensor", "dp"),
            P("tensor", "dp", None),
            P("tensor", "dp", None),
            P("tensor", "dp"),
            P("tensor", "dp"),
            P("dp"),
            P("dp", "tensor"),
            P("dp", "tensor"),
            P("tensor", "dp"),
        ),
        check_vma=False,
    )
```

```python
import functools

import jax
import jax.numpy as jnp
from jax import lax
from jax.experimental import pallas as pl
from jax.experimental.pallas import tpu as pltpu
from jax.sharding import PartitionSpec as P

TAPS = 4
EPSILON = 1e-06
GUARD = 0.001
GELU_SCALE = 0.7978845608028654
GELU_CUBE = 0.044715
MESH = pl.DeviceIdType.MESH
F32, BF16 = jnp.float32, jnp.bfloat16
ANY = pl.BlockSpec(memory_space=pl.ANY)
VMEM = pl.BlockSpec(memory_space=pltpu.VMEM)
GRANT = 60 * 1024 * 1024
NT = (((1,), (1,)), ((), ()))
TN = (((0,), (0,)), ((), ()))
CHUNK = 256


def spot():
    dp, tensor = lax.axis_index("dp"), lax.axis_index("tensor")
    return dp // 2, dp % 2, tensor // 2, tensor % 2


def seat(line, side, deck, core):
    return (line * 2 + side, deck * 2 + core)


def rank(side, deck, core):
    return side * 4 + deck * 2 + core


def greet(peers):
    barrier = pltpu.get_barrier_semaphore()
    for peer in peers:
        pl.semaphore_signal(barrier, inc=1, device_id=peer, device_id_type=MESH)
    pl.semaphore_wait(barrier, len(peers))


def remote(source, target, send, receive, peer):
    return pltpu.make_async_remote_copy(
        src_ref=source,
        dst_ref=target,
        send_sem=send,
        recv_sem=receive,
        device_id=peer,
        device_id_type=MESH,
    )


def line_peers(count):
    line, side, deck, core = spot()
    return [seat((line + k) % count, side, deck, core) for k in range(1, count)]


def group_peers():
    line, side, deck, core = spot()
    return [
        seat(line, side, deck, 1 - core),
        seat(line, 1 - side, deck, core),
        seat(line, side, 1 - deck, core),
    ]


class Freight:
    def __init__(self, count, halves, target, sems, start=0):
        self.count, self.halves, self.target = count, halves, target
        self.start_column = start
        self.cross, self.local, self.send, self.receive = sems
        self.line, self.side, self.deck, self.core = spot()

    @staticmethod
    def scratch(count):
        steps = 5 if count == 4 else count - 1
        return [
            pltpu.SemaphoreType.DMA((2,)),
            pltpu.SemaphoreType.DMA,
            pltpu.SemaphoreType.DMA((steps, 2)),
            pltpu.SemaphoreType.DMA((count, 2)),
        ]

    def half(self, which):
        if len(self.halves.shape) == 3:
            return self.halves.at[which]
        offset = which * (self.halves.shape[1] // 2) + self.start_column
        return self.halves.at[:, pl.ds(pl.multiple_of(offset, 128), self.target.shape[2])]

    def place(self, origin, part):
        rows = self.target.shape[1] // 2
        return self.target.at[origin, pl.ds(pl.multiple_of(part * rows, rows), rows)]

    def seat(self, line):
        return seat(line, self.side, self.deck, self.core)

    def swap(self):
        return remote(
            self.half(1 - self.side),
            self.place(self.line, self.side),
            self.cross.at[0],
            self.cross.at[1],
            seat(self.line, 1 - self.side, self.deck, self.core),
        )

    def keep(self):
        return pltpu.make_async_copy(
            self.half(self.side), self.place(self.line, self.side), self.local
        )

    def copy(self, origin, line, index, part, source):
        return remote(
            source,
            self.place(origin, part),
            self.send.at[index, part],
            self.receive.at[origin, part],
            self.seat(line),
        )

    def own(self, line, index, part):
        source = self.half(self.side)
        if part is not self.side:
            source = self.place(self.line, part)
        return self.copy(self.line, line, index, part, source)

    def arrival(self, origin, part):
        return self.copy(origin, origin, 0, part, self.half(self.side))

    def each_step(self, action, phases=(0, 1)):
        if self.count == 4:
            line = self.line
            for index, step in enumerate((1, -1, 2, -2)):
                if index == 0:
                    when = [line == 2, line < 2]
                elif index == 1:
                    when = [line == 1, line > 1]
                else:
                    when = [(line + step >= 0) & (line + step < 4), None]
                for phase in phases:
                    if when[phase] is not None:

                        @pl.when(when[phase])
                        def _(index=index, step=step):
                            action(index, line + step)

        elif 0 in phases:
            for step in range(1, self.count):
                action(step - 1, (self.line + step) % self.count)

    def start(self):
        self.swap().start()
        self.each_step(lambda index, line: self.own(line, index, self.side).start(), (0,))
        self.keep().start()

    def second(self):
        self.swap().wait_recv()
        self.each_step(lambda index, line: self.own(line, index, 1 - self.side).start(), (0,))

    def middle(self, action):
        if self.count == 4:

            @pl.when((self.line == 1) | (self.line == 2))
            def _():
                action(6 - 3 * self.line, 3 * self.line - 3)

    def onward(self, origin, line, part):
        return self.copy(origin, line, 4, part, self.place(origin, part))

    def forward(self):
        for part in (self.side, 1 - self.side):
            self.each_step(
                lambda index, line, part=part: self.own(line, index, part).start(), (1,)
            )

            def action(origin, line, part=part):
                self.arrival(origin, part).wait_recv()
                self.onward(origin, line, part).start()

            self.middle(action)

    def finish(self):
        for part in (self.side, 1 - self.side):
            self.each_step(
                lambda index, line, part=part: self.own(line, index, part).wait_send()
            )
            self.middle(
                lambda origin, line, part=part: self.onward(origin, line, part).wait_send()
            )
            for origin in range(self.count):
                pending = self.line != origin
                if self.count == 4 and origin == 0:
                    pending = pending & (self.line != 2)
                if self.count == 4 and origin == 3:
                    pending = pending & (self.line != 1)

                @pl.when(pending)
                def _(origin=origin, part=part):
                    self.arrival(origin, part).wait_recv()

        self.keep().wait()
        self.swap().wait_send()


class Stream:
    def __init__(self, source, target, sems, from_row=0, to_row=0, columns=None):
        self.source, self.target, self.sems = source, target, sems
        self.from_row, self.to_row, self.columns = from_row, to_row, columns
        self.pieces = sems.shape[0]

    def copy(self, r):
        source = (pl.ds(r + self.from_row, CHUNK),)
        if self.columns is not None:
            source += (self.columns,)
        return pltpu.make_async_copy(
            self.source.at[source],
            self.target.at[pl.ds(r + self.to_row, CHUNK)],
            self.sems.at[r // CHUNK],
        )

    def start(self, r):
        self.copy(r).start()

    def wait(self, r):
        self.copy(r).wait()

    def start_all(self):
        for k in range(self.pieces):
            self.start(k * CHUNK)

    def wait_all(self):
        for k in range(self.pieces):
            self.wait(k * CHUNK)


class Swap:
    def __init__(self, values, outs, send, receive, local):
        line, side, deck, core = spot()
        self.copies = []
        for k, (value, out) in enumerate(zip(values, outs)):
            self.copies.append(
                remote(
                    value.at[1 - side],
                    out.at[side],
                    send.at[k],
                    receive.at[k],
                    seat(line, 1 - side, deck, core),
                )
            )
            self.copies.append(
                pltpu.make_async_copy(value.at[side], out.at[side], local.at[k])
            )

    @staticmethod
    def scratch(values):
        return [pltpu.SemaphoreType.DMA((len(values),))] * 3 if values else []

    def start(self):
        for copy in self.copies:
            copy.start()

    def finish(self):
        for copy in self.copies:
            copy.wait()


def cargo_peers(count):
    return group_peers() + line_peers(count)


def piece_shape(count, piece):
    if isinstance(piece, tuple):
        return count, 2 * piece[0].shape[0], piece[2]
    return count, 2 * piece.shape[1], piece.shape[2]


def cargo_outs(count, cargo):
    return [(piece_shape(count, piece), BF16, ANY) for piece in cargo]


def cargo_ins(cargo):
    return [(piece[0] if isinstance(piece, tuple) else piece, ANY) for piece in cargo]


def cargo_starts(cargo):
    return [piece[1] if isinstance(piece, tuple) else 0 for piece in cargo]


def cargo_scratch(count, cargo):
    return [sem for _ in cargo for sem in Freight.scratch(count)]


def load(count, starts, halves, targets, sems):
    return [
        Freight(count, half, target, sems[4 * k : 4 * k + 4], starts[k])
        for k, (half, target) in enumerate(zip(halves, targets))
    ]


def flat_rows(values):
    return [value.reshape(-1, value.shape[2]) for value in values]


def call(kernel, outs, ins, scratch, identity, name):
    results = pl.pallas_call(
        kernel,
        out_shape=[jax.ShapeDtypeStruct(shape, kind) for shape, kind, _ in outs],
        in_specs=[space for _, space in ins],
        out_specs=[space for _, _, space in outs],
        scratch_shapes=scratch,
        compiler_params=pltpu.CompilerParams(
            collective_id=identity, has_side_effects=True, vmem_limit_bytes=GRANT
        ),
        name=name,
    )(*[value for value, _ in ins])
    return list(results)


class GroupGather:
    def __init__(self, source, target, send, receive, local):
        self.source, self.target = source, target
        self.send, self.receive = send, receive
        self.local = local
        self.here = spot()

    @staticmethod
    def scratch():
        return [
            pltpu.SemaphoreType.DMA((11,)),
            pltpu.SemaphoreType.DMA((11,)),
            pltpu.SemaphoreType.DMA,
        ]

    def half(self, ref, h):
        rows = self.source.shape[0] // 2
        return ref.at[pl.ds(h * rows, rows)]

    def make(self):
        line, side, deck, core = self.here
        sibling, across, above = group_peers()
        mine = rank(side, deck, core)
        beside = rank(1 - side, deck, core)
        over = rank(side, 1 - deck, core)
        corner = rank(1 - side, 1 - deck, core)

        def own(h, peer, index):
            return remote(
                self.half(self.source, h),
                self.half(self.target.at[mine], h),
                self.send.at[index],
                self.receive.at[index],
                peer,
            )

        def relay(block, h, peer, index):
            ref = self.half(self.target.at[block], h)
            return remote(ref, ref, self.send.at[index], self.receive.at[index], peer)

        self.keep = pltpu.make_async_copy(self.source, self.target.at[mine], self.local)
        self.first = [
            own(0, across, 0),
            own(1, above, 1),
            own(0, above, 2),
            own(1, across, 3),
        ]
        self.near = remote(
            self.source, self.target.at[mine], self.send.at[4], self.receive.at[4], sibling
        )
        self.second = [relay(beside, 0, above, 5), relay(over, 1, across, 6)]
        self.last = [
            relay(beside, 0, sibling, 7),
            relay(over, 1, sibling, 8),
            relay(over, 0, sibling, 9),
            relay(beside, 1, sibling, 10),
        ]
        self.corner = corner

    def start(self):
        self.make()
        self.first[1].start()
        self.first[2].start()
        self.near.start()
        self.keep.start()

    def start_across(self):
        self.first[0].start()
        self.first[3].start()

    def landed(self):
        self.near.wait_recv()
        self.keep.wait()

    def landed_relays(self):
        for copy in self.last:
            copy.wait_recv()

    def forward(self):
        for k in range(2):
            self.first[k].wait_recv()
            self.second[k].start()
            self.last[k].start()
        for k in range(2, 4):
            self.first[k].wait_recv()
            self.last[k].start()


def corner_relay(gather, send, receive):
    sibling = group_peers()[0]
    out = []
    for h in range(2):
        ref = gather.half(gather.target.at[gather.corner], h)
        out.append(remote(ref, ref, send.at[h], receive.at[h], sibling))
    return out


def group_finish(gather, send, receive, early=False):
    relays = corner_relay(gather, send, receive)
    for k in range(2):
        gather.second[k].wait_recv()
        relays[k].start()
    if not early:
        gather.landed()
        gather.landed_relays()
    for copy in [gather.near] + gather.first + gather.second + gather.last:
        copy.wait_send()
    for copy in relays:
        copy.wait()


def rows_scratch():
    return GroupGather.scratch() + [
        pltpu.SemaphoreType.DMA((2,)),
        pltpu.SemaphoreType.DMA((2,)),
    ]


SMALL_GAINS = 5


def first_kernel(count, starts, small_top, *refs):
    loads = len(starts)
    rows = refs[0]
    halves, refs = refs[1 : 1 + loads], refs[1 + loads :]
    everything, normed, pre = refs[:3]
    targets, refs = refs[3 : 3 + loads], refs[3 + loads :]
    incoming, table, weights, result, tails = refs[:5]
    incoming_sems, out_sems, weight_sems, result_sems, tail_sem = refs[5:10]
    sems = refs[10:]
    gather = GroupGather(rows, everything, *sems[:3])
    corner_sems = sems[3:5]
    small, branch, *others = load(count, starts, halves, targets, sems[5:])
    shares = 2 * count
    line, side, deck, core = spot()
    greet(cargo_peers(count))
    small.start()
    branch.start()
    gather.start()
    small.second()
    gather.start_across()
    small.forward()
    branch.second()
    small.finish()
    tail = pltpu.make_async_copy(targets[0], tails, tail_sem)
    tail.start()
    tail.wait()

    block_rows, features = rows.shape
    gain = jnp.concatenate(
        [
            tails[
                k // 2,
                (k % 2) * (small_top + 16) + small_top : (k % 2 + 1) * (small_top + 16),
                : features // shares,
            ].astype(F32)[SMALL_GAINS : SMALL_GAINS + 1]
            for k in range(shares)
        ],
        axis=1,
    )

    def block(ref, g):
        return ref.at[pl.ds(pl.multiple_of(g * block_rows, block_rows), block_rows)]

    def norm_blocks(pair):
        fetches = [
            pltpu.make_async_copy(everything.at[g], incoming.at[k], incoming_sems.at[k])
            for k, g in enumerate(pair)
        ]
        for fetch in fetches:
            fetch.start()
        for k, g in enumerate(pair):
            fetches[k].wait()

            def norm_rows(i, carry, k=k, g=g):
                r = pl.multiple_of(i * 32, 32)
                value = incoming[k, pl.ds(r, 32), :].astype(F32)
                mean = jnp.mean(value * value, axis=1, keepdims=True)
                unit = value * lax.rsqrt(mean + EPSILON)
                base = pl.multiple_of(g * block_rows + r, 32)
                table[pl.ds(base, 32), :] = (unit * gain).astype(BF16)
                return carry

            lax.fori_loop(0, block_rows // 32, norm_rows, 0)
            pltpu.make_async_copy(block(table, g), block(normed, g), out_sems.at[g]).start()

    def both_cores(s, d):
        return [rank(s, d, core), rank(s, d, 1 - core)]

    gather.landed()
    norm_blocks(both_cores(side, deck))
    gather.forward()
    branch.forward()
    for freight in others:
        freight.start()
    gather.landed_relays()
    norm_blocks(both_cores(1 - side, deck))
    norm_blocks(both_cores(side, 1 - deck))
    for freight in others:
        freight.second()
    group_finish(gather, *corner_sems, early=True)
    norm_blocks(both_cores(1 - side, 1 - deck))
    branch.finish()
    depth = targets[1].shape[1]
    loading = [
        pltpu.make_async_copy(
            targets[1].at[k], weights.at[pl.ds(k * depth, depth)], weight_sems.at[k]
        )
        for k in range(count)
    ]
    for copy in loading:
        copy.start()
    for freight in others:
        freight.forward()
    for copy in loading:
        copy.wait()
    lanes, width = weights.shape[1] // 2, pre.shape[1] // 2
    shift = 2 * lanes - width
    inside = lax.broadcasted_iota(jnp.int32, (CHUNK, width), 1) < lanes
    writes = Stream(result, pre, result_sems)

    def product(r):
        where = pl.ds(r, CHUNK)
        both = jnp.dot(table[where, :], weights[...], preferred_element_type=F32)
        result[where, :width] = jnp.where(inside, both[:, :width], 0.0)
        later = pltpu.roll(both[:, shift:], lanes, 1)
        result[where, width:] = jnp.where(inside, later, 0.0)
        writes.start(r)

    chunks(pre.shape[0], product)
    for g in range(8):
        pltpu.make_async_copy(block(table, g), block(normed, g), out_sems.at[g]).wait()
    writes.wait_all()
    for freight in others:
        freight.finish()


def first(count, rows, cargo, width):
    total = 8 * rows.shape[0]
    small, branch = cargo[:2]
    out = call(
        functools.partial(first_kernel, count, cargo_starts(cargo), small.shape[1] - 16),
        [
            ((8,) + rows.shape, BF16, ANY),
            ((total, rows.shape[1]), BF16, ANY),
            ((total, 2 * width), F32, ANY),
        ]
        + cargo_outs(count, cargo),
        [(rows, ANY)] + cargo_ins(cargo),
        [
            pltpu.VMEM((2,) + rows.shape, BF16),
            pltpu.VMEM((total, rows.shape[1]), BF16),
            pltpu.VMEM((rows.shape[1], branch.shape[2]), BF16),
            pltpu.VMEM((total, 2 * width), F32),
            pltpu.VMEM(piece_shape(count, small), BF16),
            pltpu.SemaphoreType.DMA((2,)),
            pltpu.SemaphoreType.DMA((8,)),
            pltpu.SemaphoreType.DMA((count,)),
            pltpu.SemaphoreType.DMA((total // CHUNK,)),
            pltpu.SemaphoreType.DMA,
        ]
        + rows_scratch()
        + cargo_scratch(count, cargo),
        0,
        "first",
    )
    return out[1:4] + flat_rows(out[4:])


def rows_kernel(count, starts, *refs):
    loads = len(starts)
    rows, halves = refs[0], refs[1 : 1 + loads]
    everything, targets = refs[1 + loads], refs[2 + loads : 2 + 2 * loads]
    sems = refs[2 + 2 * loads :]
    gather = GroupGather(rows, everything, *sems[:3])
    freights = load(count, starts, halves, targets, sems[5:])
    greet(cargo_peers(count))
    for freight in freights:
        freight.start()
    gather.start()
    for freight in freights:
        freight.second()
    gather.start_across()
    gather.forward()
    for freight in freights:
        freight.forward()
    group_finish(gather, *sems[3:5])
    for freight in freights:
        freight.finish()


def gather_rows(count, rows, cargo, identity):
    out = call(
        functools.partial(rows_kernel, count, cargo_starts(cargo)),
        [((8,) + rows.shape, BF16, ANY)] + cargo_outs(count, cargo),
        [(rows, ANY)] + cargo_ins(cargo),
        rows_scratch() + cargo_scratch(count, cargo),
        identity,
        "gather_rows",
    )
    return [out[0].reshape(-1, rows.shape[1])] + flat_rows(out[1:])


def plain_rows_kernel(rows, everything, *sems):
    gather = GroupGather(rows, everything, *sems[:3])
    greet(group_peers())
    gather.start()
    gather.start_across()
    gather.forward()
    group_finish(gather, *sems[3:5])


def gather_plain(rows, identity):
    out = call(
        plain_rows_kernel,
        [((8,) + rows.shape, BF16, ANY)],
        [(rows, ANY)],
        rows_scratch(),
        identity,
        "gather_rows",
    )
    return out[0].reshape(-1, rows.shape[1])


def flip(value, bit):
    return 1 - value if bit else value


def whole_group():
    line, side, deck, core = spot()
    return [
        seat(line, flip(side, k & 4), flip(deck, k & 2), flip(core, k & 1)) for k in range(1, 8)
    ]


class GainSum:
    def __init__(self, count, gains, totals, near, far, send, receive, far_send, far_receive):
        self.gains, self.totals, self.near, self.far = gains, totals, near, far
        self.first = [
            remote(gains, near.at[k], send.at[k], receive.at[k], peer)
            for k, peer in enumerate(whole_group())
        ]
        self.second_copies = [
            remote(far.at[0], far.at[1 + k], far_send.at[k], far_receive.at[k], peer)
            for k, peer in enumerate(line_peers(count))
        ]

    @staticmethod
    def scratch(count, gains):
        return [
            pltpu.VMEM((7,) + gains.shape, F32),
            pltpu.VMEM((count,) + gains.shape, F32),
            pltpu.SemaphoreType.DMA((7,)),
            pltpu.SemaphoreType.DMA((7,)),
            pltpu.SemaphoreType.DMA((count,)),
            pltpu.SemaphoreType.DMA((count,)),
        ]

    def start(self):
        for copy in self.first:
            copy.start()

    def second(self):
        for copy in self.first:
            copy.wait()
        total = self.gains[...]
        for k in range(7):
            total = total + self.near[k]
        self.far[0] = total
        for copy in self.second_copies:
            copy.start()

    def finish(self):
        for copy in self.second_copies:
            copy.wait()
        total = self.far[0]
        for k in range(len(self.second_copies)):
            total = total + self.far[1 + k]
        self.totals[...] = total


def fold_kernel(count, plan, starts, swaps, *refs):
    gained = swaps > 0
    loads = len(starts)
    lefts = refs[: plan[-1][0] + 1]
    rights = refs[len(lefts) : len(lefts) + len(plan)]
    refs = refs[len(lefts) + len(rights) :]
    halves, refs = refs[:loads], refs[loads:]
    gains = None
    if gained:
        gains, values, refs = refs[0], refs[1 : 1 + swaps], refs[1 + swaps :]
    out, refs = refs[0], refs[1:]
    targets, refs = refs[:loads], refs[loads:]
    if gained:
        totals, swapped, refs = refs[0], refs[1 : 1 + swaps], refs[1 + swaps :]
        gain_sum = GainSum(count, gains, totals, *refs[-6:])
        swap = Swap(values, swapped, *refs[-9:-6])
    mine, stage, near, leaving, arriving, refs = *refs[:5], refs[5:]
    send, receive, near_send, near_receive = refs[:4]
    line, side, deck, core = spot()
    sibling, across, above = group_peers()
    freights = load(count, starts, halves, targets, refs[4:])
    if gained:
        greet(whole_group() + line_peers(count))
        gain_sum.start()
        swap.start()
    else:
        greet(cargo_peers(count) if loads else group_peers())
    for freight in freights:
        freight.start()
    rows = out.shape[0]
    half = rows // 2
    width = out.shape[1]
    step = 512

    def product(which, store):
        base = pl.multiple_of(which * rows, rows)

        def body(j, carry):
            columns = pl.ds(pl.multiple_of(j * step, step), step)
            total = None
            for (which_left, start), right in zip(plan, rights):
                part = lax.dot_general(
                    lefts[which_left][pl.ds(base, rows), start : start + right.shape[1]],
                    right[columns, :],
                    NT,
                    preferred_element_type=F32,
                )
                total = part if total is None else total + part
            store(columns, total)
            return carry

        lax.fori_loop(0, width // step, body, 0)

    def sweep(action):
        def body(i, carry):
            action(pl.multiple_of(i * 16, 16))
            return carry

        lax.fori_loop(0, half // 16, body, 0)

    def chip_sum(q, h, r):
        place = pl.ds(h * half + r, 16)
        return mine[q, place, :] + near[q, place, :].astype(F32)

    def ship(index, peer):
        return remote(
            leaving.at[index], arriving.at[index], send.at[index], receive.at[index], peer
        )

    ships = [ship(k, peer) for k, peer in enumerate((above, across, above, across, across, above))]
    OWN, ACROSS, ABOVE, CORNER = 0, 1, 2, 3
    seats = {
        CORNER: (1 - side, 1 - deck),
        ABOVE: (side, 1 - deck),
        ACROSS: (1 - side, deck),
        OWN: (side, deck),
    }
    nears = []
    for q in (CORNER, ABOVE, ACROSS, OWN):
        s, d = seats[q]

        def put_stage(columns, total, q=q):
            stage[q, :, columns] = total.astype(BF16)

        def put_mine(columns, total, q=q):
            mine[q, :, columns] = total

        product(rank(s, d, 1 - core), put_stage)
        copy = remote(stage.at[q], near.at[q], near_send.at[q], near_receive.at[q], sibling)
        copy.start()
        nears.append(copy)
        product(rank(s, d, core), put_mine)
        copy.wait_recv()
        if q == CORNER:

            def corner_sum(r):
                for h in range(2):
                    leaving[h, pl.ds(r, 16), :] = chip_sum(CORNER, h, r).astype(BF16)

            sweep(corner_sum)
            ships[0].start()
            ships[1].start()
        if q == ABOVE:

            def above_sum(r):
                leaving[2, pl.ds(r, 16), :] = chip_sum(ABOVE, 0, r).astype(BF16)

            sweep(above_sum)
            ships[2].start()
            for freight in freights:
                freight.second()
            if gained:
                gain_sum.second()
        if q == ACROSS:

            def across_sum(r):
                leaving[3, pl.ds(r, 16), :] = chip_sum(ACROSS, 1, r).astype(BF16)

            sweep(across_sum)
            ships[3].start()
    ships[0].wait_recv()

    def pass_across(r):
        total = chip_sum(ACROSS, 0, r) + arriving[0, pl.ds(r, 16), :].astype(F32)
        leaving[4, pl.ds(r, 16), :] = total.astype(BF16)

    sweep(pass_across)
    ships[4].start()
    ships[1].wait_recv()

    def pass_above(r):
        total = chip_sum(ABOVE, 1, r) + arriving[1, pl.ds(r, 16), :].astype(F32)
        leaving[5, pl.ds(r, 16), :] = total.astype(BF16)

    sweep(pass_above)
    ships[5].start()
    for freight in freights:
        freight.forward()
    if gained:
        gain_sum.finish()
        swap.finish()
    for k in range(2, 6):
        ships[k].wait_recv()

    def finish(r):
        place = pl.ds(r, 16)
        first = arriving[2, place, :].astype(F32) + arriving[4, place, :].astype(F32)
        out[place, :] = chip_sum(OWN, 0, r) + first
        second = arriving[3, place, :].astype(F32) + arriving[5, place, :].astype(F32)
        out[pl.ds(half + r, 16), :] = chip_sum(OWN, 1, r) + second

    sweep(finish)
    for k in range(6):
        ships[k].wait_send()
    for copy in nears:
        copy.wait_send()
    for freight in freights:
        freight.finish()


def fold(count, pairs, identity, cargo=(), gains=None, swaps=()):
    lefts, rights, plan = [], [], []
    for k, (left, parts) in enumerate(pairs):
        lefts.append(left)
        start = 0
        for part in parts:
            rights.append(part)
            plan.append((k, start))
            start += part.shape[1]
    rows, width = lefts[0].shape[0] // 8, rights[0].shape[0]
    outs = [((rows, width), F32, VMEM)]
    ins = [(value, VMEM) for value in list(lefts) + list(rights)]
    scratch = [
        pltpu.VMEM((4, rows, width), F32),
        pltpu.VMEM((4, rows, width), BF16),
        pltpu.VMEM((4, rows, width), BF16),
        pltpu.VMEM((6, rows // 2, width), BF16),
        pltpu.VMEM((6, rows // 2, width), BF16),
        pltpu.SemaphoreType.DMA((6,)),
        pltpu.SemaphoreType.DMA((6,)),
        pltpu.SemaphoreType.DMA((4,)),
        pltpu.SemaphoreType.DMA((4,)),
    ]
    outs += cargo_outs(count, cargo)
    ins += cargo_ins(cargo)
    scratch += cargo_scratch(count, cargo)
    if gains is not None:
        outs.append((gains.shape, F32, VMEM))
        ins.append((gains, VMEM))
        outs += [(value.shape, BF16, ANY) for value in swaps]
        ins += [(value, ANY) for value in swaps]
        scratch += Swap.scratch(swaps)
        scratch += GainSum.scratch(count, gains)
    out = call(
        functools.partial(fold_kernel, count, plan, cargo_starts(cargo), len(swaps)),
        outs,
        ins,
        scratch,
        identity,
        "fold",
    )
    if gains is not None:
        return out
    return out[:1] + flat_rows(out[1:])


def gelu_both(value):
    square = value * value
    bend = jnp.tanh(GELU_SCALE * value * (1.0 + GELU_CUBE * square))
    act = 0.5 * value * (1.0 + bend)
    slope = 0.5 * (1.0 + bend) + 0.5 * value * (1.0 - bend * bend) * GELU_SCALE * (
        1.0 + 3.0 * GELU_CUBE * square
    )
    return act, slope


def chunks(rows, action, size=CHUNK):
    def body(i, carry):
        action(pl.multiple_of(i * size, size))
        return carry

    lax.fori_loop(0, rows // size, body, 0)


def spans(low, high, action):
    def body(i, carry):
        action(pl.multiple_of(i * CHUNK, CHUNK))
        return carry

    lax.fori_loop(low, high, body, 0)


def tile_scan(mults, adds, rows, width, backward):
    place = lax.broadcasted_iota(jnp.int32, (8, width), 0)

    def inside(base):
        where = pl.ds(base, 8)
        a, b = mults[where, :], adds[where, :]
        for k in (1, 2, 4):
            if backward:
                away, mask = pltpu.roll(a, 8 - k, 0), place < 8 - k
                back = pltpu.roll(b, 8 - k, 0)
            else:
                away, mask = pltpu.roll(a, k, 0), place >= k
                back = pltpu.roll(b, k, 0)
            b = jnp.where(mask, b + a * back, b)
            a = jnp.where(mask, a * away, a)
        return where, a, b

    unroll = 4
    tiles = rows // 8

    def body(i, carry):
        prod, total = carry
        work = []
        for u in range(unroll):
            index = i * unroll + u
            if backward:
                index = tiles - 1 - index
            work.append(inside(pl.multiple_of(index * 8, 8)))
        for where, a, b in work:
            edge = 0 if backward else 7
            adds[where, :] = b + a * total
            mults[where, :] = a * prod
            whole = jnp.broadcast_to(a[edge : edge + 1, :], (8, width))
            extra = jnp.broadcast_to(b[edge : edge + 1, :], (8, width))
            total = extra + whole * total
            prod = whole * prod
        return prod, total

    return lax.fori_loop(
        0, tiles // unroll, body, (jnp.ones((8, width), F32), jnp.zeros((8, width), F32))
    )


def pool(count, prod, total, outgoing, slots, send, receive, backward):
    line, side, deck, core = spot()
    outgoing[0:8, :] = prod
    outgoing[8:16, :] = total
    slots[line, 0:8, :] = prod
    slots[line, 8:16, :] = total
    copies = []
    for k in range(1, count):
        copy = remote(
            outgoing,
            slots.at[line],
            send.at[k],
            receive.at[k],
            seat((line + k) % count, side, deck, core),
        )
        copy.start()
        copies.append(copy)
    for copy in copies:
        copy.wait()
    entering = jnp.zeros_like(prod)
    order = range(count - 1, -1, -1) if backward else range(count)
    for place in order:
        longer = slots[place, 8:16, :] + slots[place, 0:8, :] * entering
        before = (line < place) if backward else (line > place)
        entering = jnp.where(before, longer, entering)
    return entering


def sigmoid(value):
    return 0.5 + 0.5 * jnp.tanh(0.5 * value)


def gates(recur, soft):
    decay = jnp.exp(-8.0 * recur * soft)
    square = (1.0 + GUARD) - decay * decay
    inverse = lax.rsqrt(square)
    return decay, square * inverse, inverse


def scan_kernel(count, starts, *refs):
    loads = len(starts)
    pre, masks, table, gate_weights, cotangent = refs[:5]
    halves, refs = refs[5 : 5 + loads], refs[5 + loads :]
    everything, targets, refs = refs[6], refs[7 : 7 + loads], refs[:6] + refs[7 + loads :]
    saved, refs = refs[:6], refs[6:]
    gate, entry, conv, recur_out, admit_out, state, merged = refs[:7]
    prods, sums, halo, outgoing, slots, edge_sems, send, receive = refs[7:15]
    in_sems, out_sems, head_sems = refs[15:18]
    sems = refs[18:]
    line, side, deck, core = spot()
    rows, width = conv.shape
    gather = GroupGather(cotangent, everything, *sems[:3])
    freights = load(count, starts, halves, targets, sems[5:])
    gate_reads = Stream(pre, gate, in_sems.at[0], columns=pl.ds(0, width))
    entry_reads = Stream(pre, entry, in_sems.at[1], to_row=8, columns=pl.ds(width, width))
    conv_writes = Stream(conv, saved[0], out_sems.at[0])
    recur_writes = Stream(recur_out, saved[1], out_sems.at[1])
    admit_writes = Stream(admit_out, saved[2], out_sems.at[2])
    state_writes = Stream(state, saved[3], out_sems.at[3], 8, 8)
    merged_writes = Stream(merged, saved[4], out_sems.at[4])
    entry_writes = Stream(entry, saved[5], out_sems.at[5], 8, 8)
    heads = [
        pltpu.make_async_copy(local.at[pl.ds(0, 8)], away.at[pl.ds(0, 8)], head_sems.at[k])
        for k, (local, away) in enumerate([(state, saved[3]), (entry, saved[5])])
    ]
    entry_reads.start_all()
    gate_reads.start_all()
    greet(cargo_peers(count))

    def edge(place):
        return remote(
            pre.at[pl.ds(rows - 8, 8), pl.ds(width, width)],
            halo,
            edge_sems.at[0],
            edge_sems.at[1],
            seat(place, side, deck, core),
        )

    @pl.when(line < count - 1)
    def _():
        edge(line + 1).start()

    for freight in freights:
        freight.start()
    gather.start()

    @pl.when(line > 0)
    def _():
        edge(line - 1).wait_recv()
        entry[0:8, :] = halo[...]

    @pl.when(line == 0)
    def _():
        entry[0:8, :] = jnp.zeros((8, width), F32)

    @pl.when(line < count - 1)
    def _():
        edge(line + 1).wait_send()

    heads[1].start()

    def gate_chunk(r):
        entry_reads.wait(r)
        wide = entry[pl.ds(r, CHUNK + 8), :]
        mask = masks[pl.ds(r, CHUNK), :]
        value = table[0:1, :] * wide[8:, :]
        for k in range(1, TAPS):
            value = (
                value + table[k : k + 1, :] * wide[8 - k : 8 - k + CHUNK, :] * mask[:, k - 1 : k]
            )
        where = pl.ds(r, CHUNK)
        conv[where, :] = value
        both = jnp.dot(value.astype(BF16), gate_weights[...], preferred_element_type=F32)
        recur = sigmoid(both[:, :width])
        admit = sigmoid(both[:, width:])
        recur_out[where, :] = recur
        admit_out[where, :] = admit
        decay, root, _ = gates(recur, table[4:5, :])
        opened = mask[:, 3:4]
        norm = root * opened + (1.0 - opened)
        prods[where, :] = decay * opened
        sums[where, :] = norm * admit * value
        for stream in (entry_writes, conv_writes, recur_writes, admit_writes):
            stream.start(r)

    pieces = rows // CHUNK
    spans(0, pieces // 4, gate_chunk)
    for freight in freights:
        freight.second()
    gather.start_across()
    spans(pieces // 4, pieces, gate_chunk)
    prod, total = tile_scan(prods, sums, rows, width, False)
    gather.forward()
    entering = pool(count, prod, total, outgoing, slots, send, receive, False)
    for freight in freights:
        freight.forward()
    state[0:8, :] = entering
    heads[0].start()

    def state_chunk(r):
        gate_reads.wait(r)
        where = pl.ds(r, CHUNK)
        value = sums[where, :] + prods[where, :] * entering[0:1, :]
        state[pl.ds(r + 8, CHUNK), :] = value
        act, _ = gelu_both(gate[where, :])
        merged[where, :] = (value * act).astype(BF16)
        state_writes.start(r)
        merged_writes.start(r)

    chunks(rows, state_chunk)
    for stream in (
        entry_writes,
        conv_writes,
        recur_writes,
        admit_writes,
        state_writes,
        merged_writes,
    ):
        stream.wait_all()
    for copy in heads:
        copy.wait()
    group_finish(gather, *sems[3:5])
    for freight in freights:
        freight.finish()


def scan_forward(count, pre, masks, table, gate_weights, cotangent, cargo):
    rows, width = pre.shape[0], pre.shape[1] // 2
    pieces = rows // CHUNK
    tall = (rows + 8, width)
    saved = [
        ((rows, width), F32),
        ((rows, width), F32),
        ((rows, width), F32),
        (tall, F32),
        ((rows, width), BF16),
        (tall, F32),
    ]
    out = call(
        functools.partial(scan_kernel, count, cargo_starts(cargo)),
        [(shape, kind, ANY) for shape, kind in saved]
        + [((8,) + cotangent.shape, BF16, ANY)]
        + cargo_outs(count, cargo),
        [(pre, ANY), (masks, VMEM), (table, VMEM), (gate_weights, VMEM), (cotangent, ANY)]
        + cargo_ins(cargo),
        [
            pltpu.VMEM((rows, width), F32),
            pltpu.VMEM(tall, F32),
            pltpu.VMEM((rows, width), F32),
            pltpu.VMEM((rows, width), F32),
            pltpu.VMEM((rows, width), F32),
            pltpu.VMEM(tall, F32),
            pltpu.VMEM((rows, width), BF16),
            pltpu.VMEM((rows, width), F32),
            pltpu.VMEM((rows, width), F32),
            pltpu.VMEM((8, width), F32),
            pltpu.VMEM((16, width), F32),
            pltpu.VMEM((count, 16, width), F32),
            pltpu.SemaphoreType.DMA((2,)),
            pltpu.SemaphoreType.DMA((count,)),
            pltpu.SemaphoreType.DMA((count,)),
            pltpu.SemaphoreType.DMA((2, pieces)),
            pltpu.SemaphoreType.DMA((6, pieces)),
            pltpu.SemaphoreType.DMA((2,)),
        ]
        + rows_scratch()
        + cargo_scratch(count, cargo),
        2,
        "scan_forward",
    )
    return out[:6] + [out[6].reshape(-1, cotangent.shape[1])] + flat_rows(out[7:])


def back_kernel(count, lanes, swaps, *refs):
    pre, low, outlet = refs[:3]
    saved, refs = refs[3:8], refs[8:]
    masks, table, gate_weights = refs[:3]
    values, refs = refs[3 : 3 + swaps], refs[3 + swaps :]
    grad_pre, grad_gates, grad_table = refs[:3]
    swapped, refs = refs[3 : 3 + swaps], refs[3 + swaps :]
    gate, conv, recur_in, admit_in, state, entry, lows = refs[:7]
    prods, sums, mixes, outgoing, slots, edge_sems, send, receive = refs[7:15]
    in_sems, low_sems, head_sems = refs[15:18]
    line, side, deck, core = spot()
    rows, width = conv.shape
    pieces = rows // CHUNK
    swap = Swap(values, swapped, *refs[18:])
    conv_reads = Stream(saved[0], conv, in_sems.at[0])
    recur_reads = Stream(saved[1], recur_in, in_sems.at[1])
    admit_reads = Stream(saved[2], admit_in, in_sems.at[2])
    state_reads = Stream(saved[3], state, in_sems.at[3], 8, 8)
    entry_reads = Stream(saved[4], entry, in_sems.at[4], 8, 8)
    gate_reads = Stream(pre, gate, in_sems.at[5], columns=pl.ds(0, width))
    heads = [
        pltpu.make_async_copy(away.at[pl.ds(0, 8)], local.at[pl.ds(0, 8)], head_sems.at[k])
        for k, (local, away) in enumerate([(state, saved[3]), (entry, saved[4])])
    ]

    def fetch(i):
        slot = i % 2
        start = pl.multiple_of(i * CHUNK, CHUNK)
        return pltpu.make_async_copy(
            low.at[pl.ds(start, CHUNK)], lows.at[slot], low_sems.at[slot]
        )

    fetch(0).start()
    for k in range(pieces):
        for stream in (gate_reads, recur_reads, state_reads):
            stream.start(k * CHUNK)
    for copy in heads:
        copy.start()
    for stream in (conv_reads, admit_reads, entry_reads):
        stream.start_all()
    greet(line_peers(count) + ([seat(line, 1 - side, deck, core)] if swaps else []))
    swap.start()

    def direct(i, carry):
        r = pl.multiple_of(i * CHUNK, CHUNK)

        @pl.when(i + 1 < pieces)
        def _():
            fetch(i + 1).start()

        fetch(i).wait()
        for stream in (gate_reads, recur_reads, state_reads):
            stream.wait(r)
        where = pl.ds(r, CHUNK)
        grad = jnp.dot(lows[i % 2], outlet[...], preferred_element_type=F32)
        act, slope = gelu_both(gate[where, :])
        gate[where, :] = grad * state[pl.ds(r + 8, CHUNK), :] * slope
        straight = grad * act
        carried = jnp.exp(-8.0 * recur_in[where, :] * table[4:5, :]) * masks[where, 3:4]
        mixes[where, :] = straight
        prods[where, :] = carried
        sums[where, :] = carried * straight
        return carry

    lax.fori_loop(0, pieces, direct, 0)
    prods[rows : rows + 8, :] = jnp.ones((8, width), F32)
    sums[rows : rows + 8, :] = jnp.zeros((8, width), F32)
    prod, total = tile_scan(prods, sums, rows, width, True)
    entering = pool(count, prod, total, outgoing, slots, send, receive, True)
    for copy in heads:
        copy.wait()
    grad_gates[...] = jnp.zeros_like(grad_gates)
    grad_table[...] = jnp.zeros_like(grad_table)

    def fold_rows(value):
        return jnp.sum(value, axis=0, keepdims=True)

    def gate_chunk(r):
        conv_reads.wait(r)
        admit_reads.wait(r)
        where = pl.ds(r, CHUNK)
        wide = pl.ds(r, CHUNK + 8)
        later = sums[wide, :] + prods[wide, :] * entering[0:1, :]
        grad = mixes[where, :] + later[1 : CHUNK + 1, :]
        before = state[wide, :][7 : CHUNK + 7, :]
        soft = table[4:5, :]
        recur, admit, value = recur_in[where, :], admit_in[where, :], conv[where, :]
        decay, root, inverse = gates(recur, soft)
        opened = masks[where, 3:4]
        norm = root * opened + (1.0 - opened)
        flow = grad * admit
        grad_log = opened * (grad * before * decay - flow * value * decay * decay * inverse)
        grad_table[4:5, :] += fold_rows(grad_log * (-8.0 * recur))
        grad_rate = (grad_log * (-8.0 * soft) * recur * (1.0 - recur)).astype(BF16)
        grad_inlet = (flow * norm * value * (1.0 - admit)).astype(BF16)
        both = jnp.concatenate([grad_rate, grad_inlet], axis=1)
        grad_gates[...] += lax.dot_general(
            value.astype(BF16), both, TN, preferred_element_type=F32
        )
        mixes[where, :] = flow * norm + lax.dot_general(
            both, gate_weights[...], NT, preferred_element_type=F32
        )

    gate_chunk(0)

    def edge(place):
        return remote(
            mixes.at[pl.ds(0, 8)],
            mixes.at[pl.ds(rows, 8)],
            edge_sems.at[0],
            edge_sems.at[1],
            seat(place, side, deck, core),
        )

    @pl.when(line > 0)
    def _():
        edge(line - 1).start()

    spans(1, pieces, gate_chunk)

    @pl.when(line < count - 1)
    def _():
        edge(line + 1).wait_recv()

    @pl.when(line == count - 1)
    def _():
        mixes[rows : rows + 8, :] = jnp.zeros((8, width), F32)

    spare = width - lanes
    shift = 2 * lanes - width

    def entry_chunk(r):
        entry_reads.wait(r)
        where, wide = pl.ds(r, CHUNK), pl.ds(r, CHUNK + 8)
        ahead, mask = mixes[wide, :], masks[where, :]
        source = entry[wide, :]
        here = ahead[:CHUNK, :]
        total = table[0:1, :] * here
        grad_table[0:1, :] += fold_rows(here * source[8:, :])
        for k in range(1, TAPS):
            total = total + table[k : k + 1, :] * ahead[k : k + CHUNK, :] * mask[:, 3 + k : 4 + k]
            grad_table[k : k + 1, :] += fold_rows(
                here * source[8 - k : 8 - k + CHUNK, :] * mask[:, k - 1 : k]
            )
        total = pltpu.roll(total, spare, 1)
        first = gate[where, :]
        middle = first[:, shift:] + total[:, : width - shift]
        grad_pre[where, :shift] = first[:, :shift].astype(BF16)
        grad_pre[where, shift:width] = middle.astype(BF16)
        grad_pre[where, width:] = total[:, width - shift :].astype(BF16)

    chunks(rows, entry_chunk)

    @pl.when(line > 0)
    def _():
        edge(line - 1).wait_send()

    swap.finish()


def scan_backward(count, lanes, pre, low, outlet, saved, masks, table, gate_weights, swaps):
    rows, width = pre.shape[0], pre.shape[1] // 2
    pieces = rows // CHUNK
    tall = (rows + 8, width)
    return call(
        functools.partial(back_kernel, count, lanes, len(swaps)),
        [
            ((rows, 2 * lanes), BF16, VMEM),
            ((width, 2 * width), F32, VMEM),
            ((8, width), F32, VMEM),
        ]
        + [(value.shape, BF16, ANY) for value in swaps],
        [(pre, ANY), (low, ANY), (outlet, VMEM)]
        + [(value, ANY) for value in saved]
        + [(value, VMEM) for value in (masks, table, gate_weights)]
        + [(value, ANY) for value in swaps],
        [
            pltpu.VMEM((rows, width), F32),
            pltpu.VMEM((rows, width), F32),
            pltpu.VMEM((rows, width), F32),
            pltpu.VMEM((rows, width), F32),
            pltpu.VMEM(tall, F32),
            pltpu.VMEM(tall, F32),
            pltpu.VMEM((2, CHUNK, low.shape[1]), BF16),
            pltpu.VMEM(tall, F32),
            pltpu.VMEM(tall, F32),
            pltpu.VMEM(tall, F32),
            pltpu.VMEM((16, width), F32),
            pltpu.VMEM((count, 16, width), F32),
            pltpu.SemaphoreType.DMA((2,)),
            pltpu.SemaphoreType.DMA((count,)),
            pltpu.SemaphoreType.DMA((count,)),
            pltpu.SemaphoreType.DMA((6, pieces)),
            pltpu.SemaphoreType.DMA((2,)),
            pltpu.SemaphoreType.DMA((2,)),
        ]
        + Swap.scratch(swaps),
        7,
        "scan_backward",
    )


def feed_kernel(count, early, starts, *refs):
    loads = len(starts)
    normed, cotangent = refs[:2]
    gate_parts, up_parts, down_parts = refs[2:4], refs[4:6], refs[6 : 6 + early]
    refs = refs[6 + early :]
    halves, refs = refs[:loads], refs[loads:]
    results, targets, refs = refs[:3], refs[3 : 3 + loads], refs[3 + loads :]
    table, gate_up, acts, slopes, down, hidden, grad_gating, grad_lifting = refs[:8]
    table_sems, back_sems, write_sems, weight_sems, down_sems = refs[8:13]
    freights = load(count, starts, halves, targets, refs[13:])
    rows, width = hidden.shape
    pieces = rows // CHUNK
    reads = Stream(normed, table, table_sems)
    again = Stream(cotangent, table, back_sems)
    writes = [
        Stream(local, away, write_sems.at[k])
        for k, (local, away) in enumerate(zip((hidden, grad_gating, grad_lifting), results))
    ]
    weights = []
    for which, parts in enumerate((gate_parts, up_parts)):
        start = 0
        for part in parts:
            weights.append(
                pltpu.make_async_copy(
                    part,
                    gate_up.at[which, :, pl.ds(start, part.shape[1])],
                    weight_sems.at[len(weights)],
                )
            )
            start += part.shape[1]
    for copy in weights:
        copy.start()
    reads.start_all()
    greet(cargo_peers(count))
    for freight in freights:
        freight.start()
    for copy in weights:
        copy.wait()

    def forward_chunk(r):
        reads.wait(r)
        where = pl.ds(r, CHUNK)
        gating = jnp.dot(table[where, :], gate_up[0], preferred_element_type=F32)
        lifting = jnp.dot(table[where, :], gate_up[1], preferred_element_type=F32)
        act, slope = gelu_both(gating)
        hidden[where, :] = (act * lifting).astype(BF16)
        acts[where, :] = act
        slopes[where, :] = lifting * slope
        writes[0].start(r)
        again.start(r)

    spans(0, pieces // 4, forward_chunk)
    for freight in freights:
        freight.second()
    spans(pieces // 4, pieces, forward_chunk)
    for freight in freights:
        freight.forward()
    rows_in = down.shape[0] // count
    copies, start = [], 0
    for k, part in enumerate(down_parts):
        copies.append(
            pltpu.make_async_copy(
                part, down.at[:, pl.ds(start, part.shape[1])], down_sems.at[k]
            )
        )
        start += part.shape[1]
    for k, target in enumerate(targets):
        for place in range(count):
            copies.append(
                pltpu.make_async_copy(
                    target.at[place],
                    down.at[pl.ds(place * rows_in, rows_in), pl.ds(start, target.shape[2])],
                    down_sems.at[early + k * count + place],
                )
            )
        start += target.shape[2]

    def back(low, high):
        def chunk(r):
            where = pl.ds(r, CHUNK)
            columns = slice(low, high)
            grad = jnp.dot(table[where, :], down[:, columns], preferred_element_type=F32)
            grad_gating[where, columns] = (grad * slopes[where, columns]).astype(BF16)
            grad_lifting[where, columns] = (grad * acts[where, columns]).astype(BF16)
            if high == width:
                writes[1].start(r)
                writes[2].start(r)

        chunks(rows, chunk)

    for copy in copies[:early]:
        copy.start()
    again.wait_all()
    for copy in copies[:early]:
        copy.wait()
    ready = sum(part.shape[1] for part in down_parts)
    back(0, ready)
    for freight in freights:
        freight.finish()
    for copy in copies[early:]:
        copy.start()
    for copy in copies[early:]:
        copy.wait()
    back(ready, width)
    for stream in writes:
        stream.wait_all()


def feed(count, normed, cotangent, gate_parts, up_parts, down_parts, cargo):
    rows = normed.shape[0]
    width = sum(part.shape[1] for part in gate_parts)
    pieces = rows // CHUNK
    out = call(
        functools.partial(feed_kernel, count, len(down_parts), cargo_starts(cargo)),
        [((rows, width), BF16, ANY)] * 3 + cargo_outs(count, cargo),
        [(normed, ANY), (cotangent, ANY)]
        + [(part, ANY) for part in list(gate_parts) + list(up_parts) + list(down_parts)]
        + cargo_ins(cargo),
        [
            pltpu.VMEM(normed.shape, BF16),
            pltpu.VMEM((2, normed.shape[1], width), BF16),
            pltpu.VMEM((rows, width), F32),
            pltpu.VMEM((rows, width), F32),
            pltpu.VMEM((normed.shape[1], width), BF16),
            pltpu.VMEM((rows, width), BF16),
            pltpu.VMEM((rows, width), BF16),
            pltpu.VMEM((rows, width), BF16),
            pltpu.SemaphoreType.DMA((pieces,)),
            pltpu.SemaphoreType.DMA((pieces,)),
            pltpu.SemaphoreType.DMA((3, pieces)),
            pltpu.SemaphoreType.DMA((4,)),
            pltpu.SemaphoreType.DMA((len(down_parts) + count * len(cargo),)),
        ]
        + cargo_scratch(count, cargo),
        5,
        "feed",
    )
    return out[:3] + flat_rows(out[3:])


def doc_index(places, doc_starts):
    return jnp.sum((doc_starts[None, :] <= places[:, None]).astype(jnp.int32), axis=1)


def norm_back(grad_unit, unit_rows, scale_rows):
    return scale_rows * (
        grad_unit - unit_rows * jnp.mean(grad_unit * unit_rows, axis=1, keepdims=True)
    )


def unit_norm(values):
    scale = lax.rsqrt(jnp.mean(values * values, axis=1, keepdims=True) + EPSILON)
    return values * scale, scale


def split_columns(value):
    rows, columns = value.shape
    return value.reshape(rows, 2, columns // 2).transpose(1, 0, 2)


def widen(value, width):
    return jnp.pad(value, [(0, 0)] * (value.ndim - 1) + [(0, width - value.shape[-1])])


def by_rows(left, right):
    return lax.dot_general(left, right, TN, preferred_element_type=F32).astype(BF16)


def shards(
    layer_input,
    out_grad,
    doc_starts,
    mixer_gain,
    branch_gate,
    branch_input,
    conv_taps,
    rate_gate,
    input_gate,
    decay_param,
    mixer_out,
    feed_gain,
    feed_gate,
    feed_up,
    feed_down,
):
    shares = lax.axis_size("dp")
    count = shares // 2
    side = lax.axis_index("dp") % 2
    slim, feature_count = mixer_gain.shape[0], layer_input.shape[1]
    heads, piece, head_width = rate_gate.shape
    half_heads = heads // 2
    lanes = half_heads * head_width
    width = -(-lanes // 128) * 128
    row_count = layer_input.shape[0]
    rows = row_count * 8
    line_groups = [[2 * k + s for k in range(count)] for s in range(2)]

    branch_halves = jnp.concatenate(
        [split_columns(branch_gate), split_columns(branch_input)], axis=2
    )
    mixer_halves = widen(split_columns(mixer_out.T), width)
    down_rows = feed_down.T
    narrow = feed_gate.shape[1] // 6
    broad = 2 * narrow

    mine = lax.axis_index("dp")
    blocks = jnp.concatenate([rate_gate, input_gate], axis=2)
    blocks = widen(blocks.reshape(2, half_heads * piece, 2 * head_width), width)
    own = jnp.concatenate([conv_taps, decay_param[None]], axis=0)
    own = jnp.pad(own, ((0, 0), (0, 0), (0, head_width - piece)))
    own = jnp.roll(own, mine * piece, axis=2)
    own = own.reshape(TAPS + 1, 2, lanes).transpose(1, 0, 2)
    gains_own = jnp.pad(
        jnp.stack([mixer_gain, feed_gain]), ((0, 16 - TAPS - 3), (0, width - slim))
    )
    tail = jnp.concatenate(
        [widen(own, width), jnp.broadcast_to(gains_own, (2,) + gains_own.shape)], axis=1
    )
    small_top = -(-half_heads * piece // 16) * 16
    small = jnp.concatenate(
        [jnp.pad(blocks, ((0, 0), (0, small_top - half_heads * piece), (0, 0))), tail], axis=1
    )

    normed_one, pre, small_all, branch_all, gate_first = first(
        count, layer_input, [small, branch_halves, (feed_gate, 0, narrow)], width
    )

    small_all = small_all.reshape(shares, -1, width)
    tails = small_all[:, small_top:].astype(F32)
    gain_first = tails[:, SMALL_GAINS, :slim].reshape(feature_count)
    gain_second = tails[:, SMALL_GAINS + 1, :slim].reshape(feature_count)
    sums = jnp.sum(tails[:, : TAPS + 1], axis=0)
    decay_flat = sums[TAPS, :lanes]
    inside = (jnp.arange(width) < lanes)[None]
    table = jnp.concatenate(
        [
            sums[:TAPS],
            jnp.where(inside, jax.nn.softplus(-sums[TAPS:]), 0.0),
            jnp.zeros((3, width), F32),
        ]
    )
    blocks = (
        small_all[:, : half_heads * piece, : 2 * head_width]
        .reshape(shares, half_heads, piece, 2 * head_width)
        .transpose(1, 0, 2, 3)
        .reshape(lanes, 2 * head_width)
    )
    head_of = jnp.arange(width) // head_width
    same = (head_of[:lanes, None] == head_of[None, :]) & (jnp.arange(width) < lanes)[None]

    def diagonal(part):
        wide = widen(jnp.concatenate([part] * half_heads, axis=1), width)
        return jnp.where(same, wide, 0)

    gate_weights = jnp.concatenate(
        [diagonal(blocks[:, :head_width]), diagonal(blocks[:, head_width:])], axis=1
    )
    gate_weights = jnp.pad(gate_weights, ((0, width - lanes), (0, 0)))

    anchor = lax.axis_index("dp") // 2 * rows
    places = anchor + jnp.arange(rows, dtype=jnp.int32)
    here = doc_index(places, doc_starts)
    columns = [doc_index(places - k, doc_starts) == here for k in range(1, TAPS)]
    columns.append(~jnp.any(doc_starts[None, :] == places[:, None], axis=1))
    columns += [doc_index(places + k, doc_starts) == here for k in range(1, TAPS)]
    columns.append(columns[0])
    masks = jnp.stack(columns, axis=1).astype(F32)

    residual = layer_input.astype(F32)
    unit_one, scale_one = unit_norm(residual)
    conv, recur, admit, state, merged, entry, cot_all, mixer_all, up_first = scan_forward(
        count, pre, masks, table, gate_weights, out_grad, [mixer_halves, (feed_up, 0, narrow)]
    )
    mixer_own, gate_second, down_first = fold(
        count, [(merged, [mixer_all])], 3, [(feed_gate, narrow, broad), (down_rows, 0, narrow)]
    )
    hidden_one = residual + mixer_own
    unit_two, scale_two = unit_norm(hidden_one)
    normed_two, up_second = gather_rows(
        count, (unit_two * gain_second).astype(BF16), [(feed_up, narrow, broad)], 4
    )
    gate_parts, up_parts = [gate_first, gate_second], [up_first, up_second]
    hidden, grad_gating, grad_lifting, down_second = feed(
        count, normed_two, cot_all, gate_parts, up_parts, [down_first], [(down_rows, narrow, broad)]
    )
    down_parts = [down_first, down_second]

    def line_sum(value):
        return lax.psum_scatter(
            value, "dp", scatter_dimension=0, axis_index_groups=line_groups, tiled=True
        )

    down_grads = by_rows(cot_all, hidden)
    grad_gating, grad_lifting, down_grads = lax.optimization_barrier(
        (grad_gating, grad_lifting, down_grads)
    )
    gate_grads = by_rows(normed_two, grad_gating)
    up_grads = by_rows(normed_two, grad_lifting)
    grad_gating, grad_lifting, down_grads, gate_grads, up_grads = lax.optimization_barrier(
        (grad_gating, grad_lifting, down_grads, gate_grads, up_grads)
    )
    down_sum, gate_sum, up_sum = line_sum(down_grads), line_sum(gate_grads), line_sum(up_grads)
    grad_normed_two = fold(count, [(grad_gating, gate_parts), (grad_lifting, up_parts)], 6)[0]
    grad_hidden_one = out_grad.astype(F32) + norm_back(
        grad_normed_two * gain_second, unit_two, scale_two
    )
    grad_hidden_one, down_sum = lax.optimization_barrier((grad_hidden_one, down_sum))
    back_low = gather_plain(grad_hidden_one.astype(BF16), 8)
    outlet_grads = by_rows(back_low, merged)

    def by_side(value):
        return value.reshape(2, -1, value.shape[1])

    back_low, outlet_grads, gate_sum = lax.optimization_barrier(
        (back_low, outlet_grads, gate_sum)
    )
    grad_pre, grad_gates, grad_table, down_both, gate_both = scan_backward(
        count,
        lanes,
        pre,
        back_low,
        mixer_all,
        [conv, recur, admit, state, entry],
        masks,
        table,
        gate_weights,
        [by_side(down_sum), by_side(gate_sum)],
    )
    branch_grads = by_rows(normed_one, grad_pre)

    def spots(value):
        blocks = [
            value[
                h * head_width : (h + 1) * head_width, h * head_width : (h + 1) * head_width
            ].reshape(shares, -1)
            for h in range(half_heads)
        ]
        return jnp.concatenate(blocks, axis=1)

    grad_decay = -jax.nn.sigmoid(-decay_flat) * grad_table[4, :lanes]
    grad_small = jnp.concatenate(
        [
            spots(grad_gates[:, :width]),
            spots(grad_gates[:, width:]),
            grad_table[:TAPS, :lanes]
            .reshape(TAPS * half_heads, shares, piece)
            .transpose(1, 0, 2)
            .reshape(shares, -1),
            grad_decay.reshape(half_heads, shares, piece).transpose(1, 0, 2).reshape(shares, -1),
        ],
        axis=1,
    )
    flat_size = grad_small.shape[1]
    spare = width - lanes
    grad_small = widen(grad_small, slim * spare).reshape(feature_count, spare).astype(BF16)
    last_grads = jnp.concatenate([outlet_grads[:, :lanes], grad_small, branch_grads], axis=1)
    grad_pre, last_grads = lax.optimization_barrier((grad_pre, last_grads))
    last_sum = line_sum(last_grads)
    grad_normed_one = fold(count, [(grad_pre, [branch_all])], 10)[0]
    hidden, grad_normed_one, up_sum = lax.optimization_barrier(
        (hidden, grad_normed_one, up_sum)
    )
    gains = jnp.concatenate(
        [
            jnp.sum(grad_normed_one * unit_one, axis=0).reshape(shares, slim),
            jnp.sum(grad_normed_two * unit_two, axis=0).reshape(shares, slim),
        ]
    )
    feed_own, gains, up_both = fold(
        count, [(hidden, down_parts)], 9, gains=gains, swaps=[by_side(up_sum)]
    )
    first_gain_grad = lax.dynamic_index_in_dim(gains, mine, 0, False)
    second_gain_grad = lax.dynamic_index_in_dim(gains, shares + mine, 0, False)
    layer_output = (hidden_one + feed_own).astype(BF16)
    input_grad = (
        grad_hidden_one + norm_back(grad_normed_one * gain_first, unit_one, scale_one)
    ).astype(BF16)

    pair = by_side(last_sum)
    kept = lax.dynamic_index_in_dim(pair, side, 0, False)
    given = lax.dynamic_index_in_dim(pair, 1 - side, 0, False)
    other = lax.ppermute(given, "dp", [(k, k ^ 1) for k in range(shares)])
    lasts = [
        jnp.where(side == 0, kept, other).astype(F32),
        jnp.where(side == 0, other, kept).astype(F32),
    ]

    def columns(start, stop):
        return jnp.concatenate([value[:, start:stop] for value in lasts], axis=1)

    mixer_out_grad = columns(0, lanes).T
    branch_gate_grad = columns(width, width + lanes)
    branch_input_grad = columns(width + lanes, width + 2 * lanes)
    smalls = [value[:, lanes:width].reshape(-1)[:flat_size] for value in lasts]
    one = half_heads * piece * head_width
    tap_size = TAPS * half_heads * piece
    rate_grad = jnp.concatenate([v[:one].reshape(half_heads, piece, head_width) for v in smalls])
    inlet_grad = jnp.concatenate(
        [v[one : 2 * one].reshape(half_heads, piece, head_width) for v in smalls]
    )
    taps_grad = jnp.concatenate(
        [v[2 * one : 2 * one + tap_size].reshape(TAPS, half_heads, piece) for v in smalls], axis=1
    )
    decay_grad = jnp.concatenate(
        [v[2 * one + tap_size :].reshape(half_heads, piece) for v in smalls]
    )

    def joined(value):
        return jnp.concatenate([value[0], value[1]], axis=1).astype(F32)

    return (
        layer_output,
        input_grad,
        first_gain_grad,
        branch_gate_grad,
        branch_input_grad,
        taps_grad,
        rate_grad,
        inlet_grad,
        decay_grad,
        mixer_out_grad,
        second_gain_grad,
        joined(gate_both),
        joined(up_both),
        joined(down_both).T,
    )


def solution(mesh):
    placed = (
        P(("dp", "tensor"), None),
        P(("dp", "tensor"), None),
        P(),
        P("dp"),
        P("dp", "tensor"),
        P("dp", "tensor"),
        P(None, "tensor", "dp"),
        P("tensor", "dp", None),
        P("tensor", "dp", None),
        P("tensor", "dp"),
        P("tensor", "dp"),
        P("dp"),
        P("dp", "tensor"),
        P("dp", "tensor"),
        P("tensor", "dp"),
    )
    return jax.shard_map(
        shards,
        mesh=mesh,
        in_specs=placed,
        out_specs=(
            P(("dp", "tensor"), None),
            P(("dp", "tensor"), None),
            P("dp"),
            P("dp", "tensor"),
            P("dp", "tensor"),
            P(None, "tensor", "dp"),
            P("tensor", "dp", None),
            P("tensor", "dp", None),
            P("tensor", "dp"),
            P("tensor", "dp"),
            P("dp"),
            P("dp", "tensor"),
            P("dp", "tensor"),
            P("tensor", "dp"),
        ),
        check_vma=False,
    )
```

```python
import functools

import jax
import jax.numpy as jnp
from jax import lax
from jax.experimental import pallas as pl
from jax.experimental.pallas import tpu as pltpu
from jax.sharding import PartitionSpec as P

TAPS = 4
EPSILON = 1e-06
GUARD = 0.001
GELU_SCALE = 0.7978845608028654
GELU_CUBE = 0.044715
MESH = pl.DeviceIdType.MESH
F32, BF16 = jnp.float32, jnp.bfloat16
ANY = pl.BlockSpec(memory_space=pl.ANY)
VMEM = pl.BlockSpec(memory_space=pltpu.VMEM)
GRANT = 60 * 1024 * 1024
NT = (((1,), (1,)), ((), ()))
TN = (((0,), (0,)), ((), ()))
CHUNK = 256


def spot():
    dp, tensor = lax.axis_index("dp"), lax.axis_index("tensor")
    return dp // 2, dp % 2, tensor // 2, tensor % 2


def seat(line, side, deck, core):
    return (line * 2 + side, deck * 2 + core)


def rank(side, deck, core):
    return side * 4 + deck * 2 + core


def greet(peers):
    barrier = pltpu.get_barrier_semaphore()
    for peer in peers:
        pl.semaphore_signal(barrier, inc=1, device_id=peer, device_id_type=MESH)
    pl.semaphore_wait(barrier, len(peers))


def remote(source, target, send, receive, peer):
    return pltpu.make_async_remote_copy(
        src_ref=source,
        dst_ref=target,
        send_sem=send,
        recv_sem=receive,
        device_id=peer,
        device_id_type=MESH,
    )


def line_peers(count):
    line, side, deck, core = spot()
    return [seat((line + k) % count, side, deck, core) for k in range(1, count)]


def group_peers():
    line, side, deck, core = spot()
    return [
        seat(line, side, deck, 1 - core),
        seat(line, 1 - side, deck, core),
        seat(line, side, 1 - deck, core),
    ]


class Freight:
    def __init__(self, count, halves, target, sems, start=0):
        self.count, self.halves, self.target = count, halves, target
        self.start_column = start
        self.cross, self.local, self.send, self.receive = sems
        self.line, self.side, self.deck, self.core = spot()

    @staticmethod
    def scratch(count):
        steps = 5 if count == 4 else count - 1
        return [
            pltpu.SemaphoreType.DMA((2,)),
            pltpu.SemaphoreType.DMA,
            pltpu.SemaphoreType.DMA((steps, 2)),
            pltpu.SemaphoreType.DMA((count, 2)),
        ]

    def half(self, which):
        if len(self.halves.shape) == 3:
            return self.halves.at[which]
        offset = which * (self.halves.shape[1] // 2) + self.start_column
        return self.halves.at[:, pl.ds(pl.multiple_of(offset, 128), self.target.shape[2])]

    def place(self, origin, part):
        rows = self.target.shape[1] // 2
        return self.target.at[origin, pl.ds(pl.multiple_of(part * rows, rows), rows)]

    def seat(self, line):
        return seat(line, self.side, self.deck, self.core)

    def swap(self):
        return remote(
            self.half(1 - self.side),
            self.place(self.line, self.side),
            self.cross.at[0],
            self.cross.at[1],
            seat(self.line, 1 - self.side, self.deck, self.core),
        )

    def keep(self):
        return pltpu.make_async_copy(
            self.half(self.side), self.place(self.line, self.side), self.local
        )

    def copy(self, origin, line, index, part, source):
        return remote(
            source,
            self.place(origin, part),
            self.send.at[index, part],
            self.receive.at[origin, part],
            self.seat(line),
        )

    def own(self, line, index, part):
        source = self.half(self.side)
        if part is not self.side:
            source = self.place(self.line, part)
        return self.copy(self.line, line, index, part, source)

    def arrival(self, origin, part):
        return self.copy(origin, origin, 0, part, self.half(self.side))

    def each_step(self, action, phases=(0, 1)):
        if self.count == 4:
            line = self.line
            for index, step in enumerate((1, -1, 2, -2)):
                if index == 0:
                    when = [line == 2, line < 2]
                elif index == 1:
                    when = [line == 1, line > 1]
                else:
                    when = [(line + step >= 0) & (line + step < 4), None]
                for phase in phases:
                    if when[phase] is not None:

                        @pl.when(when[phase])
                        def _(index=index, step=step):
                            action(index, line + step)

        elif 0 in phases:
            for step in range(1, self.count):
                action(step - 1, (self.line + step) % self.count)

    def start(self):
        self.swap().start()
        self.each_step(lambda index, line: self.own(line, index, self.side).start(), (0,))
        self.keep().start()

    def second(self):
        self.swap().wait_recv()
        self.each_step(lambda index, line: self.own(line, index, 1 - self.side).start(), (0,))

    def middle(self, action):
        if self.count == 4:

            @pl.when((self.line == 1) | (self.line == 2))
            def _():
                action(6 - 3 * self.line, 3 * self.line - 3)

    def onward(self, origin, line, part):
        return self.copy(origin, line, 4, part, self.place(origin, part))

    def forward(self):
        for part in (self.side, 1 - self.side):
            self.each_step(
                lambda index, line, part=part: self.own(line, index, part).start(), (1,)
            )

            def action(origin, line, part=part):
                self.arrival(origin, part).wait_recv()
                self.onward(origin, line, part).start()

            self.middle(action)

    def finish(self):
        for part in (self.side, 1 - self.side):
            self.each_step(
                lambda index, line, part=part: self.own(line, index, part).wait_send()
            )
            self.middle(
                lambda origin, line, part=part: self.onward(origin, line, part).wait_send()
            )
            for origin in range(self.count):
                pending = self.line != origin
                if self.count == 4 and origin == 0:
                    pending = pending & (self.line != 2)
                if self.count == 4 and origin == 3:
                    pending = pending & (self.line != 1)

                @pl.when(pending)
                def _(origin=origin, part=part):
                    self.arrival(origin, part).wait_recv()

        self.keep().wait()
        self.swap().wait_send()


class Stream:
    def __init__(self, source, target, sems, from_row=0, to_row=0, columns=None):
        self.source, self.target, self.sems = source, target, sems
        self.from_row, self.to_row, self.columns = from_row, to_row, columns
        self.pieces = sems.shape[0]

    def copy(self, r):
        source = (pl.ds(r + self.from_row, CHUNK),)
        if self.columns is not None:
            source += (self.columns,)
        return pltpu.make_async_copy(
            self.source.at[source],
            self.target.at[pl.ds(r + self.to_row, CHUNK)],
            self.sems.at[r // CHUNK],
        )

    def start(self, r):
        self.copy(r).start()

    def wait(self, r):
        self.copy(r).wait()

    def start_all(self):
        for k in range(self.pieces):
            self.start(k * CHUNK)

    def wait_all(self):
        for k in range(self.pieces):
            self.wait(k * CHUNK)


class Swap:
    def __init__(self, values, outs, send, receive, local):
        line, side, deck, core = spot()
        self.copies = []
        for k, (value, out) in enumerate(zip(values, outs)):
            self.copies.append(
                remote(
                    value.at[1 - side],
                    out.at[side],
                    send.at[k],
                    receive.at[k],
                    seat(line, 1 - side, deck, core),
                )
            )
            self.copies.append(
                pltpu.make_async_copy(value.at[side], out.at[side], local.at[k])
            )

    @staticmethod
    def scratch(values):
        return [pltpu.SemaphoreType.DMA((len(values),))] * 3 if values else []

    def start(self):
        for copy in self.copies:
            copy.start()

    def finish(self):
        for copy in self.copies:
            copy.wait()


def cargo_peers(count):
    return group_peers() + line_peers(count)


def piece_shape(count, piece):
    if isinstance(piece, tuple):
        return count, 2 * piece[0].shape[0], piece[2]
    return count, 2 * piece.shape[1], piece.shape[2]


def cargo_outs(count, cargo):
    return [(piece_shape(count, piece), BF16, ANY) for piece in cargo]


def cargo_ins(cargo):
    return [(piece[0] if isinstance(piece, tuple) else piece, ANY) for piece in cargo]


def cargo_starts(cargo):
    return [piece[1] if isinstance(piece, tuple) else 0 for piece in cargo]


def cargo_scratch(count, cargo):
    return [sem for _ in cargo for sem in Freight.scratch(count)]


def load(count, starts, halves, targets, sems):
    return [
        Freight(count, half, target, sems[4 * k : 4 * k + 4], starts[k])
        for k, (half, target) in enumerate(zip(halves, targets))
    ]


def flat_rows(values):
    return [value.reshape(-1, value.shape[2]) for value in values]


def call(kernel, outs, ins, scratch, identity, name):
    results = pl.pallas_call(
        kernel,
        out_shape=[jax.ShapeDtypeStruct(shape, kind) for shape, kind, _ in outs],
        in_specs=[space for _, space in ins],
        out_specs=[space for _, _, space in outs],
        scratch_shapes=scratch,
        compiler_params=pltpu.CompilerParams(
            collective_id=identity, has_side_effects=True, vmem_limit_bytes=GRANT
        ),
        name=name,
    )(*[value for value, _ in ins])
    return list(results)


class GroupGather:
    def __init__(self, source, target, send, receive, local):
        self.source, self.target = source, target
        self.send, self.receive = send, receive
        self.local = local
        self.here = spot()

    @staticmethod
    def scratch():
        return [
            pltpu.SemaphoreType.DMA((11,)),
            pltpu.SemaphoreType.DMA((11,)),
            pltpu.SemaphoreType.DMA,
        ]

    def half(self, ref, h):
        rows = self.source.shape[0] // 2
        return ref.at[pl.ds(h * rows, rows)]

    def make(self):
        line, side, deck, core = self.here
        sibling, across, above = group_peers()
        mine = rank(side, deck, core)
        beside = rank(1 - side, deck, core)
        over = rank(side, 1 - deck, core)
        corner = rank(1 - side, 1 - deck, core)

        def own(h, peer, index):
            return remote(
                self.half(self.source, h),
                self.half(self.target.at[mine], h),
                self.send.at[index],
                self.receive.at[index],
                peer,
            )

        def relay(block, h, peer, index):
            ref = self.half(self.target.at[block], h)
            return remote(ref, ref, self.send.at[index], self.receive.at[index], peer)

        self.keep = pltpu.make_async_copy(self.source, self.target.at[mine], self.local)
        self.first = [
            own(0, across, 0),
            own(1, above, 1),
            own(0, above, 2),
            own(1, across, 3),
        ]
        self.near = remote(
            self.source, self.target.at[mine], self.send.at[4], self.receive.at[4], sibling
        )
        self.second = [relay(beside, 0, above, 5), relay(over, 1, across, 6)]
        self.last = [
            relay(beside, 0, sibling, 7),
            relay(over, 1, sibling, 8),
            relay(over, 0, sibling, 9),
            relay(beside, 1, sibling, 10),
        ]
        self.corner = corner

    def start(self):
        self.make()
        self.first[1].start()
        self.first[2].start()
        self.near.start()
        self.keep.start()

    def start_across(self):
        self.first[0].start()
        self.first[3].start()

    def landed(self):
        self.near.wait_recv()
        self.keep.wait()

    def landed_relays(self):
        for copy in self.last:
            copy.wait_recv()

    def forward(self):
        for k in range(2):
            self.first[k].wait_recv()
            self.second[k].start()
            self.last[k].start()
        for k in range(2, 4):
            self.first[k].wait_recv()
            self.last[k].start()


def corner_relay(gather, send, receive):
    sibling = group_peers()[0]
    out = []
    for h in range(2):
        ref = gather.half(gather.target.at[gather.corner], h)
        out.append(remote(ref, ref, send.at[h], receive.at[h], sibling))
    return out


def group_finish(gather, send, receive, early=False):
    relays = corner_relay(gather, send, receive)
    for k in range(2):
        gather.second[k].wait_recv()
        relays[k].start()
    if not early:
        gather.landed()
        gather.landed_relays()
    for copy in [gather.near] + gather.first + gather.second + gather.last:
        copy.wait_send()
    for copy in relays:
        copy.wait()


def rows_scratch():
    return GroupGather.scratch() + [
        pltpu.SemaphoreType.DMA((2,)),
        pltpu.SemaphoreType.DMA((2,)),
    ]


SMALL_GAINS = 5


def first_kernel(count, starts, small_top, *refs):
    loads = len(starts)
    rows = refs[0]
    halves, refs = refs[1 : 1 + loads], refs[1 + loads :]
    everything, normed, pre = refs[:3]
    targets, refs = refs[3 : 3 + loads], refs[3 + loads :]
    incoming, table, weights, result, tails = refs[:5]
    incoming_sems, out_sems, weight_sems, result_sems, tail_sem = refs[5:10]
    sems = refs[10:]
    gather = GroupGather(rows, everything, *sems[:3])
    corner_sems = sems[3:5]
    small, branch, *others = load(count, starts, halves, targets, sems[5:])
    shares = 2 * count
    line, side, deck, core = spot()
    greet(cargo_peers(count))
    small.start()
    branch.start()
    small.second()
    branch.second()
    for freight in others:
        freight.start()
    gather.start()
    gather.start_across()
    small.forward()
    for freight in others:
        freight.second()
    small.finish()
    tail = pltpu.make_async_copy(targets[0], tails, tail_sem)
    tail.start()
    tail.wait()

    block_rows, features = rows.shape
    gain = jnp.concatenate(
        [
            tails[
                k // 2,
                (k % 2) * (small_top + 16) + small_top : (k % 2 + 1) * (small_top + 16),
                : features // shares,
            ].astype(F32)[SMALL_GAINS : SMALL_GAINS + 1]
            for k in range(shares)
        ],
        axis=1,
    )

    def block(ref, g):
        return ref.at[pl.ds(pl.multiple_of(g * block_rows, block_rows), block_rows)]

    def norm_blocks(pair):
        fetches = [
            pltpu.make_async_copy(everything.at[g], incoming.at[k], incoming_sems.at[k])
            for k, g in enumerate(pair)
        ]
        for fetch in fetches:
            fetch.start()
        for k, g in enumerate(pair):
            fetches[k].wait()

            def norm_rows(i, carry, k=k, g=g):
                r = pl.multiple_of(i * 32, 32)
                value = incoming[k, pl.ds(r, 32), :].astype(F32)
                mean = jnp.mean(value * value, axis=1, keepdims=True)
                unit = value * lax.rsqrt(mean + EPSILON)
                base = pl.multiple_of(g * block_rows + r, 32)
                table[pl.ds(base, 32), :] = (unit * gain).astype(BF16)
                return carry

            lax.fori_loop(0, block_rows // 32, norm_rows, 0)
            pltpu.make_async_copy(block(table, g), block(normed, g), out_sems.at[g]).start()

    def both_cores(s, d):
        return [rank(s, d, core), rank(s, d, 1 - core)]

    gather.landed()
    branch.forward()
    gather.forward()
    for freight in others:
        freight.forward()
    norm_blocks(both_cores(side, deck))
    gather.landed_relays()
    norm_blocks(both_cores(1 - side, deck))
    norm_blocks(both_cores(side, 1 - deck))
    group_finish(gather, *corner_sems, early=True)
    norm_blocks(both_cores(1 - side, 1 - deck))
    branch.finish()
    depth = targets[1].shape[1]
    loading = [
        pltpu.make_async_copy(
            targets[1].at[k], weights.at[pl.ds(k * depth, depth)], weight_sems.at[k]
        )
        for k in range(count)
    ]
    for copy in loading:
        copy.start()
    for copy in loading:
        copy.wait()
    lanes, width = weights.shape[1] // 2, pre.shape[1] // 2
    shift = 2 * lanes - width
    inside = lax.broadcasted_iota(jnp.int32, (CHUNK, width), 1) < lanes
    writes = Stream(result, pre, result_sems)

    def product(r):
        where = pl.ds(r, CHUNK)
        both = jnp.dot(table[where, :], weights[...], preferred_element_type=F32)
        result[where, :width] = jnp.where(inside, both[:, :width], 0.0)
        later = pltpu.roll(both[:, shift:], lanes, 1)
        result[where, width:] = jnp.where(inside, later, 0.0)
        writes.start(r)

    chunks(pre.shape[0], product)
    for g in range(8):
        pltpu.make_async_copy(block(table, g), block(normed, g), out_sems.at[g]).wait()
    writes.wait_all()
    for freight in others:
        freight.finish()


def first(count, rows, cargo, width):
    total = 8 * rows.shape[0]
    small, branch = cargo[:2]
    out = call(
        functools.partial(first_kernel, count, cargo_starts(cargo), small.shape[1] - 16),
        [
            ((8,) + rows.shape, BF16, ANY),
            ((total, rows.shape[1]), BF16, ANY),
            ((total, 2 * width), F32, ANY),
        ]
        + cargo_outs(count, cargo),
        [(rows, ANY)] + cargo_ins(cargo),
        [
            pltpu.VMEM((2,) + rows.shape, BF16),
            pltpu.VMEM((total, rows.shape[1]), BF16),
            pltpu.VMEM((rows.shape[1], branch.shape[2]), BF16),
            pltpu.VMEM((total, 2 * width), F32),
            pltpu.VMEM(piece_shape(count, small), BF16),
            pltpu.SemaphoreType.DMA((2,)),
            pltpu.SemaphoreType.DMA((8,)),
            pltpu.SemaphoreType.DMA((count,)),
            pltpu.SemaphoreType.DMA((total // CHUNK,)),
            pltpu.SemaphoreType.DMA,
        ]
        + rows_scratch()
        + cargo_scratch(count, cargo),
        0,
        "first",
    )
    return out[1:4] + flat_rows(out[4:])


def rows_kernel(count, starts, *refs):
    loads = len(starts)
    rows, halves = refs[0], refs[1 : 1 + loads]
    everything, targets = refs[1 + loads], refs[2 + loads : 2 + 2 * loads]
    sems = refs[2 + 2 * loads :]
    gather = GroupGather(rows, everything, *sems[:3])
    freights = load(count, starts, halves, targets, sems[5:])
    greet(cargo_peers(count))
    for freight in freights:
        freight.start()
    gather.start()
    for freight in freights:
        freight.second()
    gather.start_across()
    gather.forward()
    for freight in freights:
        freight.forward()
    group_finish(gather, *sems[3:5])
    for freight in freights:
        freight.finish()


def gather_rows(count, rows, cargo, identity):
    out = call(
        functools.partial(rows_kernel, count, cargo_starts(cargo)),
        [((8,) + rows.shape, BF16, ANY)] + cargo_outs(count, cargo),
        [(rows, ANY)] + cargo_ins(cargo),
        rows_scratch() + cargo_scratch(count, cargo),
        identity,
        "gather_rows",
    )
    return [out[0].reshape(-1, rows.shape[1])] + flat_rows(out[1:])


def turned(left, right, out, tiles, low, high):
    size = left.shape[1] // tiles

    def body(i, carry):
        place = pl.ds(pl.multiple_of(i * size, size), size)
        total = lax.dot_general(left[:, place], right[...], TN, preferred_element_type=F32)
        out[place, :] = total.astype(BF16)
        return carry

    lax.fori_loop(low, high, body, 0)


def plain_rows_kernel(rows, left, right, everything, product, left_here, right_here, *sems):
    gather = GroupGather(rows, everything, *sems[1:4])
    loading = [
        pltpu.make_async_copy(left, left_here, sems[0].at[0]),
        pltpu.make_async_copy(right, right_here, sems[0].at[1]),
    ]
    greet(group_peers())
    gather.start()
    gather.start_across()
    for copy in loading:
        copy.start()
    for copy in loading:
        copy.wait()
    turned(left_here, right_here, product, 4, 0, 4)
    gather.forward()
    group_finish(gather, *sems[4:6])


def gather_plain(rows, left, right, identity):
    out = call(
        plain_rows_kernel,
        [((8,) + rows.shape, BF16, ANY), ((left.shape[1], right.shape[1]), BF16, VMEM)],
        [(rows, ANY), (left, ANY), (right, ANY)],
        [
            pltpu.VMEM(left.shape, BF16),
            pltpu.VMEM(right.shape, BF16),
            pltpu.SemaphoreType.DMA((2,)),
        ]
        + rows_scratch(),
        identity,
        "gather_rows",
    )
    return out[0].reshape(-1, rows.shape[1]), out[1]


def flip(value, bit):
    return 1 - value if bit else value


def whole_group():
    line, side, deck, core = spot()
    return [
        seat(line, flip(side, k & 4), flip(deck, k & 2), flip(core, k & 1)) for k in range(1, 8)
    ]


class GainSum:
    def __init__(self, count, gains, totals, near, far, send, receive, far_send, far_receive):
        self.gains, self.totals, self.near, self.far = gains, totals, near, far
        self.first = [
            remote(gains, near.at[k], send.at[k], receive.at[k], peer)
            for k, peer in enumerate(whole_group())
        ]
        self.second_copies = [
            remote(far.at[0], far.at[1 + k], far_send.at[k], far_receive.at[k], peer)
            for k, peer in enumerate(line_peers(count))
        ]

    @staticmethod
    def scratch(count, gains):
        return [
            pltpu.VMEM((7,) + gains.shape, F32),
            pltpu.VMEM((count,) + gains.shape, F32),
            pltpu.SemaphoreType.DMA((7,)),
            pltpu.SemaphoreType.DMA((7,)),
            pltpu.SemaphoreType.DMA((count,)),
            pltpu.SemaphoreType.DMA((count,)),
        ]

    def start(self):
        for copy in self.first:
            copy.start()

    def second(self):
        for copy in self.first:
            copy.wait()
        total = self.gains[...]
        for k in range(7):
            total = total + self.near[k]
        self.far[0] = total
        for copy in self.second_copies:
            copy.start()

    def finish(self):
        for copy in self.second_copies:
            copy.wait()
        total = self.far[0]
        for k in range(len(self.second_copies)):
            total = total + self.far[1 + k]
        self.totals[...] = total


class Fold:
    OWN, ACROSS, ABOVE, CORNER = 0, 1, 2, 3

    def __init__(self, plan, lefts, rights, out, refs):
        self.plan, self.lefts, self.rights, self.out = plan, lefts, rights, out
        self.mine, self.stage, self.near = refs[:3]
        self.across_sum, self.above_sum, self.leaving, self.arriving = refs[3:7]
        send, receive, self.near_send, self.near_receive = refs[7:11]
        self.line, self.side, self.deck, self.core = spot()
        sibling, across, above = group_peers()
        self.sibling = sibling
        self.rows, self.width = out.shape
        self.half = self.rows // 2
        self.ships = [
            remote(
                self.leaving.at[k], self.arriving.at[k], send.at[k], receive.at[k], peer
            )
            for k, peer in enumerate((above, across, above, across, across, above))
        ]

    @staticmethod
    def scratch(rows, width):
        half = rows // 2
        return [
            pltpu.VMEM((rows, width), F32),
            pltpu.VMEM((2, rows, width), BF16),
            pltpu.VMEM((4, rows, width), BF16),
            pltpu.VMEM((half, width), F32),
            pltpu.VMEM((half, width), F32),
            pltpu.VMEM((6, half, width), BF16),
            pltpu.VMEM((6, half, width), BF16),
            pltpu.SemaphoreType.DMA((6,)),
            pltpu.SemaphoreType.DMA((6,)),
            pltpu.SemaphoreType.DMA((4,)),
            pltpu.SemaphoreType.DMA((4,)),
        ]

    def product(self, which, store):
        base = pl.multiple_of(which * self.rows, self.rows)
        step = 512

        def body(j, carry):
            columns = pl.ds(pl.multiple_of(j * step, step), step)
            total = None
            for (which_left, start), right in zip(self.plan, self.rights):
                part = lax.dot_general(
                    self.lefts[which_left][pl.ds(base, self.rows), start : start + right.shape[1]],
                    right[columns, :],
                    NT,
                    preferred_element_type=F32,
                )
                total = part if total is None else total + part
            store(columns, total)
            return carry

        lax.fori_loop(0, self.width // step, body, 0)

    def sweep(self, action):
        def body(i, carry):
            action(pl.multiple_of(i * 16, 16))
            return carry

        lax.fori_loop(0, self.half // 16, body, 0)

    def near_copy(self, q):
        return remote(
            self.stage.at[q % 2],
            self.near.at[q],
            self.near_send.at[q],
            self.near_receive.at[q],
            self.sibling,
        )

    def chip_sum(self, q, h, r):
        place = pl.ds(h * self.half + r, 16)
        return self.mine[place, :] + self.near[q, place, :].astype(F32)

    def block(self, q):
        s, d = [
            (self.side, self.deck),
            (1 - self.side, self.deck),
            (self.side, 1 - self.deck),
            (1 - self.side, 1 - self.deck),
        ][q]
        if q < 2:
            self.near_copy(q + 2).wait_send()

        def put_stage(columns, total):
            self.stage[q % 2, :, columns] = total.astype(BF16)

        def put_mine(columns, total):
            target = self.out if q == self.OWN else self.mine
            target[:, columns] = total

        self.product(rank(s, d, 1 - self.core), put_stage)
        self.near_copy(q).start()
        self.product(rank(s, d, self.core), put_mine)
        self.near_copy(q).wait_recv()

    def send(self, k):
        self.ships[k].start()

    def begin(self, freights=()):
        self.block(self.CORNER)

        def corner(r):
            for h in range(2):
                self.leaving[h, pl.ds(r, 16), :] = self.chip_sum(self.CORNER, h, r).astype(BF16)

        self.sweep(corner)
        self.send(0)
        self.send(1)
        self.block(self.ABOVE)

        def above(r):
            place = pl.ds(r, 16)
            self.leaving[2, place, :] = self.chip_sum(self.ABOVE, 0, r).astype(BF16)
            self.above_sum[place, :] = self.chip_sum(self.ABOVE, 1, r)

        self.sweep(above)
        self.send(2)
        for freight in freights:
            freight.second()
        self.block(self.ACROSS)

        def across(r):
            place = pl.ds(r, 16)
            self.leaving[3, place, :] = self.chip_sum(self.ACROSS, 1, r).astype(BF16)
            self.across_sum[place, :] = self.chip_sum(self.ACROSS, 0, r)

        self.sweep(across)
        self.send(3)
        self.block(self.OWN)

    def middle(self):
        self.ships[0].wait_recv()

        def across(r):
            place = pl.ds(r, 16)
            total = self.across_sum[place, :] + self.arriving[0, place, :].astype(F32)
            self.leaving[4, place, :] = total.astype(BF16)

        self.sweep(across)
        self.send(4)
        self.ships[1].wait_recv()

        def above(r):
            place = pl.ds(r, 16)
            total = self.above_sum[place, :] + self.arriving[1, place, :].astype(F32)
            self.leaving[5, place, :] = total.astype(BF16)

        self.sweep(above)
        self.send(5)

    def finish(self, store):
        for k in range(2, 6):
            self.ships[k].wait_recv()

        def total(r):
            for h, pair in enumerate(((2, 4), (3, 5))):
                place, here = pl.ds(r, 16), pl.ds(h * self.half + r, 16)
                value = self.out[here, :] + self.near[self.OWN, here, :].astype(F32)
                for k in pair:
                    value = value + self.arriving[k, place, :].astype(F32)
                store(here, value)

        self.sweep(total)
        for k in range(6):
            self.ships[k].wait_send()
        for q in range(2):
            self.near_copy(q).wait_send()


def unit_rows(value):
    scale = lax.rsqrt(jnp.mean(value * value, axis=1, keepdims=True) + EPSILON)
    return value * scale, scale


def norm_back_rows(grad, unit, scale, gain):
    grad_unit = grad * gain
    inner = jnp.mean(grad_unit * unit, axis=1, keepdims=True)
    return scale * (grad_unit - unit * inner), jnp.sum(grad * unit, axis=0, keepdims=True)


def mixer_fold_kernel(count, jobs, starts, left, right, *refs):
    loads = len(starts)
    inputs, gain, refs = refs[0], refs[1], refs[2:]
    halves, refs = refs[:loads], refs[loads:]
    out, normed, refs = refs[0], refs[1], refs[2:]
    targets, refs = refs[:loads], refs[loads:]
    fold = Fold(jobs[0], [left], [right], out, refs[:11])
    freights = load(count, starts, halves, targets, refs[11:])
    greet(cargo_peers(count))
    for freight in freights:
        freight.start()
    fold.begin(freights)
    fold.middle()
    for freight in freights:
        freight.forward()

    def store(here, value):
        value = value + inputs[here, :].astype(F32)
        out[here, :] = value
        normed[here, :] = (unit_rows(value)[0] * gain[...]).astype(BF16)

    fold.finish(store)
    for freight in freights:
        freight.finish()


def plan_of(lefts_rights):
    lefts, rights, plan = [], [], []
    for k, (left, parts) in enumerate(lefts_rights):
        lefts.append((left, VMEM))
        start = 0
        for part in parts:
            rights.append((part, VMEM))
            plan.append((k, start))
            start += part.shape[1]
    return plan, lefts + rights


def mixer_fold(count, merged, mixer, inputs, gain, cargo):
    plan, ins = plan_of([(merged, [mixer])])
    rows, width = inputs.shape
    out = call(
        functools.partial(mixer_fold_kernel, count, [plan], cargo_starts(cargo)),
        [((rows, width), F32, VMEM), ((rows, width), BF16, VMEM)] + cargo_outs(count, cargo),
        ins + [(inputs, VMEM), (gain, VMEM)] + cargo_ins(cargo),
        Fold.scratch(rows, width) + cargo_scratch(count, cargo),
        3,
        "mixer_fold",
    )
    return out[:2] + flat_rows(out[2:])


def feed_fold_kernel(plan, parts, left, other, *refs):
    rights, refs = refs[:parts], refs[parts:]
    normed, hidden, cotangent, gain, refs = *refs[:4], refs[4:]
    out, low, gain_sum, grads = refs[:4]
    fold = Fold(plan, [left, other], rights, out, refs[4:15])
    normed_here, load_sem = refs[15:]
    greet(group_peers())
    loading = pltpu.make_async_copy(normed, normed_here, load_sem)
    loading.start()
    fold.begin()
    fold.middle()
    loading.wait()
    turned(normed_here, left, grads, 4, 0, 4)
    gain_sum[...] = jnp.zeros_like(gain_sum)

    def store(here, value):
        unit, scale = unit_rows(hidden[here, :])
        back, terms = norm_back_rows(value, unit, scale, gain[...])
        gain_sum[0:1, :] += terms
        back = cotangent[here, :].astype(F32) + back
        out[here, :] = back
        low[here, :] = back.astype(BF16)

    fold.finish(store)


def feed_fold(grad_gating, grad_lifting, gates, ups, normed, hidden, cotangent, gain):
    plan, ins = plan_of([(grad_gating, gates), (grad_lifting, ups)])
    rows, width = hidden.shape
    return call(
        functools.partial(feed_fold_kernel, plan, len(gates) + len(ups)),
        [
            ((rows, width), F32, VMEM),
            ((rows, width), BF16, VMEM),
            ((8, width), F32, VMEM),
            ((normed.shape[1], grad_gating.shape[1]), BF16, VMEM),
        ],
        ins + [(normed, ANY), (hidden, VMEM), (cotangent, VMEM), (gain, VMEM)],
        Fold.scratch(rows, width)
        + [pltpu.VMEM(normed.shape, BF16), pltpu.SemaphoreType.DMA],
        6,
        "feed_fold",
    )


def last_fold_kernel(count, plans, parts, swaps, left, right, feed_left, *refs):
    rights, refs = refs[:parts], refs[parts:]
    inputs, gain, grad_hidden, hidden, second, refs = *refs[:5], refs[5:]
    values, refs = refs[:swaps], refs[swaps:]
    input_grad, output, totals = refs[:3]
    swapped, refs = refs[3 : 3 + swaps], refs[3 + swaps :]
    out, feed_out, sums, terms_here, refs = *refs[:4], refs[4:]
    fold = Fold(plans[0], [left], [right], out, refs[:11])
    feed = Fold(plans[1], [feed_left], rights, feed_out, refs[11:22])
    swap = Swap(values, swapped, *refs[22:25])
    gain_sum = GainSum(count, sums, totals, *refs[25:])
    greet(whole_group() + line_peers(count))
    swap.start()
    fold.begin()
    feed.begin()
    fold.middle()
    feed.middle()
    terms_here[...] = jnp.zeros_like(terms_here)

    def store(here, value):
        unit, scale = unit_rows(inputs[here, :].astype(F32))
        back, terms = norm_back_rows(value, unit, scale, gain[...])
        terms_here[0:1, :] += terms
        input_grad[here, :] = (grad_hidden[here, :] + back).astype(BF16)

    fold.finish(store)
    shares, slim = sums.shape[0] // 2, sums.shape[1]
    for k in range(shares):
        columns = slice(k * slim, (k + 1) * slim)
        sums[k : k + 1, :] = terms_here[0:1, columns]
        sums[shares + k : shares + k + 1, :] = second[0:1, columns]
    gain_sum.start()
    gain_sum.second()

    def store_output(here, value):
        output[here, :] = (hidden[here, :] + value).astype(BF16)

    feed.finish(store_output)
    gain_sum.finish()
    swap.finish()


def last_fold(count, grads, branch, feed_left, downs, inputs, gain, grad_hidden, hidden, second, swaps):
    plan, ins = plan_of([(grads, [branch])])
    feed_plan, feed_ins = plan_of([(feed_left, downs)])
    rows, width = hidden.shape
    both = jax.ShapeDtypeStruct((4 * count, width // (2 * count)), F32)
    return call(
        functools.partial(last_fold_kernel, count, (plan, feed_plan), len(downs), len(swaps)),
        [
            ((rows, width), BF16, VMEM),
            ((rows, width), BF16, VMEM),
            (both.shape, F32, VMEM),
        ]
        + [(value.shape, BF16, ANY) for value in swaps],
        ins
        + feed_ins
        + [(value, VMEM) for value in (inputs, gain, grad_hidden, hidden, second)]
        + [(value, ANY) for value in swaps],
        [
            pltpu.VMEM((rows, width), F32),
            pltpu.VMEM((rows, width), F32),
            pltpu.VMEM(both.shape, F32),
            pltpu.VMEM((8, width), F32),
        ]
        + Fold.scratch(rows, width) * 2
        + Swap.scratch(swaps)
        + GainSum.scratch(count, both),
        9,
        "last_fold",
    )


def gelu_both(value):
    square = value * value
    bend = jnp.tanh(GELU_SCALE * value * (1.0 + GELU_CUBE * square))
    act = 0.5 * value * (1.0 + bend)
    slope = 0.5 * (1.0 + bend) + 0.5 * value * (1.0 - bend * bend) * GELU_SCALE * (
        1.0 + 3.0 * GELU_CUBE * square
    )
    return act, slope


def chunks(rows, action, size=CHUNK):
    def body(i, carry):
        action(pl.multiple_of(i * size, size))
        return carry

    lax.fori_loop(0, rows // size, body, 0)


def spans(low, high, action):
    def body(i, carry):
        action(pl.multiple_of(i * CHUNK, CHUNK))
        return carry

    lax.fori_loop(low, high, body, 0)


def tile_scan(mults, adds, rows, width, backward):
    place = lax.broadcasted_iota(jnp.int32, (8, width), 0)

    def inside(base):
        where = pl.ds(base, 8)
        a, b = mults[where, :], adds[where, :]
        for k in (1, 2, 4):
            if backward:
                away, mask = pltpu.roll(a, 8 - k, 0), place < 8 - k
                back = pltpu.roll(b, 8 - k, 0)
            else:
                away, mask = pltpu.roll(a, k, 0), place >= k
                back = pltpu.roll(b, k, 0)
            b = jnp.where(mask, b + a * back, b)
            a = jnp.where(mask, a * away, a)
        return where, a, b

    unroll = 4
    tiles = rows // 8

    def body(i, carry):
        prod, total = carry
        work = []
        for u in range(unroll):
            index = i * unroll + u
            if backward:
                index = tiles - 1 - index
            work.append(inside(pl.multiple_of(index * 8, 8)))
        for where, a, b in work:
            edge = 0 if backward else 7
            adds[where, :] = b + a * total
            mults[where, :] = a * prod
            whole = jnp.broadcast_to(a[edge : edge + 1, :], (8, width))
            extra = jnp.broadcast_to(b[edge : edge + 1, :], (8, width))
            total = extra + whole * total
            prod = whole * prod
        return prod, total

    return lax.fori_loop(
        0, tiles // unroll, body, (jnp.ones((8, width), F32), jnp.zeros((8, width), F32))
    )


def pool(count, prod, total, outgoing, slots, send, receive, backward):
    line, side, deck, core = spot()
    outgoing[0:8, :] = prod
    outgoing[8:16, :] = total
    slots[line, 0:8, :] = prod
    slots[line, 8:16, :] = total
    copies = []
    for k in range(1, count):
        copy = remote(
            outgoing,
            slots.at[line],
            send.at[k],
            receive.at[k],
            seat((line + k) % count, side, deck, core),
        )
        copy.start()
        copies.append(copy)
    for copy in copies:
        copy.wait()
    entering = jnp.zeros_like(prod)
    order = range(count - 1, -1, -1) if backward else range(count)
    for place in order:
        longer = slots[place, 8:16, :] + slots[place, 0:8, :] * entering
        before = (line < place) if backward else (line > place)
        entering = jnp.where(before, longer, entering)
    return entering


def sigmoid(value):
    return 0.5 + 0.5 * jnp.tanh(0.5 * value)


def gates(recur, soft):
    decay = jnp.exp(-8.0 * recur * soft)
    square = (1.0 + GUARD) - decay * decay
    inverse = lax.rsqrt(square)
    return decay, square * inverse, inverse


def scan_kernel(count, starts, *refs):
    loads = len(starts)
    pre, masks, table, gate_weights, cotangent = refs[:5]
    halves, refs = refs[5 : 5 + loads], refs[5 + loads :]
    everything, targets, refs = refs[6], refs[7 : 7 + loads], refs[:6] + refs[7 + loads :]
    saved, refs = refs[:6], refs[6:]
    gate, entry, conv, recur_out, admit_out, state, merged = refs[:7]
    prods, sums, halo, outgoing, slots, edge_sems, send, receive = refs[7:15]
    in_sems, out_sems, head_sems = refs[15:18]
    sems = refs[18:]
    line, side, deck, core = spot()
    rows, width = conv.shape
    gather = GroupGather(cotangent, everything, *sems[:3])
    freights = load(count, starts, halves, targets, sems[5:])
    gate_reads = Stream(pre, gate, in_sems.at[0], columns=pl.ds(0, width))
    entry_reads = Stream(pre, entry, in_sems.at[1], to_row=8, columns=pl.ds(width, width))
    conv_writes = Stream(conv, saved[0], out_sems.at[0])
    recur_writes = Stream(recur_out, saved[1], out_sems.at[1])
    admit_writes = Stream(admit_out, saved[2], out_sems.at[2])
    state_writes = Stream(state, saved[3], out_sems.at[3], 8, 8)
    merged_writes = Stream(merged, saved[4], out_sems.at[4])
    entry_writes = Stream(entry, saved[5], out_sems.at[5], 8, 8)
    heads = [
        pltpu.make_async_copy(local.at[pl.ds(0, 8)], away.at[pl.ds(0, 8)], head_sems.at[k])
        for k, (local, away) in enumerate([(state, saved[3]), (entry, saved[5])])
    ]
    entry_reads.start_all()
    gate_reads.start_all()
    greet(cargo_peers(count))

    def edge(place):
        return remote(
            pre.at[pl.ds(rows - 8, 8), pl.ds(width, width)],
            halo,
            edge_sems.at[0],
            edge_sems.at[1],
            seat(place, side, deck, core),
        )

    @pl.when(line < count - 1)
    def _():
        edge(line + 1).start()

    for freight in freights:
        freight.start()
    gather.start()

    @pl.when(line > 0)
    def _():
        edge(line - 1).wait_recv()
        entry[0:8, :] = halo[...]

    @pl.when(line == 0)
    def _():
        entry[0:8, :] = jnp.zeros((8, width), F32)

    @pl.when(line < count - 1)
    def _():
        edge(line + 1).wait_send()

    heads[1].start()

    def gate_chunk(r):
        entry_reads.wait(r)
        wide = entry[pl.ds(r, CHUNK + 8), :]
        mask = masks[pl.ds(r, CHUNK), :]
        value = table[0:1, :] * wide[8:, :]
        for k in range(1, TAPS):
            value = (
                value + table[k : k + 1, :] * wide[8 - k : 8 - k + CHUNK, :] * mask[:, k - 1 : k]
            )
        where = pl.ds(r, CHUNK)
        conv[where, :] = value
        both = jnp.dot(value.astype(BF16), gate_weights[...], preferred_element_type=F32)
        recur = sigmoid(both[:, :width])
        admit = sigmoid(both[:, width:])
        recur_out[where, :] = recur
        admit_out[where, :] = admit
        decay, root, _ = gates(recur, table[4:5, :])
        opened = mask[:, 3:4]
        norm = root * opened + (1.0 - opened)
        prods[where, :] = decay * opened
        sums[where, :] = norm * admit * value
        for stream in (entry_writes, conv_writes, recur_writes, admit_writes):
            stream.start(r)

    pieces = rows // CHUNK
    spans(0, pieces // 4, gate_chunk)
    for freight in freights:
        freight.second()
    gather.start_across()
    spans(pieces // 4, pieces, gate_chunk)
    prod, total = tile_scan(prods, sums, rows, width, False)
    gather.forward()
    entering = pool(count, prod, total, outgoing, slots, send, receive, False)
    for freight in freights:
        freight.forward()
    state[0:8, :] = entering
    heads[0].start()

    def state_chunk(r):
        gate_reads.wait(r)
        where = pl.ds(r, CHUNK)
        value = sums[where, :] + prods[where, :] * entering[0:1, :]
        state[pl.ds(r + 8, CHUNK), :] = value
        act, _ = gelu_both(gate[where, :])
        merged[where, :] = (value * act).astype(BF16)
        state_writes.start(r)
        merged_writes.start(r)

    chunks(rows, state_chunk)
    for stream in (
        entry_writes,
        conv_writes,
        recur_writes,
        admit_writes,
        state_writes,
        merged_writes,
    ):
        stream.wait_all()
    for copy in heads:
        copy.wait()
    group_finish(gather, *sems[3:5])
    for freight in freights:
        freight.finish()


def scan_forward(count, pre, masks, table, gate_weights, cotangent, cargo):
    rows, width = pre.shape[0], pre.shape[1] // 2
    pieces = rows // CHUNK
    tall = (rows + 8, width)
    saved = [
        ((rows, width), F32),
        ((rows, width), F32),
        ((rows, width), F32),
        (tall, F32),
        ((rows, width), BF16),
        (tall, F32),
    ]
    out = call(
        functools.partial(scan_kernel, count, cargo_starts(cargo)),
        [(shape, kind, ANY) for shape, kind in saved]
        + [((8,) + cotangent.shape, BF16, ANY)]
        + cargo_outs(count, cargo),
        [(pre, ANY), (masks, VMEM), (table, VMEM), (gate_weights, VMEM), (cotangent, ANY)]
        + cargo_ins(cargo),
        [
            pltpu.VMEM((rows, width), F32),
            pltpu.VMEM(tall, F32),
            pltpu.VMEM((rows, width), F32),
            pltpu.VMEM((rows, width), F32),
            pltpu.VMEM((rows, width), F32),
            pltpu.VMEM(tall, F32),
            pltpu.VMEM((rows, width), BF16),
            pltpu.VMEM((rows, width), F32),
            pltpu.VMEM((rows, width), F32),
            pltpu.VMEM((8, width), F32),
            pltpu.VMEM((16, width), F32),
            pltpu.VMEM((count, 16, width), F32),
            pltpu.SemaphoreType.DMA((2,)),
            pltpu.SemaphoreType.DMA((count,)),
            pltpu.SemaphoreType.DMA((count,)),
            pltpu.SemaphoreType.DMA((2, pieces)),
            pltpu.SemaphoreType.DMA((6, pieces)),
            pltpu.SemaphoreType.DMA((2,)),
        ]
        + rows_scratch()
        + cargo_scratch(count, cargo),
        2,
        "scan_forward",
    )
    return out[:6] + [out[6].reshape(-1, cotangent.shape[1])] + flat_rows(out[7:])


def back_kernel(count, lanes, swaps, *refs):
    pre, low, outlet = refs[:3]
    saved, refs = refs[3:8], refs[8:]
    masks, table, gate_weights = refs[:3]
    values, refs = refs[3 : 3 + swaps], refs[3 + swaps :]
    grad_pre, grad_gates, grad_table = refs[:3]
    swapped, refs = refs[3 : 3 + swaps], refs[3 + swaps :]
    gate, conv, recur_in, admit_in, state, entry, lows = refs[:7]
    prods, sums, mixes, outgoing, slots, edge_sems, send, receive = refs[7:15]
    in_sems, low_sems, head_sems = refs[15:18]
    line, side, deck, core = spot()
    rows, width = conv.shape
    pieces = rows // CHUNK
    swap = Swap(values, swapped, *refs[18:])
    conv_reads = Stream(saved[0], conv, in_sems.at[0])
    recur_reads = Stream(saved[1], recur_in, in_sems.at[1])
    admit_reads = Stream(saved[2], admit_in, in_sems.at[2])
    state_reads = Stream(saved[3], state, in_sems.at[3], 8, 8)
    entry_reads = Stream(saved[4], entry, in_sems.at[4], 8, 8)
    gate_reads = Stream(pre, gate, in_sems.at[5], columns=pl.ds(0, width))
    heads = [
        pltpu.make_async_copy(away.at[pl.ds(0, 8)], local.at[pl.ds(0, 8)], head_sems.at[k])
        for k, (local, away) in enumerate([(state, saved[3]), (entry, saved[4])])
    ]

    def fetch(i):
        slot = i % 2
        start = pl.multiple_of(i * CHUNK, CHUNK)
        return pltpu.make_async_copy(
            low.at[pl.ds(start, CHUNK)], lows.at[slot], low_sems.at[slot]
        )

    fetch(0).start()
    for k in range(pieces):
        for stream in (gate_reads, recur_reads, state_reads):
            stream.start(k * CHUNK)
    for copy in heads:
        copy.start()
    for stream in (conv_reads, admit_reads, entry_reads):
        stream.start_all()
    greet(line_peers(count) + ([seat(line, 1 - side, deck, core)] if swaps else []))
    swap.start()

    def direct(i, carry):
        r = pl.multiple_of(i * CHUNK, CHUNK)

        @pl.when(i + 1 < pieces)
        def _():
            fetch(i + 1).start()

        fetch(i).wait()
        for stream in (gate_reads, recur_reads, state_reads):
            stream.wait(r)
        where = pl.ds(r, CHUNK)
        grad = jnp.dot(lows[i % 2], outlet[...], preferred_element_type=F32)
        act, slope = gelu_both(gate[where, :])
        gate[where, :] = grad * state[pl.ds(r + 8, CHUNK), :] * slope
        straight = grad * act
        carried = jnp.exp(-8.0 * recur_in[where, :] * table[4:5, :]) * masks[where, 3:4]
        mixes[where, :] = straight
        prods[where, :] = carried
        sums[where, :] = carried * straight
        return carry

    lax.fori_loop(0, pieces, direct, 0)
    prods[rows : rows + 8, :] = jnp.ones((8, width), F32)
    sums[rows : rows + 8, :] = jnp.zeros((8, width), F32)
    prod, total = tile_scan(prods, sums, rows, width, True)
    entering = pool(count, prod, total, outgoing, slots, send, receive, True)
    for copy in heads:
        copy.wait()
    grad_gates[...] = jnp.zeros_like(grad_gates)
    grad_table[...] = jnp.zeros_like(grad_table)

    def fold_rows(value):
        return jnp.sum(value, axis=0, keepdims=True)

    def gate_chunk(r):
        conv_reads.wait(r)
        admit_reads.wait(r)
        where = pl.ds(r, CHUNK)
        wide = pl.ds(r, CHUNK + 8)
        later = sums[wide, :] + prods[wide, :] * entering[0:1, :]
        grad = mixes[where, :] + later[1 : CHUNK + 1, :]
        before = state[wide, :][7 : CHUNK + 7, :]
        soft = table[4:5, :]
        recur, admit, value = recur_in[where, :], admit_in[where, :], conv[where, :]
        decay, root, inverse = gates(recur, soft)
        opened = masks[where, 3:4]
        norm = root * opened + (1.0 - opened)
        flow = grad * admit
        grad_log = opened * (grad * before * decay - flow * value * decay * decay * inverse)
        grad_table[4:5, :] += fold_rows(grad_log * (-8.0 * recur))
        grad_rate = (grad_log * (-8.0 * soft) * recur * (1.0 - recur)).astype(BF16)
        grad_inlet = (flow * norm * value * (1.0 - admit)).astype(BF16)
        both = jnp.concatenate([grad_rate, grad_inlet], axis=1)
        grad_gates[...] += lax.dot_general(
            value.astype(BF16), both, TN, preferred_element_type=F32
        )
        mixes[where, :] = flow * norm + lax.dot_general(
            both, gate_weights[...], NT, preferred_element_type=F32
        )

    gate_chunk(0)

    def edge(place):
        return remote(
            mixes.at[pl.ds(0, 8)],
            mixes.at[pl.ds(rows, 8)],
            edge_sems.at[0],
            edge_sems.at[1],
            seat(place, side, deck, core),
        )

    @pl.when(line > 0)
    def _():
        edge(line - 1).start()

    spans(1, pieces, gate_chunk)

    @pl.when(line < count - 1)
    def _():
        edge(line + 1).wait_recv()

    @pl.when(line == count - 1)
    def _():
        mixes[rows : rows + 8, :] = jnp.zeros((8, width), F32)

    spare = width - lanes
    shift = 2 * lanes - width

    def entry_chunk(r):
        entry_reads.wait(r)
        where, wide = pl.ds(r, CHUNK), pl.ds(r, CHUNK + 8)
        ahead, mask = mixes[wide, :], masks[where, :]
        source = entry[wide, :]
        here = ahead[:CHUNK, :]
        total = table[0:1, :] * here
        grad_table[0:1, :] += fold_rows(here * source[8:, :])
        for k in range(1, TAPS):
            total = total + table[k : k + 1, :] * ahead[k : k + CHUNK, :] * mask[:, 3 + k : 4 + k]
            grad_table[k : k + 1, :] += fold_rows(
                here * source[8 - k : 8 - k + CHUNK, :] * mask[:, k - 1 : k]
            )
        total = pltpu.roll(total, spare, 1)
        first = gate[where, :]
        middle = first[:, shift:] + total[:, : width - shift]
        grad_pre[where, :shift] = first[:, :shift].astype(BF16)
        grad_pre[where, shift:width] = middle.astype(BF16)
        grad_pre[where, width:] = total[:, width - shift :].astype(BF16)

    chunks(rows, entry_chunk)

    @pl.when(line > 0)
    def _():
        edge(line - 1).wait_send()

    swap.finish()


def scan_backward(count, lanes, pre, low, outlet, saved, masks, table, gate_weights, swaps):
    rows, width = pre.shape[0], pre.shape[1] // 2
    pieces = rows // CHUNK
    tall = (rows + 8, width)
    return call(
        functools.partial(back_kernel, count, lanes, len(swaps)),
        [
            ((rows, 2 * lanes), BF16, VMEM),
            ((width, 2 * width), F32, VMEM),
            ((8, width), F32, VMEM),
        ]
        + [(value.shape, BF16, ANY) for value in swaps],
        [(pre, ANY), (low, ANY), (outlet, VMEM)]
        + [(value, ANY) for value in saved]
        + [(value, VMEM) for value in (masks, table, gate_weights)]
        + [(value, ANY) for value in swaps],
        [
            pltpu.VMEM((rows, width), F32),
            pltpu.VMEM((rows, width), F32),
            pltpu.VMEM((rows, width), F32),
            pltpu.VMEM((rows, width), F32),
            pltpu.VMEM(tall, F32),
            pltpu.VMEM(tall, F32),
            pltpu.VMEM((2, CHUNK, low.shape[1]), BF16),
            pltpu.VMEM(tall, F32),
            pltpu.VMEM(tall, F32),
            pltpu.VMEM(tall, F32),
            pltpu.VMEM((16, width), F32),
            pltpu.VMEM((count, 16, width), F32),
            pltpu.SemaphoreType.DMA((2,)),
            pltpu.SemaphoreType.DMA((count,)),
            pltpu.SemaphoreType.DMA((count,)),
            pltpu.SemaphoreType.DMA((6, pieces)),
            pltpu.SemaphoreType.DMA((2,)),
            pltpu.SemaphoreType.DMA((2,)),
        ]
        + Swap.scratch(swaps),
        7,
        "scan_backward",
    )


def feed_kernel(count, early, starts, *refs):
    loads = len(starts)
    normed, cotangent = refs[:2]
    gate_parts, up_parts, down_parts = refs[2:4], refs[4:6], refs[6 : 6 + early]
    refs = refs[6 + early :]
    halves, refs = refs[:loads], refs[loads:]
    results, down_grads = refs[:3], refs[3]
    targets, refs = refs[4 : 4 + loads], refs[4 + loads :]
    table, gate_up, acts, slopes, down, hidden, grad_gating, grad_lifting = refs[:8]
    table_sems, back_sems, write_sems, weight_sems, down_sems = refs[8:13]
    freights = load(count, starts, halves, targets, refs[13:])
    rows, width = hidden.shape
    pieces = rows // CHUNK
    reads = Stream(normed, table, table_sems)
    again = Stream(cotangent, table, back_sems)
    writes = [
        Stream(local, away, write_sems.at[k])
        for k, (local, away) in enumerate(zip((hidden, grad_gating, grad_lifting), results))
    ]
    weights = []
    for which, parts in enumerate((gate_parts, up_parts)):
        start = 0
        for part in parts:
            weights.append(
                pltpu.make_async_copy(
                    part,
                    gate_up.at[which, :, pl.ds(start, part.shape[1])],
                    weight_sems.at[len(weights)],
                )
            )
            start += part.shape[1]
    for copy in weights:
        copy.start()
    reads.start_all()
    greet(cargo_peers(count))
    for freight in freights:
        freight.start()
    for copy in weights:
        copy.wait()

    def forward_chunk(r):
        reads.wait(r)
        where = pl.ds(r, CHUNK)
        gating = jnp.dot(table[where, :], gate_up[0], preferred_element_type=F32)
        lifting = jnp.dot(table[where, :], gate_up[1], preferred_element_type=F32)
        act, slope = gelu_both(gating)
        hidden[where, :] = (act * lifting).astype(BF16)
        acts[where, :] = act
        slopes[where, :] = lifting * slope
        writes[0].start(r)
        again.start(r)

    spans(0, pieces // 4, forward_chunk)
    for freight in freights:
        freight.second()
    spans(pieces // 4, pieces, forward_chunk)
    for freight in freights:
        freight.forward()
    rows_in = down.shape[0] // count
    copies, start = [], 0
    for k, part in enumerate(down_parts):
        copies.append(
            pltpu.make_async_copy(
                part, down.at[:, pl.ds(start, part.shape[1])], down_sems.at[k]
            )
        )
        start += part.shape[1]
    for k, target in enumerate(targets):
        for place in range(count):
            copies.append(
                pltpu.make_async_copy(
                    target.at[place],
                    down.at[pl.ds(place * rows_in, rows_in), pl.ds(start, target.shape[2])],
                    down_sems.at[early + k * count + place],
                )
            )
        start += target.shape[2]

    def back(low, high):
        def chunk(r):
            where = pl.ds(r, CHUNK)
            columns = slice(low, high)
            grad = jnp.dot(table[where, :], down[:, columns], preferred_element_type=F32)
            grad_gating[where, columns] = (grad * slopes[where, columns]).astype(BF16)
            grad_lifting[where, columns] = (grad * acts[where, columns]).astype(BF16)
            if high == width:
                writes[1].start(r)
                writes[2].start(r)

        chunks(rows, chunk)

    for copy in copies[:early]:
        copy.start()
    again.wait_all()
    for copy in copies[:early]:
        copy.wait()
    turned(table, hidden, down_grads, 4, 0, 4)
    ready = sum(part.shape[1] for part in down_parts)
    back(0, ready)
    for freight in freights:
        freight.finish()
    for copy in copies[early:]:
        copy.start()
    for copy in copies[early:]:
        copy.wait()
    back(ready, width)
    for stream in writes:
        stream.wait_all()


def feed(count, normed, cotangent, gate_parts, up_parts, down_parts, cargo):
    rows = normed.shape[0]
    width = sum(part.shape[1] for part in gate_parts)
    pieces = rows // CHUNK
    out = call(
        functools.partial(feed_kernel, count, len(down_parts), cargo_starts(cargo)),
        [((rows, width), BF16, ANY)] * 3
        + [((normed.shape[1], width), BF16, VMEM)]
        + cargo_outs(count, cargo),
        [(normed, ANY), (cotangent, ANY)]
        + [(part, ANY) for part in list(gate_parts) + list(up_parts) + list(down_parts)]
        + cargo_ins(cargo),
        [
            pltpu.VMEM(normed.shape, BF16),
            pltpu.VMEM((2, normed.shape[1], width), BF16),
            pltpu.VMEM((rows, width), F32),
            pltpu.VMEM((rows, width), F32),
            pltpu.VMEM((normed.shape[1], width), BF16),
            pltpu.VMEM((rows, width), BF16),
            pltpu.VMEM((rows, width), BF16),
            pltpu.VMEM((rows, width), BF16),
            pltpu.SemaphoreType.DMA((pieces,)),
            pltpu.SemaphoreType.DMA((pieces,)),
            pltpu.SemaphoreType.DMA((3, pieces)),
            pltpu.SemaphoreType.DMA((4,)),
            pltpu.SemaphoreType.DMA((len(down_parts) + count * len(cargo),)),
        ]
        + cargo_scratch(count, cargo),
        5,
        "feed",
    )
    return out[:4] + flat_rows(out[4:])


def doc_index(places, doc_starts):
    return jnp.sum((doc_starts[None, :] <= places[:, None]).astype(jnp.int32), axis=1)


def split_columns(value):
    rows, columns = value.shape
    return value.reshape(rows, 2, columns // 2).transpose(1, 0, 2)


def widen(value, width):
    return jnp.pad(value, [(0, 0)] * (value.ndim - 1) + [(0, width - value.shape[-1])])


def by_rows(left, right):
    return lax.dot_general(left, right, TN, preferred_element_type=F32).astype(BF16)


def shards(
    layer_input,
    out_grad,
    doc_starts,
    mixer_gain,
    branch_gate,
    branch_input,
    conv_taps,
    rate_gate,
    input_gate,
    decay_param,
    mixer_out,
    feed_gain,
    feed_gate,
    feed_up,
    feed_down,
):
    shares = lax.axis_size("dp")
    count = shares // 2
    side = lax.axis_index("dp") % 2
    slim, feature_count = mixer_gain.shape[0], layer_input.shape[1]
    heads, piece, head_width = rate_gate.shape
    half_heads = heads // 2
    lanes = half_heads * head_width
    width = -(-lanes // 128) * 128
    row_count = layer_input.shape[0]
    rows = row_count * 8
    line_groups = [[2 * k + s for k in range(count)] for s in range(2)]

    branch_halves = jnp.concatenate(
        [split_columns(branch_gate), split_columns(branch_input)], axis=2
    )
    mixer_halves = widen(split_columns(mixer_out.T), width)
    down_rows = feed_down.T
    narrow = feed_gate.shape[1] // 6
    broad = 2 * narrow

    mine = lax.axis_index("dp")
    blocks = jnp.concatenate([rate_gate, input_gate], axis=2)
    blocks = widen(blocks.reshape(2, half_heads * piece, 2 * head_width), width)
    own = jnp.concatenate([conv_taps, decay_param[None]], axis=0)
    own = jnp.pad(own, ((0, 0), (0, 0), (0, head_width - piece)))
    own = jnp.roll(own, mine * piece, axis=2)
    own = own.reshape(TAPS + 1, 2, lanes).transpose(1, 0, 2)
    gains_own = jnp.pad(
        jnp.stack([mixer_gain, feed_gain]), ((0, 16 - TAPS - 3), (0, width - slim))
    )
    tail = jnp.concatenate(
        [widen(own, width), jnp.broadcast_to(gains_own, (2,) + gains_own.shape)], axis=1
    )
    small_top = -(-half_heads * piece // 16) * 16
    small = jnp.concatenate(
        [jnp.pad(blocks, ((0, 0), (0, small_top - half_heads * piece), (0, 0))), tail], axis=1
    )

    normed_one, pre, small_all, branch_all, gate_first = first(
        count, layer_input, [small, branch_halves, (feed_gate, 0, narrow)], width
    )

    small_all = small_all.reshape(shares, -1, width)
    tails = small_all[:, small_top:].astype(F32)
    gain_first = tails[:, SMALL_GAINS, :slim].reshape(feature_count)
    gain_second = tails[:, SMALL_GAINS + 1, :slim].reshape(feature_count)
    sums = jnp.sum(tails[:, : TAPS + 1], axis=0)
    decay_flat = sums[TAPS, :lanes]
    inside = (jnp.arange(width) < lanes)[None]
    table = jnp.concatenate(
        [
            sums[:TAPS],
            jnp.where(inside, jax.nn.softplus(-sums[TAPS:]), 0.0),
            jnp.zeros((3, width), F32),
        ]
    )
    blocks = (
        small_all[:, : half_heads * piece, : 2 * head_width]
        .reshape(shares, half_heads, piece, 2 * head_width)
        .transpose(1, 0, 2, 3)
        .reshape(lanes, 2 * head_width)
    )
    head_of = jnp.arange(width) // head_width
    same = (head_of[:lanes, None] == head_of[None, :]) & (jnp.arange(width) < lanes)[None]

    def diagonal(part):
        wide = widen(jnp.concatenate([part] * half_heads, axis=1), width)
        return jnp.where(same, wide, 0)

    gate_weights = jnp.concatenate(
        [diagonal(blocks[:, :head_width]), diagonal(blocks[:, head_width:])], axis=1
    )
    gate_weights = jnp.pad(gate_weights, ((0, width - lanes), (0, 0)))

    anchor = lax.axis_index("dp") // 2 * rows
    places = anchor + jnp.arange(rows, dtype=jnp.int32)
    here = doc_index(places, doc_starts)
    columns = [doc_index(places - k, doc_starts) == here for k in range(1, TAPS)]
    columns.append(~jnp.any(doc_starts[None, :] == places[:, None], axis=1))
    columns += [doc_index(places + k, doc_starts) == here for k in range(1, TAPS)]
    columns.append(columns[0])
    masks = jnp.stack(columns, axis=1).astype(F32)

    conv, recur, admit, state, merged, entry, cot_all, mixer_all, up_first = scan_forward(
        count, pre, masks, table, gate_weights, out_grad, [mixer_halves, (feed_up, 0, narrow)]
    )
    hidden_one, normed_own, gate_second, down_first = mixer_fold(
        count,
        merged,
        mixer_all,
        layer_input,
        gain_second[None],
        [(feed_gate, narrow, broad), (down_rows, 0, narrow)],
    )
    normed_two, up_second = gather_rows(count, normed_own, [(feed_up, narrow, broad)], 4)
    gate_parts, up_parts = [gate_first, gate_second], [up_first, up_second]
    hidden, grad_gating, grad_lifting, down_grads, down_second = feed(
        count,
        normed_two,
        cot_all,
        gate_parts,
        up_parts,
        [down_first],
        [(down_rows, narrow, broad)],
    )
    down_parts = [down_first, down_second]

    def line_sum(value):
        return lax.psum_scatter(
            value, "dp", scatter_dimension=0, axis_index_groups=line_groups, tiled=True
        )

    down_sum = line_sum(down_grads)
    grad_hidden_one, low_own, second_terms, gate_grads = feed_fold(
        grad_gating,
        grad_lifting,
        gate_parts,
        up_parts,
        normed_two,
        hidden_one,
        out_grad,
        gain_second[None],
    )
    low_own, down_sum = lax.optimization_barrier((low_own, down_sum))
    gate_sum = line_sum(gate_grads)
    back_low, up_grads = gather_plain(low_own, normed_two, grad_lifting, 8)
    up_sum = line_sum(up_grads)
    outlet_grads = by_rows(back_low, merged)

    def by_side(value):
        return value.reshape(2, -1, value.shape[1])

    back_low, outlet_grads, gate_sum = lax.optimization_barrier(
        (back_low, outlet_grads, gate_sum)
    )
    grad_pre, grad_gates, grad_table, down_both, gate_both = scan_backward(
        count,
        lanes,
        pre,
        back_low,
        mixer_all,
        [conv, recur, admit, state, entry],
        masks,
        table,
        gate_weights,
        [by_side(down_sum), by_side(gate_sum)],
    )
    branch_grads = by_rows(normed_one, grad_pre)

    def spots(value):
        blocks = [
            value[
                h * head_width : (h + 1) * head_width, h * head_width : (h + 1) * head_width
            ].reshape(shares, -1)
            for h in range(half_heads)
        ]
        return jnp.concatenate(blocks, axis=1)

    grad_decay = -jax.nn.sigmoid(-decay_flat) * grad_table[4, :lanes]
    grad_small = jnp.concatenate(
        [
            spots(grad_gates[:, :width]),
            spots(grad_gates[:, width:]),
            grad_table[:TAPS, :lanes]
            .reshape(TAPS * half_heads, shares, piece)
            .transpose(1, 0, 2)
            .reshape(shares, -1),
            grad_decay.reshape(half_heads, shares, piece).transpose(1, 0, 2).reshape(shares, -1),
        ],
        axis=1,
    )
    flat_size = grad_small.shape[1]
    spare = width - lanes
    grad_small = widen(grad_small, slim * spare).reshape(feature_count, spare).astype(BF16)
    last_grads = jnp.concatenate([outlet_grads[:, :lanes], grad_small, branch_grads], axis=1)
    grad_pre, last_grads = lax.optimization_barrier((grad_pre, last_grads))
    last_sum = line_sum(last_grads)
    input_grad, layer_output, gains, up_both = last_fold(
        count,
        grad_pre,
        branch_all,
        hidden,
        down_parts,
        layer_input,
        gain_first[None],
        grad_hidden_one,
        hidden_one,
        second_terms,
        [by_side(up_sum)],
    )
    first_gain_grad = lax.dynamic_index_in_dim(gains, mine, 0, False)
    second_gain_grad = lax.dynamic_index_in_dim(gains, shares + mine, 0, False)

    def swap(value):
        pair = by_side(value)
        kept = lax.dynamic_index_in_dim(pair, side, 0, False)
        given = lax.dynamic_index_in_dim(pair, 1 - side, 0, False)
        other = lax.ppermute(given, "dp", [(k, k ^ 1) for k in range(shares)])
        return [
            jnp.where(side == 0, kept, other).astype(F32),
            jnp.where(side == 0, other, kept).astype(F32),
        ]

    lasts = swap(last_sum)

    def columns(start, stop):
        return jnp.concatenate([value[:, start:stop] for value in lasts], axis=1)

    mixer_out_grad = columns(0, lanes).T
    branch_gate_grad = columns(width, width + lanes)
    branch_input_grad = columns(width + lanes, width + 2 * lanes)
    smalls = [value[:, lanes:width].reshape(-1)[:flat_size] for value in lasts]
    one = half_heads * piece * head_width
    tap_size = TAPS * half_heads * piece
    rate_grad = jnp.concatenate([v[:one].reshape(half_heads, piece, head_width) for v in smalls])
    inlet_grad = jnp.concatenate(
        [v[one : 2 * one].reshape(half_heads, piece, head_width) for v in smalls]
    )
    taps_grad = jnp.concatenate(
        [v[2 * one : 2 * one + tap_size].reshape(TAPS, half_heads, piece) for v in smalls], axis=1
    )
    decay_grad = jnp.concatenate(
        [v[2 * one + tap_size :].reshape(half_heads, piece) for v in smalls]
    )

    def joined(value):
        return jnp.concatenate([value[0], value[1]], axis=1).astype(F32)

    return (
        layer_output,
        input_grad,
        first_gain_grad,
        branch_gate_grad,
        branch_input_grad,
        taps_grad,
        rate_grad,
        inlet_grad,
        decay_grad,
        mixer_out_grad,
        second_gain_grad,
        joined(gate_both),
        joined(up_both),
        joined(down_both).T,
    )


def solution(mesh):
    placed = (
        P(("dp", "tensor"), None),
        P(("dp", "tensor"), None),
        P(),
        P("dp"),
        P("dp", "tensor"),
        P("dp", "tensor"),
        P(None, "tensor", "dp"),
        P("tensor", "dp", None),
        P("tensor", "dp", None),
        P("tensor", "dp"),
        P("tensor", "dp"),
        P("dp"),
        P("dp", "tensor"),
        P("dp", "tensor"),
        P("tensor", "dp"),
    )
    return jax.shard_map(
        shards,
        mesh=mesh,
        in_specs=placed,
        out_specs=(
            P(("dp", "tensor"), None),
            P(("dp", "tensor"), None),
            P("dp"),
            P("dp", "tensor"),
            P("dp", "tensor"),
            P(None, "tensor", "dp"),
            P("tensor", "dp", None),
            P("tensor", "dp", None),
            P("tensor", "dp"),
            P("tensor", "dp"),
            P("dp"),
            P("dp", "tensor"),
            P("dp", "tensor"),
            P("tensor", "dp"),
        ),
        check_vma=False,
    )
```

```python
import functools

import jax
import jax.numpy as jnp
from jax import lax
from jax.experimental import pallas as pl
from jax.experimental.pallas import tpu as pltpu
from jax.sharding import PartitionSpec as P

TAPS = 4
EPSILON = 1e-06
GUARD = 0.001
GELU_SCALE = 0.7978845608028654
GELU_CUBE = 0.044715
MESH = pl.DeviceIdType.MESH
F32, BF16 = jnp.float32, jnp.bfloat16
ANY = pl.BlockSpec(memory_space=pl.ANY)
VMEM = pl.BlockSpec(memory_space=pltpu.VMEM)
LATE = pl.BlockSpec(memory_space=pl.ANY)
GRANT = 60 * 1024 * 1024
NT = (((1,), (1,)), ((), ()))
TN = (((0,), (0,)), ((), ()))
CHUNK = 256


def spot():
    dp, tensor = lax.axis_index("dp"), lax.axis_index("tensor")
    return dp // 2, dp % 2, tensor // 2, tensor % 2


def seat(line, side, deck, core):
    return (line * 2 + side, deck * 2 + core)


def rank(side, deck, core):
    return side * 4 + deck * 2 + core


def greet(peers):
    barrier = pltpu.get_barrier_semaphore()
    for peer in peers:
        pl.semaphore_signal(barrier, inc=1, device_id=peer, device_id_type=MESH)
    pl.semaphore_wait(barrier, len(peers))


def remote(source, target, send, receive, peer):
    return pltpu.make_async_remote_copy(
        src_ref=source,
        dst_ref=target,
        send_sem=send,
        recv_sem=receive,
        device_id=peer,
        device_id_type=MESH,
    )


def line_peers(count):
    line, side, deck, core = spot()
    return [seat((line + k) % count, side, deck, core) for k in range(1, count)]


def group_peers():
    line, side, deck, core = spot()
    return [
        seat(line, side, deck, 1 - core),
        seat(line, 1 - side, deck, core),
        seat(line, side, 1 - deck, core),
    ]


class Freight:
    def __init__(self, count, halves, target, sems, start=0):
        self.count, self.halves, self.target = count, halves, target
        self.start_column = start
        self.cross, self.local, self.send, self.receive = sems
        self.line, self.side, self.deck, self.core = spot()

    @staticmethod
    def scratch(count):
        steps = 5 if count == 4 else count - 1
        return [
            pltpu.SemaphoreType.DMA((2,)),
            pltpu.SemaphoreType.DMA,
            pltpu.SemaphoreType.DMA((steps, 2)),
            pltpu.SemaphoreType.DMA((count, 2)),
        ]

    def half(self, which):
        if len(self.halves.shape) == 3:
            return self.halves.at[which]
        offset = which * (self.halves.shape[1] // 2) + self.start_column
        return self.halves.at[:, pl.ds(pl.multiple_of(offset, 128), self.target.shape[2])]

    def place(self, origin, part):
        rows = self.target.shape[1] // 2
        return self.target.at[origin, pl.ds(pl.multiple_of(part * rows, rows), rows)]

    def seat(self, line):
        return seat(line, self.side, self.deck, self.core)

    def swap(self):
        return remote(
            self.half(1 - self.side),
            self.place(self.line, self.side),
            self.cross.at[0],
            self.cross.at[1],
            seat(self.line, 1 - self.side, self.deck, self.core),
        )

    def keep(self):
        return pltpu.make_async_copy(
            self.half(self.side), self.place(self.line, self.side), self.local
        )

    def copy(self, origin, line, index, part, source):
        return remote(
            source,
            self.place(origin, part),
            self.send.at[index, part],
            self.receive.at[origin, part],
            self.seat(line),
        )

    def own(self, line, index, part):
        source = self.half(self.side)
        if part is not self.side:
            source = self.place(self.line, part)
        return self.copy(self.line, line, index, part, source)

    def arrival(self, origin, part):
        return self.copy(origin, origin, 0, part, self.half(self.side))

    def each_step(self, action, phases=(0, 1)):
        if self.count == 4:
            line = self.line
            for index, step in enumerate((1, -1, 2, -2)):
                if index == 0:
                    when = [line == 2, line < 2]
                elif index == 1:
                    when = [line == 1, line > 1]
                else:
                    when = [(line + step >= 0) & (line + step < 4), None]
                for phase in phases:
                    if when[phase] is not None:

                        @pl.when(when[phase])
                        def _(index=index, step=step):
                            action(index, line + step)

        elif 0 in phases:
            for step in range(1, self.count):
                action(step - 1, (self.line + step) % self.count)

    def start(self):
        self.swap().start()
        self.each_step(lambda index, line: self.own(line, index, self.side).start(), (0,))
        self.keep().start()

    def second(self):
        self.swap().wait_recv()
        self.each_step(lambda index, line: self.own(line, index, 1 - self.side).start(), (0,))

    def middle(self, action):
        if self.count == 4:

            @pl.when((self.line == 1) | (self.line == 2))
            def _():
                action(6 - 3 * self.line, 3 * self.line - 3)

    def onward(self, origin, line, part):
        return self.copy(origin, line, 4, part, self.place(origin, part))

    def forward(self):
        for part in (self.side, 1 - self.side):
            self.each_step(
                lambda index, line, part=part: self.own(line, index, part).start(), (1,)
            )

            def action(origin, line, part=part):
                self.arrival(origin, part).wait_recv()
                self.onward(origin, line, part).start()

            self.middle(action)

    def finish(self):
        for part in (self.side, 1 - self.side):
            self.each_step(
                lambda index, line, part=part: self.own(line, index, part).wait_send()
            )
            self.middle(
                lambda origin, line, part=part: self.onward(origin, line, part).wait_send()
            )
            for origin in range(self.count):
                pending = self.line != origin
                if self.count == 4 and origin == 0:
                    pending = pending & (self.line != 2)
                if self.count == 4 and origin == 3:
                    pending = pending & (self.line != 1)

                @pl.when(pending)
                def _(origin=origin, part=part):
                    self.arrival(origin, part).wait_recv()

        self.keep().wait()
        self.swap().wait_send()


class Stream:
    def __init__(self, source, target, sems, from_row=0, to_row=0, columns=None):
        self.source, self.target, self.sems = source, target, sems
        self.from_row, self.to_row, self.columns = from_row, to_row, columns
        self.pieces = sems.shape[0]

    def copy(self, r):
        source = (pl.ds(r + self.from_row, CHUNK),)
        if self.columns is not None:
            source += (self.columns,)
        return pltpu.make_async_copy(
            self.source.at[source],
            self.target.at[pl.ds(r + self.to_row, CHUNK)],
            self.sems.at[r // CHUNK],
        )

    def start(self, r):
        self.copy(r).start()

    def wait(self, r):
        self.copy(r).wait()

    def start_all(self):
        for k in range(self.pieces):
            self.start(k * CHUNK)

    def wait_all(self):
        for k in range(self.pieces):
            self.wait(k * CHUNK)


class Swap:
    def __init__(self, values, outs, send, receive, local):
        line, side, deck, core = spot()
        self.copies = []
        for k, (value, out) in enumerate(zip(values, outs)):
            self.copies.append(
                remote(
                    value.at[1 - side],
                    out.at[side],
                    send.at[k],
                    receive.at[k],
                    seat(line, 1 - side, deck, core),
                )
            )
            self.copies.append(
                pltpu.make_async_copy(value.at[side], out.at[side], local.at[k])
            )

    @staticmethod
    def scratch(values):
        return [pltpu.SemaphoreType.DMA((len(values),))] * 3 if values else []

    def start(self):
        for copy in self.copies:
            copy.start()

    def finish(self):
        for copy in self.copies:
            copy.wait()


def cargo_peers(count):
    return group_peers() + line_peers(count)


def piece_shape(count, piece):
    if isinstance(piece, tuple):
        return count, 2 * piece[0].shape[0], piece[2]
    return count, 2 * piece.shape[1], piece.shape[2]


def cargo_outs(count, cargo):
    return [(piece_shape(count, piece), BF16, ANY) for piece in cargo]


def cargo_ins(cargo):
    return [(piece[0] if isinstance(piece, tuple) else piece, ANY) for piece in cargo]


def cargo_starts(cargo):
    return [piece[1] if isinstance(piece, tuple) else 0 for piece in cargo]


def cargo_scratch(count, cargo):
    return [sem for _ in cargo for sem in Freight.scratch(count)]


def load(count, starts, halves, targets, sems):
    return [
        Freight(count, half, target, sems[4 * k : 4 * k + 4], starts[k])
        for k, (half, target) in enumerate(zip(halves, targets))
    ]


def flat_rows(values):
    return [value.reshape(-1, value.shape[2]) for value in values]


def call(kernel, outs, ins, scratch, identity, name):
    late = [k for k, (_, space) in enumerate(ins) if space is LATE]
    body = kernel
    if late:
        held = [pltpu.VMEM(ins[k][0].shape, ins[k][0].dtype) for k in late]
        scratch = scratch + held + [pltpu.SemaphoreType.DMA((len(late),))]

        def body(*refs):
            inputs, rest = list(refs[: len(ins)]), refs[len(ins) : -len(late) - 1]
            fetches = []
            for i, (k, buffer) in enumerate(zip(late, refs[-len(late) - 1 : -1])):
                fetches.append(pltpu.make_async_copy(inputs[k], buffer, refs[-1].at[i]))
                inputs[k] = buffer
            for fetch in fetches:
                fetch.start()
            kernel(*inputs, *rest, fetches=fetches)

    results = pl.pallas_call(
        body,
        out_shape=[jax.ShapeDtypeStruct(shape, kind) for shape, kind, _ in outs],
        in_specs=[space for _, space in ins],
        out_specs=[space for _, _, space in outs],
        scratch_shapes=scratch,
        compiler_params=pltpu.CompilerParams(
            collective_id=identity, has_side_effects=True, vmem_limit_bytes=GRANT
        ),
        name=name,
    )(*[value for value, _ in ins])
    return list(results)


class GroupGather:
    def __init__(self, source, target, send, receive, local):
        self.source, self.target = source, target
        self.send, self.receive = send, receive
        self.local = local
        self.here = spot()

    @staticmethod
    def scratch():
        return [
            pltpu.SemaphoreType.DMA((11,)),
            pltpu.SemaphoreType.DMA((11,)),
            pltpu.SemaphoreType.DMA,
        ]

    def half(self, ref, h):
        rows = self.source.shape[0] // 2
        return ref.at[pl.ds(h * rows, rows)]

    def make(self):
        line, side, deck, core = self.here
        sibling, across, above = group_peers()
        mine = rank(side, deck, core)
        beside = rank(1 - side, deck, core)
        over = rank(side, 1 - deck, core)
        corner = rank(1 - side, 1 - deck, core)

        def own(h, peer, index):
            return remote(
                self.half(self.source, h),
                self.half(self.target.at[mine], h),
                self.send.at[index],
                self.receive.at[index],
                peer,
            )

        def relay(block, h, peer, index):
            ref = self.half(self.target.at[block], h)
            return remote(ref, ref, self.send.at[index], self.receive.at[index], peer)

        self.keep = pltpu.make_async_copy(self.source, self.target.at[mine], self.local)
        self.first = [
            own(0, across, 0),
            own(1, above, 1),
            own(0, above, 2),
            own(1, across, 3),
        ]
        self.near = remote(
            self.source, self.target.at[mine], self.send.at[4], self.receive.at[4], sibling
        )
        self.second = [relay(beside, 0, above, 5), relay(over, 1, across, 6)]
        self.last = [
            relay(beside, 0, sibling, 7),
            relay(over, 1, sibling, 8),
            relay(over, 0, sibling, 9),
            relay(beside, 1, sibling, 10),
        ]
        self.corner = corner

    def start(self):
        self.make()
        self.first[1].start()
        self.first[2].start()
        self.near.start()
        self.keep.start()

    def start_across(self):
        self.first[0].start()
        self.first[3].start()

    def landed(self):
        self.near.wait_recv()
        self.keep.wait()

    def landed_relays(self):
        for copy in self.last:
            copy.wait_recv()

    def forward(self):
        for k in range(2):
            self.first[k].wait_recv()
            self.second[k].start()
            self.last[k].start()
        for k in range(2, 4):
            self.first[k].wait_recv()
            self.last[k].start()


def corner_relay(gather, send, receive):
    sibling = group_peers()[0]
    out = []
    for h in range(2):
        ref = gather.half(gather.target.at[gather.corner], h)
        out.append(remote(ref, ref, send.at[h], receive.at[h], sibling))
    return out


def group_finish(gather, send, receive, early=False):
    relays = corner_relay(gather, send, receive)
    for k in range(2):
        gather.second[k].wait_recv()
        relays[k].start()
    if not early:
        gather.landed()
        gather.landed_relays()
    for copy in [gather.near] + gather.first + gather.second + gather.last:
        copy.wait_send()
    for copy in relays:
        copy.wait()


def rows_scratch():
    return GroupGather.scratch() + [
        pltpu.SemaphoreType.DMA((2,)),
        pltpu.SemaphoreType.DMA((2,)),
    ]


def first_kernel(count, starts, *refs):
    loads = len(starts)
    rows, gains = refs[:2]
    halves, refs = refs[2 : 2 + loads], refs[2 + loads :]
    normed, pre, gains_all = refs[:3]
    targets, refs = refs[3 : 3 + loads], refs[3 + loads :]
    own, table, weights, result = refs[:4]
    gain_send, gain_receive, gain_local, out_sems, weight_sems, result_sems = refs[4:10]
    sems = refs[10:]
    dp, tensor = lax.axis_index("dp"), lax.axis_index("tensor")
    gather = GroupGather(own, table, *sems[:3])
    corner_sems = sems[3:5]
    branch, small, *others = load(count, starts, halves, targets, sems[5:])
    shares = 2 * count
    line, side, deck, core = spot()
    greet(
        [((dp + k) % shares, tensor) for k in range(1, shares)]
        + [seat(line, side, deck, 1 - core), seat(line, side, 1 - deck, core)]
    )
    gain_copies = [
        remote(
            gains,
            gains_all.at[dp],
            gain_send.at[k],
            gain_receive.at[k],
            ((dp + k) % shares, tensor),
        )
        for k in range(1, shares)
    ]
    gain_copies.append(pltpu.make_async_copy(gains, gains_all.at[dp], gain_local))
    for copy in gain_copies:
        copy.start()
    branch.start()
    small.start()
    for copy in gain_copies:
        copy.wait()

    block_rows, features = rows.shape
    slim = features // shares
    gain = jnp.concatenate(
        [gains_all[k].astype(F32)[0:1] for k in range(shares)], axis=1
    )

    def norm_rows(i, carry):
        where = pl.ds(pl.multiple_of(i * 32, 32), 32)
        value = rows[where, :].astype(F32)
        mean = jnp.mean(value * value, axis=1, keepdims=True)
        own[where, :] = (value * lax.rsqrt(mean + EPSILON) * gain).astype(BF16)
        return carry

    lax.fori_loop(0, block_rows // 32, norm_rows, 0)
    branch.second()
    small.second()
    gather.start()
    gather.start_across()
    small.forward()
    gather.forward()
    branch.forward()
    for freight in others:
        freight.start()
    for freight in others:
        freight.second()
    small.finish()
    group_finish(gather, *corner_sems)
    copies = [
        pltpu.make_async_copy(
            table.at[g], normed.at[pl.ds(g * block_rows, block_rows)], out_sems.at[g]
        )
        for g in range(8)
    ]
    for copy in copies:
        copy.start()
    branch.finish()
    depth = targets[0].shape[1]
    loading = [
        pltpu.make_async_copy(
            targets[0].at[k], weights.at[pl.ds(k * depth, depth)], weight_sems.at[k]
        )
        for k in range(count)
    ]
    for copy in loading:
        copy.start()
    for freight in others:
        freight.forward()
    for copy in loading:
        copy.wait()
    lanes, width = weights.shape[1] // 2, pre.shape[1] // 2
    shift = 2 * lanes - width
    inside = lax.broadcasted_iota(jnp.int32, (block_rows, width), 1) < lanes

    def write(g):
        where = pl.ds(pl.multiple_of(g * block_rows, block_rows), block_rows)
        return pltpu.make_async_copy(result.at[where], pre.at[where], result_sems.at[g])

    def product(g, carry):
        where = pl.ds(pl.multiple_of(g * block_rows, block_rows), block_rows)
        both = jnp.dot(table[g], weights[...], preferred_element_type=F32)
        result[where, :width] = jnp.where(inside, both[:, :width], 0.0)
        later = pltpu.roll(both[:, shift:], lanes, 1)
        result[where, width:] = jnp.where(inside, later, 0.0)
        write(g).start()
        return carry

    lax.fori_loop(0, 8, product, 0)
    for g in range(8):
        copies[g].wait()
        write(g).wait()
    for freight in others:
        freight.finish()


def first(count, rows, gains, cargo, width):
    total = 8 * rows.shape[0]
    shares = 2 * count
    branch = cargo[0]
    out = call(
        functools.partial(first_kernel, count, cargo_starts(cargo)),
        [
            ((total, rows.shape[1]), BF16, ANY),
            ((total, 2 * width), F32, ANY),
            ((shares,) + gains.shape, BF16, VMEM),
        ]
        + cargo_outs(count, cargo),
        [(rows, VMEM), (gains, VMEM)] + cargo_ins(cargo),
        [
            pltpu.VMEM(rows.shape, BF16),
            pltpu.VMEM((8,) + rows.shape, BF16),
            pltpu.VMEM((rows.shape[1], branch.shape[2]), BF16),
            pltpu.VMEM((total, 2 * width), F32),
            pltpu.SemaphoreType.DMA((shares,)),
            pltpu.SemaphoreType.DMA((shares,)),
            pltpu.SemaphoreType.DMA,
            pltpu.SemaphoreType.DMA((8,)),
            pltpu.SemaphoreType.DMA((count,)),
            pltpu.SemaphoreType.DMA((8,)),
        ]
        + rows_scratch()
        + cargo_scratch(count, cargo),
        0,
        "first",
    )
    return out[:3] + flat_rows(out[3:])


def rows_kernel(count, starts, *refs):
    loads = len(starts)
    rows, halves = refs[0], refs[1 : 1 + loads]
    everything, targets = refs[1 + loads], refs[2 + loads : 2 + 2 * loads]
    sems = refs[2 + 2 * loads :]
    gather = GroupGather(rows, everything, *sems[:3])
    freights = load(count, starts, halves, targets, sems[5:])
    greet(cargo_peers(count))
    for freight in freights:
        freight.start()
    gather.start()
    gather.start_across()
    for freight in freights:
        freight.second()
    for freight in freights:
        freight.forward()
    gather.forward()
    group_finish(gather, *sems[3:5])
    for freight in freights:
        freight.finish()


def gather_rows(count, rows, cargo, identity):
    out = call(
        functools.partial(rows_kernel, count, cargo_starts(cargo)),
        [((8,) + rows.shape, BF16, ANY)] + cargo_outs(count, cargo),
        [(rows, ANY)] + cargo_ins(cargo),
        rows_scratch() + cargo_scratch(count, cargo),
        identity,
        "gather_rows",
    )
    return [out[0].reshape(-1, rows.shape[1])] + flat_rows(out[1:])


def turned(left, right, out, tiles, low, high):
    size = left.shape[1] // tiles

    def body(i, carry):
        place = pl.ds(pl.multiple_of(i * size, size), size)
        total = lax.dot_general(left[:, place], right[...], TN, preferred_element_type=F32)
        out[place, :] = total.astype(BF16)
        return carry

    lax.fori_loop(low, high, body, 0)


def plain_rows_kernel(rows, left, right, everything, product_out, product, *sems, fetches):
    gather = GroupGather(rows, everything, *sems[1:4])
    greet(group_peers())
    gather.start()
    gather.start_across()
    for fetch in fetches:
        fetch.wait()
    turned(left, right, product, 4, 0, 4)
    writing = pltpu.make_async_copy(product, product_out, sems[0])
    writing.start()
    gather.forward()
    group_finish(gather, *sems[4:6])
    writing.wait()


def gather_plain(rows, left, right, identity):
    out = call(
        plain_rows_kernel,
        [((8,) + rows.shape, BF16, ANY), ((left.shape[1], right.shape[1]), BF16, ANY)],
        [(rows, ANY), (left, LATE), (right, LATE)],
        [pltpu.VMEM((left.shape[1], right.shape[1]), BF16), pltpu.SemaphoreType.DMA]
        + rows_scratch(),
        identity,
        "gather_rows",
    )
    return out[0].reshape(-1, rows.shape[1]), out[1]


def flip(value, bit):
    return 1 - value if bit else value


def whole_group():
    line, side, deck, core = spot()
    return [
        seat(line, flip(side, k & 4), flip(deck, k & 2), flip(core, k & 1)) for k in range(1, 8)
    ]


class GainSum:
    def __init__(self, count, gains, totals, near, far, send, receive, far_send, far_receive):
        self.gains, self.totals, self.near, self.far = gains, totals, near, far
        self.first = [
            remote(gains, near.at[k], send.at[k], receive.at[k], peer)
            for k, peer in enumerate(whole_group())
        ]
        self.second_copies = [
            remote(far.at[0], far.at[1 + k], far_send.at[k], far_receive.at[k], peer)
            for k, peer in enumerate(line_peers(count))
        ]

    @staticmethod
    def scratch(count, gains):
        return [
            pltpu.VMEM((7,) + gains.shape, F32),
            pltpu.VMEM((count,) + gains.shape, F32),
            pltpu.SemaphoreType.DMA((7,)),
            pltpu.SemaphoreType.DMA((7,)),
            pltpu.SemaphoreType.DMA((count,)),
            pltpu.SemaphoreType.DMA((count,)),
        ]

    def start(self):
        for copy in self.first:
            copy.start()

    def second(self):
        for copy in self.first:
            copy.wait()
        total = self.gains[...]
        for k in range(7):
            total = total + self.near[k]
        self.far[0] = total
        for copy in self.second_copies:
            copy.start()

    def finish(self):
        for copy in self.second_copies:
            copy.wait()
        total = self.far[0]
        for k in range(len(self.second_copies)):
            total = total + self.far[1 + k]
        self.totals[...] = total


class Fold:
    OWN, ACROSS, ABOVE, CORNER = 0, 1, 2, 3

    def __init__(self, plan, lefts, rights, out, refs):
        self.plan, self.lefts, self.rights, self.out = plan, lefts, rights, out
        self.mine, self.stage, self.near = refs[:3]
        self.across_sum, self.above_sum, self.leaving, self.arriving = refs[3:7]
        send, receive, self.near_send, self.near_receive = refs[7:11]
        self.line, self.side, self.deck, self.core = spot()
        sibling, across, above = group_peers()
        self.sibling = sibling
        self.rows, self.width = out.shape
        self.half = self.rows // 2
        self.ships = [
            remote(
                self.leaving.at[k], self.arriving.at[k], send.at[k], receive.at[k], peer
            )
            for k, peer in enumerate((above, across, above, across, across, above))
        ]

    @staticmethod
    def scratch(rows, width):
        half = rows // 2
        return [
            pltpu.VMEM((rows, width), F32),
            pltpu.VMEM((2, rows, width), BF16),
            pltpu.VMEM((4, rows, width), BF16),
            pltpu.VMEM((half, width), F32),
            pltpu.VMEM((half, width), F32),
            pltpu.VMEM((6, half, width), BF16),
            pltpu.VMEM((6, half, width), BF16),
            pltpu.SemaphoreType.DMA((6,)),
            pltpu.SemaphoreType.DMA((6,)),
            pltpu.SemaphoreType.DMA((4,)),
            pltpu.SemaphoreType.DMA((4,)),
        ]

    def product(self, which, store):
        base = pl.multiple_of(which * self.rows, self.rows)
        step = 512

        def body(j, carry):
            columns = pl.ds(pl.multiple_of(j * step, step), step)
            total = None
            for (which_left, start), right in zip(self.plan, self.rights):
                part = lax.dot_general(
                    self.lefts[which_left][pl.ds(base, self.rows), start : start + right.shape[1]],
                    right[columns, :],
                    NT,
                    preferred_element_type=F32,
                )
                total = part if total is None else total + part
            store(columns, total)
            return carry

        lax.fori_loop(0, self.width // step, body, 0)

    def sweep(self, action):
        def body(i, carry):
            action(pl.multiple_of(i * 16, 16))
            return carry

        lax.fori_loop(0, self.half // 16, body, 0)

    def near_copy(self, q):
        return remote(
            self.stage.at[q % 2],
            self.near.at[q],
            self.near_send.at[q],
            self.near_receive.at[q],
            self.sibling,
        )

    def chip_sum(self, q, h, r):
        place = pl.ds(h * self.half + r, 16)
        return self.mine[place, :] + self.near[q, place, :].astype(F32)

    def block(self, q):
        s, d = [
            (self.side, self.deck),
            (1 - self.side, self.deck),
            (self.side, 1 - self.deck),
            (1 - self.side, 1 - self.deck),
        ][q]
        if q < 2:
            self.near_copy(q + 2).wait_send()

        def put_stage(columns, total):
            self.stage[q % 2, :, columns] = total.astype(BF16)

        def put_mine(columns, total):
            target = self.out if q == self.OWN else self.mine
            target[:, columns] = total

        self.product(rank(s, d, 1 - self.core), put_stage)
        self.near_copy(q).start()
        self.product(rank(s, d, self.core), put_mine)
        self.near_copy(q).wait_recv()

    def send(self, k):
        self.ships[k].start()

    def begin(self, freights=()):
        self.block(self.CORNER)

        def corner(r):
            for h in range(2):
                self.leaving[h, pl.ds(r, 16), :] = self.chip_sum(self.CORNER, h, r).astype(BF16)

        self.sweep(corner)
        self.send(0)
        self.send(1)
        self.block(self.ABOVE)

        def above(r):
            place = pl.ds(r, 16)
            self.leaving[2, place, :] = self.chip_sum(self.ABOVE, 0, r).astype(BF16)
            self.above_sum[place, :] = self.chip_sum(self.ABOVE, 1, r)

        self.sweep(above)
        self.send(2)
        for freight in freights:
            freight.second()
        self.block(self.ACROSS)

        def across(r):
            place = pl.ds(r, 16)
            self.leaving[3, place, :] = self.chip_sum(self.ACROSS, 1, r).astype(BF16)
            self.across_sum[place, :] = self.chip_sum(self.ACROSS, 0, r)

        self.sweep(across)
        self.send(3)
        self.block(self.OWN)

    def middle(self):
        self.ships[0].wait_recv()

        def across(r):
            place = pl.ds(r, 16)
            total = self.across_sum[place, :] + self.arriving[0, place, :].astype(F32)
            self.leaving[4, place, :] = total.astype(BF16)

        self.sweep(across)
        self.send(4)
        self.ships[1].wait_recv()

        def above(r):
            place = pl.ds(r, 16)
            total = self.above_sum[place, :] + self.arriving[1, place, :].astype(F32)
            self.leaving[5, place, :] = total.astype(BF16)

        self.sweep(above)
        self.send(5)

    def finish(self, store):
        for k in range(2, 6):
            self.ships[k].wait_recv()

        def total(r):
            for h, pair in enumerate(((2, 4), (3, 5))):
                place, here = pl.ds(r, 16), pl.ds(h * self.half + r, 16)
                value = self.out[here, :] + self.near[self.OWN, here, :].astype(F32)
                for k in pair:
                    value = value + self.arriving[k, place, :].astype(F32)
                store(here, value)

        self.sweep(total)
        for k in range(6):
            self.ships[k].wait_send()
        for q in range(2):
            self.near_copy(q).wait_send()


def unit_rows(value):
    scale = lax.rsqrt(jnp.mean(value * value, axis=1, keepdims=True) + EPSILON)
    return value * scale, scale


def norm_back_rows(grad, unit, scale, gain):
    grad_unit = grad * gain
    inner = jnp.mean(grad_unit * unit, axis=1, keepdims=True)
    return scale * (grad_unit - unit * inner), jnp.sum(grad * unit, axis=0, keepdims=True)


def mixer_fold_kernel(count, jobs, starts, left, right, *refs, fetches):
    loads = len(starts)
    inputs, gain, refs = refs[0], refs[1], refs[2:]
    halves, refs = refs[:loads], refs[loads:]
    out, normed, refs = refs[0], refs[1], refs[2:]
    targets, refs = refs[:loads], refs[loads:]
    fold = Fold(jobs[0], [left], [right], out, refs[:11])
    freights = load(count, starts, halves, targets, refs[11:])
    greet(cargo_peers(count))
    for freight in freights:
        freight.start()
    for fetch in fetches[:2]:
        fetch.wait()
    fold.begin(freights)
    fold.middle()
    for freight in freights:
        freight.forward()

    fetches[2].wait()

    def store(here, value):
        value = value + inputs[here, :].astype(F32)
        out[here, :] = value
        normed[here, :] = (unit_rows(value)[0] * gain[...]).astype(BF16)

    fold.finish(store)
    for freight in freights:
        freight.finish()


def plan_of(lefts_rights):
    lefts, rights, plan = [], [], []
    for k, (left, parts) in enumerate(lefts_rights):
        lefts.append((left, LATE))
        start = 0
        for part in parts:
            rights.append((part, LATE))
            plan.append((k, start))
            start += part.shape[1]
    return plan, lefts + rights


def mixer_fold(count, merged, mixer, inputs, gain, cargo):
    plan, ins = plan_of([(merged, [mixer])])
    rows, width = inputs.shape
    out = call(
        functools.partial(mixer_fold_kernel, count, [plan], cargo_starts(cargo)),
        [((rows, width), F32, VMEM), ((rows, width), BF16, VMEM)] + cargo_outs(count, cargo),
        ins + [(inputs, LATE), (gain, VMEM)] + cargo_ins(cargo),
        Fold.scratch(rows, width) + cargo_scratch(count, cargo),
        3,
        "mixer_fold",
    )
    return out[:2] + flat_rows(out[2:])


def feed_fold_kernel(plan, parts, left, other, *refs, fetches):
    rights, refs = refs[:parts], refs[parts:]
    normed, hidden, cotangent, gain, refs = *refs[:4], refs[4:]
    out, low, gain_sum, grads_out = refs[:4]
    fold = Fold(plan, [left, other], rights, out, refs[4:15])
    grads, write_sem = refs[15:]
    greet(group_peers())
    for fetch in fetches[: 2 + parts]:
        fetch.wait()
    fold.begin()
    fold.middle()
    for fetch in fetches[2 + parts :]:
        fetch.wait()
    turned(normed, left, grads, 4, 0, 4)
    writing = pltpu.make_async_copy(grads, grads_out, write_sem)
    writing.start()
    gain_sum[...] = jnp.zeros_like(gain_sum)

    def store(here, value):
        unit, scale = unit_rows(hidden[here, :])
        back, terms = norm_back_rows(value, unit, scale, gain[...])
        gain_sum[0:1, :] += terms
        back = cotangent[here, :].astype(F32) + back
        out[here, :] = back
        low[here, :] = back.astype(BF16)

    fold.finish(store)
    writing.wait()


def feed_fold(grad_gating, grad_lifting, gates, ups, normed, hidden, cotangent, gain):
    plan, ins = plan_of([(grad_gating, gates), (grad_lifting, ups)])
    rows, width = hidden.shape
    return call(
        functools.partial(feed_fold_kernel, plan, len(gates) + len(ups)),
        [
            ((rows, width), F32, VMEM),
            ((rows, width), BF16, VMEM),
            ((8, width), F32, VMEM),
            ((normed.shape[1], grad_gating.shape[1]), BF16, ANY),
        ],
        ins + [(normed, LATE), (hidden, LATE), (cotangent, LATE), (gain, VMEM)],
        Fold.scratch(rows, width)
        + [
            pltpu.VMEM((normed.shape[1], grad_gating.shape[1]), BF16),
            pltpu.SemaphoreType.DMA,
        ],
        6,
        "feed_fold",
    )


def last_fold_kernel(count, plans, parts, swaps, left, right, feed_left, *refs, fetches):
    rights, refs = refs[:parts], refs[parts:]
    inputs, gain, grad_hidden, hidden, second, refs = *refs[:5], refs[5:]
    values, refs = refs[:swaps], refs[swaps:]
    input_grad, output, totals = refs[:3]
    swapped, refs = refs[3 : 3 + swaps], refs[3 + swaps :]
    out, feed_out, sums, terms_here, refs = *refs[:4], refs[4:]
    fold = Fold(plans[0], [left], [right], out, refs[:11])
    feed = Fold(plans[1], [feed_left], rights, feed_out, refs[11:22])
    swap = Swap(values, swapped, *refs[22:25])
    gain_sum = GainSum(count, sums, totals, *refs[25:])
    greet(whole_group() + line_peers(count))
    swap.start()
    for fetch in fetches[:2]:
        fetch.wait()
    fold.begin()
    for fetch in fetches[2:]:
        fetch.wait()
    feed.begin()
    fold.middle()
    feed.middle()
    terms_here[...] = jnp.zeros_like(terms_here)

    def store(here, value):
        unit, scale = unit_rows(inputs[here, :].astype(F32))
        back, terms = norm_back_rows(value, unit, scale, gain[...])
        terms_here[0:1, :] += terms
        input_grad[here, :] = (grad_hidden[here, :] + back).astype(BF16)

    fold.finish(store)
    shares, slim = sums.shape[0] // 2, sums.shape[1]
    for k in range(shares):
        columns = slice(k * slim, (k + 1) * slim)
        sums[k : k + 1, :] = terms_here[0:1, columns]
        sums[shares + k : shares + k + 1, :] = second[0:1, columns]
    gain_sum.start()
    gain_sum.second()

    def store_output(here, value):
        output[here, :] = (hidden[here, :] + value).astype(BF16)

    feed.finish(store_output)
    gain_sum.finish()
    swap.finish()


def last_fold(count, grads, branch, feed_left, downs, inputs, gain, grad_hidden, hidden, second, swaps):
    plan, ins = plan_of([(grads, [branch])])
    feed_plan, feed_ins = plan_of([(feed_left, downs)])
    rows, width = hidden.shape
    both = jax.ShapeDtypeStruct((4 * count, width // (2 * count)), F32)
    return call(
        functools.partial(last_fold_kernel, count, (plan, feed_plan), len(downs), len(swaps)),
        [
            ((rows, width), BF16, VMEM),
            ((rows, width), BF16, VMEM),
            (both.shape, F32, VMEM),
        ]
        + [(value.shape, BF16, ANY) for value in swaps],
        ins
        + feed_ins
        + [
            (inputs, LATE),
            (gain, VMEM),
            (grad_hidden, LATE),
            (hidden, LATE),
            (second, VMEM),
        ]
        + [(value, ANY) for value in swaps],
        [
            pltpu.VMEM((rows, width), F32),
            pltpu.VMEM((rows, width), F32),
            pltpu.VMEM(both.shape, F32),
            pltpu.VMEM((8, width), F32),
        ]
        + Fold.scratch(rows, width) * 2
        + Swap.scratch(swaps)
        + GainSum.scratch(count, both),
        9,
        "last_fold",
    )


def gelu_both(value):
    square = value * value
    bend = jnp.tanh(GELU_SCALE * value * (1.0 + GELU_CUBE * square))
    act = 0.5 * value * (1.0 + bend)
    slope = 0.5 * (1.0 + bend) + 0.5 * value * (1.0 - bend * bend) * GELU_SCALE * (
        1.0 + 3.0 * GELU_CUBE * square
    )
    return act, slope


def chunks(rows, action, size=CHUNK):
    def body(i, carry):
        action(pl.multiple_of(i * size, size))
        return carry

    lax.fori_loop(0, rows // size, body, 0)


def spans(low, high, action):
    def body(i, carry):
        action(pl.multiple_of(i * CHUNK, CHUNK))
        return carry

    lax.fori_loop(low, high, body, 0)


def tile_scan(mults, adds, rows, width, backward):
    place = lax.broadcasted_iota(jnp.int32, (8, width), 0)

    def inside(base):
        where = pl.ds(base, 8)
        a, b = mults[where, :], adds[where, :]
        for k in (1, 2, 4):
            if backward:
                away, mask = pltpu.roll(a, 8 - k, 0), place < 8 - k
                back = pltpu.roll(b, 8 - k, 0)
            else:
                away, mask = pltpu.roll(a, k, 0), place >= k
                back = pltpu.roll(b, k, 0)
            b = jnp.where(mask, b + a * back, b)
            a = jnp.where(mask, a * away, a)
        return where, a, b

    unroll = 4
    tiles = rows // 8

    def body(i, carry):
        prod, total = carry
        work = []
        for u in range(unroll):
            index = i * unroll + u
            if backward:
                index = tiles - 1 - index
            work.append(inside(pl.multiple_of(index * 8, 8)))
        for where, a, b in work:
            edge = 0 if backward else 7
            adds[where, :] = b + a * total
            mults[where, :] = a * prod
            whole = jnp.broadcast_to(a[edge : edge + 1, :], (8, width))
            extra = jnp.broadcast_to(b[edge : edge + 1, :], (8, width))
            total = extra + whole * total
            prod = whole * prod
        return prod, total

    return lax.fori_loop(
        0, tiles // unroll, body, (jnp.ones((8, width), F32), jnp.zeros((8, width), F32))
    )


def pool(count, prod, total, outgoing, slots, send, receive, backward):
    line, side, deck, core = spot()
    outgoing[0:8, :] = prod
    outgoing[8:16, :] = total
    slots[line, 0:8, :] = prod
    slots[line, 8:16, :] = total
    copies = []
    for k in range(1, count):
        copy = remote(
            outgoing,
            slots.at[line],
            send.at[k],
            receive.at[k],
            seat((line + k) % count, side, deck, core),
        )
        copy.start()
        copies.append(copy)
    for copy in copies:
        copy.wait()
    entering = jnp.zeros_like(prod)
    order = range(count - 1, -1, -1) if backward else range(count)
    for place in order:
        longer = slots[place, 8:16, :] + slots[place, 0:8, :] * entering
        before = (line < place) if backward else (line > place)
        entering = jnp.where(before, longer, entering)
    return entering


def sigmoid(value):
    return 0.5 + 0.5 * jnp.tanh(0.5 * value)


def gates(recur, soft):
    decay = jnp.exp(-8.0 * recur * soft)
    square = (1.0 + GUARD) - decay * decay
    inverse = lax.rsqrt(square)
    return decay, square * inverse, inverse


def scan_kernel(count, starts, *refs):
    loads = len(starts)
    pre, masks, table, gate_weights, cotangent = refs[:5]
    halves, refs = refs[5 : 5 + loads], refs[5 + loads :]
    everything, targets, refs = refs[6], refs[7 : 7 + loads], refs[:6] + refs[7 + loads :]
    saved, refs = refs[:6], refs[6:]
    gate, entry, conv, recur_out, admit_out, state, merged = refs[:7]
    prods, sums, halo, outgoing, slots, edge_sems, send, receive = refs[7:15]
    in_sems, out_sems, head_sems = refs[15:18]
    sems = refs[18:]
    line, side, deck, core = spot()
    rows, width = conv.shape
    gather = GroupGather(cotangent, everything, *sems[:3])
    freights = load(count, starts, halves, targets, sems[5:])
    gate_reads = Stream(pre, gate, in_sems.at[0], columns=pl.ds(0, width))
    entry_reads = Stream(pre, entry, in_sems.at[1], to_row=8, columns=pl.ds(width, width))
    conv_writes = Stream(conv, saved[0], out_sems.at[0])
    recur_writes = Stream(recur_out, saved[1], out_sems.at[1])
    admit_writes = Stream(admit_out, saved[2], out_sems.at[2])
    state_writes = Stream(state, saved[3], out_sems.at[3], 8, 8)
    merged_writes = Stream(merged, saved[4], out_sems.at[4])
    entry_writes = Stream(entry, saved[5], out_sems.at[5], 8, 8)
    heads = [
        pltpu.make_async_copy(local.at[pl.ds(0, 8)], away.at[pl.ds(0, 8)], head_sems.at[k])
        for k, (local, away) in enumerate([(state, saved[3]), (entry, saved[5])])
    ]
    entry_reads.start_all()
    gate_reads.start_all()
    greet(cargo_peers(count))

    def edge(place):
        return remote(
            pre.at[pl.ds(rows - 8, 8), pl.ds(width, width)],
            halo,
            edge_sems.at[0],
            edge_sems.at[1],
            seat(place, side, deck, core),
        )

    @pl.when(line < count - 1)
    def _():
        edge(line + 1).start()

    for freight in freights:
        freight.start()
    gather.start()

    @pl.when(line > 0)
    def _():
        edge(line - 1).wait_recv()
        entry[0:8, :] = halo[...]

    @pl.when(line == 0)
    def _():
        entry[0:8, :] = jnp.zeros((8, width), F32)

    @pl.when(line < count - 1)
    def _():
        edge(line + 1).wait_send()

    heads[1].start()

    def gate_chunk(r):
        entry_reads.wait(r)
        wide = entry[pl.ds(r, CHUNK + 8), :]
        mask = masks[pl.ds(r, CHUNK), :]
        value = table[0:1, :] * wide[8:, :]
        for k in range(1, TAPS):
            value = (
                value + table[k : k + 1, :] * wide[8 - k : 8 - k + CHUNK, :] * mask[:, k - 1 : k]
            )
        where = pl.ds(r, CHUNK)
        conv[where, :] = value
        both = jnp.dot(value.astype(BF16), gate_weights[...], preferred_element_type=F32)
        recur = sigmoid(both[:, :width])
        admit = sigmoid(both[:, width:])
        recur_out[where, :] = recur
        admit_out[where, :] = admit
        decay, root, _ = gates(recur, table[4:5, :])
        opened = mask[:, 3:4]
        norm = root * opened + (1.0 - opened)
        prods[where, :] = decay * opened
        sums[where, :] = norm * admit * value
        for stream in (entry_writes, conv_writes, recur_writes, admit_writes):
            stream.start(r)

    pieces = rows // CHUNK
    spans(0, 1, gate_chunk)
    for freight in freights:
        freight.second()
    gather.start_across()
    spans(1, pieces, gate_chunk)
    prod, total = tile_scan(prods, sums, rows, width, False)
    entering = pool(count, prod, total, outgoing, slots, send, receive, False)
    for freight in freights:
        freight.forward()
    gather.forward()
    state[0:8, :] = entering
    heads[0].start()

    def state_chunk(r):
        gate_reads.wait(r)
        where = pl.ds(r, CHUNK)
        value = sums[where, :] + prods[where, :] * entering[0:1, :]
        state[pl.ds(r + 8, CHUNK), :] = value
        act, _ = gelu_both(gate[where, :])
        merged[where, :] = (value * act).astype(BF16)
        state_writes.start(r)
        merged_writes.start(r)

    chunks(rows, state_chunk)
    for stream in (
        entry_writes,
        conv_writes,
        recur_writes,
        admit_writes,
        state_writes,
        merged_writes,
    ):
        stream.wait_all()
    for copy in heads:
        copy.wait()
    group_finish(gather, *sems[3:5])
    for freight in freights:
        freight.finish()


def scan_forward(count, pre, masks, table, gate_weights, cotangent, cargo):
    rows, width = pre.shape[0], pre.shape[1] // 2
    pieces = rows // CHUNK
    tall = (rows + 8, width)
    saved = [
        ((rows, width), F32),
        ((rows, width), F32),
        ((rows, width), F32),
        (tall, F32),
        ((rows, width), BF16),
        (tall, F32),
    ]
    out = call(
        functools.partial(scan_kernel, count, cargo_starts(cargo)),
        [(shape, kind, ANY) for shape, kind in saved]
        + [((8,) + cotangent.shape, BF16, ANY)]
        + cargo_outs(count, cargo),
        [(pre, ANY), (masks, VMEM), (table, VMEM), (gate_weights, VMEM), (cotangent, ANY)]
        + cargo_ins(cargo),
        [
            pltpu.VMEM((rows, width), F32),
            pltpu.VMEM(tall, F32),
            pltpu.VMEM((rows, width), F32),
            pltpu.VMEM((rows, width), F32),
            pltpu.VMEM((rows, width), F32),
            pltpu.VMEM(tall, F32),
            pltpu.VMEM((rows, width), BF16),
            pltpu.VMEM((rows, width), F32),
            pltpu.VMEM((rows, width), F32),
            pltpu.VMEM((8, width), F32),
            pltpu.VMEM((16, width), F32),
            pltpu.VMEM((count, 16, width), F32),
            pltpu.SemaphoreType.DMA((2,)),
            pltpu.SemaphoreType.DMA((count,)),
            pltpu.SemaphoreType.DMA((count,)),
            pltpu.SemaphoreType.DMA((2, pieces)),
            pltpu.SemaphoreType.DMA((6, pieces)),
            pltpu.SemaphoreType.DMA((2,)),
        ]
        + rows_scratch()
        + cargo_scratch(count, cargo),
        2,
        "scan_forward",
    )
    return out[:6] + [out[6].reshape(-1, cotangent.shape[1])] + flat_rows(out[7:])


def back_kernel(count, lanes, swaps, *refs, fetches):
    pre, low, outlet = refs[:3]
    saved, refs = refs[3:8], refs[8:]
    masks, table, gate_weights = refs[:3]
    values, refs = refs[3 : 3 + swaps], refs[3 + swaps :]
    grad_pre, grad_gates, grad_table = refs[:3]
    swapped, refs = refs[3 : 3 + swaps], refs[3 + swaps :]
    gate, conv, recur_in, admit_in, state, entry, lows = refs[:7]
    prods, sums, mixes, outgoing, slots, edge_sems, send, receive = refs[7:15]
    in_sems, low_sems, head_sems = refs[15:18]
    line, side, deck, core = spot()
    rows, width = conv.shape
    pieces = rows // CHUNK
    swap = Swap(values, swapped, *refs[18:])
    conv_reads = Stream(saved[0], conv, in_sems.at[0])
    recur_reads = Stream(saved[1], recur_in, in_sems.at[1])
    admit_reads = Stream(saved[2], admit_in, in_sems.at[2])
    state_reads = Stream(saved[3], state, in_sems.at[3], 8, 8)
    entry_reads = Stream(saved[4], entry, in_sems.at[4], 8, 8)
    gate_reads = Stream(pre, gate, in_sems.at[5], columns=pl.ds(0, width))
    heads = [
        pltpu.make_async_copy(away.at[pl.ds(0, 8)], local.at[pl.ds(0, 8)], head_sems.at[k])
        for k, (local, away) in enumerate([(state, saved[3]), (entry, saved[4])])
    ]

    def fetch(i):
        slot = i % 2
        start = pl.multiple_of(i * CHUNK, CHUNK)
        return pltpu.make_async_copy(
            low.at[pl.ds(start, CHUNK)], lows.at[slot], low_sems.at[slot]
        )

    fetch(0).start()
    for k in range(pieces):
        for stream in (gate_reads, recur_reads, state_reads):
            stream.start(k * CHUNK)
    for copy in heads:
        copy.start()
    for stream in (conv_reads, admit_reads, entry_reads):
        stream.start_all()
    greet(line_peers(count) + ([seat(line, 1 - side, deck, core)] if swaps else []))
    swap.start()
    for copy in fetches:
        copy.wait()

    def direct(i, carry):
        r = pl.multiple_of(i * CHUNK, CHUNK)

        @pl.when(i + 1 < pieces)
        def _():
            fetch(i + 1).start()

        fetch(i).wait()
        for stream in (gate_reads, recur_reads, state_reads):
            stream.wait(r)
        where = pl.ds(r, CHUNK)
        grad = jnp.dot(lows[i % 2], outlet[...], preferred_element_type=F32)
        act, slope = gelu_both(gate[where, :])
        gate[where, :] = grad * state[pl.ds(r + 8, CHUNK), :] * slope
        straight = grad * act
        carried = jnp.exp(-8.0 * recur_in[where, :] * table[4:5, :]) * masks[where, 3:4]
        mixes[where, :] = straight
        prods[where, :] = carried
        sums[where, :] = carried * straight
        return carry

    lax.fori_loop(0, pieces, direct, 0)
    prods[rows : rows + 8, :] = jnp.ones((8, width), F32)
    sums[rows : rows + 8, :] = jnp.zeros((8, width), F32)
    prod, total = tile_scan(prods, sums, rows, width, True)
    entering = pool(count, prod, total, outgoing, slots, send, receive, True)
    for copy in heads:
        copy.wait()
    grad_gates[...] = jnp.zeros_like(grad_gates)
    grad_table[...] = jnp.zeros_like(grad_table)

    def fold_rows(value):
        return jnp.sum(value, axis=0, keepdims=True)

    def gate_chunk(r):
        conv_reads.wait(r)
        admit_reads.wait(r)
        where = pl.ds(r, CHUNK)
        wide = pl.ds(r, CHUNK + 8)
        later = sums[wide, :] + prods[wide, :] * entering[0:1, :]
        grad = mixes[where, :] + later[1 : CHUNK + 1, :]
        before = state[wide, :][7 : CHUNK + 7, :]
        soft = table[4:5, :]
        recur, admit, value = recur_in[where, :], admit_in[where, :], conv[where, :]
        decay, root, inverse = gates(recur, soft)
        opened = masks[where, 3:4]
        norm = root * opened + (1.0 - opened)
        flow = grad * admit
        grad_log = opened * (grad * before * decay - flow * value * decay * decay * inverse)
        grad_table[4:5, :] += fold_rows(grad_log * (-8.0 * recur))
        grad_rate = (grad_log * (-8.0 * soft) * recur * (1.0 - recur)).astype(BF16)
        grad_inlet = (flow * norm * value * (1.0 - admit)).astype(BF16)
        both = jnp.concatenate([grad_rate, grad_inlet], axis=1)
        grad_gates[...] += lax.dot_general(
            value.astype(BF16), both, TN, preferred_element_type=F32
        )
        mixes[where, :] = flow * norm + lax.dot_general(
            both, gate_weights[...], NT, preferred_element_type=F32
        )

    gate_chunk(0)

    def edge(place):
        return remote(
            mixes.at[pl.ds(0, 8)],
            mixes.at[pl.ds(rows, 8)],
            edge_sems.at[0],
            edge_sems.at[1],
            seat(place, side, deck, core),
        )

    @pl.when(line > 0)
    def _():
        edge(line - 1).start()

    spans(1, pieces, gate_chunk)

    @pl.when(line < count - 1)
    def _():
        edge(line + 1).wait_recv()

    @pl.when(line == count - 1)
    def _():
        mixes[rows : rows + 8, :] = jnp.zeros((8, width), F32)

    spare = width - lanes
    shift = 2 * lanes - width

    def entry_chunk(r):
        entry_reads.wait(r)
        where, wide = pl.ds(r, CHUNK), pl.ds(r, CHUNK + 8)
        ahead, mask = mixes[wide, :], masks[where, :]
        source = entry[wide, :]
        here = ahead[:CHUNK, :]
        total = table[0:1, :] * here
        grad_table[0:1, :] += fold_rows(here * source[8:, :])
        for k in range(1, TAPS):
            total = total + table[k : k + 1, :] * ahead[k : k + CHUNK, :] * mask[:, 3 + k : 4 + k]
            grad_table[k : k + 1, :] += fold_rows(
                here * source[8 - k : 8 - k + CHUNK, :] * mask[:, k - 1 : k]
            )
        total = pltpu.roll(total, spare, 1)
        first = gate[where, :]
        middle = first[:, shift:] + total[:, : width - shift]
        grad_pre[where, :shift] = first[:, :shift].astype(BF16)
        grad_pre[where, shift:width] = middle.astype(BF16)
        grad_pre[where, width:] = total[:, width - shift :].astype(BF16)

    chunks(rows, entry_chunk)

    @pl.when(line > 0)
    def _():
        edge(line - 1).wait_send()

    swap.finish()


def scan_backward(count, lanes, pre, low, outlet, saved, masks, table, gate_weights, swaps):
    rows, width = pre.shape[0], pre.shape[1] // 2
    pieces = rows // CHUNK
    tall = (rows + 8, width)
    return call(
        functools.partial(back_kernel, count, lanes, len(swaps)),
        [
            ((rows, 2 * lanes), BF16, VMEM),
            ((width, 2 * width), F32, VMEM),
            ((8, width), F32, VMEM),
        ]
        + [(value.shape, BF16, ANY) for value in swaps],
        [(pre, ANY), (low, ANY), (outlet, LATE)]
        + [(value, ANY) for value in saved]
        + [(masks, LATE), (table, VMEM), (gate_weights, LATE)]
        + [(value, ANY) for value in swaps],
        [
            pltpu.VMEM((rows, width), F32),
            pltpu.VMEM((rows, width), F32),
            pltpu.VMEM((rows, width), F32),
            pltpu.VMEM((rows, width), F32),
            pltpu.VMEM(tall, F32),
            pltpu.VMEM(tall, F32),
            pltpu.VMEM((2, CHUNK, low.shape[1]), BF16),
            pltpu.VMEM(tall, F32),
            pltpu.VMEM(tall, F32),
            pltpu.VMEM(tall, F32),
            pltpu.VMEM((16, width), F32),
            pltpu.VMEM((count, 16, width), F32),
            pltpu.SemaphoreType.DMA((2,)),
            pltpu.SemaphoreType.DMA((count,)),
            pltpu.SemaphoreType.DMA((count,)),
            pltpu.SemaphoreType.DMA((6, pieces)),
            pltpu.SemaphoreType.DMA((2,)),
            pltpu.SemaphoreType.DMA((2,)),
        ]
        + Swap.scratch(swaps),
        7,
        "scan_backward",
    )


def feed_kernel(count, early, starts, *refs):
    loads = len(starts)
    normed, cotangent = refs[:2]
    gate_parts, up_parts, down_parts = refs[2:4], refs[4:6], refs[6 : 6 + early]
    refs = refs[6 + early :]
    halves, refs = refs[:loads], refs[loads:]
    results, down_grads = refs[:3], refs[3]
    targets, refs = refs[4 : 4 + loads], refs[4 + loads :]
    table, gate_up, acts, slopes, down, hidden, grad_gating, grad_lifting = refs[:8]
    table_sems, back_sems, write_sems, weight_sems, down_sems = refs[8:13]
    freights = load(count, starts, halves, targets, refs[13:])
    rows, width = hidden.shape
    pieces = rows // CHUNK
    reads = Stream(normed, table, table_sems)
    again = Stream(cotangent, table, back_sems)
    writes = [
        Stream(local, away, write_sems.at[k])
        for k, (local, away) in enumerate(zip((hidden, grad_gating, grad_lifting), results))
    ]
    weights = []
    for which, parts in enumerate((gate_parts, up_parts)):
        start = 0
        for part in parts:
            weights.append(
                pltpu.make_async_copy(
                    part,
                    gate_up.at[which, :, pl.ds(start, part.shape[1])],
                    weight_sems.at[len(weights)],
                )
            )
            start += part.shape[1]
    for copy in weights:
        copy.start()
    reads.start_all()
    greet(cargo_peers(count))
    for freight in freights:
        freight.start()
    for copy in weights:
        copy.wait()

    def forward_chunk(r):
        reads.wait(r)
        where = pl.ds(r, CHUNK)
        gating = jnp.dot(table[where, :], gate_up[0], preferred_element_type=F32)
        lifting = jnp.dot(table[where, :], gate_up[1], preferred_element_type=F32)
        act, slope = gelu_both(gating)
        hidden[where, :] = (act * lifting).astype(BF16)
        acts[where, :] = act
        slopes[where, :] = lifting * slope
        writes[0].start(r)
        again.start(r)

    spans(0, pieces // 4, forward_chunk)
    for freight in freights:
        freight.second()
    spans(pieces // 4, pieces, forward_chunk)
    for freight in freights:
        freight.forward()
    rows_in = down.shape[0] // count
    copies, start = [], 0
    for k, part in enumerate(down_parts):
        copies.append(
            pltpu.make_async_copy(
                part, down.at[:, pl.ds(start, part.shape[1])], down_sems.at[k]
            )
        )
        start += part.shape[1]
    for k, target in enumerate(targets):
        for place in range(count):
            copies.append(
                pltpu.make_async_copy(
                    target.at[place],
                    down.at[pl.ds(place * rows_in, rows_in), pl.ds(start, target.shape[2])],
                    down_sems.at[early + k * count + place],
                )
            )
        start += target.shape[2]

    def back(low, high):
        def chunk(r):
            where = pl.ds(r, CHUNK)
            columns = slice(low, high)
            grad = jnp.dot(table[where, :], down[:, columns], preferred_element_type=F32)
            grad_gating[where, columns] = (grad * slopes[where, columns]).astype(BF16)
            grad_lifting[where, columns] = (grad * acts[where, columns]).astype(BF16)
            if high == width:
                writes[1].start(r)
                writes[2].start(r)

        chunks(rows, chunk)

    for copy in copies[:early]:
        copy.start()
    again.wait_all()
    for copy in copies[:early]:
        copy.wait()
    turned(table, hidden, down_grads, 4, 0, 4)
    ready = sum(part.shape[1] for part in down_parts)
    back(0, ready)
    for freight in freights:
        freight.finish()
    for copy in copies[early:]:
        copy.start()
    for copy in copies[early:]:
        copy.wait()
    back(ready, width)
    for stream in writes:
        stream.wait_all()


def feed(count, normed, cotangent, gate_parts, up_parts, down_parts, cargo):
    rows = normed.shape[0]
    width = sum(part.shape[1] for part in gate_parts)
    pieces = rows // CHUNK
    out = call(
        functools.partial(feed_kernel, count, len(down_parts), cargo_starts(cargo)),
        [((rows, width), BF16, ANY)] * 3
        + [((normed.shape[1], width), BF16, VMEM)]
        + cargo_outs(count, cargo),
        [(normed, ANY), (cotangent, ANY)]
        + [(part, ANY) for part in list(gate_parts) + list(up_parts) + list(down_parts)]
        + cargo_ins(cargo),
        [
            pltpu.VMEM(normed.shape, BF16),
            pltpu.VMEM((2, normed.shape[1], width), BF16),
            pltpu.VMEM((rows, width), F32),
            pltpu.VMEM((rows, width), F32),
            pltpu.VMEM((normed.shape[1], width), BF16),
            pltpu.VMEM((rows, width), BF16),
            pltpu.VMEM((rows, width), BF16),
            pltpu.VMEM((rows, width), BF16),
            pltpu.SemaphoreType.DMA((pieces,)),
            pltpu.SemaphoreType.DMA((pieces,)),
            pltpu.SemaphoreType.DMA((3, pieces)),
            pltpu.SemaphoreType.DMA((4,)),
            pltpu.SemaphoreType.DMA((len(down_parts) + count * len(cargo),)),
        ]
        + cargo_scratch(count, cargo),
        5,
        "feed",
    )
    return out[:4] + flat_rows(out[4:])


def doc_index(places, doc_starts):
    return jnp.sum((doc_starts[None, :] <= places[:, None]).astype(jnp.int32), axis=1)


def split_columns(value):
    rows, columns = value.shape
    return value.reshape(rows, 2, columns // 2).transpose(1, 0, 2)


def widen(value, width):
    return jnp.pad(value, [(0, 0)] * (value.ndim - 1) + [(0, width - value.shape[-1])])


def by_rows(left, right):
    return lax.dot_general(left, right, TN, preferred_element_type=F32).astype(BF16)


def shards(
    layer_input,
    out_grad,
    doc_starts,
    mixer_gain,
    branch_gate,
    branch_input,
    conv_taps,
    rate_gate,
    input_gate,
    decay_param,
    mixer_out,
    feed_gain,
    feed_gate,
    feed_up,
    feed_down,
):
    shares = lax.axis_size("dp")
    count = shares // 2
    side = lax.axis_index("dp") % 2
    slim, feature_count = mixer_gain.shape[0], layer_input.shape[1]
    heads, piece, head_width = rate_gate.shape
    half_heads = heads // 2
    lanes = half_heads * head_width
    width = -(-lanes // 128) * 128
    row_count = layer_input.shape[0]
    rows = row_count * 8
    line_groups = [[2 * k + s for k in range(count)] for s in range(2)]

    branch_halves = jnp.concatenate(
        [split_columns(branch_gate), split_columns(branch_input)], axis=2
    )
    mixer_halves = widen(split_columns(mixer_out.T), width)
    down_rows = feed_down.T
    narrow = feed_gate.shape[1] // 6
    broad = 2 * narrow

    mine = lax.axis_index("dp")
    blocks = jnp.concatenate([rate_gate, input_gate], axis=2)
    blocks = widen(blocks.reshape(2, half_heads * piece, 2 * head_width), width)
    own = jnp.concatenate([conv_taps, decay_param[None]], axis=0)
    own = jnp.pad(own, ((0, 0), (0, 0), (0, head_width - piece)))
    own = jnp.roll(own, mine * piece, axis=2)
    own = own.reshape(TAPS + 1, 2, lanes).transpose(1, 0, 2)
    gains_own = jnp.pad(jnp.stack([mixer_gain, feed_gain]), ((0, 14), (0, 0)))
    tail = jnp.pad(widen(own, width), ((0, 0), (0, 15 - TAPS), (0, 0)))
    small_top = -(-half_heads * piece // 16) * 16
    small = jnp.concatenate(
        [jnp.pad(blocks, ((0, 0), (0, small_top - half_heads * piece), (0, 0))), tail], axis=1
    )

    normed_one, pre, gains_all, branch_all, small_all, gate_first = first(
        count, layer_input, gains_own, [branch_halves, small, (feed_gate, 0, narrow)], width
    )

    small_all = small_all.reshape(shares, -1, width)
    tails = small_all[:, small_top:].astype(F32)
    gain_first = gains_all[:, 0].reshape(feature_count).astype(F32)
    gain_second = gains_all[:, 1].reshape(feature_count).astype(F32)
    sums = jnp.sum(tails[:, : TAPS + 1], axis=0)
    decay_flat = sums[TAPS, :lanes]
    inside = (jnp.arange(width) < lanes)[None]
    table = jnp.concatenate(
        [
            sums[:TAPS],
            jnp.where(inside, jax.nn.softplus(-sums[TAPS:]), 0.0),
            jnp.zeros((3, width), F32),
        ]
    )
    blocks = (
        small_all[:, : half_heads * piece, : 2 * head_width]
        .reshape(shares, half_heads, piece, 2 * head_width)
        .transpose(1, 0, 2, 3)
        .reshape(lanes, 2 * head_width)
    )
    head_of = jnp.arange(width) // head_width
    same = (head_of[:lanes, None] == head_of[None, :]) & (jnp.arange(width) < lanes)[None]

    def diagonal(part):
        wide = widen(jnp.concatenate([part] * half_heads, axis=1), width)
        return jnp.where(same, wide, 0)

    gate_weights = jnp.concatenate(
        [diagonal(blocks[:, :head_width]), diagonal(blocks[:, head_width:])], axis=1
    )
    gate_weights = jnp.pad(gate_weights, ((0, width - lanes), (0, 0)))

    anchor = lax.axis_index("dp") // 2 * rows
    places = anchor + jnp.arange(rows, dtype=jnp.int32)
    here = doc_index(places, doc_starts)
    columns = [doc_index(places - k, doc_starts) == here for k in range(1, TAPS)]
    columns.append(~jnp.any(doc_starts[None, :] == places[:, None], axis=1))
    columns += [doc_index(places + k, doc_starts) == here for k in range(1, TAPS)]
    columns.append(columns[0])
    masks = jnp.stack(columns, axis=1).astype(F32)

    conv, recur, admit, state, merged, entry, cot_all, mixer_all, up_first = scan_forward(
        count, pre, masks, table, gate_weights, out_grad, [mixer_halves, (feed_up, 0, narrow)]
    )
    hidden_one, normed_own, gate_second, down_first = mixer_fold(
        count,
        merged,
        mixer_all,
        layer_input,
        gain_second[None],
        [(feed_gate, narrow, broad), (down_rows, 0, narrow)],
    )
    normed_two, up_second = gather_rows(count, normed_own, [(feed_up, narrow, broad)], 4)
    gate_parts, up_parts = [gate_first, gate_second], [up_first, up_second]
    hidden, grad_gating, grad_lifting, down_grads, down_second = feed(
        count,
        normed_two,
        cot_all,
        gate_parts,
        up_parts,
        [down_first],
        [(down_rows, narrow, broad)],
    )
    down_parts = [down_first, down_second]

    def line_sum(value):
        return lax.psum_scatter(
            value, "dp", scatter_dimension=0, axis_index_groups=line_groups, tiled=True
        )

    down_sum = line_sum(down_grads)
    grad_hidden_one, low_own, second_terms, gate_grads = feed_fold(
        grad_gating,
        grad_lifting,
        gate_parts,
        up_parts,
        normed_two,
        hidden_one,
        out_grad,
        gain_second[None],
    )
    low_own, down_sum = lax.optimization_barrier((low_own, down_sum))
    gate_sum = line_sum(gate_grads)
    back_low, up_grads = gather_plain(low_own, normed_two, grad_lifting, 8)
    up_sum = line_sum(up_grads)
    outlet_grads = by_rows(back_low, merged)

    def by_side(value):
        return value.reshape(2, -1, value.shape[1])

    back_low, outlet_grads, gate_sum = lax.optimization_barrier(
        (back_low, outlet_grads, gate_sum)
    )
    grad_pre, grad_gates, grad_table, down_both, gate_both = scan_backward(
        count,
        lanes,
        pre,
        back_low,
        mixer_all,
        [conv, recur, admit, state, entry],
        masks,
        table,
        gate_weights,
        [by_side(down_sum), by_side(gate_sum)],
    )
    branch_grads = by_rows(normed_one, grad_pre)

    def spots(value):
        blocks = [
            value[
                h * head_width : (h + 1) * head_width, h * head_width : (h + 1) * head_width
            ].reshape(shares, -1)
            for h in range(half_heads)
        ]
        return jnp.concatenate(blocks, axis=1)

    grad_decay = -jax.nn.sigmoid(-decay_flat) * grad_table[4, :lanes]
    grad_small = jnp.concatenate(
        [
            spots(grad_gates[:, :width]),
            spots(grad_gates[:, width:]),
            grad_table[:TAPS, :lanes]
            .reshape(TAPS * half_heads, shares, piece)
            .transpose(1, 0, 2)
            .reshape(shares, -1),
            grad_decay.reshape(half_heads, shares, piece).transpose(1, 0, 2).reshape(shares, -1),
        ],
        axis=1,
    )
    flat_size = grad_small.shape[1]
    spare = width - lanes
    grad_small = widen(grad_small, slim * spare).reshape(feature_count, spare).astype(BF16)
    last_grads = jnp.concatenate([outlet_grads[:, :lanes], grad_small, branch_grads], axis=1)
    grad_pre, last_grads = lax.optimization_barrier((grad_pre, last_grads))
    last_sum = line_sum(last_grads)
    input_grad, layer_output, gains, up_both = last_fold(
        count,
        grad_pre,
        branch_all,
        hidden,
        down_parts,
        layer_input,
        gain_first[None],
        grad_hidden_one,
        hidden_one,
        second_terms,
        [by_side(up_sum)],
    )
    first_gain_grad = lax.dynamic_index_in_dim(gains, mine, 0, False)
    second_gain_grad = lax.dynamic_index_in_dim(gains, shares + mine, 0, False)

    def swap(value):
        pair = by_side(value)
        kept = lax.dynamic_index_in_dim(pair, side, 0, False)
        given = lax.dynamic_index_in_dim(pair, 1 - side, 0, False)
        other = lax.ppermute(given, "dp", [(k, k ^ 1) for k in range(shares)])
        return [
            jnp.where(side == 0, kept, other).astype(F32),
            jnp.where(side == 0, other, kept).astype(F32),
        ]

    lasts = swap(last_sum)

    def columns(start, stop):
        return jnp.concatenate([value[:, start:stop] for value in lasts], axis=1)

    mixer_out_grad = columns(0, lanes).T
    branch_gate_grad = columns(width, width + lanes)
    branch_input_grad = columns(width + lanes, width + 2 * lanes)
    smalls = [value[:, lanes:width].reshape(-1)[:flat_size] for value in lasts]
    one = half_heads * piece * head_width
    tap_size = TAPS * half_heads * piece
    rate_grad = jnp.concatenate([v[:one].reshape(half_heads, piece, head_width) for v in smalls])
    inlet_grad = jnp.concatenate(
        [v[one : 2 * one].reshape(half_heads, piece, head_width) for v in smalls]
    )
    taps_grad = jnp.concatenate(
        [v[2 * one : 2 * one + tap_size].reshape(TAPS, half_heads, piece) for v in smalls], axis=1
    )
    decay_grad = jnp.concatenate(
        [v[2 * one + tap_size :].reshape(half_heads, piece) for v in smalls]
    )

    def joined(value):
        return jnp.concatenate([value[0], value[1]], axis=1).astype(F32)

    return (
        layer_output,
        input_grad,
        first_gain_grad,
        branch_gate_grad,
        branch_input_grad,
        taps_grad,
        rate_grad,
        inlet_grad,
        decay_grad,
        mixer_out_grad,
        second_gain_grad,
        joined(gate_both),
        joined(up_both),
        joined(down_both).T,
    )


def solution(mesh):
    placed = (
        P(("dp", "tensor"), None),
        P(("dp", "tensor"), None),
        P(),
        P("dp"),
        P("dp", "tensor"),
        P("dp", "tensor"),
        P(None, "tensor", "dp"),
        P("tensor", "dp", None),
        P("tensor", "dp", None),
        P("tensor", "dp"),
        P("tensor", "dp"),
        P("dp"),
        P("dp", "tensor"),
        P("dp", "tensor"),
        P("tensor", "dp"),
    )
    return jax.shard_map(
        shards,
        mesh=mesh,
        in_specs=placed,
        out_specs=(
            P(("dp", "tensor"), None),
            P(("dp", "tensor"), None),
            P("dp"),
            P("dp", "tensor"),
            P("dp", "tensor"),
            P(None, "tensor", "dp"),
            P("tensor", "dp", None),
            P("tensor", "dp", None),
            P("tensor", "dp"),
            P("tensor", "dp"),
            P("dp"),
            P("dp", "tensor"),
            P("dp", "tensor"),
            P("tensor", "dp"),
        ),
        check_vma=False,
    )
```

```python
import functools

import jax
import jax.numpy as jnp
from jax import lax
from jax.experimental import pallas as pl
from jax.experimental.layout import Layout, with_layout_constraint
from jax.experimental.pallas import tpu as pltpu
from jax.sharding import PartitionSpec as P

TAPS = 4
EPSILON = 1e-06
GUARD = 0.001
GELU_SCALE = 0.7978845608028654
GELU_CUBE = 0.044715
MESH = pl.DeviceIdType.MESH
F32, BF16 = jnp.float32, jnp.bfloat16
ANY = pl.BlockSpec(memory_space=pl.ANY)
VMEM = pl.BlockSpec(memory_space=pltpu.VMEM)
LATE = pl.BlockSpec(memory_space=pl.ANY)
GRANT = 60 * 1024 * 1024
NT = (((1,), (1,)), ((), ()))
TN = (((0,), (0,)), ((), ()))
CHUNK = 512


def spot():
    dp, tensor = lax.axis_index("dp"), lax.axis_index("tensor")
    return dp // 2, dp % 2, tensor // 2, tensor % 2


def seat(line, side, deck, core):
    return (line * 2 + side, deck * 2 + core)


def rank(side, deck, core):
    return side * 4 + deck * 2 + core


def greet(peers):
    barrier = pltpu.get_barrier_semaphore()
    for peer in peers:
        pl.semaphore_signal(barrier, inc=1, device_id=peer, device_id_type=MESH)
    pl.semaphore_wait(barrier, len(peers))


def remote(source, target, send, receive, peer):
    return pltpu.make_async_remote_copy(
        src_ref=source,
        dst_ref=target,
        send_sem=send,
        recv_sem=receive,
        device_id=peer,
        device_id_type=MESH,
    )


def line_peers(count):
    line, side, deck, core = spot()
    return [seat((line + k) % count, side, deck, core) for k in range(1, count)]


def group_peers():
    line, side, deck, core = spot()
    return [
        seat(line, side, deck, 1 - core),
        seat(line, 1 - side, deck, core),
        seat(line, side, 1 - deck, core),
    ]


class Freight:
    def __init__(self, count, halves, target, sems, start=0):
        self.count, self.halves, self.target = count, halves, target
        self.start_column = start
        self.cross, self.local, self.send, self.receive = sems
        self.line, self.side, self.deck, self.core = spot()

    @staticmethod
    def scratch(count):
        steps = 5 if count == 4 else count - 1
        return [
            pltpu.SemaphoreType.DMA((2,)),
            pltpu.SemaphoreType.DMA,
            pltpu.SemaphoreType.DMA((steps, 2)),
            pltpu.SemaphoreType.DMA((count, 2)),
        ]

    def half(self, which):
        if len(self.halves.shape) == 3:
            return self.halves.at[which]
        offset = which * (self.halves.shape[1] // 2) + self.start_column
        return self.halves.at[:, pl.ds(pl.multiple_of(offset, 128), self.target.shape[2])]

    def place(self, origin, part):
        rows = self.target.shape[1] // 2
        return self.target.at[origin, pl.ds(pl.multiple_of(part * rows, rows), rows)]

    def seat(self, line):
        return seat(line, self.side, self.deck, self.core)

    def swap(self):
        return remote(
            self.half(1 - self.side),
            self.place(self.line, self.side),
            self.cross.at[0],
            self.cross.at[1],
            seat(self.line, 1 - self.side, self.deck, self.core),
        )

    def keep(self):
        return pltpu.make_async_copy(
            self.half(self.side), self.place(self.line, self.side), self.local
        )

    def copy(self, origin, line, index, part, source):
        return remote(
            source,
            self.place(origin, part),
            self.send.at[index, part],
            self.receive.at[origin, part],
            self.seat(line),
        )

    def own(self, line, index, part):
        source = self.half(self.side)
        if part is not self.side:
            source = self.place(self.line, part)
        return self.copy(self.line, line, index, part, source)

    def arrival(self, origin, part):
        return self.copy(origin, origin, 0, part, self.half(self.side))

    def each_step(self, action, phases=(0, 1)):
        if self.count == 4:
            line = self.line
            for index, step in enumerate((1, -1, 2, -2)):
                if index == 0:
                    when = [line == 2, line < 2]
                elif index == 1:
                    when = [line == 1, line > 1]
                else:
                    when = [(line + step >= 0) & (line + step < 4), None]
                for phase in phases:
                    if when[phase] is not None:

                        @pl.when(when[phase])
                        def _(index=index, step=step):
                            action(index, line + step)

        elif 0 in phases:
            for step in range(1, self.count):
                action(step - 1, (self.line + step) % self.count)

    def start(self):
        self.swap().start()
        self.each_step(lambda index, line: self.own(line, index, self.side).start(), (0,))
        self.keep().start()

    def second(self):
        self.swap().wait_recv()
        self.each_step(lambda index, line: self.own(line, index, 1 - self.side).start(), (0,))

    def middle(self, action):
        if self.count == 4:

            @pl.when((self.line == 1) | (self.line == 2))
            def _():
                action(6 - 3 * self.line, 3 * self.line - 3)

    def onward(self, origin, line, part):
        return self.copy(origin, line, 4, part, self.place(origin, part))

    def forward(self):
        for part in (self.side, 1 - self.side):
            self.each_step(
                lambda index, line, part=part: self.own(line, index, part).start(), (1,)
            )

            def action(origin, line, part=part):
                self.arrival(origin, part).wait_recv()
                self.onward(origin, line, part).start()

            self.middle(action)

    def finish(self):
        for part in (self.side, 1 - self.side):
            self.each_step(
                lambda index, line, part=part: self.own(line, index, part).wait_send()
            )
            self.middle(
                lambda origin, line, part=part: self.onward(origin, line, part).wait_send()
            )
            for origin in range(self.count):
                pending = self.line != origin
                if self.count == 4 and origin == 0:
                    pending = pending & (self.line != 2)
                if self.count == 4 and origin == 3:
                    pending = pending & (self.line != 1)

                @pl.when(pending)
                def _(origin=origin, part=part):
                    self.arrival(origin, part).wait_recv()

        self.keep().wait()
        self.swap().wait_send()


class Stream:
    def __init__(self, source, target, sems, from_row=0, to_row=0, columns=None):
        self.source, self.target, self.sems = source, target, sems
        self.from_row, self.to_row, self.columns = from_row, to_row, columns
        self.pieces = sems.shape[0]

    def copy(self, r):
        source = (pl.ds(r + self.from_row, CHUNK),)
        if self.columns is not None:
            source += (self.columns,)
        return pltpu.make_async_copy(
            self.source.at[source],
            self.target.at[pl.ds(r + self.to_row, CHUNK)],
            self.sems.at[r // CHUNK],
        )

    def start(self, r):
        self.copy(r).start()

    def wait(self, r):
        self.copy(r).wait()

    def start_all(self):
        for k in range(self.pieces):
            self.start(k * CHUNK)

    def wait_all(self):
        for k in range(self.pieces):
            self.wait(k * CHUNK)


class Swap:
    def __init__(self, values, outs, send, receive, local):
        line, side, deck, core = spot()
        self.copies = []
        for k, (value, out) in enumerate(zip(values, outs)):
            self.copies.append(
                remote(
                    value.at[1 - side],
                    out.at[side],
                    send.at[k],
                    receive.at[k],
                    seat(line, 1 - side, deck, core),
                )
            )
            self.copies.append(
                pltpu.make_async_copy(value.at[side], out.at[side], local.at[k])
            )

    @staticmethod
    def scratch(values):
        return [pltpu.SemaphoreType.DMA((len(values),))] * 3 if values else []

    def start(self):
        for copy in self.copies:
            copy.start()

    def finish(self):
        for copy in self.copies:
            copy.wait()


def cargo_peers(count):
    return group_peers() + line_peers(count)


def piece_shape(count, piece):
    if isinstance(piece, tuple):
        return count, 2 * piece[0].shape[0], piece[2]
    return count, 2 * piece.shape[1], piece.shape[2]


def cargo_outs(count, cargo):
    return [(piece_shape(count, piece), BF16, ANY) for piece in cargo]


def cargo_ins(cargo):
    return [(piece[0] if isinstance(piece, tuple) else piece, ANY) for piece in cargo]


def cargo_starts(cargo):
    return [piece[1] if isinstance(piece, tuple) else 0 for piece in cargo]


def cargo_scratch(count, cargo):
    return [sem for _ in cargo for sem in Freight.scratch(count)]


def load(count, starts, halves, targets, sems):
    return [
        Freight(count, half, target, sems[4 * k : 4 * k + 4], starts[k])
        for k, (half, target) in enumerate(zip(halves, targets))
    ]


def flat_rows(values):
    return [value.reshape(-1, value.shape[2]) for value in values]


def call(kernel, outs, ins, scratch, identity, name):
    late = [k for k, (_, space) in enumerate(ins) if space is LATE]
    body = kernel
    if late:
        held = [pltpu.VMEM(ins[k][0].shape, ins[k][0].dtype) for k in late]
        scratch = scratch + held + [pltpu.SemaphoreType.DMA((len(late),))]

        def body(*refs):
            inputs, rest = list(refs[: len(ins)]), refs[len(ins) : -len(late) - 1]
            fetches = []
            for i, (k, buffer) in enumerate(zip(late, refs[-len(late) - 1 : -1])):
                fetches.append(pltpu.make_async_copy(inputs[k], buffer, refs[-1].at[i]))
                inputs[k] = buffer
            for fetch in fetches:
                fetch.start()
            kernel(*inputs, *rest, fetches=fetches)

    results = pl.pallas_call(
        body,
        out_shape=[jax.ShapeDtypeStruct(shape, kind) for shape, kind, _ in outs],
        in_specs=[space for _, space in ins],
        out_specs=[space for _, _, space in outs],
        scratch_shapes=scratch,
        compiler_params=pltpu.CompilerParams(
            collective_id=identity, has_side_effects=True, vmem_limit_bytes=GRANT
        ),
        name=name,
    )(*[value for value, _ in ins])
    return list(results)


class GroupGather:
    def __init__(self, source, target, send, receive, local):
        self.source, self.target = source, target
        self.send, self.receive = send, receive
        self.local = local
        self.here = spot()

    @staticmethod
    def scratch():
        return [
            pltpu.SemaphoreType.DMA((11,)),
            pltpu.SemaphoreType.DMA((11,)),
            pltpu.SemaphoreType.DMA,
        ]

    def half(self, ref, h):
        rows = self.source.shape[0] // 2
        return ref.at[pl.ds(h * rows, rows)]

    def make(self):
        line, side, deck, core = self.here
        sibling, across, above = group_peers()
        mine = rank(side, deck, core)
        beside = rank(1 - side, deck, core)
        over = rank(side, 1 - deck, core)
        corner = rank(1 - side, 1 - deck, core)

        def own(h, peer, index):
            return remote(
                self.half(self.source, h),
                self.half(self.target.at[mine], h),
                self.send.at[index],
                self.receive.at[index],
                peer,
            )

        def relay(block, h, peer, index):
            ref = self.half(self.target.at[block], h)
            return remote(ref, ref, self.send.at[index], self.receive.at[index], peer)

        self.keep = pltpu.make_async_copy(self.source, self.target.at[mine], self.local)
        self.first = [
            own(0, across, 0),
            own(1, above, 1),
            own(0, above, 2),
            own(1, across, 3),
        ]
        self.near = remote(
            self.source, self.target.at[mine], self.send.at[4], self.receive.at[4], sibling
        )
        self.second = [relay(beside, 0, above, 5), relay(over, 1, across, 6)]
        self.last = [
            relay(beside, 0, sibling, 7),
            relay(over, 1, sibling, 8),
            relay(over, 0, sibling, 9),
            relay(beside, 1, sibling, 10),
        ]
        self.corner = corner

    def start(self):
        self.make()
        self.first[1].start()
        self.first[2].start()
        self.near.start()
        self.keep.start()

    def start_across(self):
        self.first[0].start()
        self.first[3].start()

    def landed(self):
        self.near.wait_recv()
        self.keep.wait()

    def landed_relays(self):
        for copy in self.last:
            copy.wait_recv()

    def forward(self):
        for k in range(2):
            self.first[k].wait_recv()
            self.second[k].start()
            self.last[k].start()
        for k in range(2, 4):
            self.first[k].wait_recv()
            self.last[k].start()


def corner_relay(gather, send, receive):
    sibling = group_peers()[0]
    out = []
    for h in range(2):
        ref = gather.half(gather.target.at[gather.corner], h)
        out.append(remote(ref, ref, send.at[h], receive.at[h], sibling))
    return out


def group_finish(gather, send, receive, early=False):
    relays = corner_relay(gather, send, receive)
    for k in range(2):
        gather.second[k].wait_recv()
        relays[k].start()
    if not early:
        gather.landed()
        gather.landed_relays()
    for copy in [gather.near] + gather.first + gather.second + gather.last:
        copy.wait_send()
    for copy in relays:
        copy.wait()


def rows_scratch():
    return GroupGather.scratch() + [
        pltpu.SemaphoreType.DMA((2,)),
        pltpu.SemaphoreType.DMA((2,)),
    ]


def first_kernel(count, starts, *refs):
    loads = len(starts)
    rows, gains = refs[:2]
    halves, refs = refs[2 : 2 + loads], refs[2 + loads :]
    normed, pre, gains_all = refs[:3]
    targets, refs = refs[3 : 3 + loads], refs[3 + loads :]
    own, table, weights, result = refs[:4]
    gain_send, gain_receive, gain_local, out_sems, weight_sems, result_sems = refs[4:10]
    sems = refs[10:]
    dp, tensor = lax.axis_index("dp"), lax.axis_index("tensor")
    gather = GroupGather(own, table, *sems[:3])
    corner_sems = sems[3:5]
    branch, small, *others = load(count, starts, halves, targets, sems[5:])
    shares = 2 * count
    line, side, deck, core = spot()
    greet(
        [((dp + k) % shares, tensor) for k in range(1, shares)]
        + [seat(line, side, deck, 1 - core), seat(line, side, 1 - deck, core)]
    )
    gain_copies = [
        remote(
            gains,
            gains_all.at[dp],
            gain_send.at[k],
            gain_receive.at[k],
            ((dp + k) % shares, tensor),
        )
        for k in range(1, shares)
    ]
    gain_copies.append(pltpu.make_async_copy(gains, gains_all.at[dp], gain_local))
    for copy in gain_copies:
        copy.start()
    branch.start()
    small.start()
    for copy in gain_copies:
        copy.wait()

    block_rows, features = rows.shape
    slim = features // shares
    gain = jnp.concatenate(
        [gains_all[k].astype(F32)[0:1] for k in range(shares)], axis=1
    )

    def norm_rows(i, carry):
        where = pl.ds(pl.multiple_of(i * 32, 32), 32)
        value = rows[where, :].astype(F32)
        mean = jnp.mean(value * value, axis=1, keepdims=True)
        own[where, :] = (value * lax.rsqrt(mean + EPSILON) * gain).astype(BF16)
        return carry

    lax.fori_loop(0, block_rows // 32, norm_rows, 0)
    branch.second()
    small.second()
    gather.start()
    gather.start_across()
    small.forward()
    gather.forward()
    branch.forward()
    for freight in others:
        freight.start()
    for freight in others:
        freight.second()
    small.finish()
    group_finish(gather, *corner_sems)
    copies = [
        pltpu.make_async_copy(
            table.at[g], normed.at[pl.ds(g * block_rows, block_rows)], out_sems.at[g]
        )
        for g in range(8)
    ]
    for copy in copies:
        copy.start()
    branch.finish()
    depth = targets[0].shape[1]
    loading = [
        pltpu.make_async_copy(
            targets[0].at[k], weights.at[pl.ds(k * depth, depth)], weight_sems.at[k]
        )
        for k in range(count)
    ]
    for copy in loading:
        copy.start()
    for freight in others:
        freight.forward()
    for copy in loading:
        copy.wait()
    lanes, width = weights.shape[1] // 2, pre.shape[1] // 2
    shift = 2 * lanes - width
    inside = lax.broadcasted_iota(jnp.int32, (block_rows, width), 1) < lanes

    def write(g):
        where = pl.ds(pl.multiple_of(g * block_rows, block_rows), block_rows)
        return pltpu.make_async_copy(result.at[where], pre.at[where], result_sems.at[g])

    def product(g, carry):
        where = pl.ds(pl.multiple_of(g * block_rows, block_rows), block_rows)
        both = jnp.dot(table[g], weights[...], preferred_element_type=F32)
        result[where, :width] = jnp.where(inside, both[:, :width], 0.0)
        later = pltpu.roll(both[:, shift:], lanes, 1)
        result[where, width:] = jnp.where(inside, later, 0.0)
        write(g).start()
        return carry

    lax.fori_loop(0, 8, product, 0)
    for g in range(8):
        copies[g].wait()
        write(g).wait()
    for freight in others:
        freight.finish()


def first(count, rows, gains, cargo, width):
    total = 8 * rows.shape[0]
    shares = 2 * count
    branch = cargo[0]
    out = call(
        functools.partial(first_kernel, count, cargo_starts(cargo)),
        [
            ((total, rows.shape[1]), BF16, ANY),
            ((total, 2 * width), F32, ANY),
            ((shares,) + gains.shape, BF16, VMEM),
        ]
        + cargo_outs(count, cargo),
        [(rows, VMEM), (gains, VMEM)] + cargo_ins(cargo),
        [
            pltpu.VMEM(rows.shape, BF16),
            pltpu.VMEM((8,) + rows.shape, BF16),
            pltpu.VMEM((rows.shape[1], branch.shape[2]), BF16),
            pltpu.VMEM((total, 2 * width), F32),
            pltpu.SemaphoreType.DMA((shares,)),
            pltpu.SemaphoreType.DMA((shares,)),
            pltpu.SemaphoreType.DMA,
            pltpu.SemaphoreType.DMA((8,)),
            pltpu.SemaphoreType.DMA((count,)),
            pltpu.SemaphoreType.DMA((8,)),
        ]
        + rows_scratch()
        + cargo_scratch(count, cargo),
        0,
        "first",
    )
    return out[:3] + flat_rows(out[3:])


def rows_kernel(count, starts, *refs):
    loads = len(starts)
    rows, halves = refs[0], refs[1 : 1 + loads]
    everything, targets = refs[1 + loads], refs[2 + loads : 2 + 2 * loads]
    sems = refs[2 + 2 * loads :]
    gather = GroupGather(rows, everything, *sems[:3])
    freights = load(count, starts, halves, targets, sems[5:])
    greet(cargo_peers(count))
    for freight in freights:
        freight.start()
    gather.start()
    gather.start_across()
    for freight in freights:
        freight.second()
    for freight in freights:
        freight.forward()
    gather.forward()
    group_finish(gather, *sems[3:5])
    for freight in freights:
        freight.finish()


def gather_rows(count, rows, cargo, identity):
    out = call(
        functools.partial(rows_kernel, count, cargo_starts(cargo)),
        [((8,) + rows.shape, BF16, ANY)] + cargo_outs(count, cargo),
        [(rows, ANY)] + cargo_ins(cargo),
        rows_scratch() + cargo_scratch(count, cargo),
        identity,
        "gather_rows",
    )
    return [out[0].reshape(-1, rows.shape[1])] + flat_rows(out[1:])


def turned(left, right, out, tiles, low, high):
    size = left.shape[1] // tiles

    def body(i, carry):
        place = pl.ds(pl.multiple_of(i * size, size), size)
        total = lax.dot_general(left[:, place], right[...], TN, preferred_element_type=F32)
        out[place, :] = total.astype(BF16)
        return carry

    lax.fori_loop(low, high, body, 0)


def plain_rows_kernel(rows, left, right, everything, product_out, product, *sems, fetches):
    gather = GroupGather(rows, everything, *sems[1:4])
    greet(group_peers())
    gather.start()
    gather.start_across()
    for fetch in fetches:
        fetch.wait()
    turned(left, right, product, 4, 0, 4)
    writing = pltpu.make_async_copy(product, product_out, sems[0])
    writing.start()
    gather.forward()
    group_finish(gather, *sems[4:6])
    writing.wait()


def gather_plain(rows, left, right, identity):
    out = call(
        plain_rows_kernel,
        [((8,) + rows.shape, BF16, ANY), ((left.shape[1], right.shape[1]), BF16, ANY)],
        [(rows, ANY), (left, LATE), (right, LATE)],
        [pltpu.VMEM((left.shape[1], right.shape[1]), BF16), pltpu.SemaphoreType.DMA]
        + rows_scratch(),
        identity,
        "gather_rows",
    )
    return out[0].reshape(-1, rows.shape[1]), out[1]


def flip(value, bit):
    return 1 - value if bit else value


def whole_group():
    line, side, deck, core = spot()
    return [
        seat(line, flip(side, k & 4), flip(deck, k & 2), flip(core, k & 1)) for k in range(1, 8)
    ]


class GainSum:
    def __init__(self, count, gains, totals, near, far, send, receive, far_send, far_receive):
        self.gains, self.totals, self.near, self.far = gains, totals, near, far
        self.first = [
            remote(gains, near.at[k], send.at[k], receive.at[k], peer)
            for k, peer in enumerate(whole_group())
        ]
        self.second_copies = [
            remote(far.at[0], far.at[1 + k], far_send.at[k], far_receive.at[k], peer)
            for k, peer in enumerate(line_peers(count))
        ]

    @staticmethod
    def scratch(count, gains):
        return [
            pltpu.VMEM((7,) + gains.shape, F32),
            pltpu.VMEM((count,) + gains.shape, F32),
            pltpu.SemaphoreType.DMA((7,)),
            pltpu.SemaphoreType.DMA((7,)),
            pltpu.SemaphoreType.DMA((count,)),
            pltpu.SemaphoreType.DMA((count,)),
        ]

    def start(self):
        for copy in self.first:
            copy.start()

    def second(self):
        for copy in self.first:
            copy.wait()
        total = self.gains[...]
        for k in range(7):
            total = total + self.near[k]
        self.far[0] = total
        for copy in self.second_copies:
            copy.start()

    def finish(self):
        for copy in self.second_copies:
            copy.wait()
        total = self.far[0]
        for k in range(len(self.second_copies)):
            total = total + self.far[1 + k]
        self.totals[...] = total


class Fold:
    OWN, ACROSS, ABOVE, CORNER = 0, 1, 2, 3

    def __init__(self, plan, lefts, rights, out, refs, uneven=0):
        self.plan, self.lefts, self.rights, self.out = plan, lefts, rights, out
        self.mine, self.stage, self.near = refs[:3]
        self.across_sum, self.above_sum, self.leaving, self.arriving = refs[3:7]
        send, receive, self.near_send, self.near_receive = refs[7:11]
        self.line, self.side, self.deck, self.core = spot()
        sibling, across, above = group_peers()
        self.sibling = sibling
        self.rows, self.width = out.shape
        self.cut = (self.rows // 2 + uneven, self.rows // 2 - uneven)
        self.ships = [
            remote(
                self.leaving.at[k, pl.ds(0, self.cut[k % 2])],
                self.arriving.at[k, pl.ds(0, self.cut[k % 2])],
                send.at[k],
                receive.at[k],
                peer,
            )
            for k, peer in enumerate((above, across, above, across, across, above))
        ]

    @staticmethod
    def scratch(rows, width, uneven=0):
        half = rows // 2 + uneven
        return [
            pltpu.VMEM((rows, width), F32),
            pltpu.VMEM((2, rows, width), BF16),
            pltpu.VMEM((4, rows, width), BF16),
            pltpu.VMEM((half, width), F32),
            pltpu.VMEM((half, width), F32),
            pltpu.VMEM((6, half, width), BF16),
            pltpu.VMEM((6, half, width), BF16),
            pltpu.SemaphoreType.DMA((6,)),
            pltpu.SemaphoreType.DMA((6,)),
            pltpu.SemaphoreType.DMA((4,)),
            pltpu.SemaphoreType.DMA((4,)),
        ]

    def product(self, which, store):
        base = pl.multiple_of(which * self.rows, self.rows)
        step = 512

        def body(j, carry):
            columns = pl.ds(pl.multiple_of(j * step, step), step)
            total = None
            for (which_left, start), right in zip(self.plan, self.rights):
                part = lax.dot_general(
                    self.lefts[which_left][pl.ds(base, self.rows), start : start + right.shape[1]],
                    right[columns, :],
                    NT,
                    preferred_element_type=F32,
                )
                total = part if total is None else total + part
            store(columns, total)
            return carry

        lax.fori_loop(0, self.width // step, body, 0)

    def sweep(self, part, action):
        def body(i, carry):
            action(pl.multiple_of(i * 16, 16))
            return carry

        lax.fori_loop(0, self.cut[part] // 16, body, 0)

    def near_copy(self, q):
        return remote(
            self.stage.at[q % 2],
            self.near.at[q],
            self.near_send.at[q],
            self.near_receive.at[q],
            self.sibling,
        )

    def chip_sum(self, q, h, r):
        place = pl.ds(h * self.cut[0] + r, 16)
        return self.mine[place, :] + self.near[q, place, :].astype(F32)

    def block(self, q):
        s, d = [
            (self.side, self.deck),
            (1 - self.side, self.deck),
            (self.side, 1 - self.deck),
            (1 - self.side, 1 - self.deck),
        ][q]
        if q < 2:
            self.near_copy(q + 2).wait_send()

        def put_stage(columns, total):
            self.stage[q % 2, :, columns] = total.astype(BF16)

        def put_mine(columns, total):
            target = self.out if q == self.OWN else self.mine
            target[:, columns] = total

        self.product(rank(s, d, 1 - self.core), put_stage)
        self.near_copy(q).start()
        self.product(rank(s, d, self.core), put_mine)
        self.near_copy(q).wait_recv()

    def send(self, k):
        self.ships[k].start()

    def begin(self, freights=()):
        self.block(self.CORNER)

        def depart(k, q, part):
            def action(r):
                self.leaving[k, pl.ds(r, 16), :] = self.chip_sum(q, part, r).astype(BF16)

            self.sweep(part, action)
            self.send(k)

        def stay(sums, q, part):
            def action(r):
                sums[pl.ds(r, 16), :] = self.chip_sum(q, part, r)

            self.sweep(part, action)

        depart(0, self.CORNER, 0)
        depart(1, self.CORNER, 1)
        self.block(self.ABOVE)
        depart(2, self.ABOVE, 0)
        stay(self.above_sum, self.ABOVE, 1)
        for freight in freights:
            freight.second()
        self.block(self.ACROSS)
        depart(3, self.ACROSS, 1)
        stay(self.across_sum, self.ACROSS, 0)
        self.block(self.OWN)

    def middle(self):
        for k, sums in enumerate((self.across_sum, self.above_sum)):
            self.ships[k].wait_recv()

            def action(r, k=k, sums=sums):
                place = pl.ds(r, 16)
                total = sums[place, :] + self.arriving[k, place, :].astype(F32)
                self.leaving[4 + k, place, :] = total.astype(BF16)

            self.sweep(k, action)
            self.send(4 + k)

    def finish(self, store):
        for k in range(2, 6):
            self.ships[k].wait_recv()

        for part in range(2):

            def total(r, part=part):
                place = pl.ds(r, 16)
                here = pl.ds(pl.multiple_of(part * self.cut[0] + r, 16), 16)
                value = self.out[here, :] + self.near[self.OWN, here, :].astype(F32)
                for k in (2 + part, 4 + part):
                    value = value + self.arriving[k, place, :].astype(F32)
                store(here, value)

            self.sweep(part, total)

        for k in range(6):
            self.ships[k].wait_send()
        for q in range(2):
            self.near_copy(q).wait_send()


def unit_rows(value):
    scale = lax.rsqrt(jnp.mean(value * value, axis=1, keepdims=True) + EPSILON)
    return value * scale, scale


def norm_back_rows(grad, unit, scale, gain):
    grad_unit = grad * gain
    inner = jnp.mean(grad_unit * unit, axis=1, keepdims=True)
    return scale * (grad_unit - unit * inner), jnp.sum(grad * unit, axis=0, keepdims=True)


def mixer_fold_kernel(count, jobs, starts, left, right, *refs, fetches):
    loads = len(starts)
    inputs, gain, refs = refs[0], refs[1], refs[2:]
    halves, refs = refs[:loads], refs[loads:]
    out, normed, refs = refs[0], refs[1], refs[2:]
    targets, refs = refs[:loads], refs[loads:]
    fold = Fold(jobs[0], [left], [right], out, refs[:11])
    freights = load(count, starts, halves, targets, refs[11:])
    greet(cargo_peers(count))
    for freight in freights:
        freight.start()
    for fetch in fetches[:2]:
        fetch.wait()
    fold.begin(freights)
    fold.middle()
    for freight in freights:
        freight.forward()

    fetches[2].wait()

    def store(here, value):
        value = value + inputs[here, :].astype(F32)
        out[here, :] = value
        normed[here, :] = (unit_rows(value)[0] * gain[...]).astype(BF16)

    fold.finish(store)
    for freight in freights:
        freight.finish()


def plan_of(lefts_rights):
    lefts, rights, plan = [], [], []
    for k, (left, parts) in enumerate(lefts_rights):
        lefts.append((left, LATE))
        start = 0
        for part in parts:
            rights.append((part, LATE))
            plan.append((k, start))
            start += part.shape[1]
    return plan, lefts + rights


def mixer_fold(count, merged, mixer, inputs, gain, cargo):
    plan, ins = plan_of([(merged, [mixer])])
    rows, width = inputs.shape
    out = call(
        functools.partial(mixer_fold_kernel, count, [plan], cargo_starts(cargo)),
        [((rows, width), F32, VMEM), ((rows, width), BF16, VMEM)] + cargo_outs(count, cargo),
        ins + [(inputs, LATE), (gain, VMEM)] + cargo_ins(cargo),
        Fold.scratch(rows, width) + cargo_scratch(count, cargo),
        3,
        "mixer_fold",
    )
    return out[:2] + flat_rows(out[2:])


def feed_fold_kernel(plan, parts, left, other, *refs, fetches):
    rights, refs = refs[:parts], refs[parts:]
    normed, hidden, cotangent, gain, refs = *refs[:4], refs[4:]
    out, low, gain_sum, grads_out = refs[:4]
    fold = Fold(plan, [left, other], rights, out, refs[4:15])
    grads, write_sem = refs[15:]
    greet(group_peers())
    for fetch in fetches[: 2 + parts]:
        fetch.wait()
    fold.begin()
    fold.middle()
    for fetch in fetches[2 + parts :]:
        fetch.wait()
    turned(normed, left, grads, 4, 0, 4)
    writing = pltpu.make_async_copy(grads, grads_out, write_sem)
    writing.start()
    gain_sum[...] = jnp.zeros_like(gain_sum)

    def store(here, value):
        unit, scale = unit_rows(hidden[here, :])
        back, terms = norm_back_rows(value, unit, scale, gain[...])
        gain_sum[0:1, :] += terms
        back = cotangent[here, :].astype(F32) + back
        out[here, :] = back
        low[here, :] = back.astype(BF16)

    fold.finish(store)
    writing.wait()


def feed_fold(grad_gating, grad_lifting, gates, ups, normed, hidden, cotangent, gain):
    plan, ins = plan_of([(grad_gating, gates), (grad_lifting, ups)])
    rows, width = hidden.shape
    return call(
        functools.partial(feed_fold_kernel, plan, len(gates) + len(ups)),
        [
            ((rows, width), F32, VMEM),
            ((rows, width), BF16, VMEM),
            ((8, width), F32, VMEM),
            ((normed.shape[1], grad_gating.shape[1]), BF16, ANY),
        ],
        ins + [(normed, LATE), (hidden, LATE), (cotangent, LATE), (gain, VMEM)],
        Fold.scratch(rows, width)
        + [
            pltpu.VMEM((normed.shape[1], grad_gating.shape[1]), BF16),
            pltpu.SemaphoreType.DMA,
        ],
        6,
        "feed_fold",
    )


UNEVEN = 16


def last_fold_kernel(count, plans, parts, swaps, left, right, feed_left, *refs, fetches):
    rights, refs = refs[:parts], refs[parts:]
    inputs, gain, grad_hidden, hidden, second, refs = *refs[:5], refs[5:]
    values, refs = refs[:swaps], refs[swaps:]
    input_grad, output, totals = refs[:3]
    swapped, refs = refs[3 : 3 + swaps], refs[3 + swaps :]
    out, feed_out, sums, terms_here, refs = *refs[:4], refs[4:]
    fold = Fold(plans[0], [left], [right], out, refs[:11], UNEVEN)
    feed = Fold(plans[1], [feed_left], rights, feed_out, refs[11:22], UNEVEN)
    swap = Swap(values, swapped, *refs[22:25])
    gain_sum = GainSum(count, sums, totals, *refs[25:])
    greet(whole_group() + line_peers(count))
    swap.start()
    for fetch in fetches[:2]:
        fetch.wait()
    fold.begin()
    fold.middle()
    for fetch in fetches[2:]:
        fetch.wait()
    feed.begin()
    terms_here[...] = jnp.zeros_like(terms_here)

    def store(here, value):
        unit, scale = unit_rows(inputs[here, :].astype(F32))
        back, terms = norm_back_rows(value, unit, scale, gain[...])
        terms_here[0:1, :] += terms
        input_grad[here, :] = (grad_hidden[here, :] + back).astype(BF16)

    fold.finish(store)
    shares, slim = sums.shape[0] // 2, sums.shape[1]
    for k in range(shares):
        columns = slice(k * slim, (k + 1) * slim)
        sums[k : k + 1, :] = terms_here[0:1, columns]
        sums[shares + k : shares + k + 1, :] = second[0:1, columns]
    gain_sum.start()
    feed.middle()
    gain_sum.second()

    def store_output(here, value):
        output[here, :] = (hidden[here, :] + value).astype(BF16)

    feed.finish(store_output)
    gain_sum.finish()
    swap.finish()


def last_fold(count, grads, branch, feed_left, downs, inputs, gain, grad_hidden, hidden, second, swaps):
    plan, ins = plan_of([(grads, [branch])])
    feed_plan, feed_ins = plan_of([(feed_left, downs)])
    rows, width = hidden.shape
    both = jax.ShapeDtypeStruct((4 * count, width // (2 * count)), F32)
    return call(
        functools.partial(last_fold_kernel, count, (plan, feed_plan), len(downs), len(swaps)),
        [
            ((rows, width), BF16, VMEM),
            ((rows, width), BF16, VMEM),
            (both.shape, F32, VMEM),
        ]
        + [(value.shape, BF16, ANY) for value in swaps],
        ins
        + feed_ins
        + [
            (inputs, LATE),
            (gain, VMEM),
            (grad_hidden, LATE),
            (hidden, LATE),
            (second, VMEM),
        ]
        + [(value, ANY) for value in swaps],
        [
            pltpu.VMEM((rows, width), F32),
            pltpu.VMEM((rows, width), F32),
            pltpu.VMEM(both.shape, F32),
            pltpu.VMEM((8, width), F32),
        ]
        + Fold.scratch(rows, width, UNEVEN) * 2
        + Swap.scratch(swaps)
        + GainSum.scratch(count, both),
        9,
        "last_fold",
    )


def gelu_both(value):
    square = value * value
    bend = jnp.tanh(GELU_SCALE * value * (1.0 + GELU_CUBE * square))
    act = 0.5 * value * (1.0 + bend)
    slope = 0.5 * (1.0 + bend) + 0.5 * value * (1.0 - bend * bend) * GELU_SCALE * (
        1.0 + 3.0 * GELU_CUBE * square
    )
    return act, slope


def chunks(rows, action, size=CHUNK):
    def body(i, carry):
        action(pl.multiple_of(i * size, size))
        return carry

    lax.fori_loop(0, rows // size, body, 0)


def spans(low, high, action):
    def body(i, carry):
        action(pl.multiple_of(i * CHUNK, CHUNK))
        return carry

    lax.fori_loop(low, high, body, 0)


def tile_scan(mults, adds, rows, width, backward):
    place = lax.broadcasted_iota(jnp.int32, (8, width), 0)

    def inside(base):
        where = pl.ds(base, 8)
        a, b = mults[where, :], adds[where, :]
        for k in (1, 2, 4):
            if backward:
                away, mask = pltpu.roll(a, 8 - k, 0), place < 8 - k
                back = pltpu.roll(b, 8 - k, 0)
            else:
                away, mask = pltpu.roll(a, k, 0), place >= k
                back = pltpu.roll(b, k, 0)
            b = jnp.where(mask, b + a * back, b)
            a = jnp.where(mask, a * away, a)
        return where, a, b

    unroll = 4
    tiles = rows // 8

    def body(i, carry):
        prod, total = carry
        work = []
        for u in range(unroll):
            index = i * unroll + u
            if backward:
                index = tiles - 1 - index
            work.append(inside(pl.multiple_of(index * 8, 8)))
        for where, a, b in work:
            edge = 0 if backward else 7
            adds[where, :] = b + a * total
            mults[where, :] = a * prod
            whole = jnp.broadcast_to(a[edge : edge + 1, :], (8, width))
            extra = jnp.broadcast_to(b[edge : edge + 1, :], (8, width))
            total = extra + whole * total
            prod = whole * prod
        return prod, total

    return lax.fori_loop(
        0, tiles // unroll, body, (jnp.ones((8, width), F32), jnp.zeros((8, width), F32))
    )


def pool(count, prod, total, outgoing, slots, send, receive, backward):
    line, side, deck, core = spot()
    outgoing[0:8, :] = prod
    outgoing[8:16, :] = total
    slots[line, 0:8, :] = prod
    slots[line, 8:16, :] = total
    copies = []
    for k in range(1, count):
        copy = remote(
            outgoing,
            slots.at[line],
            send.at[k],
            receive.at[k],
            seat((line + k) % count, side, deck, core),
        )
        copy.start()
        copies.append(copy)
    for copy in copies:
        copy.wait()
    entering = jnp.zeros_like(prod)
    order = range(count - 1, -1, -1) if backward else range(count)
    for place in order:
        longer = slots[place, 8:16, :] + slots[place, 0:8, :] * entering
        before = (line < place) if backward else (line > place)
        entering = jnp.where(before, longer, entering)
    return entering


def sigmoid(value):
    return 0.5 + 0.5 * jnp.tanh(0.5 * value)


def gates(recur, soft):
    decay = jnp.exp(-8.0 * recur * soft)
    square = (1.0 + GUARD) - decay * decay
    inverse = lax.rsqrt(square)
    return decay, square * inverse, inverse


def scan_kernel(count, starts, *refs):
    loads = len(starts)
    pre, masks, table, gate_weights, cotangent = refs[:5]
    halves, refs = refs[5 : 5 + loads], refs[5 + loads :]
    everything, targets, refs = refs[6], refs[7 : 7 + loads], refs[:6] + refs[7 + loads :]
    saved, refs = refs[:6], refs[6:]
    gate, entry, conv, recur_out, admit_out, state, merged = refs[:7]
    prods, sums, halo, outgoing, slots, edge_sems, send, receive = refs[7:15]
    in_sems, out_sems, head_sems = refs[15:18]
    sems = refs[18:]
    line, side, deck, core = spot()
    rows, width = conv.shape
    gather = GroupGather(cotangent, everything, *sems[:3])
    freights = load(count, starts, halves, targets, sems[5:])
    gate_reads = Stream(pre, gate, in_sems.at[0], columns=pl.ds(0, width))
    entry_reads = Stream(pre, entry, in_sems.at[1], to_row=8, columns=pl.ds(width, width))
    conv_writes = Stream(conv, saved[0], out_sems.at[0])
    recur_writes = Stream(recur_out, saved[1], out_sems.at[1])
    admit_writes = Stream(admit_out, saved[2], out_sems.at[2])
    state_writes = Stream(state, saved[3], out_sems.at[3], 8, 8)
    merged_writes = Stream(merged, saved[4], out_sems.at[4])
    entry_writes = Stream(entry, saved[5], out_sems.at[5], 8, 8)
    heads = [
        pltpu.make_async_copy(local.at[pl.ds(0, 8)], away.at[pl.ds(0, 8)], head_sems.at[k])
        for k, (local, away) in enumerate([(state, saved[3]), (entry, saved[5])])
    ]
    entry_reads.start_all()
    gate_reads.start_all()
    greet(cargo_peers(count))

    def edge(place):
        return remote(
            pre.at[pl.ds(rows - 8, 8), pl.ds(width, width)],
            halo,
            edge_sems.at[0],
            edge_sems.at[1],
            seat(place, side, deck, core),
        )

    @pl.when(line < count - 1)
    def _():
        edge(line + 1).start()

    for freight in freights:
        freight.start()
    gather.start()

    @pl.when(line > 0)
    def _():
        edge(line - 1).wait_recv()
        entry[0:8, :] = halo[...]

    @pl.when(line == 0)
    def _():
        entry[0:8, :] = jnp.zeros((8, width), F32)

    @pl.when(line < count - 1)
    def _():
        edge(line + 1).wait_send()

    heads[1].start()

    def gate_chunk(r):
        entry_reads.wait(r)
        wide = entry[pl.ds(r, CHUNK + 8), :]
        mask = masks[pl.ds(r, CHUNK), :]
        value = table[0:1, :] * wide[8:, :]
        for k in range(1, TAPS):
            value = (
                value + table[k : k + 1, :] * wide[8 - k : 8 - k + CHUNK, :] * mask[:, k - 1 : k]
            )
        where = pl.ds(r, CHUNK)
        conv[where, :] = value
        both = jnp.dot(value.astype(BF16), gate_weights[...], preferred_element_type=F32)
        recur = sigmoid(both[:, :width])
        admit = sigmoid(both[:, width:])
        recur_out[where, :] = recur
        admit_out[where, :] = admit
        decay, root, _ = gates(recur, table[4:5, :])
        opened = mask[:, 3:4]
        norm = root * opened + (1.0 - opened)
        prods[where, :] = decay * opened
        sums[where, :] = norm * admit * value
        for stream in (entry_writes, conv_writes, recur_writes, admit_writes):
            stream.start(r)

    pieces = rows // CHUNK
    spans(0, 1, gate_chunk)
    for freight in freights:
        freight.second()
    gather.start_across()
    spans(1, pieces, gate_chunk)
    prod, total = tile_scan(prods, sums, rows, width, False)
    entering = pool(count, prod, total, outgoing, slots, send, receive, False)
    for freight in freights:
        freight.forward()
    gather.forward()
    state[0:8, :] = entering
    heads[0].start()

    def state_chunk(r):
        gate_reads.wait(r)
        where = pl.ds(r, CHUNK)
        value = sums[where, :] + prods[where, :] * entering[0:1, :]
        state[pl.ds(r + 8, CHUNK), :] = value
        act, _ = gelu_both(gate[where, :])
        merged[where, :] = (value * act).astype(BF16)
        state_writes.start(r)
        merged_writes.start(r)

    chunks(rows, state_chunk)
    for stream in (
        entry_writes,
        conv_writes,
        recur_writes,
        admit_writes,
        state_writes,
        merged_writes,
    ):
        stream.wait_all()
    for copy in heads:
        copy.wait()
    group_finish(gather, *sems[3:5])
    for freight in freights:
        freight.finish()


def scan_forward(count, pre, masks, table, gate_weights, cotangent, cargo):
    rows, width = pre.shape[0], pre.shape[1] // 2
    pieces = rows // CHUNK
    tall = (rows + 8, width)
    saved = [
        ((rows, width), F32),
        ((rows, width), F32),
        ((rows, width), F32),
        (tall, F32),
        ((rows, width), BF16),
        (tall, F32),
    ]
    out = call(
        functools.partial(scan_kernel, count, cargo_starts(cargo)),
        [(shape, kind, ANY) for shape, kind in saved]
        + [((8,) + cotangent.shape, BF16, ANY)]
        + cargo_outs(count, cargo),
        [(pre, ANY), (masks, VMEM), (table, VMEM), (gate_weights, VMEM), (cotangent, ANY)]
        + cargo_ins(cargo),
        [
            pltpu.VMEM((rows, width), F32),
            pltpu.VMEM(tall, F32),
            pltpu.VMEM((rows, width), F32),
            pltpu.VMEM((rows, width), F32),
            pltpu.VMEM((rows, width), F32),
            pltpu.VMEM(tall, F32),
            pltpu.VMEM((rows, width), BF16),
            pltpu.VMEM((rows, width), F32),
            pltpu.VMEM((rows, width), F32),
            pltpu.VMEM((8, width), F32),
            pltpu.VMEM((16, width), F32),
            pltpu.VMEM((count, 16, width), F32),
            pltpu.SemaphoreType.DMA((2,)),
            pltpu.SemaphoreType.DMA((count,)),
            pltpu.SemaphoreType.DMA((count,)),
            pltpu.SemaphoreType.DMA((2, pieces)),
            pltpu.SemaphoreType.DMA((6, pieces)),
            pltpu.SemaphoreType.DMA((2,)),
        ]
        + rows_scratch()
        + cargo_scratch(count, cargo),
        2,
        "scan_forward",
    )
    return out[:6] + [out[6].reshape(-1, cotangent.shape[1])] + flat_rows(out[7:])


def back_kernel(count, lanes, swaps, *refs, fetches):
    pre, low, outlet = refs[:3]
    saved, refs = refs[3:8], refs[8:]
    masks, table, gate_weights = refs[:3]
    values, refs = refs[3 : 3 + swaps], refs[3 + swaps :]
    grad_pre, grad_gates, grad_table = refs[:3]
    swapped, refs = refs[3 : 3 + swaps], refs[3 + swaps :]
    gate, conv, recur_in, admit_in, state, entry, lows = refs[:7]
    prods, sums, mixes, outgoing, slots, edge_sems, send, receive = refs[7:15]
    in_sems, low_sems, head_sems = refs[15:18]
    line, side, deck, core = spot()
    rows, width = conv.shape
    pieces = rows // CHUNK
    swap = Swap(values, swapped, *refs[18:])
    conv_reads = Stream(saved[0], conv, in_sems.at[0])
    recur_reads = Stream(saved[1], recur_in, in_sems.at[1])
    admit_reads = Stream(saved[2], admit_in, in_sems.at[2])
    state_reads = Stream(saved[3], state, in_sems.at[3], 8, 8)
    entry_reads = Stream(saved[4], entry, in_sems.at[4], 8, 8)
    gate_reads = Stream(pre, gate, in_sems.at[5], columns=pl.ds(0, width))
    heads = [
        pltpu.make_async_copy(away.at[pl.ds(0, 8)], local.at[pl.ds(0, 8)], head_sems.at[k])
        for k, (local, away) in enumerate([(state, saved[3]), (entry, saved[4])])
    ]

    def fetch(i):
        slot = i % 2
        start = pl.multiple_of(i * CHUNK, CHUNK)
        return pltpu.make_async_copy(
            low.at[pl.ds(start, CHUNK)], lows.at[slot], low_sems.at[slot]
        )

    fetch(0).start()
    for k in range(pieces):
        for stream in (gate_reads, recur_reads, state_reads):
            stream.start(k * CHUNK)
    for copy in heads:
        copy.start()
    for stream in (conv_reads, admit_reads, entry_reads):
        stream.start_all()
    greet(line_peers(count) + ([seat(line, 1 - side, deck, core)] if swaps else []))
    swap.start()
    for copy in fetches:
        copy.wait()

    def direct(i, carry):
        r = pl.multiple_of(i * CHUNK, CHUNK)

        @pl.when(i + 1 < pieces)
        def _():
            fetch(i + 1).start()

        fetch(i).wait()
        for stream in (gate_reads, recur_reads, state_reads):
            stream.wait(r)
        where = pl.ds(r, CHUNK)
        grad = jnp.dot(lows[i % 2], outlet[...], preferred_element_type=F32)
        act, slope = gelu_both(gate[where, :])
        gate[where, :] = grad * state[pl.ds(r + 8, CHUNK), :] * slope
        straight = grad * act
        carried = jnp.exp(-8.0 * recur_in[where, :] * table[4:5, :]) * masks[where, 3:4]
        mixes[where, :] = straight
        prods[where, :] = carried
        sums[where, :] = carried * straight
        return carry

    lax.fori_loop(0, pieces, direct, 0)
    prods[rows : rows + 8, :] = jnp.ones((8, width), F32)
    sums[rows : rows + 8, :] = jnp.zeros((8, width), F32)
    prod, total = tile_scan(prods, sums, rows, width, True)
    entering = pool(count, prod, total, outgoing, slots, send, receive, True)
    for copy in heads:
        copy.wait()
    grad_gates[...] = jnp.zeros_like(grad_gates)
    grad_table[...] = jnp.zeros_like(grad_table)

    def fold_rows(value):
        return jnp.sum(value, axis=0, keepdims=True)

    def gate_chunk(r):
        conv_reads.wait(r)
        admit_reads.wait(r)
        where = pl.ds(r, CHUNK)
        wide = pl.ds(r, CHUNK + 8)
        later = sums[wide, :] + prods[wide, :] * entering[0:1, :]
        grad = mixes[where, :] + later[1 : CHUNK + 1, :]
        before = state[wide, :][7 : CHUNK + 7, :]
        soft = table[4:5, :]
        recur, admit, value = recur_in[where, :], admit_in[where, :], conv[where, :]
        decay, root, inverse = gates(recur, soft)
        opened = masks[where, 3:4]
        norm = root * opened + (1.0 - opened)
        flow = grad * admit
        grad_log = opened * (grad * before * decay - flow * value * decay * decay * inverse)
        grad_table[4:5, :] += fold_rows(grad_log * (-8.0 * recur))
        grad_rate = (grad_log * (-8.0 * soft) * recur * (1.0 - recur)).astype(BF16)
        grad_inlet = (flow * norm * value * (1.0 - admit)).astype(BF16)
        both = jnp.concatenate([grad_rate, grad_inlet], axis=1)
        grad_gates[...] += lax.dot_general(
            value.astype(BF16), both, TN, preferred_element_type=F32
        )
        mixes[where, :] = flow * norm + lax.dot_general(
            both, gate_weights[...], NT, preferred_element_type=F32
        )

    gate_chunk(0)

    def edge(place):
        return remote(
            mixes.at[pl.ds(0, 8)],
            mixes.at[pl.ds(rows, 8)],
            edge_sems.at[0],
            edge_sems.at[1],
            seat(place, side, deck, core),
        )

    @pl.when(line > 0)
    def _():
        edge(line - 1).start()

    spans(1, pieces, gate_chunk)

    @pl.when(line < count - 1)
    def _():
        edge(line + 1).wait_recv()

    @pl.when(line == count - 1)
    def _():
        mixes[rows : rows + 8, :] = jnp.zeros((8, width), F32)

    spare = width - lanes
    shift = 2 * lanes - width

    def entry_chunk(r):
        entry_reads.wait(r)
        where, wide = pl.ds(r, CHUNK), pl.ds(r, CHUNK + 8)
        ahead, mask = mixes[wide, :], masks[where, :]
        source = entry[wide, :]
        here = ahead[:CHUNK, :]
        total = table[0:1, :] * here
        grad_table[0:1, :] += fold_rows(here * source[8:, :])
        for k in range(1, TAPS):
            total = total + table[k : k + 1, :] * ahead[k : k + CHUNK, :] * mask[:, 3 + k : 4 + k]
            grad_table[k : k + 1, :] += fold_rows(
                here * source[8 - k : 8 - k + CHUNK, :] * mask[:, k - 1 : k]
            )
        total = pltpu.roll(total, spare, 1)
        first = gate[where, :]
        middle = first[:, shift:] + total[:, : width - shift]
        grad_pre[where, :shift] = first[:, :shift].astype(BF16)
        grad_pre[where, shift:width] = middle.astype(BF16)
        grad_pre[where, width:] = total[:, width - shift :].astype(BF16)

    chunks(rows, entry_chunk)

    @pl.when(line > 0)
    def _():
        edge(line - 1).wait_send()

    swap.finish()


def scan_backward(count, lanes, pre, low, outlet, saved, masks, table, gate_weights, swaps):
    rows, width = pre.shape[0], pre.shape[1] // 2
    pieces = rows // CHUNK
    tall = (rows + 8, width)
    return call(
        functools.partial(back_kernel, count, lanes, len(swaps)),
        [
            ((rows, 2 * lanes), BF16, VMEM),
            ((width, 2 * width), F32, VMEM),
            ((8, width), F32, VMEM),
        ]
        + [(value.shape, BF16, ANY) for value in swaps],
        [(pre, ANY), (low, ANY), (outlet, LATE)]
        + [(value, ANY) for value in saved]
        + [(masks, LATE), (table, VMEM), (gate_weights, LATE)]
        + [(value, ANY) for value in swaps],
        [
            pltpu.VMEM((rows, width), F32),
            pltpu.VMEM((rows, width), F32),
            pltpu.VMEM((rows, width), F32),
            pltpu.VMEM((rows, width), F32),
            pltpu.VMEM(tall, F32),
            pltpu.VMEM(tall, F32),
            pltpu.VMEM((2, CHUNK, low.shape[1]), BF16),
            pltpu.VMEM(tall, F32),
            pltpu.VMEM(tall, F32),
            pltpu.VMEM(tall, F32),
            pltpu.VMEM((16, width), F32),
            pltpu.VMEM((count, 16, width), F32),
            pltpu.SemaphoreType.DMA((2,)),
            pltpu.SemaphoreType.DMA((count,)),
            pltpu.SemaphoreType.DMA((count,)),
            pltpu.SemaphoreType.DMA((6, pieces)),
            pltpu.SemaphoreType.DMA((2,)),
            pltpu.SemaphoreType.DMA((2,)),
        ]
        + Swap.scratch(swaps),
        7,
        "scan_backward",
    )


def feed_kernel(count, early, starts, *refs):
    loads = len(starts)
    normed, cotangent = refs[:2]
    gate_parts, up_parts, down_parts = refs[2:4], refs[4:6], refs[6 : 6 + early]
    refs = refs[6 + early :]
    halves, refs = refs[:loads], refs[loads:]
    results, down_grads = refs[:3], refs[3]
    targets, refs = refs[4 : 4 + loads], refs[4 + loads :]
    table, gate_up, acts, slopes, down, hidden, grad_gating, grad_lifting = refs[:8]
    table_sems, back_sems, write_sems, weight_sems, down_sems = refs[8:13]
    freights = load(count, starts, halves, targets, refs[13:])
    rows, width = hidden.shape
    pieces = rows // CHUNK
    reads = Stream(normed, table, table_sems)
    again = Stream(cotangent, table, back_sems)
    writes = [
        Stream(local, away, write_sems.at[k])
        for k, (local, away) in enumerate(zip((hidden, grad_gating, grad_lifting), results))
    ]
    weights = []
    for which, parts in enumerate((gate_parts, up_parts)):
        start = 0
        for part in parts:
            weights.append(
                pltpu.make_async_copy(
                    part,
                    gate_up.at[which, :, pl.ds(start, part.shape[1])],
                    weight_sems.at[len(weights)],
                )
            )
            start += part.shape[1]
    for copy in weights:
        copy.start()
    reads.start_all()
    greet(cargo_peers(count))
    for freight in freights:
        freight.start()
    for copy in weights:
        copy.wait()

    def forward_chunk(r):
        reads.wait(r)
        where = pl.ds(r, CHUNK)
        gating = jnp.dot(table[where, :], gate_up[0], preferred_element_type=F32)
        lifting = jnp.dot(table[where, :], gate_up[1], preferred_element_type=F32)
        act, slope = gelu_both(gating)
        hidden[where, :] = (act * lifting).astype(BF16)
        acts[where, :] = act
        slopes[where, :] = lifting * slope
        writes[0].start(r)
        again.start(r)

    for freight in freights:
        freight.second()
    spans(0, 3 * pieces // 4, forward_chunk)
    for freight in freights:
        freight.forward()
    spans(3 * pieces // 4, pieces, forward_chunk)
    rows_in = down.shape[0] // count
    copies, start = [], 0
    for k, part in enumerate(down_parts):
        copies.append(
            pltpu.make_async_copy(
                part, down.at[:, pl.ds(start, part.shape[1])], down_sems.at[k]
            )
        )
        start += part.shape[1]
    for k, target in enumerate(targets):
        for place in range(count):
            copies.append(
                pltpu.make_async_copy(
                    target.at[place],
                    down.at[pl.ds(place * rows_in, rows_in), pl.ds(start, target.shape[2])],
                    down_sems.at[early + k * count + place],
                )
            )
        start += target.shape[2]

    def back(low, high):
        def chunk(r):
            where = pl.ds(r, CHUNK)
            columns = slice(low, high)
            grad = jnp.dot(table[where, :], down[:, columns], preferred_element_type=F32)
            grad_gating[where, columns] = (grad * slopes[where, columns]).astype(BF16)
            grad_lifting[where, columns] = (grad * acts[where, columns]).astype(BF16)
            if high == width:
                writes[1].start(r)
                writes[2].start(r)

        chunks(rows, chunk)

    for copy in copies[:early]:
        copy.start()
    again.wait_all()
    for copy in copies[:early]:
        copy.wait()
    turned(table, hidden, down_grads, 4, 0, 4)
    ready = sum(part.shape[1] for part in down_parts)
    back(0, ready)
    for freight in freights:
        freight.finish()
    for copy in copies[early:]:
        copy.start()
    for copy in copies[early:]:
        copy.wait()
    back(ready, width)
    for stream in writes:
        stream.wait_all()


def feed(count, normed, cotangent, gate_parts, up_parts, down_parts, cargo):
    rows = normed.shape[0]
    width = sum(part.shape[1] for part in gate_parts)
    pieces = rows // CHUNK
    out = call(
        functools.partial(feed_kernel, count, len(down_parts), cargo_starts(cargo)),
        [((rows, width), BF16, ANY)] * 3
        + [((normed.shape[1], width), BF16, VMEM)]
        + cargo_outs(count, cargo),
        [(normed, ANY), (cotangent, ANY)]
        + [(part, ANY) for part in list(gate_parts) + list(up_parts) + list(down_parts)]
        + cargo_ins(cargo),
        [
            pltpu.VMEM(normed.shape, BF16),
            pltpu.VMEM((2, normed.shape[1], width), BF16),
            pltpu.VMEM((rows, width), F32),
            pltpu.VMEM((rows, width), F32),
            pltpu.VMEM((normed.shape[1], width), BF16),
            pltpu.VMEM((rows, width), BF16),
            pltpu.VMEM((rows, width), BF16),
            pltpu.VMEM((rows, width), BF16),
            pltpu.SemaphoreType.DMA((pieces,)),
            pltpu.SemaphoreType.DMA((pieces,)),
            pltpu.SemaphoreType.DMA((3, pieces)),
            pltpu.SemaphoreType.DMA((4,)),
            pltpu.SemaphoreType.DMA((len(down_parts) + count * len(cargo),)),
        ]
        + cargo_scratch(count, cargo),
        5,
        "feed",
    )
    return out[:4] + flat_rows(out[4:])


def doc_index(places, doc_starts):
    return jnp.sum((doc_starts[None, :] <= places[:, None]).astype(jnp.int32), axis=1)


def split_columns(value):
    rows, columns = value.shape
    return value.reshape(rows, 2, columns // 2).transpose(1, 0, 2)


def widen(value, width):
    return jnp.pad(value, [(0, 0)] * (value.ndim - 1) + [(0, width - value.shape[-1])])


def by_rows(left, right):
    return lax.dot_general(left, right, TN, preferred_element_type=F32).astype(BF16)


def shards(
    layer_input,
    out_grad,
    doc_starts,
    mixer_gain,
    branch_gate,
    branch_input,
    conv_taps,
    rate_gate,
    input_gate,
    decay_param,
    mixer_out,
    feed_gain,
    feed_gate,
    feed_up,
    feed_down,
):
    shares = lax.axis_size("dp")
    count = shares // 2
    side = lax.axis_index("dp") % 2
    slim, feature_count = mixer_gain.shape[0], layer_input.shape[1]
    heads, piece, head_width = rate_gate.shape
    half_heads = heads // 2
    lanes = half_heads * head_width
    width = -(-lanes // 128) * 128
    row_count = layer_input.shape[0]
    rows = row_count * 8
    line_groups = [[2 * k + s for k in range(count)] for s in range(2)]

    branch_halves = jnp.concatenate(
        [split_columns(branch_gate), split_columns(branch_input)], axis=2
    )
    mixer_halves = widen(split_columns(mixer_out.T), width)
    down_rows = feed_down.T
    narrow = feed_gate.shape[1] // 6
    broad = 2 * narrow

    mine = lax.axis_index("dp")
    blocks = jnp.concatenate([rate_gate, input_gate], axis=2)
    blocks = widen(blocks.reshape(2, half_heads * piece, 2 * head_width), width)
    own = jnp.concatenate([conv_taps, decay_param[None]], axis=0)
    own = jnp.pad(own, ((0, 0), (0, 0), (0, head_width - piece)))
    own = jnp.roll(own, mine * piece, axis=2)
    own = own.reshape(TAPS + 1, 2, lanes).transpose(1, 0, 2)
    gains_own = jnp.pad(jnp.stack([mixer_gain, feed_gain]), ((0, 14), (0, 0)))
    tail = widen(own, width)
    small_top = half_heads * piece
    small_rows = -(-(small_top + TAPS + 1) // 16) * 16
    small = jnp.concatenate([blocks, tail], axis=1)
    small = jnp.pad(small, ((0, 0), (0, small_rows - small.shape[1]), (0, 0)))

    normed_one, pre, gains_all, branch_all, small_all, gate_first = first(
        count, layer_input, gains_own, [branch_halves, small, (feed_gate, 0, narrow)], width
    )

    small_all = small_all.reshape(shares, -1, width)
    tails = small_all[:, small_top : small_top + TAPS + 1].astype(F32)
    gain_first = gains_all[:, 0].reshape(feature_count).astype(F32)
    gain_second = gains_all[:, 1].reshape(feature_count).astype(F32)
    sums = jnp.sum(tails, axis=0)
    decay_flat = sums[TAPS, :lanes]
    inside = (jnp.arange(width) < lanes)[None]
    table = jnp.concatenate(
        [
            sums[:TAPS],
            jnp.where(inside, jax.nn.softplus(-sums[TAPS:]), 0.0),
            jnp.zeros((3, width), F32),
        ]
    )
    blocks = (
        small_all[:, : half_heads * piece, : 2 * head_width]
        .reshape(shares, half_heads, piece, 2 * head_width)
        .transpose(1, 0, 2, 3)
        .reshape(lanes, 2 * head_width)
    )
    head_of = jnp.arange(width) // head_width
    same = (head_of[:lanes, None] == head_of[None, :]) & (jnp.arange(width) < lanes)[None]

    def diagonal(part):
        wide = widen(jnp.concatenate([part] * half_heads, axis=1), width)
        return jnp.where(same, wide, 0)

    gate_weights = jnp.concatenate(
        [diagonal(blocks[:, :head_width]), diagonal(blocks[:, head_width:])], axis=1
    )
    gate_weights = jnp.pad(gate_weights, ((0, width - lanes), (0, 0)))

    anchor = lax.axis_index("dp") // 2 * rows
    places = anchor + jnp.arange(rows, dtype=jnp.int32)
    here = doc_index(places, doc_starts)
    columns = [doc_index(places - k, doc_starts) == here for k in range(1, TAPS)]
    columns.append(~jnp.any(doc_starts[None, :] == places[:, None], axis=1))
    columns += [doc_index(places + k, doc_starts) == here for k in range(1, TAPS)]
    columns.append(columns[0])
    masks = jnp.stack(columns, axis=1).astype(F32)

    conv, recur, admit, state, merged, entry, cot_all, mixer_all, up_first = scan_forward(
        count, pre, masks, table, gate_weights, out_grad, [mixer_halves, (feed_up, 0, narrow)]
    )
    hidden_one, normed_own, gate_second, down_first = mixer_fold(
        count,
        merged,
        mixer_all,
        layer_input,
        gain_second[None],
        [(feed_gate, narrow, broad), (down_rows, 0, narrow)],
    )
    normed_two, up_second = gather_rows(count, normed_own, [(feed_up, narrow, broad)], 4)
    gate_parts, up_parts = [gate_first, gate_second], [up_first, up_second]
    hidden, grad_gating, grad_lifting, down_grads, down_second = feed(
        count,
        normed_two,
        cot_all,
        gate_parts,
        up_parts,
        [down_first],
        [(down_rows, narrow, broad)],
    )
    down_parts = [down_first, down_second]

    def line_sum(value):
        return lax.psum_scatter(
            value, "dp", scatter_dimension=0, axis_index_groups=line_groups, tiled=True
        )

    down_sum = line_sum(down_grads)
    grad_hidden_one, low_own, second_terms, gate_grads = feed_fold(
        grad_gating,
        grad_lifting,
        gate_parts,
        up_parts,
        normed_two,
        hidden_one,
        out_grad,
        gain_second[None],
    )
    low_own, down_sum = lax.optimization_barrier((low_own, down_sum))
    gate_sum = line_sum(gate_grads)
    back_low, up_grads = gather_plain(low_own, normed_two, grad_lifting, 8)
    up_sum = line_sum(up_grads)
    outlet_grads = by_rows(back_low, merged)

    def by_side(value):
        return value.reshape(2, -1, value.shape[1])

    back_low, outlet_grads, gate_sum = lax.optimization_barrier(
        (back_low, outlet_grads, gate_sum)
    )
    grad_pre, grad_gates, grad_table, down_both, gate_both = scan_backward(
        count,
        lanes,
        pre,
        back_low,
        mixer_all,
        [conv, recur, admit, state, entry],
        masks,
        table,
        gate_weights,
        [by_side(down_sum), by_side(gate_sum)],
    )
    branch_grads = by_rows(normed_one, grad_pre)

    def spots(value):
        blocks = [
            value[
                h * head_width : (h + 1) * head_width, h * head_width : (h + 1) * head_width
            ].reshape(shares, -1)
            for h in range(half_heads)
        ]
        return jnp.concatenate(blocks, axis=1)

    grad_decay = -jax.nn.sigmoid(-decay_flat) * grad_table[4, :lanes]
    grad_small = jnp.concatenate(
        [
            spots(grad_gates[:, :width]),
            spots(grad_gates[:, width:]),
            grad_table[:TAPS, :lanes]
            .reshape(TAPS * half_heads, shares, piece)
            .transpose(1, 0, 2)
            .reshape(shares, -1),
            grad_decay.reshape(half_heads, shares, piece).transpose(1, 0, 2).reshape(shares, -1),
        ],
        axis=1,
    )
    flat_size = grad_small.shape[1]
    spare = width - lanes
    grad_small = widen(grad_small, slim * spare).reshape(feature_count, spare).astype(BF16)
    last_grads = jnp.concatenate([outlet_grads[:, :lanes], grad_small, branch_grads], axis=1)
    grad_pre, last_grads = lax.optimization_barrier((grad_pre, last_grads))
    last_sum = line_sum(with_layout_constraint(last_grads, Layout(major_to_minor=(0, 1))))
    last_sum = with_layout_constraint(last_sum, Layout(major_to_minor=(0, 1)))
    input_grad, layer_output, gains, up_both = last_fold(
        count,
        grad_pre,
        branch_all,
        hidden,
        down_parts,
        layer_input,
        gain_first[None],
        grad_hidden_one,
        hidden_one,
        second_terms,
        [by_side(up_sum)],
    )
    first_gain_grad = lax.dynamic_index_in_dim(gains, mine, 0, False)
    second_gain_grad = lax.dynamic_index_in_dim(gains, shares + mine, 0, False)

    def swap(value):
        pair = by_side(value)
        kept = lax.dynamic_index_in_dim(pair, side, 0, False)
        given = lax.dynamic_index_in_dim(pair, 1 - side, 0, False)
        other = lax.ppermute(given, "dp", [(k, k ^ 1) for k in range(shares)])
        return [
            jnp.where(side == 0, kept, other).astype(F32),
            jnp.where(side == 0, other, kept).astype(F32),
        ]

    lasts = swap(last_sum)

    def columns(start, stop):
        return jnp.concatenate([value[:, start:stop] for value in lasts], axis=1)

    mixer_out_grad = columns(0, lanes).T
    branch_gate_grad = columns(width, width + lanes)
    branch_input_grad = columns(width + lanes, width + 2 * lanes)
    smalls = [value[:, lanes:width].reshape(-1)[:flat_size] for value in lasts]
    one = half_heads * piece * head_width
    tap_size = TAPS * half_heads * piece
    rate_grad = jnp.concatenate([v[:one].reshape(half_heads, piece, head_width) for v in smalls])
    inlet_grad = jnp.concatenate(
        [v[one : 2 * one].reshape(half_heads, piece, head_width) for v in smalls]
    )
    taps_grad = jnp.concatenate(
        [v[2 * one : 2 * one + tap_size].reshape(TAPS, half_heads, piece) for v in smalls], axis=1
    )
    decay_grad = jnp.concatenate(
        [v[2 * one + tap_size :].reshape(half_heads, piece) for v in smalls]
    )

    def joined(value):
        return jnp.concatenate([value[0], value[1]], axis=1).astype(F32)

    return (
        layer_output,
        input_grad,
        first_gain_grad,
        branch_gate_grad,
        branch_input_grad,
        taps_grad,
        rate_grad,
        inlet_grad,
        decay_grad,
        mixer_out_grad,
        second_gain_grad,
        joined(gate_both),
        joined(up_both),
        joined(down_both).T,
    )


def solution(mesh):
    placed = (
        P(("dp", "tensor"), None),
        P(("dp", "tensor"), None),
        P(),
        P("dp"),
        P("dp", "tensor"),
        P("dp", "tensor"),
        P(None, "tensor", "dp"),
        P("tensor", "dp", None),
        P("tensor", "dp", None),
        P("tensor", "dp"),
        P("tensor", "dp"),
        P("dp"),
        P("dp", "tensor"),
        P("dp", "tensor"),
        P("tensor", "dp"),
    )
    return jax.shard_map(
        shards,
        mesh=mesh,
        in_specs=placed,
        out_specs=(
            P(("dp", "tensor"), None),
            P(("dp", "tensor"), None),
            P("dp"),
            P("dp", "tensor"),
            P("dp", "tensor"),
            P(None, "tensor", "dp"),
            P("tensor", "dp", None),
            P("tensor", "dp", None),
            P("tensor", "dp"),
            P("tensor", "dp"),
            P("dp"),
            P("dp", "tensor"),
            P("dp", "tensor"),
            P("tensor", "dp"),
        ),
        check_vma=False,
    )
```

```python
import functools

import jax
import jax.numpy as jnp
from jax import lax
from jax.experimental import pallas as pl
from jax.experimental.layout import Layout, with_layout_constraint
from jax.experimental.pallas import tpu as pltpu
from jax.sharding import PartitionSpec as P

TAPS = 4
EPSILON = 1e-06
GUARD = 0.001
GELU_SCALE = 0.7978845608028654
GELU_CUBE = 0.044715
MESH = pl.DeviceIdType.MESH
F32, BF16 = jnp.float32, jnp.bfloat16
ANY = pl.BlockSpec(memory_space=pl.ANY)
VMEM = pl.BlockSpec(memory_space=pltpu.VMEM)
LATE = pl.BlockSpec(memory_space=pl.ANY)
GRANT = 60 * 1024 * 1024
NT = (((1,), (1,)), ((), ()))
TN = (((0,), (0,)), ((), ()))
CHUNK = 512


def spot():
    dp, tensor = lax.axis_index("dp"), lax.axis_index("tensor")
    return dp // 2, dp % 2, tensor // 2, tensor % 2


def seat(line, side, deck, core):
    return (line * 2 + side, deck * 2 + core)


def rank(side, deck, core):
    return side * 4 + deck * 2 + core


def greet(peers):
    barrier = pltpu.get_barrier_semaphore()
    for peer in peers:
        pl.semaphore_signal(barrier, inc=1, device_id=peer, device_id_type=MESH)
    pl.semaphore_wait(barrier, len(peers))


def remote(source, target, send, receive, peer):
    return pltpu.make_async_remote_copy(
        src_ref=source,
        dst_ref=target,
        send_sem=send,
        recv_sem=receive,
        device_id=peer,
        device_id_type=MESH,
    )


def line_peers(count):
    line, side, deck, core = spot()
    return [seat((line + k) % count, side, deck, core) for k in range(1, count)]


def group_peers():
    line, side, deck, core = spot()
    return [
        seat(line, side, deck, 1 - core),
        seat(line, 1 - side, deck, core),
        seat(line, side, 1 - deck, core),
    ]


class Freight:
    def __init__(self, count, halves, target, sems, start=0):
        self.count, self.halves, self.target = count, halves, target
        self.start_column = start
        self.cross, self.local, self.send, self.receive = sems
        self.line, self.side, self.deck, self.core = spot()

    @staticmethod
    def scratch(count):
        steps = 5 if count == 4 else count - 1
        return [
            pltpu.SemaphoreType.DMA((2,)),
            pltpu.SemaphoreType.DMA,
            pltpu.SemaphoreType.DMA((steps, 2)),
            pltpu.SemaphoreType.DMA((count, 2)),
        ]

    def half(self, which):
        if len(self.halves.shape) == 3:
            return self.halves.at[which]
        offset = which * (self.halves.shape[1] // 2) + self.start_column
        return self.halves.at[:, pl.ds(pl.multiple_of(offset, 128), self.target.shape[2])]

    def place(self, origin, part):
        rows = self.target.shape[1] // 2
        return self.target.at[origin, pl.ds(pl.multiple_of(part * rows, rows), rows)]

    def seat(self, line):
        return seat(line, self.side, self.deck, self.core)

    def swap(self):
        return remote(
            self.half(1 - self.side),
            self.place(self.line, self.side),
            self.cross.at[0],
            self.cross.at[1],
            seat(self.line, 1 - self.side, self.deck, self.core),
        )

    def keep(self):
        return pltpu.make_async_copy(
            self.half(self.side), self.place(self.line, self.side), self.local
        )

    def copy(self, origin, line, index, part, source):
        return remote(
            source,
            self.place(origin, part),
            self.send.at[index, part],
            self.receive.at[origin, part],
            self.seat(line),
        )

    def own(self, line, index, part):
        source = self.half(self.side)
        if part is not self.side:
            source = self.place(self.line, part)
        return self.copy(self.line, line, index, part, source)

    def arrival(self, origin, part):
        return self.copy(origin, origin, 0, part, self.half(self.side))

    def each_step(self, action, phases=(0, 1)):
        if self.count == 4:
            line = self.line
            for index, step in enumerate((1, -1, 2, -2)):
                if index == 0:
                    when = [line == 2, line < 2]
                elif index == 1:
                    when = [line == 1, line > 1]
                else:
                    when = [(line + step >= 0) & (line + step < 4), None]
                for phase in phases:
                    if when[phase] is not None:

                        @pl.when(when[phase])
                        def _(index=index, step=step):
                            action(index, line + step)

        elif 0 in phases:
            for step in range(1, self.count):
                action(step - 1, (self.line + step) % self.count)

    def start(self):
        self.swap().start()
        self.each_step(lambda index, line: self.own(line, index, self.side).start(), (0,))
        self.keep().start()

    def second(self):
        self.swap().wait_recv()
        self.each_step(lambda index, line: self.own(line, index, 1 - self.side).start(), (0,))

    def middle(self, action):
        if self.count == 4:

            @pl.when((self.line == 1) | (self.line == 2))
            def _():
                action(6 - 3 * self.line, 3 * self.line - 3)

    def onward(self, origin, line, part):
        return self.copy(origin, line, 4, part, self.place(origin, part))

    def forward(self):
        for part in (self.side, 1 - self.side):
            self.each_step(
                lambda index, line, part=part: self.own(line, index, part).start(), (1,)
            )

            def action(origin, line, part=part):
                self.arrival(origin, part).wait_recv()
                self.onward(origin, line, part).start()

            self.middle(action)

    def finish(self):
        for part in (self.side, 1 - self.side):
            self.each_step(
                lambda index, line, part=part: self.own(line, index, part).wait_send()
            )
            self.middle(
                lambda origin, line, part=part: self.onward(origin, line, part).wait_send()
            )
            for origin in range(self.count):
                pending = self.line != origin
                if self.count == 4 and origin == 0:
                    pending = pending & (self.line != 2)
                if self.count == 4 and origin == 3:
                    pending = pending & (self.line != 1)

                @pl.when(pending)
                def _(origin=origin, part=part):
                    self.arrival(origin, part).wait_recv()

        self.keep().wait()
        self.swap().wait_send()


class Stream:
    def __init__(self, source, target, sems, from_row=0, to_row=0, columns=None):
        self.source, self.target, self.sems = source, target, sems
        self.from_row, self.to_row, self.columns = from_row, to_row, columns
        self.pieces = sems.shape[0]

    def copy(self, r):
        source = (pl.ds(r + self.from_row, CHUNK),)
        if self.columns is not None:
            source += (self.columns,)
        return pltpu.make_async_copy(
            self.source.at[source],
            self.target.at[pl.ds(r + self.to_row, CHUNK)],
            self.sems.at[r // CHUNK],
        )

    def start(self, r):
        self.copy(r).start()

    def wait(self, r):
        self.copy(r).wait()

    def start_all(self):
        for k in range(self.pieces):
            self.start(k * CHUNK)

    def wait_all(self):
        for k in range(self.pieces):
            self.wait(k * CHUNK)


class Swap:
    def __init__(self, values, outs, send, receive, local):
        line, side, deck, core = spot()
        self.copies = []
        for k, (value, out) in enumerate(zip(values, outs)):
            self.copies.append(
                remote(
                    value.at[1 - side],
                    out.at[side],
                    send.at[k],
                    receive.at[k],
                    seat(line, 1 - side, deck, core),
                )
            )
            self.copies.append(
                pltpu.make_async_copy(value.at[side], out.at[side], local.at[k])
            )

    @staticmethod
    def scratch(values):
        return [pltpu.SemaphoreType.DMA((len(values),))] * 3 if values else []

    def start(self):
        for copy in self.copies:
            copy.start()

    def finish(self):
        for copy in self.copies:
            copy.wait()


def cargo_peers(count):
    return group_peers() + line_peers(count)


def piece_shape(count, piece):
    if isinstance(piece, tuple):
        return count, 2 * piece[0].shape[0], piece[2]
    return count, 2 * piece.shape[1], piece.shape[2]


def cargo_outs(count, cargo):
    return [(piece_shape(count, piece), BF16, ANY) for piece in cargo]


def cargo_ins(cargo):
    return [(piece[0] if isinstance(piece, tuple) else piece, ANY) for piece in cargo]


def cargo_starts(cargo):
    return [piece[1] if isinstance(piece, tuple) else 0 for piece in cargo]


def cargo_scratch(count, cargo):
    return [sem for _ in cargo for sem in Freight.scratch(count)]


def load(count, starts, halves, targets, sems):
    return [
        Freight(count, half, target, sems[4 * k : 4 * k + 4], starts[k])
        for k, (half, target) in enumerate(zip(halves, targets))
    ]


def flat_rows(values):
    return [value.reshape(-1, value.shape[2]) for value in values]


def call(kernel, outs, ins, scratch, identity, name):
    late = [k for k, (_, space) in enumerate(ins) if space is LATE]
    body = kernel
    if late:
        held = [pltpu.VMEM(ins[k][0].shape, ins[k][0].dtype) for k in late]
        scratch = scratch + held + [pltpu.SemaphoreType.DMA((len(late),))]

        def body(*refs):
            inputs, rest = list(refs[: len(ins)]), refs[len(ins) : -len(late) - 1]
            fetches = []
            for i, (k, buffer) in enumerate(zip(late, refs[-len(late) - 1 : -1])):
                fetches.append(pltpu.make_async_copy(inputs[k], buffer, refs[-1].at[i]))
                inputs[k] = buffer
            for fetch in fetches:
                fetch.start()
            kernel(*inputs, *rest, fetches=fetches)

    results = pl.pallas_call(
        body,
        out_shape=[jax.ShapeDtypeStruct(shape, kind) for shape, kind, _ in outs],
        in_specs=[space for _, space in ins],
        out_specs=[space for _, _, space in outs],
        scratch_shapes=scratch,
        compiler_params=pltpu.CompilerParams(
            collective_id=identity, has_side_effects=True, vmem_limit_bytes=GRANT
        ),
        name=name,
    )(*[value for value, _ in ins])
    return list(results)


class GroupGather:
    def __init__(self, source, target, send, receive, local):
        self.source, self.target = source, target
        self.send, self.receive = send, receive
        self.local = local
        self.here = spot()

    @staticmethod
    def scratch():
        return [
            pltpu.SemaphoreType.DMA((11,)),
            pltpu.SemaphoreType.DMA((11,)),
            pltpu.SemaphoreType.DMA,
        ]

    def half(self, ref, h):
        rows = self.source.shape[0] // 2
        return ref.at[pl.ds(h * rows, rows)]

    def make(self):
        line, side, deck, core = self.here
        sibling, across, above = group_peers()
        mine = rank(side, deck, core)
        beside = rank(1 - side, deck, core)
        over = rank(side, 1 - deck, core)
        corner = rank(1 - side, 1 - deck, core)

        def own(h, peer, index):
            return remote(
                self.half(self.source, h),
                self.half(self.target.at[mine], h),
                self.send.at[index],
                self.receive.at[index],
                peer,
            )

        def relay(block, h, peer, index):
            ref = self.half(self.target.at[block], h)
            return remote(ref, ref, self.send.at[index], self.receive.at[index], peer)

        self.keep = pltpu.make_async_copy(self.source, self.target.at[mine], self.local)
        self.first = [
            own(0, across, 0),
            own(1, above, 1),
            own(0, above, 2),
            own(1, across, 3),
        ]
        self.near = remote(
            self.source, self.target.at[mine], self.send.at[4], self.receive.at[4], sibling
        )
        self.second = [relay(beside, 0, above, 5), relay(over, 1, across, 6)]
        self.last = [
            relay(beside, 0, sibling, 7),
            relay(over, 1, sibling, 8),
            relay(over, 0, sibling, 9),
            relay(beside, 1, sibling, 10),
        ]
        self.corner = corner

    def start(self):
        self.make()
        self.first[1].start()
        self.first[2].start()
        self.near.start()
        self.keep.start()

    def start_across(self):
        self.first[0].start()
        self.first[3].start()

    def landed(self):
        self.near.wait_recv()
        self.keep.wait()

    def landed_relays(self):
        for copy in self.last:
            copy.wait_recv()

    def forward(self):
        for k in range(2):
            self.first[k].wait_recv()
            self.second[k].start()
            self.last[k].start()
        for k in range(2, 4):
            self.first[k].wait_recv()
            self.last[k].start()


def corner_relay(gather, send, receive):
    sibling = group_peers()[0]
    out = []
    for h in range(2):
        ref = gather.half(gather.target.at[gather.corner], h)
        out.append(remote(ref, ref, send.at[h], receive.at[h], sibling))
    return out


def group_finish(gather, send, receive, early=False):
    relays = corner_relay(gather, send, receive)
    for k in range(2):
        gather.second[k].wait_recv()
        relays[k].start()
    if not early:
        gather.landed()
        gather.landed_relays()
    for copy in [gather.near] + gather.first + gather.second + gather.last:
        copy.wait_send()
    for copy in relays:
        copy.wait()


def rows_scratch():
    return GroupGather.scratch() + [
        pltpu.SemaphoreType.DMA((2,)),
        pltpu.SemaphoreType.DMA((2,)),
    ]


def first_kernel(count, starts, *refs):
    loads = len(starts)
    rows, gains = refs[:2]
    halves, refs = refs[2 : 2 + loads], refs[2 + loads :]
    normed, pre, gains_all = refs[:3]
    targets, refs = refs[3 : 3 + loads], refs[3 + loads :]
    own, table, weights, result = refs[:4]
    gain_send, gain_receive, gain_local, out_sems, weight_sems, result_sems = refs[4:10]
    sems = refs[10:]
    dp, tensor = lax.axis_index("dp"), lax.axis_index("tensor")
    gather = GroupGather(own, table, *sems[:3])
    corner_sems = sems[3:5]
    branch, small, *others = load(count, starts, halves, targets, sems[5:])
    shares = 2 * count
    line, side, deck, core = spot()
    greet(
        [((dp + k) % shares, tensor) for k in range(1, shares)]
        + [seat(line, side, deck, 1 - core), seat(line, side, 1 - deck, core)]
    )
    gain_copies = [
        remote(
            gains,
            gains_all.at[dp],
            gain_send.at[k],
            gain_receive.at[k],
            ((dp + k) % shares, tensor),
        )
        for k in range(1, shares)
    ]
    gain_copies.append(pltpu.make_async_copy(gains, gains_all.at[dp], gain_local))
    for copy in gain_copies:
        copy.start()
    branch.start()
    small.start()
    for copy in gain_copies:
        copy.wait()

    block_rows, features = rows.shape
    slim = features // shares
    gain = jnp.concatenate(
        [gains_all[k].astype(F32)[0:1] for k in range(shares)], axis=1
    )

    def norm_rows(i, carry):
        where = pl.ds(pl.multiple_of(i * 32, 32), 32)
        value = rows[where, :].astype(F32)
        mean = jnp.mean(value * value, axis=1, keepdims=True)
        own[where, :] = (value * lax.rsqrt(mean + EPSILON) * gain).astype(BF16)
        return carry

    lax.fori_loop(0, block_rows // 32, norm_rows, 0)
    branch.second()
    small.second()
    gather.start()
    gather.start_across()
    small.forward()
    gather.forward()
    branch.forward()
    for freight in others:
        freight.start()
    for freight in others:
        freight.second()
    small.finish()
    group_finish(gather, *corner_sems)
    copies = [
        pltpu.make_async_copy(
            table.at[g], normed.at[pl.ds(g * block_rows, block_rows)], out_sems.at[g]
        )
        for g in range(8)
    ]
    for copy in copies:
        copy.start()
    branch.finish()
    depth = targets[0].shape[1]
    loading = [
        pltpu.make_async_copy(
            targets[0].at[k], weights.at[pl.ds(k * depth, depth)], weight_sems.at[k]
        )
        for k in range(count)
    ]
    for copy in loading:
        copy.start()
    for freight in others:
        freight.forward()
    for copy in loading:
        copy.wait()
    lanes, width = weights.shape[1] // 2, pre.shape[1] // 2
    shift = 2 * lanes - width
    inside = lax.broadcasted_iota(jnp.int32, (block_rows, width), 1) < lanes

    def write(g):
        where = pl.ds(pl.multiple_of(g * block_rows, block_rows), block_rows)
        return pltpu.make_async_copy(result.at[where], pre.at[where], result_sems.at[g])

    def product(g, carry):
        where = pl.ds(pl.multiple_of(g * block_rows, block_rows), block_rows)
        both = jnp.dot(table[g], weights[...], preferred_element_type=F32)
        result[where, :width] = jnp.where(inside, both[:, :width], 0.0)
        later = pltpu.roll(both[:, shift:], lanes, 1)
        result[where, width:] = jnp.where(inside, later, 0.0)
        write(g).start()
        return carry

    lax.fori_loop(0, 8, product, 0)
    for g in range(8):
        copies[g].wait()
        write(g).wait()
    for freight in others:
        freight.finish()


def first(count, rows, gains, cargo, width):
    total = 8 * rows.shape[0]
    shares = 2 * count
    branch = cargo[0]
    out = call(
        functools.partial(first_kernel, count, cargo_starts(cargo)),
        [
            ((total, rows.shape[1]), BF16, ANY),
            ((total, 2 * width), F32, ANY),
            ((shares,) + gains.shape, BF16, VMEM),
        ]
        + cargo_outs(count, cargo),
        [(rows, VMEM), (gains, VMEM)] + cargo_ins(cargo),
        [
            pltpu.VMEM(rows.shape, BF16),
            pltpu.VMEM((8,) + rows.shape, BF16),
            pltpu.VMEM((rows.shape[1], branch.shape[2]), BF16),
            pltpu.VMEM((total, 2 * width), F32),
            pltpu.SemaphoreType.DMA((shares,)),
            pltpu.SemaphoreType.DMA((shares,)),
            pltpu.SemaphoreType.DMA,
            pltpu.SemaphoreType.DMA((8,)),
            pltpu.SemaphoreType.DMA((count,)),
            pltpu.SemaphoreType.DMA((8,)),
        ]
        + rows_scratch()
        + cargo_scratch(count, cargo),
        0,
        "first",
    )
    return out[:3] + flat_rows(out[3:])


def rows_kernel(count, starts, *refs):
    loads = len(starts)
    rows, halves = refs[0], refs[1 : 1 + loads]
    everything, targets = refs[1 + loads], refs[2 + loads : 2 + 2 * loads]
    sems = refs[2 + 2 * loads :]
    gather = GroupGather(rows, everything, *sems[:3])
    freights = load(count, starts, halves, targets, sems[5:])
    greet(cargo_peers(count))
    for freight in freights:
        freight.start()
    gather.start()
    gather.start_across()
    for freight in freights:
        freight.second()
    for freight in freights:
        freight.forward()
    gather.forward()
    group_finish(gather, *sems[3:5])
    for freight in freights:
        freight.finish()


def gather_rows(count, rows, cargo, identity):
    out = call(
        functools.partial(rows_kernel, count, cargo_starts(cargo)),
        [((8,) + rows.shape, BF16, ANY)] + cargo_outs(count, cargo),
        [(rows, ANY)] + cargo_ins(cargo),
        rows_scratch() + cargo_scratch(count, cargo),
        identity,
        "gather_rows",
    )
    return [out[0].reshape(-1, rows.shape[1])] + flat_rows(out[1:])


def turned(left, right, out, tiles, low, high):
    size = left.shape[1] // tiles

    def body(i, carry):
        place = pl.ds(pl.multiple_of(i * size, size), size)
        total = lax.dot_general(left[:, place], right[...], TN, preferred_element_type=F32)
        out[place, :] = total.astype(BF16)
        return carry

    lax.fori_loop(low, high, body, 0)


def plain_rows_kernel(rows, left, right, everything, product_out, product, *sems, fetches):
    gather = GroupGather(rows, everything, *sems[1:4])
    greet(group_peers())
    gather.start()
    gather.start_across()
    for fetch in fetches:
        fetch.wait()
    turned(left, right, product, 4, 0, 4)
    writing = pltpu.make_async_copy(product, product_out, sems[0])
    writing.start()
    gather.forward()
    group_finish(gather, *sems[4:6])
    writing.wait()


def gather_plain(rows, left, right, identity):
    out = call(
        plain_rows_kernel,
        [((8,) + rows.shape, BF16, ANY), ((left.shape[1], right.shape[1]), BF16, ANY)],
        [(rows, ANY), (left, LATE), (right, LATE)],
        [pltpu.VMEM((left.shape[1], right.shape[1]), BF16), pltpu.SemaphoreType.DMA]
        + rows_scratch(),
        identity,
        "gather_rows",
    )
    return out[0].reshape(-1, rows.shape[1]), out[1]


def flip(value, bit):
    return 1 - value if bit else value


def whole_group():
    line, side, deck, core = spot()
    return [
        seat(line, flip(side, k & 4), flip(deck, k & 2), flip(core, k & 1)) for k in range(1, 8)
    ]


class GainSum:
    def __init__(self, count, gains, totals, near, far, send, receive, far_send, far_receive):
        self.gains, self.totals, self.near, self.far = gains, totals, near, far
        self.first = [
            remote(gains, near.at[k], send.at[k], receive.at[k], peer)
            for k, peer in enumerate(whole_group())
        ]
        self.second_copies = [
            remote(far.at[0], far.at[1 + k], far_send.at[k], far_receive.at[k], peer)
            for k, peer in enumerate(line_peers(count))
        ]

    @staticmethod
    def scratch(count, gains):
        return [
            pltpu.VMEM((7,) + gains.shape, F32),
            pltpu.VMEM((count,) + gains.shape, F32),
            pltpu.SemaphoreType.DMA((7,)),
            pltpu.SemaphoreType.DMA((7,)),
            pltpu.SemaphoreType.DMA((count,)),
            pltpu.SemaphoreType.DMA((count,)),
        ]

    def start(self):
        for copy in self.first:
            copy.start()

    def second(self):
        for copy in self.first:
            copy.wait()
        total = self.gains[...]
        for k in range(7):
            total = total + self.near[k]
        self.far[0] = total
        for copy in self.second_copies:
            copy.start()

    def finish(self):
        for copy in self.second_copies:
            copy.wait()
        total = self.far[0]
        for k in range(len(self.second_copies)):
            total = total + self.far[1 + k]
        self.totals[...] = total


class Fold:
    OWN, ACROSS, ABOVE, CORNER = 0, 1, 2, 3

    def __init__(self, plan, lefts, rights, out, refs, uneven=0):
        self.plan, self.lefts, self.rights, self.out = plan, lefts, rights, out
        self.mine, self.stage, self.near = refs[:3]
        self.across_sum, self.above_sum, self.leaving, self.arriving = refs[3:7]
        send, receive, self.near_send, self.near_receive = refs[7:11]
        self.line, self.side, self.deck, self.core = spot()
        sibling, across, above = group_peers()
        self.sibling = sibling
        self.rows, self.width = out.shape
        self.cut = (self.rows // 2 + uneven, self.rows // 2 - uneven)
        self.ships = [
            remote(
                self.leaving.at[k, pl.ds(0, self.cut[k % 2])],
                self.arriving.at[k, pl.ds(0, self.cut[k % 2])],
                send.at[k],
                receive.at[k],
                peer,
            )
            for k, peer in enumerate((above, across, above, across, across, above))
        ]

    @staticmethod
    def scratch(rows, width, uneven=0):
        half = rows // 2 + uneven
        return [
            pltpu.VMEM((rows, width), F32),
            pltpu.VMEM((2, rows, width), BF16),
            pltpu.VMEM((4, rows, width), BF16),
            pltpu.VMEM((half, width), F32),
            pltpu.VMEM((half, width), F32),
            pltpu.VMEM((6, half, width), BF16),
            pltpu.VMEM((6, half, width), BF16),
            pltpu.SemaphoreType.DMA((6,)),
            pltpu.SemaphoreType.DMA((6,)),
            pltpu.SemaphoreType.DMA((4,)),
            pltpu.SemaphoreType.DMA((4,)),
        ]

    def product(self, which, store):
        base = pl.multiple_of(which * self.rows, self.rows)
        step = 512

        def body(j, carry):
            columns = pl.ds(pl.multiple_of(j * step, step), step)
            total = None
            for (which_left, start), right in zip(self.plan, self.rights):
                part = lax.dot_general(
                    self.lefts[which_left][pl.ds(base, self.rows), start : start + right.shape[1]],
                    right[columns, :],
                    NT,
                    preferred_element_type=F32,
                )
                total = part if total is None else total + part
            store(columns, total)
            return carry

        lax.fori_loop(0, self.width // step, body, 0)

    def sweep(self, part, action):
        def body(i, carry):
            action(pl.multiple_of(i * 16, 16))
            return carry

        lax.fori_loop(0, self.cut[part] // 16, body, 0)

    def near_copy(self, q):
        return remote(
            self.stage.at[q % 2],
            self.near.at[q],
            self.near_send.at[q],
            self.near_receive.at[q],
            self.sibling,
        )

    def chip_sum(self, q, h, r):
        place = pl.ds(h * self.cut[0] + r, 16)
        return self.mine[place, :] + self.near[q, place, :].astype(F32)

    def block(self, q):
        s, d = [
            (self.side, self.deck),
            (1 - self.side, self.deck),
            (self.side, 1 - self.deck),
            (1 - self.side, 1 - self.deck),
        ][q]
        if q < 2:
            self.near_copy(q + 2).wait_send()

        def put_stage(columns, total):
            self.stage[q % 2, :, columns] = total.astype(BF16)

        def put_mine(columns, total):
            target = self.out if q == self.OWN else self.mine
            target[:, columns] = total

        self.product(rank(s, d, 1 - self.core), put_stage)
        self.near_copy(q).start()
        self.product(rank(s, d, self.core), put_mine)
        self.near_copy(q).wait_recv()

    def send(self, k):
        self.ships[k].start()

    def begin(self, freights=()):
        self.block(self.CORNER)

        def depart(k, q, part):
            def action(r):
                self.leaving[k, pl.ds(r, 16), :] = self.chip_sum(q, part, r).astype(BF16)

            self.sweep(part, action)
            self.send(k)

        def stay(sums, q, part):
            def action(r):
                sums[pl.ds(r, 16), :] = self.chip_sum(q, part, r)

            self.sweep(part, action)

        depart(0, self.CORNER, 0)
        depart(1, self.CORNER, 1)
        self.block(self.ABOVE)
        depart(2, self.ABOVE, 0)
        stay(self.above_sum, self.ABOVE, 1)
        for freight in freights:
            freight.second()
        self.block(self.ACROSS)
        depart(3, self.ACROSS, 1)
        stay(self.across_sum, self.ACROSS, 0)
        self.block(self.OWN)

    def middle(self):
        for k, sums in enumerate((self.across_sum, self.above_sum)):
            self.ships[k].wait_recv()

            def action(r, k=k, sums=sums):
                place = pl.ds(r, 16)
                total = sums[place, :] + self.arriving[k, place, :].astype(F32)
                self.leaving[4 + k, place, :] = total.astype(BF16)

            self.sweep(k, action)
            self.send(4 + k)

    def finish(self, store):
        for k in range(2, 6):
            self.ships[k].wait_recv()

        for part in range(2):

            def total(r, part=part):
                place = pl.ds(r, 16)
                here = pl.ds(pl.multiple_of(part * self.cut[0] + r, 16), 16)
                value = self.out[here, :] + self.near[self.OWN, here, :].astype(F32)
                for k in (2 + part, 4 + part):
                    value = value + self.arriving[k, place, :].astype(F32)
                store(here, value)

            self.sweep(part, total)

        for k in range(6):
            self.ships[k].wait_send()
        for q in range(2):
            self.near_copy(q).wait_send()


def unit_rows(value):
    scale = lax.rsqrt(jnp.mean(value * value, axis=1, keepdims=True) + EPSILON)
    return value * scale, scale


def norm_back_rows(grad, unit, scale, gain):
    grad_unit = grad * gain
    inner = jnp.mean(grad_unit * unit, axis=1, keepdims=True)
    return scale * (grad_unit - unit * inner), jnp.sum(grad * unit, axis=0, keepdims=True)


def mixer_fold_kernel(count, jobs, starts, left, right, *refs, fetches):
    loads = len(starts)
    inputs, gain, refs = refs[0], refs[1], refs[2:]
    halves, refs = refs[:loads], refs[loads:]
    out, normed, refs = refs[0], refs[1], refs[2:]
    targets, refs = refs[:loads], refs[loads:]
    fold = Fold(jobs[0], [left], [right], out, refs[:11])
    freights = load(count, starts, halves, targets, refs[11:])
    greet(cargo_peers(count))
    for freight in freights:
        freight.start()
    for fetch in fetches[:2]:
        fetch.wait()
    fold.begin(freights)
    fold.middle()
    for freight in freights:
        freight.forward()

    fetches[2].wait()

    def store(here, value):
        value = value + inputs[here, :].astype(F32)
        out[here, :] = value
        normed[here, :] = (unit_rows(value)[0] * gain[...]).astype(BF16)

    fold.finish(store)
    for freight in freights:
        freight.finish()


def plan_of(lefts_rights):
    lefts, rights, plan = [], [], []
    for k, (left, parts) in enumerate(lefts_rights):
        lefts.append((left, LATE))
        start = 0
        for part in parts:
            rights.append((part, LATE))
            plan.append((k, start))
            start += part.shape[1]
    return plan, lefts + rights


def mixer_fold(count, merged, mixer, inputs, gain, cargo):
    plan, ins = plan_of([(merged, [mixer])])
    rows, width = inputs.shape
    out = call(
        functools.partial(mixer_fold_kernel, count, [plan], cargo_starts(cargo)),
        [((rows, width), F32, VMEM), ((rows, width), BF16, VMEM)] + cargo_outs(count, cargo),
        ins + [(inputs, LATE), (gain, VMEM)] + cargo_ins(cargo),
        Fold.scratch(rows, width) + cargo_scratch(count, cargo),
        3,
        "mixer_fold",
    )
    return out[:2] + flat_rows(out[2:])


def feed_fold_kernel(plan, parts, left, other, *refs, fetches):
    rights, refs = refs[:parts], refs[parts:]
    normed, hidden, cotangent, gain, refs = *refs[:4], refs[4:]
    out, low, gain_sum, grads_out = refs[:4]
    fold = Fold(plan, [left, other], rights, out, refs[4:15])
    grads, write_sem = refs[15:]
    greet(group_peers())
    for fetch in fetches[: 2 + parts]:
        fetch.wait()
    fold.begin()
    fold.middle()
    for fetch in fetches[2 + parts :]:
        fetch.wait()
    turned(normed, left, grads, 4, 0, 4)
    writing = pltpu.make_async_copy(grads, grads_out, write_sem)
    writing.start()
    gain_sum[...] = jnp.zeros_like(gain_sum)

    def store(here, value):
        unit, scale = unit_rows(hidden[here, :])
        back, terms = norm_back_rows(value, unit, scale, gain[...])
        gain_sum[0:1, :] += terms
        back = cotangent[here, :].astype(F32) + back
        out[here, :] = back
        low[here, :] = back.astype(BF16)

    fold.finish(store)
    writing.wait()


def feed_fold(grad_gating, grad_lifting, gates, ups, normed, hidden, cotangent, gain):
    plan, ins = plan_of([(grad_gating, gates), (grad_lifting, ups)])
    rows, width = hidden.shape
    return call(
        functools.partial(feed_fold_kernel, plan, len(gates) + len(ups)),
        [
            ((rows, width), F32, VMEM),
            ((rows, width), BF16, VMEM),
            ((8, width), F32, VMEM),
            ((normed.shape[1], grad_gating.shape[1]), BF16, ANY),
        ],
        ins + [(normed, LATE), (hidden, LATE), (cotangent, LATE), (gain, VMEM)],
        Fold.scratch(rows, width)
        + [
            pltpu.VMEM((normed.shape[1], grad_gating.shape[1]), BF16),
            pltpu.SemaphoreType.DMA,
        ],
        6,
        "feed_fold",
    )


UNEVEN = 16


def last_fold_kernel(count, plans, parts, swaps, left, right, feed_left, *refs, fetches):
    rights, refs = refs[:parts], refs[parts:]
    inputs, gain, grad_hidden, hidden, second, refs = *refs[:5], refs[5:]
    values, refs = refs[:swaps], refs[swaps:]
    input_grad, output, totals = refs[:3]
    swapped, refs = refs[3 : 3 + swaps], refs[3 + swaps :]
    out, feed_out, sums, terms_here, refs = *refs[:4], refs[4:]
    fold = Fold(plans[0], [left], [right], out, refs[:11], UNEVEN)
    feed = Fold(plans[1], [feed_left], rights, feed_out, refs[11:22], UNEVEN)
    swap = Swap(values, swapped, *refs[22:25])
    gain_sum = GainSum(count, sums, totals, *refs[25:])
    greet(whole_group() + line_peers(count))
    swap.start()
    for fetch in fetches[:2]:
        fetch.wait()
    fold.begin()
    fold.middle()
    for fetch in fetches[2:]:
        fetch.wait()
    feed.begin()
    terms_here[...] = jnp.zeros_like(terms_here)

    def store(here, value):
        unit, scale = unit_rows(inputs[here, :].astype(F32))
        back, terms = norm_back_rows(value, unit, scale, gain[...])
        terms_here[0:1, :] += terms
        input_grad[here, :] = (grad_hidden[here, :] + back).astype(BF16)

    fold.finish(store)
    shares, slim = sums.shape[0] // 2, sums.shape[1]
    for k in range(shares):
        columns = slice(k * slim, (k + 1) * slim)
        sums[k : k + 1, :] = terms_here[0:1, columns]
        sums[shares + k : shares + k + 1, :] = second[0:1, columns]
    gain_sum.start()
    feed.middle()
    gain_sum.second()

    def store_output(here, value):
        output[here, :] = (hidden[here, :] + value).astype(BF16)

    feed.finish(store_output)
    gain_sum.finish()
    swap.finish()


def last_fold(count, grads, branch, feed_left, downs, inputs, gain, grad_hidden, hidden, second, swaps):
    plan, ins = plan_of([(grads, [branch])])
    feed_plan, feed_ins = plan_of([(feed_left, downs)])
    rows, width = hidden.shape
    both = jax.ShapeDtypeStruct((4 * count, width // (2 * count)), F32)
    return call(
        functools.partial(last_fold_kernel, count, (plan, feed_plan), len(downs), len(swaps)),
        [
            ((rows, width), BF16, VMEM),
            ((rows, width), BF16, VMEM),
            (both.shape, F32, VMEM),
        ]
        + [(value.shape, BF16, ANY) for value in swaps],
        ins
        + feed_ins
        + [
            (inputs, LATE),
            (gain, VMEM),
            (grad_hidden, LATE),
            (hidden, LATE),
            (second, VMEM),
        ]
        + [(value, ANY) for value in swaps],
        [
            pltpu.VMEM((rows, width), F32),
            pltpu.VMEM((rows, width), F32),
            pltpu.VMEM(both.shape, F32),
            pltpu.VMEM((8, width), F32),
        ]
        + Fold.scratch(rows, width, UNEVEN) * 2
        + Swap.scratch(swaps)
        + GainSum.scratch(count, both),
        9,
        "last_fold",
    )


def gelu_both(value):
    square = value * value
    bend = jnp.tanh(GELU_SCALE * value * (1.0 + GELU_CUBE * square))
    act = 0.5 * value * (1.0 + bend)
    slope = 0.5 * (1.0 + bend) + 0.5 * value * (1.0 - bend * bend) * GELU_SCALE * (
        1.0 + 3.0 * GELU_CUBE * square
    )
    return act, slope


def chunks(rows, action, size=CHUNK):
    def body(i, carry):
        action(pl.multiple_of(i * size, size))
        return carry

    lax.fori_loop(0, rows // size, body, 0)


def spans(low, high, action):
    def body(i, carry):
        action(pl.multiple_of(i * CHUNK, CHUNK))
        return carry

    lax.fori_loop(low, high, body, 0)


def tile_scan(mults, adds, rows, width, backward):
    place = lax.broadcasted_iota(jnp.int32, (8, width), 0)

    def inside(base):
        where = pl.ds(base, 8)
        a, b = mults[where, :], adds[where, :]
        for k in (1, 2, 4):
            if backward:
                away, mask = pltpu.roll(a, 8 - k, 0), place < 8 - k
                back = pltpu.roll(b, 8 - k, 0)
            else:
                away, mask = pltpu.roll(a, k, 0), place >= k
                back = pltpu.roll(b, k, 0)
            b = jnp.where(mask, b + a * back, b)
            a = jnp.where(mask, a * away, a)
        return where, a, b

    unroll = 4
    tiles = rows // 8

    def body(i, carry):
        prod, total = carry
        work = []
        for u in range(unroll):
            index = i * unroll + u
            if backward:
                index = tiles - 1 - index
            work.append(inside(pl.multiple_of(index * 8, 8)))
        for where, a, b in work:
            edge = 0 if backward else 7
            adds[where, :] = b + a * total
            mults[where, :] = a * prod
            whole = jnp.broadcast_to(a[edge : edge + 1, :], (8, width))
            extra = jnp.broadcast_to(b[edge : edge + 1, :], (8, width))
            total = extra + whole * total
            prod = whole * prod
        return prod, total

    return lax.fori_loop(
        0, tiles // unroll, body, (jnp.ones((8, width), F32), jnp.zeros((8, width), F32))
    )


def pool(count, prod, total, outgoing, slots, send, receive, backward):
    line, side, deck, core = spot()
    outgoing[0:8, :] = prod
    outgoing[8:16, :] = total
    slots[line, 0:8, :] = prod
    slots[line, 8:16, :] = total
    copies = []
    for k in range(1, count):
        copy = remote(
            outgoing,
            slots.at[line],
            send.at[k],
            receive.at[k],
            seat((line + k) % count, side, deck, core),
        )
        copy.start()
        copies.append(copy)
    for copy in copies:
        copy.wait()
    entering = jnp.zeros_like(prod)
    order = range(count - 1, -1, -1) if backward else range(count)
    for place in order:
        longer = slots[place, 8:16, :] + slots[place, 0:8, :] * entering
        before = (line < place) if backward else (line > place)
        entering = jnp.where(before, longer, entering)
    return entering


def sigmoid(value):
    return 0.5 + 0.5 * jnp.tanh(0.5 * value)


def gates(recur, soft):
    decay = jnp.exp(-8.0 * recur * soft)
    square = (1.0 + GUARD) - decay * decay
    inverse = lax.rsqrt(square)
    return decay, square * inverse, inverse


def scan_kernel(count, starts, *refs):
    loads = len(starts)
    pre, masks, table, gate_weights, cotangent = refs[:5]
    halves, refs = refs[5 : 5 + loads], refs[5 + loads :]
    everything, targets, refs = refs[6], refs[7 : 7 + loads], refs[:6] + refs[7 + loads :]
    saved, refs = refs[:6], refs[6:]
    gate, entry, conv, recur_out, admit_out, state, merged = refs[:7]
    prods, sums, halo, outgoing, slots, edge_sems, send, receive = refs[7:15]
    in_sems, out_sems, head_sems = refs[15:18]
    sems = refs[18:]
    line, side, deck, core = spot()
    rows, width = conv.shape
    gather = GroupGather(cotangent, everything, *sems[:3])
    freights = load(count, starts, halves, targets, sems[5:])
    gate_reads = Stream(pre, gate, in_sems.at[0], columns=pl.ds(0, width))
    entry_reads = Stream(pre, entry, in_sems.at[1], to_row=8, columns=pl.ds(width, width))
    conv_writes = Stream(conv, saved[0], out_sems.at[0])
    recur_writes = Stream(recur_out, saved[1], out_sems.at[1])
    admit_writes = Stream(admit_out, saved[2], out_sems.at[2])
    state_writes = Stream(state, saved[3], out_sems.at[3], 8, 8)
    merged_writes = Stream(merged, saved[4], out_sems.at[4])
    entry_writes = Stream(entry, saved[5], out_sems.at[5], 8, 8)
    heads = [
        pltpu.make_async_copy(local.at[pl.ds(0, 8)], away.at[pl.ds(0, 8)], head_sems.at[k])
        for k, (local, away) in enumerate([(state, saved[3]), (entry, saved[5])])
    ]
    entry_reads.start_all()
    gate_reads.start_all()
    greet(cargo_peers(count))

    def edge(place):
        return remote(
            pre.at[pl.ds(rows - 8, 8), pl.ds(width, width)],
            halo,
            edge_sems.at[0],
            edge_sems.at[1],
            seat(place, side, deck, core),
        )

    @pl.when(line < count - 1)
    def _():
        edge(line + 1).start()

    for freight in freights:
        freight.start()
    gather.start()

    @pl.when(line > 0)
    def _():
        edge(line - 1).wait_recv()
        entry[0:8, :] = halo[...]

    @pl.when(line == 0)
    def _():
        entry[0:8, :] = jnp.zeros((8, width), F32)

    @pl.when(line < count - 1)
    def _():
        edge(line + 1).wait_send()

    heads[1].start()

    def gate_chunk(r):
        entry_reads.wait(r)
        wide = entry[pl.ds(r, CHUNK + 8), :]
        mask = masks[pl.ds(r, CHUNK), :]
        value = table[0:1, :] * wide[8:, :]
        for k in range(1, TAPS):
            value = (
                value + table[k : k + 1, :] * wide[8 - k : 8 - k + CHUNK, :] * mask[:, k - 1 : k]
            )
        where = pl.ds(r, CHUNK)
        conv[where, :] = value
        both = jnp.dot(value.astype(BF16), gate_weights[...], preferred_element_type=F32)
        recur = sigmoid(both[:, :width])
        admit = sigmoid(both[:, width:])
        recur_out[where, :] = recur
        admit_out[where, :] = admit
        decay, root, _ = gates(recur, table[4:5, :])
        opened = mask[:, 3:4]
        norm = root * opened + (1.0 - opened)
        prods[where, :] = decay * opened
        sums[where, :] = norm * admit * value
        for stream in (entry_writes, conv_writes, recur_writes, admit_writes):
            stream.start(r)

    pieces = rows // CHUNK
    spans(0, 1, gate_chunk)
    for freight in freights:
        freight.second()
    gather.start_across()
    spans(1, pieces, gate_chunk)
    prod, total = tile_scan(prods, sums, rows, width, False)
    entering = pool(count, prod, total, outgoing, slots, send, receive, False)
    for freight in freights:
        freight.forward()
    gather.forward()
    state[0:8, :] = entering
    heads[0].start()

    def state_chunk(r):
        gate_reads.wait(r)
        where = pl.ds(r, CHUNK)
        value = sums[where, :] + prods[where, :] * entering[0:1, :]
        state[pl.ds(r + 8, CHUNK), :] = value
        act, _ = gelu_both(gate[where, :])
        merged[where, :] = (value * act).astype(BF16)
        state_writes.start(r)
        merged_writes.start(r)

    chunks(rows, state_chunk)
    for stream in (
        entry_writes,
        conv_writes,
        recur_writes,
        admit_writes,
        state_writes,
        merged_writes,
    ):
        stream.wait_all()
    for copy in heads:
        copy.wait()
    group_finish(gather, *sems[3:5])
    for freight in freights:
        freight.finish()


def scan_forward(count, pre, masks, table, gate_weights, cotangent, cargo):
    rows, width = pre.shape[0], pre.shape[1] // 2
    pieces = rows // CHUNK
    tall = (rows + 8, width)
    saved = [
        ((rows, width), F32),
        ((rows, width), F32),
        ((rows, width), F32),
        (tall, F32),
        ((rows, width), BF16),
        (tall, F32),
    ]
    out = call(
        functools.partial(scan_kernel, count, cargo_starts(cargo)),
        [(shape, kind, ANY) for shape, kind in saved]
        + [((8,) + cotangent.shape, BF16, ANY)]
        + cargo_outs(count, cargo),
        [(pre, ANY), (masks, VMEM), (table, VMEM), (gate_weights, VMEM), (cotangent, ANY)]
        + cargo_ins(cargo),
        [
            pltpu.VMEM((rows, width), F32),
            pltpu.VMEM(tall, F32),
            pltpu.VMEM((rows, width), F32),
            pltpu.VMEM((rows, width), F32),
            pltpu.VMEM((rows, width), F32),
            pltpu.VMEM(tall, F32),
            pltpu.VMEM((rows, width), BF16),
            pltpu.VMEM((rows, width), F32),
            pltpu.VMEM((rows, width), F32),
            pltpu.VMEM((8, width), F32),
            pltpu.VMEM((16, width), F32),
            pltpu.VMEM((count, 16, width), F32),
            pltpu.SemaphoreType.DMA((2,)),
            pltpu.SemaphoreType.DMA((count,)),
            pltpu.SemaphoreType.DMA((count,)),
            pltpu.SemaphoreType.DMA((2, pieces)),
            pltpu.SemaphoreType.DMA((6, pieces)),
            pltpu.SemaphoreType.DMA((2,)),
        ]
        + rows_scratch()
        + cargo_scratch(count, cargo),
        2,
        "scan_forward",
    )
    return out[:6] + [out[6].reshape(-1, cotangent.shape[1])] + flat_rows(out[7:])


def back_kernel(count, lanes, swaps, *refs, fetches):
    pre, low, outlet = refs[:3]
    saved, refs = refs[3:8], refs[8:]
    masks, table, gate_weights = refs[:3]
    values, refs = refs[3 : 3 + swaps], refs[3 + swaps :]
    grad_pre, grad_gates, grad_table = refs[:3]
    swapped, refs = refs[3 : 3 + swaps], refs[3 + swaps :]
    gate, conv, recur_in, admit_in, state, entry, lows = refs[:7]
    prods, sums, mixes, outgoing, slots, edge_sems, send, receive = refs[7:15]
    in_sems, low_sems, head_sems = refs[15:18]
    line, side, deck, core = spot()
    rows, width = conv.shape
    pieces = rows // CHUNK
    swap = Swap(values, swapped, *refs[18:])
    conv_reads = Stream(saved[0], conv, in_sems.at[0])
    recur_reads = Stream(saved[1], recur_in, in_sems.at[1])
    admit_reads = Stream(saved[2], admit_in, in_sems.at[2])
    state_reads = Stream(saved[3], state, in_sems.at[3], 8, 8)
    entry_reads = Stream(saved[4], entry, in_sems.at[4], 8, 8)
    gate_reads = Stream(pre, gate, in_sems.at[5], columns=pl.ds(0, width))
    heads = [
        pltpu.make_async_copy(away.at[pl.ds(0, 8)], local.at[pl.ds(0, 8)], head_sems.at[k])
        for k, (local, away) in enumerate([(state, saved[3]), (entry, saved[4])])
    ]

    def fetch(i):
        slot = i % 2
        start = pl.multiple_of(i * CHUNK, CHUNK)
        return pltpu.make_async_copy(
            low.at[pl.ds(start, CHUNK)], lows.at[slot], low_sems.at[slot]
        )

    fetch(0).start()
    for k in range(pieces):
        for stream in (gate_reads, recur_reads, state_reads):
            stream.start(k * CHUNK)
    for copy in heads:
        copy.start()
    for stream in (conv_reads, admit_reads, entry_reads):
        stream.start_all()
    greet(line_peers(count) + ([seat(line, 1 - side, deck, core)] if swaps else []))
    swap.start()
    for copy in fetches:
        copy.wait()

    def direct(i, carry):
        r = pl.multiple_of(i * CHUNK, CHUNK)

        @pl.when(i + 1 < pieces)
        def _():
            fetch(i + 1).start()

        fetch(i).wait()
        for stream in (gate_reads, recur_reads, state_reads):
            stream.wait(r)
        where = pl.ds(r, CHUNK)
        grad = jnp.dot(lows[i % 2], outlet[...], preferred_element_type=F32)
        act, slope = gelu_both(gate[where, :])
        gate[where, :] = grad * state[pl.ds(r + 8, CHUNK), :] * slope
        straight = grad * act
        carried = jnp.exp(-8.0 * recur_in[where, :] * table[4:5, :]) * masks[where, 3:4]
        mixes[where, :] = straight
        prods[where, :] = carried
        sums[where, :] = carried * straight
        return carry

    lax.fori_loop(0, pieces, direct, 0)
    prods[rows : rows + 8, :] = jnp.ones((8, width), F32)
    sums[rows : rows + 8, :] = jnp.zeros((8, width), F32)
    prod, total = tile_scan(prods, sums, rows, width, True)
    entering = pool(count, prod, total, outgoing, slots, send, receive, True)
    for copy in heads:
        copy.wait()
    grad_gates[...] = jnp.zeros_like(grad_gates)
    grad_table[...] = jnp.zeros_like(grad_table)

    def fold_rows(value):
        return jnp.sum(value, axis=0, keepdims=True)

    def gate_chunk(r):
        conv_reads.wait(r)
        admit_reads.wait(r)
        where = pl.ds(r, CHUNK)
        wide = pl.ds(r, CHUNK + 8)
        later = sums[wide, :] + prods[wide, :] * entering[0:1, :]
        grad = mixes[where, :] + later[1 : CHUNK + 1, :]
        before = state[wide, :][7 : CHUNK + 7, :]
        soft = table[4:5, :]
        recur, admit, value = recur_in[where, :], admit_in[where, :], conv[where, :]
        decay, root, inverse = gates(recur, soft)
        opened = masks[where, 3:4]
        norm = root * opened + (1.0 - opened)
        flow = grad * admit
        grad_log = opened * (grad * before * decay - flow * value * decay * decay * inverse)
        grad_table[4:5, :] += fold_rows(grad_log * (-8.0 * recur))
        grad_rate = (grad_log * (-8.0 * soft) * recur * (1.0 - recur)).astype(BF16)
        grad_inlet = (flow * norm * value * (1.0 - admit)).astype(BF16)
        both = jnp.concatenate([grad_rate, grad_inlet], axis=1)
        grad_gates[...] += lax.dot_general(
            value.astype(BF16), both, TN, preferred_element_type=F32
        )
        mixes[where, :] = flow * norm + lax.dot_general(
            both, gate_weights[...], NT, preferred_element_type=F32
        )

    gate_chunk(0)

    def edge(place):
        return remote(
            mixes.at[pl.ds(0, 8)],
            mixes.at[pl.ds(rows, 8)],
            edge_sems.at[0],
            edge_sems.at[1],
            seat(place, side, deck, core),
        )

    @pl.when(line > 0)
    def _():
        edge(line - 1).start()

    spans(1, pieces, gate_chunk)

    @pl.when(line < count - 1)
    def _():
        edge(line + 1).wait_recv()

    @pl.when(line == count - 1)
    def _():
        mixes[rows : rows + 8, :] = jnp.zeros((8, width), F32)

    spare = width - lanes
    shift = 2 * lanes - width

    def entry_chunk(r):
        entry_reads.wait(r)
        where, wide = pl.ds(r, CHUNK), pl.ds(r, CHUNK + 8)
        ahead, mask = mixes[wide, :], masks[where, :]
        source = entry[wide, :]
        here = ahead[:CHUNK, :]
        total = table[0:1, :] * here
        grad_table[0:1, :] += fold_rows(here * source[8:, :])
        for k in range(1, TAPS):
            total = total + table[k : k + 1, :] * ahead[k : k + CHUNK, :] * mask[:, 3 + k : 4 + k]
            grad_table[k : k + 1, :] += fold_rows(
                here * source[8 - k : 8 - k + CHUNK, :] * mask[:, k - 1 : k]
            )
        total = pltpu.roll(total, spare, 1)
        first = gate[where, :]
        middle = first[:, shift:] + total[:, : width - shift]
        grad_pre[where, :shift] = first[:, :shift].astype(BF16)
        grad_pre[where, shift:width] = middle.astype(BF16)
        grad_pre[where, width:] = total[:, width - shift :].astype(BF16)

    chunks(rows, entry_chunk)

    @pl.when(line > 0)
    def _():
        edge(line - 1).wait_send()

    swap.finish()


def scan_backward(count, lanes, pre, low, outlet, saved, masks, table, gate_weights, swaps):
    rows, width = pre.shape[0], pre.shape[1] // 2
    pieces = rows // CHUNK
    tall = (rows + 8, width)
    return call(
        functools.partial(back_kernel, count, lanes, len(swaps)),
        [
            ((rows, 2 * lanes), BF16, VMEM),
            ((width, 2 * width), F32, VMEM),
            ((8, width), F32, VMEM),
        ]
        + [(value.shape, BF16, ANY) for value in swaps],
        [(pre, ANY), (low, ANY), (outlet, LATE)]
        + [(value, ANY) for value in saved]
        + [(masks, LATE), (table, VMEM), (gate_weights, LATE)]
        + [(value, ANY) for value in swaps],
        [
            pltpu.VMEM((rows, width), F32),
            pltpu.VMEM((rows, width), F32),
            pltpu.VMEM((rows, width), F32),
            pltpu.VMEM((rows, width), F32),
            pltpu.VMEM(tall, F32),
            pltpu.VMEM(tall, F32),
            pltpu.VMEM((2, CHUNK, low.shape[1]), BF16),
            pltpu.VMEM(tall, F32),
            pltpu.VMEM(tall, F32),
            pltpu.VMEM(tall, F32),
            pltpu.VMEM((16, width), F32),
            pltpu.VMEM((count, 16, width), F32),
            pltpu.SemaphoreType.DMA((2,)),
            pltpu.SemaphoreType.DMA((count,)),
            pltpu.SemaphoreType.DMA((count,)),
            pltpu.SemaphoreType.DMA((6, pieces)),
            pltpu.SemaphoreType.DMA((2,)),
            pltpu.SemaphoreType.DMA((2,)),
        ]
        + Swap.scratch(swaps),
        7,
        "scan_backward",
    )


def feed_kernel(count, early, starts, *refs):
    loads = len(starts)
    normed, cotangent = refs[:2]
    gate_parts, up_parts, down_parts = refs[2:4], refs[4:6], refs[6 : 6 + early]
    refs = refs[6 + early :]
    halves, refs = refs[:loads], refs[loads:]
    results, down_grads = refs[:3], refs[3]
    targets, refs = refs[4 : 4 + loads], refs[4 + loads :]
    table, gate_up, acts, slopes, down, hidden, grad_gating, grad_lifting = refs[:8]
    table_sems, back_sems, write_sems, weight_sems, down_sems = refs[8:13]
    freights = load(count, starts, halves, targets, refs[13:])
    rows, width = hidden.shape
    pieces = rows // CHUNK
    reads = Stream(normed, table, table_sems)
    again = Stream(cotangent, table, back_sems)
    writes = [
        Stream(local, away, write_sems.at[k])
        for k, (local, away) in enumerate(zip((hidden, grad_gating, grad_lifting), results))
    ]
    weights = []
    for which, parts in enumerate((gate_parts, up_parts)):
        start = 0
        for part in parts:
            weights.append(
                pltpu.make_async_copy(
                    part,
                    gate_up.at[which, :, pl.ds(start, part.shape[1])],
                    weight_sems.at[len(weights)],
                )
            )
            start += part.shape[1]
    for copy in weights:
        copy.start()
    reads.start_all()
    greet(cargo_peers(count))
    for freight in freights:
        freight.start()
    for copy in weights:
        copy.wait()

    def forward_chunk(r):
        reads.wait(r)
        where = pl.ds(r, CHUNK)
        gating = jnp.dot(table[where, :], gate_up[0], preferred_element_type=F32)
        lifting = jnp.dot(table[where, :], gate_up[1], preferred_element_type=F32)
        act, slope = gelu_both(gating)
        hidden[where, :] = (act * lifting).astype(BF16)
        acts[where, :] = act
        slopes[where, :] = lifting * slope
        writes[0].start(r)
        again.start(r)

    for freight in freights:
        freight.second()
    spans(0, 3 * pieces // 4, forward_chunk)
    for freight in freights:
        freight.forward()
    spans(3 * pieces // 4, pieces, forward_chunk)
    rows_in = down.shape[0] // count
    copies, start = [], 0
    for k, part in enumerate(down_parts):
        copies.append(
            pltpu.make_async_copy(
                part, down.at[:, pl.ds(start, part.shape[1])], down_sems.at[k]
            )
        )
        start += part.shape[1]
    for k, target in enumerate(targets):
        for place in range(count):
            copies.append(
                pltpu.make_async_copy(
                    target.at[place],
                    down.at[pl.ds(place * rows_in, rows_in), pl.ds(start, target.shape[2])],
                    down_sems.at[early + k * count + place],
                )
            )
        start += target.shape[2]

    def back(low, high):
        def chunk(r):
            where = pl.ds(r, CHUNK)
            columns = slice(low, high)
            grad = jnp.dot(table[where, :], down[:, columns], preferred_element_type=F32)
            grad_gating[where, columns] = (grad * slopes[where, columns]).astype(BF16)
            grad_lifting[where, columns] = (grad * acts[where, columns]).astype(BF16)
            if high == width:
                writes[1].start(r)
                writes[2].start(r)

        chunks(rows, chunk)

    for copy in copies[:early]:
        copy.start()
    again.wait_all()
    for copy in copies[:early]:
        copy.wait()
    turned(table, hidden, down_grads, 4, 0, 4)
    ready = sum(part.shape[1] for part in down_parts)
    back(0, ready)
    for freight in freights:
        freight.finish()
    for copy in copies[early:]:
        copy.start()
    for copy in copies[early:]:
        copy.wait()
    back(ready, width)
    for stream in writes:
        stream.wait_all()


def feed(count, normed, cotangent, gate_parts, up_parts, down_parts, cargo):
    rows = normed.shape[0]
    width = sum(part.shape[1] for part in gate_parts)
    pieces = rows // CHUNK
    out = call(
        functools.partial(feed_kernel, count, len(down_parts), cargo_starts(cargo)),
        [((rows, width), BF16, ANY)] * 3
        + [((normed.shape[1], width), BF16, VMEM)]
        + cargo_outs(count, cargo),
        [(normed, ANY), (cotangent, ANY)]
        + [(part, ANY) for part in list(gate_parts) + list(up_parts) + list(down_parts)]
        + cargo_ins(cargo),
        [
            pltpu.VMEM(normed.shape, BF16),
            pltpu.VMEM((2, normed.shape[1], width), BF16),
            pltpu.VMEM((rows, width), F32),
            pltpu.VMEM((rows, width), F32),
            pltpu.VMEM((normed.shape[1], width), BF16),
            pltpu.VMEM((rows, width), BF16),
            pltpu.VMEM((rows, width), BF16),
            pltpu.VMEM((rows, width), BF16),
            pltpu.SemaphoreType.DMA((pieces,)),
            pltpu.SemaphoreType.DMA((pieces,)),
            pltpu.SemaphoreType.DMA((3, pieces)),
            pltpu.SemaphoreType.DMA((4,)),
            pltpu.SemaphoreType.DMA((len(down_parts) + count * len(cargo),)),
        ]
        + cargo_scratch(count, cargo),
        5,
        "feed",
    )
    return out[:4] + flat_rows(out[4:])


def doc_index(places, doc_starts):
    return jnp.sum((doc_starts[None, :] <= places[:, None]).astype(jnp.int32), axis=1)


def split_columns(value):
    rows, columns = value.shape
    return value.reshape(rows, 2, columns // 2).transpose(1, 0, 2)


def widen(value, width):
    return jnp.pad(value, [(0, 0)] * (value.ndim - 1) + [(0, width - value.shape[-1])])


def by_rows(left, right):
    return lax.dot_general(left, right, TN, preferred_element_type=F32).astype(BF16)


def shards(
    layer_input,
    out_grad,
    doc_starts,
    mixer_gain,
    branch_gate,
    branch_input,
    conv_taps,
    rate_gate,
    input_gate,
    decay_param,
    mixer_out,
    feed_gain,
    feed_gate,
    feed_up,
    feed_down,
):
    shares = lax.axis_size("dp")
    count = shares // 2
    side = lax.axis_index("dp") % 2
    slim, feature_count = mixer_gain.shape[0], layer_input.shape[1]
    heads, piece, head_width = rate_gate.shape
    half_heads = heads // 2
    lanes = half_heads * head_width
    width = -(-lanes // 128) * 128
    row_count = layer_input.shape[0]
    rows = row_count * 8
    line_groups = [[2 * k + s for k in range(count)] for s in range(2)]

    branch_halves = jnp.concatenate(
        [split_columns(branch_gate), split_columns(branch_input)], axis=2
    )
    mixer_halves = widen(split_columns(mixer_out.T), width)
    down_rows = feed_down.T
    narrow = feed_gate.shape[1] // 6
    broad = 2 * narrow

    mine = lax.axis_index("dp")
    blocks = jnp.concatenate([rate_gate, input_gate], axis=2)
    blocks = widen(blocks.reshape(2, half_heads * piece, 2 * head_width), width)
    own = jnp.concatenate([conv_taps, decay_param[None]], axis=0)
    own = jnp.pad(own, ((0, 0), (0, 0), (0, head_width - piece)))
    own = jnp.roll(own, mine * piece, axis=2)
    own = own.reshape(TAPS + 1, 2, lanes).transpose(1, 0, 2)
    gains_own = jnp.pad(jnp.stack([mixer_gain, feed_gain]), ((0, 14), (0, 0)))
    tail = widen(own, width)
    small_top = half_heads * piece
    small_rows = -(-(small_top + TAPS + 1) // 16) * 16
    small = jnp.concatenate([blocks, tail], axis=1)
    small = jnp.pad(small, ((0, 0), (0, small_rows - small.shape[1]), (0, 0)))

    normed_one, pre, gains_all, branch_all, small_all, gate_first = first(
        count, layer_input, gains_own, [branch_halves, small, (feed_gate, 0, narrow)], width
    )

    small_all = small_all.reshape(shares, -1, width)
    tails = small_all[:, small_top : small_top + TAPS + 1].astype(F32)
    gain_first = gains_all[:, 0].reshape(feature_count).astype(F32)
    gain_second = gains_all[:, 1].reshape(feature_count).astype(F32)
    sums = jnp.sum(tails, axis=0)
    decay_flat = sums[TAPS, :lanes]
    inside = (jnp.arange(width) < lanes)[None]
    table = jnp.concatenate(
        [
            sums[:TAPS],
            jnp.where(inside, jax.nn.softplus(-sums[TAPS:]), 0.0),
            jnp.zeros((3, width), F32),
        ]
    )
    blocks = (
        small_all[:, : half_heads * piece, : 2 * head_width]
        .reshape(shares, half_heads, piece, 2 * head_width)
        .transpose(1, 0, 2, 3)
        .reshape(lanes, 2 * head_width)
    )
    head_of = jnp.arange(width) // head_width
    same = (head_of[:lanes, None] == head_of[None, :]) & (jnp.arange(width) < lanes)[None]

    def diagonal(part):
        wide = widen(jnp.concatenate([part] * half_heads, axis=1), width)
        return jnp.where(same, wide, 0)

    gate_weights = jnp.concatenate(
        [diagonal(blocks[:, :head_width]), diagonal(blocks[:, head_width:])], axis=1
    )
    gate_weights = jnp.pad(gate_weights, ((0, width - lanes), (0, 0)))

    anchor = lax.axis_index("dp") // 2 * rows
    places = anchor + jnp.arange(rows, dtype=jnp.int32)
    here = doc_index(places, doc_starts)
    columns = [doc_index(places - k, doc_starts) == here for k in range(1, TAPS)]
    columns.append(~jnp.any(doc_starts[None, :] == places[:, None], axis=1))
    columns += [doc_index(places + k, doc_starts) == here for k in range(1, TAPS)]
    columns.append(columns[0])
    masks = jnp.stack(columns, axis=1).astype(F32)

    conv, recur, admit, state, merged, entry, cot_all, mixer_all, up_first = scan_forward(
        count, pre, masks, table, gate_weights, out_grad, [mixer_halves, (feed_up, 0, narrow)]
    )
    hidden_one, normed_own, gate_second, down_first = mixer_fold(
        count,
        merged,
        mixer_all,
        layer_input,
        gain_second[None],
        [(feed_gate, narrow, broad), (down_rows, 0, narrow)],
    )
    normed_two, up_second = gather_rows(count, normed_own, [(feed_up, narrow, broad)], 4)
    gate_parts, up_parts = [gate_first, gate_second], [up_first, up_second]
    hidden, grad_gating, grad_lifting, down_grads, down_second = feed(
        count,
        normed_two,
        cot_all,
        gate_parts,
        up_parts,
        [down_first],
        [(down_rows, narrow, broad)],
    )
    down_parts = [down_first, down_second]

    def line_sum(value):
        return lax.psum_scatter(
            value, "dp", scatter_dimension=0, axis_index_groups=line_groups, tiled=True
        )

    down_sum = line_sum(down_grads)
    grad_hidden_one, low_own, second_terms, gate_grads = feed_fold(
        grad_gating,
        grad_lifting,
        gate_parts,
        up_parts,
        normed_two,
        hidden_one,
        out_grad,
        gain_second[None],
    )
    low_own, down_sum = lax.optimization_barrier((low_own, down_sum))
    gate_sum = line_sum(gate_grads)
    back_low, up_grads = gather_plain(low_own, normed_two, grad_lifting, 8)
    up_sum = line_sum(up_grads)
    outlet_grads = by_rows(back_low, merged)

    def by_side(value):
        return value.reshape(2, -1, value.shape[1])

    back_low, outlet_grads, gate_sum = lax.optimization_barrier(
        (back_low, outlet_grads, gate_sum)
    )
    grad_pre, grad_gates, grad_table, down_both, gate_both = scan_backward(
        count,
        lanes,
        pre,
        back_low,
        mixer_all,
        [conv, recur, admit, state, entry],
        masks,
        table,
        gate_weights,
        [by_side(down_sum), by_side(gate_sum)],
    )
    branch_grads = by_rows(normed_one, grad_pre)

    def spots(value):
        blocks = [
            value[
                h * head_width : (h + 1) * head_width, h * head_width : (h + 1) * head_width
            ].reshape(shares, -1)
            for h in range(half_heads)
        ]
        return jnp.concatenate(blocks, axis=1)

    grad_decay = -jax.nn.sigmoid(-decay_flat) * grad_table[4, :lanes]
    grad_small = jnp.concatenate(
        [
            spots(grad_gates[:, :width]),
            spots(grad_gates[:, width:]),
            grad_table[:TAPS, :lanes]
            .reshape(TAPS * half_heads, shares, piece)
            .transpose(1, 0, 2)
            .reshape(shares, -1),
            grad_decay.reshape(half_heads, shares, piece).transpose(1, 0, 2).reshape(shares, -1),
        ],
        axis=1,
    )
    flat_size = grad_small.shape[1]
    spare = width - lanes
    grad_small = widen(grad_small, slim * spare).reshape(feature_count, spare).astype(BF16)
    last_grads = jnp.concatenate([outlet_grads[:, :lanes], grad_small, branch_grads], axis=1)
    grad_pre, last_grads = lax.optimization_barrier((grad_pre, last_grads))
    last_sum = line_sum(with_layout_constraint(last_grads, Layout(major_to_minor=(0, 1))))
    last_sum = with_layout_constraint(last_sum, Layout(major_to_minor=(0, 1)))
    input_grad, layer_output, gains, up_both = last_fold(
        count,
        grad_pre,
        branch_all,
        hidden,
        down_parts,
        layer_input,
        gain_first[None],
        grad_hidden_one,
        hidden_one,
        second_terms,
        [by_side(up_sum)],
    )
    first_gain_grad = lax.dynamic_index_in_dim(gains, mine, 0, False)
    second_gain_grad = lax.dynamic_index_in_dim(gains, shares + mine, 0, False)

    def swap(value):
        pair = by_side(value)
        kept = lax.dynamic_index_in_dim(pair, side, 0, False)
        given = lax.dynamic_index_in_dim(pair, 1 - side, 0, False)
        other = lax.ppermute(given, "dp", [(k, k ^ 1) for k in range(shares)])
        return [
            jnp.where(side == 0, kept, other).astype(F32),
            jnp.where(side == 0, other, kept).astype(F32),
        ]

    lasts, branches = swap(last_sum[:, :width]), swap(last_sum[:, width:])

    def columns(values, start, stop):
        return jnp.concatenate([value[:, start:stop] for value in values], axis=1)

    mixer_out_grad = columns(lasts, 0, lanes).T
    branch_gate_grad = columns(branches, 0, lanes)
    branch_input_grad = columns(branches, lanes, 2 * lanes)
    smalls = [value[:, lanes:width].reshape(-1)[:flat_size] for value in lasts]
    one = half_heads * piece * head_width
    tap_size = TAPS * half_heads * piece
    rate_grad = jnp.concatenate([v[:one].reshape(half_heads, piece, head_width) for v in smalls])
    inlet_grad = jnp.concatenate(
        [v[one : 2 * one].reshape(half_heads, piece, head_width) for v in smalls]
    )
    taps_grad = jnp.concatenate(
        [v[2 * one : 2 * one + tap_size].reshape(TAPS, half_heads, piece) for v in smalls], axis=1
    )
    decay_grad = jnp.concatenate(
        [v[2 * one + tap_size :].reshape(half_heads, piece) for v in smalls]
    )

    def joined(value):
        return jnp.concatenate([value[0], value[1]], axis=1).astype(F32)

    return (
        layer_output,
        input_grad,
        first_gain_grad,
        branch_gate_grad,
        branch_input_grad,
        taps_grad,
        rate_grad,
        inlet_grad,
        decay_grad,
        mixer_out_grad,
        second_gain_grad,
        joined(gate_both),
        joined(up_both),
        joined(down_both).T,
    )


def solution(mesh):
    placed = (
        P(("dp", "tensor"), None),
        P(("dp", "tensor"), None),
        P(),
        P("dp"),
        P("dp", "tensor"),
        P("dp", "tensor"),
        P(None, "tensor", "dp"),
        P("tensor", "dp", None),
        P("tensor", "dp", None),
        P("tensor", "dp"),
        P("tensor", "dp"),
        P("dp"),
        P("dp", "tensor"),
        P("dp", "tensor"),
        P("tensor", "dp"),
    )
    return jax.shard_map(
        shards,
        mesh=mesh,
        in_specs=placed,
        out_specs=(
            P(("dp", "tensor"), None),
            P(("dp", "tensor"), None),
            P("dp"),
            P("dp", "tensor"),
            P("dp", "tensor"),
            P(None, "tensor", "dp"),
            P("tensor", "dp", None),
            P("tensor", "dp", None),
            P("tensor", "dp"),
            P("tensor", "dp"),
            P("dp"),
            P("dp", "tensor"),
            P("dp", "tensor"),
            P("tensor", "dp"),
        ),
        check_vma=False,
    )
```

```python
import functools

import jax
import jax.numpy as jnp
from jax import lax
from jax.experimental import pallas as pl
from jax.experimental.layout import Layout, with_layout_constraint
from jax.experimental.pallas import tpu as pltpu
from jax.sharding import PartitionSpec as P

TAPS = 4
EPSILON = 1e-06
GUARD = 0.001
GELU_SCALE = 0.7978845608028654
GELU_CUBE = 0.044715
MESH = pl.DeviceIdType.MESH
F32, BF16 = jnp.float32, jnp.bfloat16
ANY = pl.BlockSpec(memory_space=pl.ANY)
VMEM = pl.BlockSpec(memory_space=pltpu.VMEM)
LATE = pl.BlockSpec(memory_space=pl.ANY)
GRANT = 60 * 1024 * 1024
NT = (((1,), (1,)), ((), ()))
TN = (((0,), (0,)), ((), ()))
CHUNK = 512


def spot():
    dp, tensor = lax.axis_index("dp"), lax.axis_index("tensor")
    return dp // 2, dp % 2, tensor // 2, tensor % 2


def seat(line, side, deck, core):
    return (line * 2 + side, deck * 2 + core)


def rank(side, deck, core):
    return side * 4 + deck * 2 + core


def greet(peers):
    barrier = pltpu.get_barrier_semaphore()
    for peer in peers:
        pl.semaphore_signal(barrier, inc=1, device_id=peer, device_id_type=MESH)
    pl.semaphore_wait(barrier, len(peers))


def remote(source, target, send, receive, peer):
    return pltpu.make_async_remote_copy(
        src_ref=source,
        dst_ref=target,
        send_sem=send,
        recv_sem=receive,
        device_id=peer,
        device_id_type=MESH,
    )


def line_peers(count):
    line, side, deck, core = spot()
    return [seat((line + k) % count, side, deck, core) for k in range(1, count)]


def group_peers():
    line, side, deck, core = spot()
    return [
        seat(line, side, deck, 1 - core),
        seat(line, 1 - side, deck, core),
        seat(line, side, 1 - deck, core),
    ]


class Freight:
    def __init__(self, count, halves, target, sems, start=0):
        self.count, self.halves, self.target = count, halves, target
        self.start_column = start
        self.cross, self.local, self.send, self.receive = sems
        self.line, self.side, self.deck, self.core = spot()

    @staticmethod
    def scratch(count):
        steps = 5 if count == 4 else count - 1
        return [
            pltpu.SemaphoreType.DMA((2,)),
            pltpu.SemaphoreType.DMA,
            pltpu.SemaphoreType.DMA((steps, 2)),
            pltpu.SemaphoreType.DMA((count, 2)),
        ]

    def half(self, which):
        if len(self.halves.shape) == 3:
            return self.halves.at[which]
        offset = which * (self.halves.shape[1] // 2) + self.start_column
        return self.halves.at[:, pl.ds(pl.multiple_of(offset, 128), self.target.shape[2])]

    def place(self, origin, part):
        rows = self.target.shape[1] // 2
        return self.target.at[origin, pl.ds(pl.multiple_of(part * rows, rows), rows)]

    def seat(self, line):
        return seat(line, self.side, self.deck, self.core)

    def swap(self):
        return remote(
            self.half(1 - self.side),
            self.place(self.line, self.side),
            self.cross.at[0],
            self.cross.at[1],
            seat(self.line, 1 - self.side, self.deck, self.core),
        )

    def keep(self):
        return pltpu.make_async_copy(
            self.half(self.side), self.place(self.line, self.side), self.local
        )

    def copy(self, origin, line, index, part, source):
        return remote(
            source,
            self.place(origin, part),
            self.send.at[index, part],
            self.receive.at[origin, part],
            self.seat(line),
        )

    def own(self, line, index, part):
        source = self.half(self.side)
        if part is not self.side:
            source = self.place(self.line, part)
        return self.copy(self.line, line, index, part, source)

    def arrival(self, origin, part):
        return self.copy(origin, origin, 0, part, self.half(self.side))

    def each_step(self, action, phases=(0, 1)):
        if self.count == 4:
            line = self.line
            for index, step in enumerate((1, -1, 2, -2)):
                if index == 0:
                    when = [line == 2, line < 2]
                elif index == 1:
                    when = [line == 1, line > 1]
                else:
                    when = [(line + step >= 0) & (line + step < 4), None]
                for phase in phases:
                    if when[phase] is not None:

                        @pl.when(when[phase])
                        def _(index=index, step=step):
                            action(index, line + step)

        elif 0 in phases:
            for step in range(1, self.count):
                action(step - 1, (self.line + step) % self.count)

    def start(self):
        self.swap().start()
        self.each_step(lambda index, line: self.own(line, index, self.side).start(), (0,))
        self.keep().start()

    def second(self):
        self.swap().wait_recv()
        self.each_step(lambda index, line: self.own(line, index, 1 - self.side).start(), (0,))

    def middle(self, action):
        if self.count == 4:

            @pl.when((self.line == 1) | (self.line == 2))
            def _():
                action(6 - 3 * self.line, 3 * self.line - 3)

    def onward(self, origin, line, part):
        return self.copy(origin, line, 4, part, self.place(origin, part))

    def forward(self):
        for part in (self.side, 1 - self.side):
            self.each_step(
                lambda index, line, part=part: self.own(line, index, part).start(), (1,)
            )

            def action(origin, line, part=part):
                self.arrival(origin, part).wait_recv()
                self.onward(origin, line, part).start()

            self.middle(action)

    def finish(self):
        for part in (self.side, 1 - self.side):
            self.each_step(
                lambda index, line, part=part: self.own(line, index, part).wait_send()
            )
            self.middle(
                lambda origin, line, part=part: self.onward(origin, line, part).wait_send()
            )
            for origin in range(self.count):
                pending = self.line != origin
                if self.count == 4 and origin == 0:
                    pending = pending & (self.line != 2)
                if self.count == 4 and origin == 3:
                    pending = pending & (self.line != 1)

                @pl.when(pending)
                def _(origin=origin, part=part):
                    self.arrival(origin, part).wait_recv()

        self.keep().wait()
        self.swap().wait_send()


class Stream:
    def __init__(self, source, target, sems, from_row=0, to_row=0, columns=None):
        self.source, self.target, self.sems = source, target, sems
        self.from_row, self.to_row, self.columns = from_row, to_row, columns
        self.pieces = sems.shape[0]

    def copy(self, r):
        source = (pl.ds(r + self.from_row, CHUNK),)
        if self.columns is not None:
            source += (self.columns,)
        return pltpu.make_async_copy(
            self.source.at[source],
            self.target.at[pl.ds(r + self.to_row, CHUNK)],
            self.sems.at[r // CHUNK],
        )

    def start(self, r):
        self.copy(r).start()

    def wait(self, r):
        self.copy(r).wait()

    def start_all(self):
        for k in range(self.pieces):
            self.start(k * CHUNK)

    def wait_all(self):
        for k in range(self.pieces):
            self.wait(k * CHUNK)


class Swap:
    def __init__(self, values, outs, send, receive, local):
        line, side, deck, core = spot()
        self.copies = []
        for k, (value, out) in enumerate(zip(values, outs)):
            self.copies.append(
                remote(
                    value.at[1 - side],
                    out.at[side],
                    send.at[k],
                    receive.at[k],
                    seat(line, 1 - side, deck, core),
                )
            )
            self.copies.append(
                pltpu.make_async_copy(value.at[side], out.at[side], local.at[k])
            )

    @staticmethod
    def scratch(values):
        return [pltpu.SemaphoreType.DMA((len(values),))] * 3 if values else []

    def start(self):
        for copy in self.copies:
            copy.start()

    def finish(self):
        for copy in self.copies:
            copy.wait()


def cargo_peers(count):
    return group_peers() + line_peers(count)


def piece_shape(count, piece):
    if isinstance(piece, tuple):
        return count, 2 * piece[0].shape[0], piece[2]
    return count, 2 * piece.shape[1], piece.shape[2]


def cargo_outs(count, cargo):
    return [(piece_shape(count, piece), BF16, ANY) for piece in cargo]


def cargo_ins(cargo):
    return [(piece[0] if isinstance(piece, tuple) else piece, ANY) for piece in cargo]


def cargo_starts(cargo):
    return [piece[1] if isinstance(piece, tuple) else 0 for piece in cargo]


def cargo_scratch(count, cargo):
    return [sem for _ in cargo for sem in Freight.scratch(count)]


def load(count, starts, halves, targets, sems):
    return [
        Freight(count, half, target, sems[4 * k : 4 * k + 4], starts[k])
        for k, (half, target) in enumerate(zip(halves, targets))
    ]


def flat_rows(values):
    return [value.reshape(-1, value.shape[2]) for value in values]


def call(kernel, outs, ins, scratch, identity, name):
    late = [k for k, (_, space) in enumerate(ins) if space is LATE]
    body = kernel
    if late:
        held = [pltpu.VMEM(ins[k][0].shape, ins[k][0].dtype) for k in late]
        scratch = scratch + held + [pltpu.SemaphoreType.DMA((len(late),))]

        def body(*refs):
            inputs, rest = list(refs[: len(ins)]), refs[len(ins) : -len(late) - 1]
            fetches = []
            for i, (k, buffer) in enumerate(zip(late, refs[-len(late) - 1 : -1])):
                fetches.append(pltpu.make_async_copy(inputs[k], buffer, refs[-1].at[i]))
                inputs[k] = buffer
            for fetch in fetches:
                fetch.start()
            kernel(*inputs, *rest, fetches=fetches)

    results = pl.pallas_call(
        body,
        out_shape=[jax.ShapeDtypeStruct(shape, kind) for shape, kind, _ in outs],
        in_specs=[space for _, space in ins],
        out_specs=[space for _, _, space in outs],
        scratch_shapes=scratch,
        compiler_params=pltpu.CompilerParams(
            collective_id=identity, has_side_effects=True, vmem_limit_bytes=GRANT
        ),
        name=name,
    )(*[value for value, _ in ins])
    return list(results)


class GroupGather:
    def __init__(self, source, target, send, receive, local):
        self.source, self.target = source, target
        self.send, self.receive = send, receive
        self.local = local
        self.here = spot()

    @staticmethod
    def scratch():
        return [
            pltpu.SemaphoreType.DMA((11,)),
            pltpu.SemaphoreType.DMA((11,)),
            pltpu.SemaphoreType.DMA,
        ]

    def half(self, ref, h):
        rows = self.source.shape[0] // 2
        return ref.at[pl.ds(h * rows, rows)]

    def make(self):
        line, side, deck, core = self.here
        sibling, across, above = group_peers()
        mine = rank(side, deck, core)
        beside = rank(1 - side, deck, core)
        over = rank(side, 1 - deck, core)
        corner = rank(1 - side, 1 - deck, core)

        def own(h, peer, index):
            return remote(
                self.half(self.source, h),
                self.half(self.target.at[mine], h),
                self.send.at[index],
                self.receive.at[index],
                peer,
            )

        def relay(block, h, peer, index):
            ref = self.half(self.target.at[block], h)
            return remote(ref, ref, self.send.at[index], self.receive.at[index], peer)

        self.keep = pltpu.make_async_copy(self.source, self.target.at[mine], self.local)
        self.first = [
            own(0, across, 0),
            own(1, above, 1),
            own(0, above, 2),
            own(1, across, 3),
        ]
        self.near = remote(
            self.source, self.target.at[mine], self.send.at[4], self.receive.at[4], sibling
        )
        self.second = [relay(beside, 0, above, 5), relay(over, 1, across, 6)]
        self.last = [
            relay(beside, 0, sibling, 7),
            relay(over, 1, sibling, 8),
            relay(over, 0, sibling, 9),
            relay(beside, 1, sibling, 10),
        ]
        self.corner = corner

    def start(self):
        self.make()
        self.first[1].start()
        self.first[2].start()
        self.near.start()
        self.keep.start()

    def start_across(self):
        self.first[0].start()
        self.first[3].start()

    def landed(self):
        self.near.wait_recv()
        self.keep.wait()

    def landed_relays(self):
        for copy in self.last:
            copy.wait_recv()

    def forward(self):
        for k in range(2):
            self.first[k].wait_recv()
            self.second[k].start()
            self.last[k].start()
        for k in range(2, 4):
            self.first[k].wait_recv()
            self.last[k].start()


def corner_relay(gather, send, receive):
    sibling = group_peers()[0]
    out = []
    for h in range(2):
        ref = gather.half(gather.target.at[gather.corner], h)
        out.append(remote(ref, ref, send.at[h], receive.at[h], sibling))
    return out


def group_finish(gather, send, receive, early=False):
    relays = corner_relay(gather, send, receive)
    for k in range(2):
        gather.second[k].wait_recv()
        relays[k].start()
    if not early:
        gather.landed()
        gather.landed_relays()
    for copy in [gather.near] + gather.first + gather.second + gather.last:
        copy.wait_send()
    for copy in relays:
        copy.wait()


def rows_scratch():
    return GroupGather.scratch() + [
        pltpu.SemaphoreType.DMA((2,)),
        pltpu.SemaphoreType.DMA((2,)),
    ]


def first_kernel(count, starts, *refs):
    loads = len(starts)
    rows, gains = refs[:2]
    halves, refs = refs[2 : 2 + loads], refs[2 + loads :]
    normed, pre, gains_all = refs[:3]
    targets, refs = refs[3 : 3 + loads], refs[3 + loads :]
    own, table, weights, result = refs[:4]
    gain_send, gain_receive, gain_local, out_sems, weight_sems, result_sems = refs[4:10]
    sems = refs[10:]
    dp, tensor = lax.axis_index("dp"), lax.axis_index("tensor")
    gather = GroupGather(own, table, *sems[:3])
    corner_sems = sems[3:5]
    branch, small, *others = load(count, starts, halves, targets, sems[5:])
    shares = 2 * count
    line, side, deck, core = spot()
    greet(
        [((dp + k) % shares, tensor) for k in range(1, shares)]
        + [seat(line, side, deck, 1 - core), seat(line, side, 1 - deck, core)]
    )
    gain_copies = [
        remote(
            gains,
            gains_all.at[dp],
            gain_send.at[k],
            gain_receive.at[k],
            ((dp + k) % shares, tensor),
        )
        for k in range(1, shares)
    ]
    gain_copies.append(pltpu.make_async_copy(gains, gains_all.at[dp], gain_local))
    for copy in gain_copies:
        copy.start()
    branch.start()
    small.start()
    for copy in gain_copies:
        copy.wait()

    block_rows, features = rows.shape
    slim = features // shares
    gain = jnp.concatenate(
        [gains_all[k].astype(F32)[0:1] for k in range(shares)], axis=1
    )

    def norm_rows(i, carry):
        where = pl.ds(pl.multiple_of(i * 32, 32), 32)
        value = rows[where, :].astype(F32)
        mean = jnp.mean(value * value, axis=1, keepdims=True)
        own[where, :] = (value * lax.rsqrt(mean + EPSILON) * gain).astype(BF16)
        return carry

    lax.fori_loop(0, block_rows // 32, norm_rows, 0)
    branch.second()
    small.second()
    gather.start()
    gather.start_across()
    small.forward()
    gather.forward()
    branch.forward()
    for freight in others:
        freight.start()
    for freight in others:
        freight.second()
    small.finish()
    group_finish(gather, *corner_sems)
    copies = [
        pltpu.make_async_copy(
            table.at[g], normed.at[pl.ds(g * block_rows, block_rows)], out_sems.at[g]
        )
        for g in range(8)
    ]
    for copy in copies:
        copy.start()
    branch.finish()
    depth = targets[0].shape[1]
    loading = [
        pltpu.make_async_copy(
            targets[0].at[k], weights.at[pl.ds(k * depth, depth)], weight_sems.at[k]
        )
        for k in range(count)
    ]
    for copy in loading:
        copy.start()
    for freight in others:
        freight.forward()
    for copy in loading:
        copy.wait()
    lanes, width = weights.shape[1] // 2, pre.shape[1] // 2
    shift = 2 * lanes - width
    inside = lax.broadcasted_iota(jnp.int32, (block_rows, width), 1) < lanes

    def write(g):
        where = pl.ds(pl.multiple_of(g * block_rows, block_rows), block_rows)
        return pltpu.make_async_copy(result.at[where], pre.at[where], result_sems.at[g])

    def product(g, carry):
        where = pl.ds(pl.multiple_of(g * block_rows, block_rows), block_rows)
        both = jnp.dot(table[g], weights[...], preferred_element_type=F32)
        result[where, :width] = jnp.where(inside, both[:, :width], 0.0)
        later = pltpu.roll(both[:, shift:], lanes, 1)
        result[where, width:] = jnp.where(inside, later, 0.0)
        write(g).start()
        return carry

    lax.fori_loop(0, 8, product, 0)
    for g in range(8):
        copies[g].wait()
        write(g).wait()
    for freight in others:
        freight.finish()


def first(count, rows, gains, cargo, width):
    total = 8 * rows.shape[0]
    shares = 2 * count
    branch = cargo[0]
    out = call(
        functools.partial(first_kernel, count, cargo_starts(cargo)),
        [
            ((total, rows.shape[1]), BF16, ANY),
            ((total, 2 * width), F32, ANY),
            ((shares,) + gains.shape, BF16, VMEM),
        ]
        + cargo_outs(count, cargo),
        [(rows, VMEM), (gains, VMEM)] + cargo_ins(cargo),
        [
            pltpu.VMEM(rows.shape, BF16),
            pltpu.VMEM((8,) + rows.shape, BF16),
            pltpu.VMEM((rows.shape[1], branch.shape[2]), BF16),
            pltpu.VMEM((total, 2 * width), F32),
            pltpu.SemaphoreType.DMA((shares,)),
            pltpu.SemaphoreType.DMA((shares,)),
            pltpu.SemaphoreType.DMA,
            pltpu.SemaphoreType.DMA((8,)),
            pltpu.SemaphoreType.DMA((count,)),
            pltpu.SemaphoreType.DMA((8,)),
        ]
        + rows_scratch()
        + cargo_scratch(count, cargo),
        0,
        "first",
    )
    return out[:3] + flat_rows(out[3:])


def rows_kernel(count, starts, *refs):
    loads = len(starts)
    rows, halves = refs[0], refs[1 : 1 + loads]
    everything, targets = refs[1 + loads], refs[2 + loads : 2 + 2 * loads]
    sems = refs[2 + 2 * loads :]
    gather = GroupGather(rows, everything, *sems[:3])
    freights = load(count, starts, halves, targets, sems[5:])
    greet(cargo_peers(count))
    for freight in freights:
        freight.start()
    gather.start()
    gather.start_across()
    for freight in freights:
        freight.second()
    for freight in freights:
        freight.forward()
    gather.forward()
    group_finish(gather, *sems[3:5])
    for freight in freights:
        freight.finish()


def gather_rows(count, rows, cargo, identity):
    out = call(
        functools.partial(rows_kernel, count, cargo_starts(cargo)),
        [((8,) + rows.shape, BF16, ANY)] + cargo_outs(count, cargo),
        [(rows, ANY)] + cargo_ins(cargo),
        rows_scratch() + cargo_scratch(count, cargo),
        identity,
        "gather_rows",
    )
    return [out[0].reshape(-1, rows.shape[1])] + flat_rows(out[1:])


def turned(left, right, out, tiles, low, high):
    size = left.shape[1] // tiles

    def body(i, carry):
        place = pl.ds(pl.multiple_of(i * size, size), size)
        total = lax.dot_general(left[:, place], right[...], TN, preferred_element_type=F32)
        out[place, :] = total.astype(BF16)
        return carry

    lax.fori_loop(low, high, body, 0)


def plain_rows_kernel(rows, left, right, everything, product_out, product, *sems, fetches):
    gather = GroupGather(rows, everything, *sems[1:4])
    greet(group_peers())
    gather.start()
    gather.start_across()
    for fetch in fetches:
        fetch.wait()
    turned(left, right, product, 4, 0, 4)
    writing = pltpu.make_async_copy(product, product_out, sems[0])
    writing.start()
    gather.forward()
    group_finish(gather, *sems[4:6])
    writing.wait()


def gather_plain(rows, left, right, identity):
    out = call(
        plain_rows_kernel,
        [((8,) + rows.shape, BF16, ANY), ((left.shape[1], right.shape[1]), BF16, ANY)],
        [(rows, ANY), (left, LATE), (right, LATE)],
        [pltpu.VMEM((left.shape[1], right.shape[1]), BF16), pltpu.SemaphoreType.DMA]
        + rows_scratch(),
        identity,
        "gather_rows",
    )
    return out[0].reshape(-1, rows.shape[1]), out[1]


def flip(value, bit):
    return 1 - value if bit else value


def whole_group():
    line, side, deck, core = spot()
    return [
        seat(line, flip(side, k & 4), flip(deck, k & 2), flip(core, k & 1)) for k in range(1, 8)
    ]


class GainSum:
    def __init__(self, count, gains, totals, near, far, send, receive, far_send, far_receive):
        self.gains, self.totals, self.near, self.far = gains, totals, near, far
        self.first = [
            remote(gains, near.at[k], send.at[k], receive.at[k], peer)
            for k, peer in enumerate(whole_group())
        ]
        self.second_copies = [
            remote(far.at[0], far.at[1 + k], far_send.at[k], far_receive.at[k], peer)
            for k, peer in enumerate(line_peers(count))
        ]

    @staticmethod
    def scratch(count, gains):
        return [
            pltpu.VMEM((7,) + gains.shape, F32),
            pltpu.VMEM((count,) + gains.shape, F32),
            pltpu.SemaphoreType.DMA((7,)),
            pltpu.SemaphoreType.DMA((7,)),
            pltpu.SemaphoreType.DMA((count,)),
            pltpu.SemaphoreType.DMA((count,)),
        ]

    def start(self):
        for copy in self.first:
            copy.start()

    def second(self):
        for copy in self.first:
            copy.wait()
        total = self.gains[...]
        for k in range(7):
            total = total + self.near[k]
        self.far[0] = total
        for copy in self.second_copies:
            copy.start()

    def finish(self):
        for copy in self.second_copies:
            copy.wait()
        total = self.far[0]
        for k in range(len(self.second_copies)):
            total = total + self.far[1 + k]
        self.totals[...] = total


class Fold:
    OWN, ACROSS, ABOVE, CORNER = 0, 1, 2, 3

    def __init__(self, plan, lefts, rights, out, refs, uneven=0):
        self.plan, self.lefts, self.rights, self.out = plan, lefts, rights, out
        self.mine, self.stage, self.near = refs[:3]
        self.across_sum, self.above_sum, self.leaving, self.arriving = refs[3:7]
        send, receive, self.near_send, self.near_receive = refs[7:11]
        self.line, self.side, self.deck, self.core = spot()
        sibling, across, above = group_peers()
        self.sibling = sibling
        self.rows, self.width = out.shape
        self.cut = (self.rows // 2 + uneven, self.rows // 2 - uneven)
        self.ships = [
            remote(
                self.leaving.at[k, pl.ds(0, self.cut[k % 2])],
                self.arriving.at[k, pl.ds(0, self.cut[k % 2])],
                send.at[k],
                receive.at[k],
                peer,
            )
            for k, peer in enumerate((above, across, above, across, across, above))
        ]

    @staticmethod
    def scratch(rows, width, uneven=0):
        half = rows // 2 + uneven
        return [
            pltpu.VMEM((rows, width), F32),
            pltpu.VMEM((2, rows, width), BF16),
            pltpu.VMEM((4, rows, width), BF16),
            pltpu.VMEM((half, width), F32),
            pltpu.VMEM((half, width), F32),
            pltpu.VMEM((6, half, width), BF16),
            pltpu.VMEM((6, half, width), BF16),
            pltpu.SemaphoreType.DMA((6,)),
            pltpu.SemaphoreType.DMA((6,)),
            pltpu.SemaphoreType.DMA((4,)),
            pltpu.SemaphoreType.DMA((4,)),
        ]

    def product(self, which, store):
        base = pl.multiple_of(which * self.rows, self.rows)
        step = 512

        def body(j, carry):
            columns = pl.ds(pl.multiple_of(j * step, step), step)
            total = None
            for (which_left, start), right in zip(self.plan, self.rights):
                part = lax.dot_general(
                    self.lefts[which_left][pl.ds(base, self.rows), start : start + right.shape[1]],
                    right[columns, :],
                    NT,
                    preferred_element_type=F32,
                )
                total = part if total is None else total + part
            store(columns, total)
            return carry

        lax.fori_loop(0, self.width // step, body, 0)

    def sweep(self, part, action):
        def body(i, carry):
            action(pl.multiple_of(i * 16, 16))
            return carry

        lax.fori_loop(0, self.cut[part] // 16, body, 0)

    def near_copy(self, q):
        return remote(
            self.stage.at[q % 2],
            self.near.at[q],
            self.near_send.at[q],
            self.near_receive.at[q],
            self.sibling,
        )

    def chip_sum(self, q, h, r):
        place = pl.ds(h * self.cut[0] + r, 16)
        return self.mine[place, :] + self.near[q, place, :].astype(F32)

    def block(self, q):
        s, d = [
            (self.side, self.deck),
            (1 - self.side, self.deck),
            (self.side, 1 - self.deck),
            (1 - self.side, 1 - self.deck),
        ][q]
        if q < 2:
            self.near_copy(q + 2).wait_send()

        def put_stage(columns, total):
            self.stage[q % 2, :, columns] = total.astype(BF16)

        def put_mine(columns, total):
            target = self.out if q == self.OWN else self.mine
            target[:, columns] = total

        self.product(rank(s, d, 1 - self.core), put_stage)
        self.near_copy(q).start()
        self.product(rank(s, d, self.core), put_mine)
        self.near_copy(q).wait_recv()

    def send(self, k):
        self.ships[k].start()

    def begin(self, freights=()):
        self.block(self.CORNER)

        def depart(k, q, part):
            def action(r):
                self.leaving[k, pl.ds(r, 16), :] = self.chip_sum(q, part, r).astype(BF16)

            self.sweep(part, action)
            self.send(k)

        def stay(sums, q, part):
            def action(r):
                sums[pl.ds(r, 16), :] = self.chip_sum(q, part, r)

            self.sweep(part, action)

        depart(0, self.CORNER, 0)
        depart(1, self.CORNER, 1)
        self.block(self.ABOVE)
        depart(2, self.ABOVE, 0)
        stay(self.above_sum, self.ABOVE, 1)
        for freight in freights:
            freight.second()
        self.block(self.ACROSS)
        depart(3, self.ACROSS, 1)
        stay(self.across_sum, self.ACROSS, 0)
        self.block(self.OWN)

    def middle(self):
        for k, sums in enumerate((self.across_sum, self.above_sum)):
            self.ships[k].wait_recv()

            def action(r, k=k, sums=sums):
                place = pl.ds(r, 16)
                total = sums[place, :] + self.arriving[k, place, :].astype(F32)
                self.leaving[4 + k, place, :] = total.astype(BF16)

            self.sweep(k, action)
            self.send(4 + k)

    def finish(self, store):
        for k in range(2, 6):
            self.ships[k].wait_recv()

        for part in range(2):

            def total(r, part=part):
                place = pl.ds(r, 16)
                here = pl.ds(pl.multiple_of(part * self.cut[0] + r, 16), 16)
                value = self.out[here, :] + self.near[self.OWN, here, :].astype(F32)
                for k in (2 + part, 4 + part):
                    value = value + self.arriving[k, place, :].astype(F32)
                store(here, value)

            self.sweep(part, total)

        for k in range(6):
            self.ships[k].wait_send()
        for q in range(2):
            self.near_copy(q).wait_send()


def unit_rows(value):
    scale = lax.rsqrt(jnp.mean(value * value, axis=1, keepdims=True) + EPSILON)
    return value * scale, scale


def norm_back_rows(grad, unit, scale, gain):
    grad_unit = grad * gain
    inner = jnp.mean(grad_unit * unit, axis=1, keepdims=True)
    return scale * (grad_unit - unit * inner), jnp.sum(grad * unit, axis=0, keepdims=True)


def mixer_fold_kernel(count, jobs, starts, left, right, *refs, fetches):
    loads = len(starts)
    inputs, gain, refs = refs[0], refs[1], refs[2:]
    halves, refs = refs[:loads], refs[loads:]
    out, normed, refs = refs[0], refs[1], refs[2:]
    targets, refs = refs[:loads], refs[loads:]
    fold = Fold(jobs[0], [left], [right], out, refs[:11])
    freights = load(count, starts, halves, targets, refs[11:])
    greet(cargo_peers(count))
    for freight in freights:
        freight.start()
    for fetch in fetches[:2]:
        fetch.wait()
    fold.begin(freights)
    fold.middle()
    for freight in freights:
        freight.forward()

    fetches[2].wait()

    def store(here, value):
        value = value + inputs[here, :].astype(F32)
        out[here, :] = value
        normed[here, :] = (unit_rows(value)[0] * gain[...]).astype(BF16)

    fold.finish(store)
    for freight in freights:
        freight.finish()


def plan_of(lefts_rights):
    lefts, rights, plan = [], [], []
    for k, (left, parts) in enumerate(lefts_rights):
        lefts.append((left, LATE))
        start = 0
        for part in parts:
            rights.append((part, LATE))
            plan.append((k, start))
            start += part.shape[1]
    return plan, lefts + rights


def mixer_fold(count, merged, mixer, inputs, gain, cargo):
    plan, ins = plan_of([(merged, [mixer])])
    rows, width = inputs.shape
    out = call(
        functools.partial(mixer_fold_kernel, count, [plan], cargo_starts(cargo)),
        [((rows, width), F32, VMEM), ((rows, width), BF16, VMEM)] + cargo_outs(count, cargo),
        ins + [(inputs, LATE), (gain, VMEM)] + cargo_ins(cargo),
        Fold.scratch(rows, width) + cargo_scratch(count, cargo),
        3,
        "mixer_fold",
    )
    return out[:2] + flat_rows(out[2:])


def feed_fold_kernel(plan, parts, left, other, *refs, fetches):
    rights, refs = refs[:parts], refs[parts:]
    normed, hidden, cotangent, gain, refs = *refs[:4], refs[4:]
    out, low, gain_sum, grads_out = refs[:4]
    fold = Fold(plan, [left, other], rights, out, refs[4:15])
    grads, write_sem = refs[15:]
    greet(group_peers())
    for fetch in fetches[: 2 + parts]:
        fetch.wait()
    fold.begin()
    fold.middle()
    for fetch in fetches[2 + parts :]:
        fetch.wait()
    turned(normed, left, grads, 4, 0, 4)
    writing = pltpu.make_async_copy(grads, grads_out, write_sem)
    writing.start()
    gain_sum[...] = jnp.zeros_like(gain_sum)

    def store(here, value):
        unit, scale = unit_rows(hidden[here, :])
        back, terms = norm_back_rows(value, unit, scale, gain[...])
        gain_sum[0:1, :] += terms
        back = cotangent[here, :].astype(F32) + back
        out[here, :] = back
        low[here, :] = back.astype(BF16)

    fold.finish(store)
    writing.wait()


def feed_fold(grad_gating, grad_lifting, gates, ups, normed, hidden, cotangent, gain):
    plan, ins = plan_of([(grad_gating, gates), (grad_lifting, ups)])
    rows, width = hidden.shape
    return call(
        functools.partial(feed_fold_kernel, plan, len(gates) + len(ups)),
        [
            ((rows, width), F32, VMEM),
            ((rows, width), BF16, VMEM),
            ((8, width), F32, VMEM),
            ((normed.shape[1], grad_gating.shape[1]), BF16, ANY),
        ],
        ins + [(normed, LATE), (hidden, LATE), (cotangent, LATE), (gain, VMEM)],
        Fold.scratch(rows, width)
        + [
            pltpu.VMEM((normed.shape[1], grad_gating.shape[1]), BF16),
            pltpu.SemaphoreType.DMA,
        ],
        6,
        "feed_fold",
    )


UNEVEN = 16


def last_fold_kernel(count, plans, parts, swaps, left, right, feed_left, *refs, fetches):
    rights, refs = refs[:parts], refs[parts:]
    inputs, gain, grad_hidden, hidden, second, refs = *refs[:5], refs[5:]
    values, refs = refs[:swaps], refs[swaps:]
    input_grad, output, totals = refs[:3]
    swapped, refs = refs[3 : 3 + swaps], refs[3 + swaps :]
    out, feed_out, sums, terms_here, refs = *refs[:4], refs[4:]
    fold = Fold(plans[0], [left], [right], out, refs[:11], UNEVEN)
    feed = Fold(plans[1], [feed_left], rights, feed_out, refs[11:22], UNEVEN)
    swap = Swap(values, swapped, *refs[22:25])
    gain_sum = GainSum(count, sums, totals, *refs[25:])
    greet(whole_group() + line_peers(count))
    swap.start()
    for fetch in fetches[:2]:
        fetch.wait()
    fold.begin()
    fold.middle()
    for fetch in fetches[2:]:
        fetch.wait()
    feed.begin()
    terms_here[...] = jnp.zeros_like(terms_here)

    def store(here, value):
        unit, scale = unit_rows(inputs[here, :].astype(F32))
        back, terms = norm_back_rows(value, unit, scale, gain[...])
        terms_here[0:1, :] += terms
        input_grad[here, :] = (grad_hidden[here, :] + back).astype(BF16)

    fold.finish(store)
    shares, slim = sums.shape[0] // 2, sums.shape[1]
    for k in range(shares):
        columns = slice(k * slim, (k + 1) * slim)
        sums[k : k + 1, :] = terms_here[0:1, columns]
        sums[shares + k : shares + k + 1, :] = second[0:1, columns]
    gain_sum.start()
    feed.middle()
    gain_sum.second()

    def store_output(here, value):
        output[here, :] = (hidden[here, :] + value).astype(BF16)

    feed.finish(store_output)
    gain_sum.finish()
    swap.finish()


def last_fold(count, grads, branch, feed_left, downs, inputs, gain, grad_hidden, hidden, second, swaps):
    plan, ins = plan_of([(grads, [branch])])
    feed_plan, feed_ins = plan_of([(feed_left, downs)])
    rows, width = hidden.shape
    both = jax.ShapeDtypeStruct((4 * count, width // (2 * count)), F32)
    return call(
        functools.partial(last_fold_kernel, count, (plan, feed_plan), len(downs), len(swaps)),
        [
            ((rows, width), BF16, VMEM),
            ((rows, width), BF16, VMEM),
            (both.shape, F32, VMEM),
        ]
        + [(value.shape, BF16, ANY) for value in swaps],
        ins
        + feed_ins
        + [
            (inputs, LATE),
            (gain, VMEM),
            (grad_hidden, LATE),
            (hidden, LATE),
            (second, VMEM),
        ]
        + [(value, ANY) for value in swaps],
        [
            pltpu.VMEM((rows, width), F32),
            pltpu.VMEM((rows, width), F32),
            pltpu.VMEM(both.shape, F32),
            pltpu.VMEM((8, width), F32),
        ]
        + Fold.scratch(rows, width, UNEVEN) * 2
        + Swap.scratch(swaps)
        + GainSum.scratch(count, both),
        9,
        "last_fold",
    )


def gelu_both(value):
    square = value * value
    bend = jnp.tanh(GELU_SCALE * value * (1.0 + GELU_CUBE * square))
    act = 0.5 * value * (1.0 + bend)
    slope = 0.5 * (1.0 + bend) + 0.5 * value * (1.0 - bend * bend) * GELU_SCALE * (
        1.0 + 3.0 * GELU_CUBE * square
    )
    return act, slope


def chunks(rows, action, size=CHUNK):
    def body(i, carry):
        action(pl.multiple_of(i * size, size))
        return carry

    lax.fori_loop(0, rows // size, body, 0)


def spans(low, high, action):
    def body(i, carry):
        action(pl.multiple_of(i * CHUNK, CHUNK))
        return carry

    lax.fori_loop(low, high, body, 0)


def tile_scan(mults, adds, rows, width, backward):
    place = lax.broadcasted_iota(jnp.int32, (8, width), 0)

    def inside(base):
        where = pl.ds(base, 8)
        a, b = mults[where, :], adds[where, :]
        for k in (1, 2, 4):
            if backward:
                away, mask = pltpu.roll(a, 8 - k, 0), place < 8 - k
                back = pltpu.roll(b, 8 - k, 0)
            else:
                away, mask = pltpu.roll(a, k, 0), place >= k
                back = pltpu.roll(b, k, 0)
            b = jnp.where(mask, b + a * back, b)
            a = jnp.where(mask, a * away, a)
        return where, a, b

    unroll = 4
    tiles = rows // 8

    def body(i, carry):
        prod, total = carry
        work = []
        for u in range(unroll):
            index = i * unroll + u
            if backward:
                index = tiles - 1 - index
            work.append(inside(pl.multiple_of(index * 8, 8)))
        for where, a, b in work:
            edge = 0 if backward else 7
            adds[where, :] = b + a * total
            mults[where, :] = a * prod
            whole = jnp.broadcast_to(a[edge : edge + 1, :], (8, width))
            extra = jnp.broadcast_to(b[edge : edge + 1, :], (8, width))
            total = extra + whole * total
            prod = whole * prod
        return prod, total

    return lax.fori_loop(
        0, tiles // unroll, body, (jnp.ones((8, width), F32), jnp.zeros((8, width), F32))
    )


def pool(count, prod, total, outgoing, slots, send, receive, backward):
    line, side, deck, core = spot()
    outgoing[0:8, :] = prod
    outgoing[8:16, :] = total
    slots[line, 0:8, :] = prod
    slots[line, 8:16, :] = total
    copies = []
    for k in range(1, count):
        copy = remote(
            outgoing,
            slots.at[line],
            send.at[k],
            receive.at[k],
            seat((line + k) % count, side, deck, core),
        )
        copy.start()
        copies.append(copy)
    for copy in copies:
        copy.wait()
    entering = jnp.zeros_like(prod)
    order = range(count - 1, -1, -1) if backward else range(count)
    for place in order:
        longer = slots[place, 8:16, :] + slots[place, 0:8, :] * entering
        before = (line < place) if backward else (line > place)
        entering = jnp.where(before, longer, entering)
    return entering


def sigmoid(value):
    return 0.5 + 0.5 * jnp.tanh(0.5 * value)


def gates(recur, soft):
    decay = jnp.exp(-8.0 * recur * soft)
    square = (1.0 + GUARD) - decay * decay
    inverse = lax.rsqrt(square)
    return decay, square * inverse, inverse


def scan_kernel(count, starts, *refs):
    loads = len(starts)
    pre, masks, table, gate_weights, cotangent = refs[:5]
    halves, refs = refs[5 : 5 + loads], refs[5 + loads :]
    everything, targets, refs = refs[6], refs[7 : 7 + loads], refs[:6] + refs[7 + loads :]
    saved, refs = refs[:6], refs[6:]
    gate, entry, conv, recur_out, admit_out, state, merged = refs[:7]
    prods, sums, halo, outgoing, slots, edge_sems, send, receive = refs[7:15]
    in_sems, out_sems, head_sems = refs[15:18]
    sems = refs[18:]
    line, side, deck, core = spot()
    rows, width = conv.shape
    gather = GroupGather(cotangent, everything, *sems[:3])
    freights = load(count, starts, halves, targets, sems[5:])
    gate_reads = Stream(pre, gate, in_sems.at[0], columns=pl.ds(0, width))
    entry_reads = Stream(pre, entry, in_sems.at[1], to_row=8, columns=pl.ds(width, width))
    conv_writes = Stream(conv, saved[0], out_sems.at[0])
    recur_writes = Stream(recur_out, saved[1], out_sems.at[1])
    admit_writes = Stream(admit_out, saved[2], out_sems.at[2])
    state_writes = Stream(state, saved[3], out_sems.at[3], 8, 8)
    merged_writes = Stream(merged, saved[4], out_sems.at[4])
    entry_writes = Stream(entry, saved[5], out_sems.at[5], 8, 8)
    heads = [
        pltpu.make_async_copy(local.at[pl.ds(0, 8)], away.at[pl.ds(0, 8)], head_sems.at[k])
        for k, (local, away) in enumerate([(state, saved[3]), (entry, saved[5])])
    ]
    entry_reads.start_all()
    gate_reads.start_all()
    greet(cargo_peers(count))

    def edge(place):
        return remote(
            pre.at[pl.ds(rows - 8, 8), pl.ds(width, width)],
            halo,
            edge_sems.at[0],
            edge_sems.at[1],
            seat(place, side, deck, core),
        )

    @pl.when(line < count - 1)
    def _():
        edge(line + 1).start()

    for freight in freights:
        freight.start()
    gather.start()

    @pl.when(line > 0)
    def _():
        edge(line - 1).wait_recv()
        entry[0:8, :] = halo[...]

    @pl.when(line == 0)
    def _():
        entry[0:8, :] = jnp.zeros((8, width), F32)

    @pl.when(line < count - 1)
    def _():
        edge(line + 1).wait_send()

    heads[1].start()

    def gate_chunk(r):
        entry_reads.wait(r)
        wide = entry[pl.ds(r, CHUNK + 8), :]
        mask = masks[pl.ds(r, CHUNK), :]
        value = table[0:1, :] * wide[8:, :]
        for k in range(1, TAPS):
            value = (
                value + table[k : k + 1, :] * wide[8 - k : 8 - k + CHUNK, :] * mask[:, k - 1 : k]
            )
        where = pl.ds(r, CHUNK)
        conv[where, :] = value
        both = jnp.dot(value.astype(BF16), gate_weights[...], preferred_element_type=F32)
        recur = sigmoid(both[:, :width])
        admit = sigmoid(both[:, width:])
        recur_out[where, :] = recur
        admit_out[where, :] = admit
        decay, root, _ = gates(recur, table[4:5, :])
        opened = mask[:, 3:4]
        norm = root * opened + (1.0 - opened)
        prods[where, :] = decay * opened
        sums[where, :] = norm * admit * value
        for stream in (entry_writes, conv_writes, recur_writes, admit_writes):
            stream.start(r)

    pieces = rows // CHUNK
    for freight in freights:
        freight.second()
    gather.start_across()
    spans(0, pieces, gate_chunk)
    prod, total = tile_scan(prods, sums, rows, width, False)
    entering = pool(count, prod, total, outgoing, slots, send, receive, False)
    for freight in freights:
        freight.forward()
    gather.forward()
    state[0:8, :] = entering
    heads[0].start()

    def state_chunk(r):
        gate_reads.wait(r)
        where = pl.ds(r, CHUNK)
        value = sums[where, :] + prods[where, :] * entering[0:1, :]
        state[pl.ds(r + 8, CHUNK), :] = value
        act, _ = gelu_both(gate[where, :])
        merged[where, :] = (value * act).astype(BF16)
        state_writes.start(r)
        merged_writes.start(r)

    chunks(rows, state_chunk)
    for stream in (
        entry_writes,
        conv_writes,
        recur_writes,
        admit_writes,
        state_writes,
        merged_writes,
    ):
        stream.wait_all()
    for copy in heads:
        copy.wait()
    group_finish(gather, *sems[3:5])
    for freight in freights:
        freight.finish()


def scan_forward(count, pre, masks, table, gate_weights, cotangent, cargo):
    rows, width = pre.shape[0], pre.shape[1] // 2
    pieces = rows // CHUNK
    tall = (rows + 8, width)
    saved = [
        ((rows, width), F32),
        ((rows, width), F32),
        ((rows, width), F32),
        (tall, F32),
        ((rows, width), BF16),
        (tall, F32),
    ]
    out = call(
        functools.partial(scan_kernel, count, cargo_starts(cargo)),
        [(shape, kind, ANY) for shape, kind in saved]
        + [((8,) + cotangent.shape, BF16, ANY)]
        + cargo_outs(count, cargo),
        [(pre, ANY), (masks, VMEM), (table, VMEM), (gate_weights, VMEM), (cotangent, ANY)]
        + cargo_ins(cargo),
        [
            pltpu.VMEM((rows, width), F32),
            pltpu.VMEM(tall, F32),
            pltpu.VMEM((rows, width), F32),
            pltpu.VMEM((rows, width), F32),
            pltpu.VMEM((rows, width), F32),
            pltpu.VMEM(tall, F32),
            pltpu.VMEM((rows, width), BF16),
            pltpu.VMEM((rows, width), F32),
            pltpu.VMEM((rows, width), F32),
            pltpu.VMEM((8, width), F32),
            pltpu.VMEM((16, width), F32),
            pltpu.VMEM((count, 16, width), F32),
            pltpu.SemaphoreType.DMA((2,)),
            pltpu.SemaphoreType.DMA((count,)),
            pltpu.SemaphoreType.DMA((count,)),
            pltpu.SemaphoreType.DMA((2, pieces)),
            pltpu.SemaphoreType.DMA((6, pieces)),
            pltpu.SemaphoreType.DMA((2,)),
        ]
        + rows_scratch()
        + cargo_scratch(count, cargo),
        2,
        "scan_forward",
    )
    return out[:6] + [out[6].reshape(-1, cotangent.shape[1])] + flat_rows(out[7:])


def back_kernel(count, lanes, swaps, *refs, fetches):
    pre, low, outlet = refs[:3]
    saved, refs = refs[3:8], refs[8:]
    masks, table, gate_weights = refs[:3]
    values, refs = refs[3 : 3 + swaps], refs[3 + swaps :]
    grad_pre, grad_gates, grad_table = refs[:3]
    swapped, refs = refs[3 : 3 + swaps], refs[3 + swaps :]
    gate, conv, recur_in, admit_in, state, entry, lows = refs[:7]
    prods, sums, mixes, outgoing, slots, edge_sems, send, receive = refs[7:15]
    in_sems, low_sems, head_sems = refs[15:18]
    line, side, deck, core = spot()
    rows, width = conv.shape
    pieces = rows // CHUNK
    swap = Swap(values, swapped, *refs[18:])
    conv_reads = Stream(saved[0], conv, in_sems.at[0])
    recur_reads = Stream(saved[1], recur_in, in_sems.at[1])
    admit_reads = Stream(saved[2], admit_in, in_sems.at[2])
    state_reads = Stream(saved[3], state, in_sems.at[3], 8, 8)
    entry_reads = Stream(saved[4], entry, in_sems.at[4], 8, 8)
    gate_reads = Stream(pre, gate, in_sems.at[5], columns=pl.ds(0, width))
    heads = [
        pltpu.make_async_copy(away.at[pl.ds(0, 8)], local.at[pl.ds(0, 8)], head_sems.at[k])
        for k, (local, away) in enumerate([(state, saved[3]), (entry, saved[4])])
    ]

    def fetch(i):
        slot = i % 2
        start = pl.multiple_of(i * CHUNK, CHUNK)
        return pltpu.make_async_copy(
            low.at[pl.ds(start, CHUNK)], lows.at[slot], low_sems.at[slot]
        )

    fetch(0).start()
    for k in range(pieces):
        for stream in (gate_reads, recur_reads, state_reads):
            stream.start(k * CHUNK)
    for copy in heads:
        copy.start()
    for stream in (conv_reads, admit_reads, entry_reads):
        stream.start_all()
    greet(line_peers(count) + ([seat(line, 1 - side, deck, core)] if swaps else []))
    swap.start()
    for copy in fetches:
        copy.wait()

    def direct(i, carry):
        r = pl.multiple_of(i * CHUNK, CHUNK)

        @pl.when(i + 1 < pieces)
        def _():
            fetch(i + 1).start()

        fetch(i).wait()
        for stream in (gate_reads, recur_reads, state_reads):
            stream.wait(r)
        where = pl.ds(r, CHUNK)
        grad = jnp.dot(lows[i % 2], outlet[...], preferred_element_type=F32)
        act, slope = gelu_both(gate[where, :])
        gate[where, :] = grad * state[pl.ds(r + 8, CHUNK), :] * slope
        straight = grad * act
        carried = jnp.exp(-8.0 * recur_in[where, :] * table[4:5, :]) * masks[where, 3:4]
        mixes[where, :] = straight
        prods[where, :] = carried
        sums[where, :] = carried * straight
        return carry

    lax.fori_loop(0, pieces, direct, 0)
    prods[rows : rows + 8, :] = jnp.ones((8, width), F32)
    sums[rows : rows + 8, :] = jnp.zeros((8, width), F32)
    prod, total = tile_scan(prods, sums, rows, width, True)
    entering = pool(count, prod, total, outgoing, slots, send, receive, True)
    for copy in heads:
        copy.wait()
    grad_gates[...] = jnp.zeros_like(grad_gates)
    grad_table[...] = jnp.zeros_like(grad_table)

    def fold_rows(value):
        return jnp.sum(value, axis=0, keepdims=True)

    def gate_chunk(r):
        conv_reads.wait(r)
        admit_reads.wait(r)
        where = pl.ds(r, CHUNK)
        wide = pl.ds(r, CHUNK + 8)
        later = sums[wide, :] + prods[wide, :] * entering[0:1, :]
        grad = mixes[where, :] + later[1 : CHUNK + 1, :]
        before = state[wide, :][7 : CHUNK + 7, :]
        soft = table[4:5, :]
        recur, admit, value = recur_in[where, :], admit_in[where, :], conv[where, :]
        decay, root, inverse = gates(recur, soft)
        opened = masks[where, 3:4]
        norm = root * opened + (1.0 - opened)
        flow = grad * admit
        grad_log = opened * (grad * before * decay - flow * value * decay * decay * inverse)
        grad_table[4:5, :] += fold_rows(grad_log * (-8.0 * recur))
        grad_rate = (grad_log * (-8.0 * soft) * recur * (1.0 - recur)).astype(BF16)
        grad_inlet = (flow * norm * value * (1.0 - admit)).astype(BF16)
        both = jnp.concatenate([grad_rate, grad_inlet], axis=1)
        grad_gates[...] += lax.dot_general(
            value.astype(BF16), both, TN, preferred_element_type=F32
        )
        mixes[where, :] = flow * norm + lax.dot_general(
            both, gate_weights[...], NT, preferred_element_type=F32
        )

    gate_chunk(0)

    def edge(place):
        return remote(
            mixes.at[pl.ds(0, 8)],
            mixes.at[pl.ds(rows, 8)],
            edge_sems.at[0],
            edge_sems.at[1],
            seat(place, side, deck, core),
        )

    @pl.when(line > 0)
    def _():
        edge(line - 1).start()

    spans(1, pieces, gate_chunk)

    @pl.when(line < count - 1)
    def _():
        edge(line + 1).wait_recv()

    @pl.when(line == count - 1)
    def _():
        mixes[rows : rows + 8, :] = jnp.zeros((8, width), F32)

    spare = width - lanes
    shift = 2 * lanes - width

    def entry_chunk(r):
        entry_reads.wait(r)
        where, wide = pl.ds(r, CHUNK), pl.ds(r, CHUNK + 8)
        ahead, mask = mixes[wide, :], masks[where, :]
        source = entry[wide, :]
        here = ahead[:CHUNK, :]
        total = table[0:1, :] * here
        grad_table[0:1, :] += fold_rows(here * source[8:, :])
        for k in range(1, TAPS):
            total = total + table[k : k + 1, :] * ahead[k : k + CHUNK, :] * mask[:, 3 + k : 4 + k]
            grad_table[k : k + 1, :] += fold_rows(
                here * source[8 - k : 8 - k + CHUNK, :] * mask[:, k - 1 : k]
            )
        total = pltpu.roll(total, spare, 1)
        first = gate[where, :]
        middle = first[:, shift:] + total[:, : width - shift]
        grad_pre[where, :shift] = first[:, :shift].astype(BF16)
        grad_pre[where, shift:width] = middle.astype(BF16)
        grad_pre[where, width:] = total[:, width - shift :].astype(BF16)

    chunks(rows, entry_chunk)

    @pl.when(line > 0)
    def _():
        edge(line - 1).wait_send()

    swap.finish()


def scan_backward(count, lanes, pre, low, outlet, saved, masks, table, gate_weights, swaps):
    rows, width = pre.shape[0], pre.shape[1] // 2
    pieces = rows // CHUNK
    tall = (rows + 8, width)
    return call(
        functools.partial(back_kernel, count, lanes, len(swaps)),
        [
            ((rows, 2 * lanes), BF16, VMEM),
            ((width, 2 * width), F32, VMEM),
            ((8, width), F32, VMEM),
        ]
        + [(value.shape, BF16, ANY) for value in swaps],
        [(pre, ANY), (low, ANY), (outlet, LATE)]
        + [(value, ANY) for value in saved]
        + [(masks, LATE), (table, VMEM), (gate_weights, LATE)]
        + [(value, ANY) for value in swaps],
        [
            pltpu.VMEM((rows, width), F32),
            pltpu.VMEM((rows, width), F32),
            pltpu.VMEM((rows, width), F32),
            pltpu.VMEM((rows, width), F32),
            pltpu.VMEM(tall, F32),
            pltpu.VMEM(tall, F32),
            pltpu.VMEM((2, CHUNK, low.shape[1]), BF16),
            pltpu.VMEM(tall, F32),
            pltpu.VMEM(tall, F32),
            pltpu.VMEM(tall, F32),
            pltpu.VMEM((16, width), F32),
            pltpu.VMEM((count, 16, width), F32),
            pltpu.SemaphoreType.DMA((2,)),
            pltpu.SemaphoreType.DMA((count,)),
            pltpu.SemaphoreType.DMA((count,)),
            pltpu.SemaphoreType.DMA((6, pieces)),
            pltpu.SemaphoreType.DMA((2,)),
            pltpu.SemaphoreType.DMA((2,)),
        ]
        + Swap.scratch(swaps),
        7,
        "scan_backward",
    )


def feed_kernel(count, early, starts, *refs):
    loads = len(starts)
    normed, cotangent = refs[:2]
    gate_parts, up_parts, down_parts = refs[2:4], refs[4:6], refs[6 : 6 + early]
    refs = refs[6 + early :]
    halves, refs = refs[:loads], refs[loads:]
    results, down_grads = refs[:3], refs[3]
    targets, refs = refs[4 : 4 + loads], refs[4 + loads :]
    table, gate_up, acts, slopes, down, hidden, grad_gating, grad_lifting = refs[:8]
    table_sems, back_sems, write_sems, weight_sems, down_sems = refs[8:13]
    freights = load(count, starts, halves, targets, refs[13:])
    rows, width = hidden.shape
    pieces = rows // CHUNK
    reads = Stream(normed, table, table_sems)
    again = Stream(cotangent, table, back_sems)
    writes = [
        Stream(local, away, write_sems.at[k])
        for k, (local, away) in enumerate(zip((hidden, grad_gating, grad_lifting), results))
    ]
    weights = []
    for which, parts in enumerate((gate_parts, up_parts)):
        start = 0
        for part in parts:
            weights.append(
                pltpu.make_async_copy(
                    part,
                    gate_up.at[which, :, pl.ds(start, part.shape[1])],
                    weight_sems.at[len(weights)],
                )
            )
            start += part.shape[1]
    for copy in weights:
        copy.start()
    reads.start_all()
    greet(cargo_peers(count))
    for freight in freights:
        freight.start()
    for copy in weights:
        copy.wait()

    def forward_chunk(r):
        reads.wait(r)
        where = pl.ds(r, CHUNK)
        gating = jnp.dot(table[where, :], gate_up[0], preferred_element_type=F32)
        lifting = jnp.dot(table[where, :], gate_up[1], preferred_element_type=F32)
        act, slope = gelu_both(gating)
        hidden[where, :] = (act * lifting).astype(BF16)
        acts[where, :] = act
        slopes[where, :] = lifting * slope
        writes[0].start(r)
        again.start(r)

    for freight in freights:
        freight.second()
    spans(0, 3 * pieces // 4, forward_chunk)
    for freight in freights:
        freight.forward()
    spans(3 * pieces // 4, pieces, forward_chunk)
    rows_in = down.shape[0] // count
    copies, start = [], 0
    for k, part in enumerate(down_parts):
        copies.append(
            pltpu.make_async_copy(
                part, down.at[:, pl.ds(start, part.shape[1])], down_sems.at[k]
            )
        )
        start += part.shape[1]
    for k, target in enumerate(targets):
        for place in range(count):
            copies.append(
                pltpu.make_async_copy(
                    target.at[place],
                    down.at[pl.ds(place * rows_in, rows_in), pl.ds(start, target.shape[2])],
                    down_sems.at[early + k * count + place],
                )
            )
        start += target.shape[2]

    def back(low, high):
        def chunk(r):
            where = pl.ds(r, CHUNK)
            columns = slice(low, high)
            grad = jnp.dot(table[where, :], down[:, columns], preferred_element_type=F32)
            grad_gating[where, columns] = (grad * slopes[where, columns]).astype(BF16)
            grad_lifting[where, columns] = (grad * acts[where, columns]).astype(BF16)
            if high == width:
                writes[1].start(r)
                writes[2].start(r)

        chunks(rows, chunk)

    for copy in copies[:early]:
        copy.start()
    again.wait_all()
    for copy in copies[:early]:
        copy.wait()
    turned(table, hidden, down_grads, 4, 0, 4)
    ready = sum(part.shape[1] for part in down_parts)
    back(0, ready)
    for freight in freights:
        freight.finish()
    for copy in copies[early:]:
        copy.start()
    for copy in copies[early:]:
        copy.wait()
    back(ready, width)
    for stream in writes:
        stream.wait_all()


def feed(count, normed, cotangent, gate_parts, up_parts, down_parts, cargo):
    rows = normed.shape[0]
    width = sum(part.shape[1] for part in gate_parts)
    pieces = rows // CHUNK
    out = call(
        functools.partial(feed_kernel, count, len(down_parts), cargo_starts(cargo)),
        [((rows, width), BF16, ANY)] * 3
        + [((normed.shape[1], width), BF16, VMEM)]
        + cargo_outs(count, cargo),
        [(normed, ANY), (cotangent, ANY)]
        + [(part, ANY) for part in list(gate_parts) + list(up_parts) + list(down_parts)]
        + cargo_ins(cargo),
        [
            pltpu.VMEM(normed.shape, BF16),
            pltpu.VMEM((2, normed.shape[1], width), BF16),
            pltpu.VMEM((rows, width), F32),
            pltpu.VMEM((rows, width), F32),
            pltpu.VMEM((normed.shape[1], width), BF16),
            pltpu.VMEM((rows, width), BF16),
            pltpu.VMEM((rows, width), BF16),
            pltpu.VMEM((rows, width), BF16),
            pltpu.SemaphoreType.DMA((pieces,)),
            pltpu.SemaphoreType.DMA((pieces,)),
            pltpu.SemaphoreType.DMA((3, pieces)),
            pltpu.SemaphoreType.DMA((4,)),
            pltpu.SemaphoreType.DMA((len(down_parts) + count * len(cargo),)),
        ]
        + cargo_scratch(count, cargo),
        5,
        "feed",
    )
    return out[:4] + flat_rows(out[4:])


def doc_index(places, doc_starts):
    return jnp.sum((doc_starts[None, :] <= places[:, None]).astype(jnp.int32), axis=1)


def split_columns(value):
    rows, columns = value.shape
    return value.reshape(rows, 2, columns // 2).transpose(1, 0, 2)


def widen(value, width):
    return jnp.pad(value, [(0, 0)] * (value.ndim - 1) + [(0, width - value.shape[-1])])


def by_rows(left, right):
    return lax.dot_general(left, right, TN, preferred_element_type=F32).astype(BF16)


def shards(
    layer_input,
    out_grad,
    doc_starts,
    mixer_gain,
    branch_gate,
    branch_input,
    conv_taps,
    rate_gate,
    input_gate,
    decay_param,
    mixer_out,
    feed_gain,
    feed_gate,
    feed_up,
    feed_down,
):
    shares = lax.axis_size("dp")
    count = shares // 2
    side = lax.axis_index("dp") % 2
    slim, feature_count = mixer_gain.shape[0], layer_input.shape[1]
    heads, piece, head_width = rate_gate.shape
    half_heads = heads // 2
    lanes = half_heads * head_width
    width = -(-lanes // 128) * 128
    row_count = layer_input.shape[0]
    rows = row_count * 8
    line_groups = [[2 * k + s for k in range(count)] for s in range(2)]

    branch_halves = jnp.concatenate(
        [split_columns(branch_gate), split_columns(branch_input)], axis=2
    )
    mixer_halves = widen(split_columns(mixer_out.T), width)
    down_rows = feed_down.T
    narrow = feed_gate.shape[1] // 6
    broad = 2 * narrow

    mine = lax.axis_index("dp")
    blocks = jnp.concatenate([rate_gate, input_gate], axis=2)
    blocks = widen(blocks.reshape(2, half_heads * piece, 2 * head_width), width)
    own = jnp.concatenate([conv_taps, decay_param[None]], axis=0)
    own = jnp.pad(own, ((0, 0), (0, 0), (0, head_width - piece)))
    own = jnp.roll(own, mine * piece, axis=2)
    own = own.reshape(TAPS + 1, 2, lanes).transpose(1, 0, 2)
    gains_own = jnp.pad(jnp.stack([mixer_gain, feed_gain]), ((0, 14), (0, 0)))
    tail = widen(own, width)
    small_top = half_heads * piece
    small_rows = -(-(small_top + TAPS + 1) // 16) * 16
    small = jnp.concatenate([blocks, tail], axis=1)
    small = jnp.pad(small, ((0, 0), (0, small_rows - small.shape[1]), (0, 0)))

    normed_one, pre, gains_all, branch_all, small_all, gate_first = first(
        count, layer_input, gains_own, [branch_halves, small, (feed_gate, 0, narrow)], width
    )

    small_all = small_all.reshape(shares, -1, width)
    tails = small_all[:, small_top : small_top + TAPS + 1].astype(F32)
    gain_first = gains_all[:, 0].reshape(feature_count).astype(F32)
    gain_second = gains_all[:, 1].reshape(feature_count).astype(F32)
    sums = jnp.sum(tails, axis=0)
    decay_flat = sums[TAPS, :lanes]
    inside = (jnp.arange(width) < lanes)[None]
    table = jnp.concatenate(
        [
            sums[:TAPS],
            jnp.where(inside, jax.nn.softplus(-sums[TAPS:]), 0.0),
            jnp.zeros((3, width), F32),
        ]
    )
    blocks = (
        small_all[:, : half_heads * piece, : 2 * head_width]
        .reshape(shares, half_heads, piece, 2 * head_width)
        .transpose(1, 0, 2, 3)
        .reshape(lanes, 2 * head_width)
    )
    head_of = jnp.arange(width) // head_width
    same = (head_of[:lanes, None] == head_of[None, :]) & (jnp.arange(width) < lanes)[None]

    def diagonal(part):
        wide = widen(jnp.concatenate([part] * half_heads, axis=1), width)
        return jnp.where(same, wide, 0)

    gate_weights = jnp.concatenate(
        [diagonal(blocks[:, :head_width]), diagonal(blocks[:, head_width:])], axis=1
    )
    gate_weights = jnp.pad(gate_weights, ((0, width - lanes), (0, 0)))

    anchor = lax.axis_index("dp") // 2 * rows
    places = anchor + jnp.arange(rows, dtype=jnp.int32)
    here = doc_index(places, doc_starts)
    columns = [doc_index(places - k, doc_starts) == here for k in range(1, TAPS)]
    columns.append(~jnp.any(doc_starts[None, :] == places[:, None], axis=1))
    columns += [doc_index(places + k, doc_starts) == here for k in range(1, TAPS)]
    columns.append(columns[0])
    masks = jnp.stack(columns, axis=1).astype(F32)

    conv, recur, admit, state, merged, entry, cot_all, mixer_all, up_first = scan_forward(
        count, pre, masks, table, gate_weights, out_grad, [mixer_halves, (feed_up, 0, narrow)]
    )
    hidden_one, normed_own, gate_second, down_first = mixer_fold(
        count,
        merged,
        mixer_all,
        layer_input,
        gain_second[None],
        [(feed_gate, narrow, broad), (down_rows, 0, narrow)],
    )
    normed_two, up_second = gather_rows(count, normed_own, [(feed_up, narrow, broad)], 4)
    gate_parts, up_parts = [gate_first, gate_second], [up_first, up_second]
    hidden, grad_gating, grad_lifting, down_grads, down_second = feed(
        count,
        normed_two,
        cot_all,
        gate_parts,
        up_parts,
        [down_first],
        [(down_rows, narrow, broad)],
    )
    down_parts = [down_first, down_second]

    def line_sum(value):
        return lax.psum_scatter(
            value, "dp", scatter_dimension=0, axis_index_groups=line_groups, tiled=True
        )

    down_sum = line_sum(down_grads)
    grad_hidden_one, low_own, second_terms, gate_grads = feed_fold(
        grad_gating,
        grad_lifting,
        gate_parts,
        up_parts,
        normed_two,
        hidden_one,
        out_grad,
        gain_second[None],
    )
    low_own, down_sum = lax.optimization_barrier((low_own, down_sum))
    gate_sum = line_sum(gate_grads)
    back_low, up_grads = gather_plain(low_own, normed_two, grad_lifting, 8)
    up_sum = line_sum(up_grads)
    outlet_grads = by_rows(back_low, merged)

    def by_side(value):
        return value.reshape(2, -1, value.shape[1])

    back_low, outlet_grads, gate_sum = lax.optimization_barrier(
        (back_low, outlet_grads, gate_sum)
    )
    grad_pre, grad_gates, grad_table, down_both, gate_both = scan_backward(
        count,
        lanes,
        pre,
        back_low,
        mixer_all,
        [conv, recur, admit, state, entry],
        masks,
        table,
        gate_weights,
        [by_side(down_sum), by_side(gate_sum)],
    )
    branch_grads = by_rows(normed_one, grad_pre)

    def spots(value):
        blocks = [
            value[
                h * head_width : (h + 1) * head_width, h * head_width : (h + 1) * head_width
            ].reshape(shares, -1)
            for h in range(half_heads)
        ]
        return jnp.concatenate(blocks, axis=1)

    grad_decay = -jax.nn.sigmoid(-decay_flat) * grad_table[4, :lanes]
    grad_small = jnp.concatenate(
        [
            spots(grad_gates[:, :width]),
            spots(grad_gates[:, width:]),
            grad_table[:TAPS, :lanes]
            .reshape(TAPS * half_heads, shares, piece)
            .transpose(1, 0, 2)
            .reshape(shares, -1),
            grad_decay.reshape(half_heads, shares, piece).transpose(1, 0, 2).reshape(shares, -1),
        ],
        axis=1,
    )
    flat_size = grad_small.shape[1]
    spare = width - lanes
    grad_small = widen(grad_small, slim * spare).reshape(feature_count, spare).astype(BF16)
    last_grads = jnp.concatenate([outlet_grads[:, :lanes], grad_small, branch_grads], axis=1)
    grad_pre, last_grads = lax.optimization_barrier((grad_pre, last_grads))
    last_sum = line_sum(with_layout_constraint(last_grads, Layout(major_to_minor=(0, 1))))
    last_sum = with_layout_constraint(last_sum, Layout(major_to_minor=(0, 1)))
    input_grad, layer_output, gains, up_both = last_fold(
        count,
        grad_pre,
        branch_all,
        hidden,
        down_parts,
        layer_input,
        gain_first[None],
        grad_hidden_one,
        hidden_one,
        second_terms,
        [by_side(up_sum)],
    )
    first_gain_grad = lax.dynamic_index_in_dim(gains, mine, 0, False)
    second_gain_grad = lax.dynamic_index_in_dim(gains, shares + mine, 0, False)

    def swap(value):
        pair = by_side(value)
        kept = lax.dynamic_index_in_dim(pair, side, 0, False)
        given = lax.dynamic_index_in_dim(pair, 1 - side, 0, False)
        other = lax.ppermute(given, "dp", [(k, k ^ 1) for k in range(shares)])
        return [
            jnp.where(side == 0, kept, other).astype(F32),
            jnp.where(side == 0, other, kept).astype(F32),
        ]

    lasts, branches = swap(last_sum[:, :width]), swap(last_sum[:, width:])

    def columns(values, start, stop):
        return jnp.concatenate([value[:, start:stop] for value in values], axis=1)

    mixer_out_grad = columns(lasts, 0, lanes).T
    branch_gate_grad = columns(branches, 0, lanes)
    branch_input_grad = columns(branches, lanes, 2 * lanes)
    smalls = [value[:, lanes:width].reshape(-1)[:flat_size] for value in lasts]
    one = half_heads * piece * head_width
    tap_size = TAPS * half_heads * piece
    rate_grad = jnp.concatenate([v[:one].reshape(half_heads, piece, head_width) for v in smalls])
    inlet_grad = jnp.concatenate(
        [v[one : 2 * one].reshape(half_heads, piece, head_width) for v in smalls]
    )
    taps_grad = jnp.concatenate(
        [v[2 * one : 2 * one + tap_size].reshape(TAPS, half_heads, piece) for v in smalls], axis=1
    )
    decay_grad = jnp.concatenate(
        [v[2 * one + tap_size :].reshape(half_heads, piece) for v in smalls]
    )

    def joined(value):
        return jnp.concatenate([value[0], value[1]], axis=1).astype(F32)

    return (
        layer_output,
        input_grad,
        first_gain_grad,
        branch_gate_grad,
        branch_input_grad,
        taps_grad,
        rate_grad,
        inlet_grad,
        decay_grad,
        mixer_out_grad,
        second_gain_grad,
        joined(gate_both),
        joined(up_both),
        joined(down_both).T,
    )


def solution(mesh):
    placed = (
        P(("dp", "tensor"), None),
        P(("dp", "tensor"), None),
        P(),
        P("dp"),
        P("dp", "tensor"),
        P("dp", "tensor"),
        P(None, "tensor", "dp"),
        P("tensor", "dp", None),
        P("tensor", "dp", None),
        P("tensor", "dp"),
        P("tensor", "dp"),
        P("dp"),
        P("dp", "tensor"),
        P("dp", "tensor"),
        P("tensor", "dp"),
    )
    return jax.shard_map(
        shards,
        mesh=mesh,
        in_specs=placed,
        out_specs=(
            P(("dp", "tensor"), None),
            P(("dp", "tensor"), None),
            P("dp"),
            P("dp", "tensor"),
            P("dp", "tensor"),
            P(None, "tensor", "dp"),
            P("tensor", "dp", None),
            P("tensor", "dp", None),
            P("tensor", "dp"),
            P("tensor", "dp"),
            P("dp"),
            P("dp", "tensor"),
            P("dp", "tensor"),
            P("tensor", "dp"),
        ),
        check_vma=False,
    )
```
